32 devices in a mesh: group: 8 (over z, x), shard: 4 (over y, core).
Axes of the slice: x: 2, y: 2, z: 4, core: 2. Of those that a mesh axis runs over, the one named last changes fastest.
Arguments:
- tokens: bfloat16 [64, 1024], P(('group', 'shard')), may hold values from -6 to 6
- norm_gain: float32 [1024], replicated, may hold values from 0.5 to 1.5
- qkv_weight: bfloat16 [1024, 3072], P(None, 'shard'), may hold values from -0.1875 to 0.1875
- conv_weight: float32 [4, 3072], P(None, 'shard'), may hold values from -3 to 3
- conv_state: bfloat16 [64, 3, 3072], P('group', None, 'shard'), may hold values from -6 to 6
- mesa_gates: bfloat16 [1024, 16], replicated, may hold values from -0.1875 to 0.1875
- mesa_bias: float32 [16], replicated, may hold values from -3 to 3
- ridge_term: float32 [8], replicated, may hold values from 0.5 to 2
- key_cache: bfloat16 [128, 128, 1024], P(('group', 'shard')), may hold values from -1.25 to 1.25
- value_cache: bfloat16 [128, 128, 1024], P(('group', 'shard')), may hold values from -6 to 6
- log_weight: bfloat16 [128, 8, 128], P(('group', 'shard'))
- page_owner: int32 [128], P(('group', 'shard')), may hold values from 0 to 15, as said below
- page_fill: int32 [128], P(('group', 'shard')), may hold values from 1 to 128, as said below
- out_weight: bfloat16 [1024, 1024], P('shard'), may hold values from -0.1875 to 0.1875
- mlp_gain: float32 [1024], replicated, may hold values from 0.5 to 1.5
- gate_weight: bfloat16 [1024, 2816], P(None, 'shard'), may hold values from -0.1875 to 0.1875
- up_weight: bfloat16 [1024, 2816], P(None, 'shard'), may hold values from -0.1875 to 0.1875
- down_weight: bfloat16 [2816, 1024], P('shard'), may hold values from -0.109375 to 0.109375
Outputs:
- retrieved: bfloat16 [64, 1024], P(('group', 'shard'))
- layer_out: bfloat16 [64, 1024], P(('group', 'shard'))
The draws below stay inside these ranges and needn't reach their ends.
Inputs may be any that keep to these rules, and one draw needn't show every extreme that they name: `page_owner`: slots of a pair of groups (groups 2p and 2p + 1) belong to that pair's requests: 0 to 7 are group 2p's requests in row order, 8 to 15 group 2p + 1's. Every slot is owned, every request owns one or more slots, and a request's slots may lie on any device of either group of its pair. `page_fill`: tokens stored from the start of the slot; only a request's last page may be partly filled.
All inputs are finite; a program needn't handle non-finite values.
Results may differ from the reference program's by a relative error of at most 0.0085.
Values may be sent and summed in bfloat16 or wider, within the bound.
No kernel may reach another device: no remote copies, remote signals or barrier semaphores. Data moves between devices by JAX's collectives and lax.ppermute only.
A program may use at most 64 MiB of HBM per device.

```python
import math
import jax
import jax.numpy as jnp
from jax import lax

D = 1024
ATTENTION_COUNT = 8
DH = 128
FF = 2816
PAGE = 128
CONV = 4
ITERS = 4
COUPLED_QUERIES = 16
REQUESTS = 64
SLOTS_PAIR = 32
PAGES = 128
MOST = 8
N_GROUP = 8


def pair_layout(key):
    base_key = jax.random.fold_in(key, 101)
    spare_pages = SLOTS_PAIR - MOST - (COUPLED_QUERIES - 1)

    def one_pair(pair_index):
        pair_key = jax.random.fold_in(base_key, pair_index)
        sub_keys = jax.random.split(pair_key, 5)
        order = jax.random.permutation(sub_keys[0], COUPLED_QUERIES)
        longest = order[COUPLED_QUERIES - 1]
        others = order[:COUPLED_QUERIES - 1]
        upper = jax.random.randint(sub_keys[1], (spare_pages,), 1, COUPLED_QUERIES)
        picks = jax.random.randint(sub_keys[2], (spare_pages,), 0, upper)
        chosen = others[picks]
        members = jnp.arange(COUPLED_QUERIES)
        extra = jnp.sum((chosen[:, None] == members[None, :]).astype(jnp.int32), axis=0)
        counts = jnp.where(members == longest, MOST, 1 + extra).astype(jnp.int32)
        starts = jnp.cumsum(counts) - counts
        places = jnp.arange(SLOTS_PAIR)
        owner_seq = jnp.sum((starts[None, :] <= places[:, None]).astype(jnp.int32), axis=1) - 1
        rank_seq = places - starts[owner_seq]
        last_fill = jax.random.randint(sub_keys[3], (COUPLED_QUERIES,), 1, PAGE + 1)
        fill_seq = jnp.where(rank_seq == counts[owner_seq] - 1, last_fill[owner_seq], PAGE)
        overall_extent = (counts - 1) * PAGE + last_fill
        spots = jax.random.permutation(sub_keys[4], SLOTS_PAIR)
        inverse = jnp.argsort(spots)
        return (owner_seq[inverse].astype(jnp.int32), fill_seq[inverse].astype(jnp.int32), rank_seq[inverse].astype(jnp.int32), overall_extent.astype(jnp.int32))
    return jax.vmap(one_pair)(jnp.arange(N_GROUP // 2))


def draw_page_owner(key, part):
    holder_sequence, fill, rank, overall_extent = pair_layout(key)
    return holder_sequence.reshape(-1).astype(jnp.int32)


def draw_page_fill(key, part):
    holder_sequence, fill, rank, overall_extent = pair_layout(key)
    return fill.reshape(-1).astype(jnp.int32)


def draw_log_weight(key, part):
    holder_sequence, fill, rank, overall_extent = pair_layout(key)
    couple_number = N_GROUP // 2
    lookup_vectors_real = jax.random.split(jax.random.fold_in(key, 202), 4)
    rates = jnp.exp(jax.random.uniform(lookup_vectors_real[0], (couple_number, COUPLED_QUERIES, ATTENTION_COUNT), minval=math.log(0.0003), maxval=math.log(0.03)))
    keep_part = jax.random.uniform(lookup_vectors_real[1], (couple_number, SLOTS_PAIR, ATTENTION_COUNT, PAGE), minval=0.1, maxval=1.0)
    contiguous_spans = jax.random.randint(lookup_vectors_real[2], (couple_number, COUPLED_QUERIES, ATTENTION_COUNT, 3), 0, overall_extent[:, :, None, None])
    depths = jax.random.uniform(lookup_vectors_real[3], (couple_number, COUPLED_QUERIES, ATTENTION_COUNT, 3), minval=0.22, maxval=0.69)
    slot_rate = jnp.take_along_axis(rates, holder_sequence[:, :, None], axis=1)
    slot_total = jnp.take_along_axis(overall_extent, holder_sequence, axis=1)
    entry_contiguous_spans = jnp.take_along_axis(contiguous_spans, holder_sequence[:, :, None, None], axis=1)
    slot_depths = jnp.take_along_axis(depths, holder_sequence[:, :, None, None], axis=1)
    sequence_offset = rank[:, :, None] * PAGE + jnp.arange(PAGE)[None, None, :]
    distance = jnp.maximum(slot_total[:, :, None] - 1 - sequence_offset, 0).astype(jnp.float32)
    log_decay = -slot_rate[:, :, :, None] * distance[:, :, None, :]
    equality_indicator = (sequence_offset[:, :, None, :, None] < entry_contiguous_spans[:, :, :, None, :]).astype(jnp.float32)
    lost = jnp.sum(equality_indicator * slot_depths[:, :, :, None, :], axis=-1)
    values = jnp.log(keep_part) + log_decay - lost
    return values.reshape(couple_number * SLOTS_PAIR, ATTENTION_COUNT, PAGE).astype(jnp.bfloat16)


def block_scale(stream_key, dims, cuts, smallest, high):
    factor_of = 1.0
    for position, parts in cuts:
        steps = jax.random.uniform(jax.random.fold_in(jax.random.fold_in(stream_key, 6), position), (parts,), jnp.float32, smallest / len(cuts), high / len(cuts))
        factor_of = factor_of * jnp.repeat(jnp.exp(steps), dims[position] // parts).reshape((-1,) + (1,) * (len(dims) - 1 - position))
    return factor_of


def scatter_about(stream_key, dims, scale, bound, pieces=(), held_as=jnp.bfloat16):
    level = block_scale(stream_key, dims, pieces, -0.22, 0.18) if pieces else 1.0
    values = jax.random.normal(stream_key, dims, jnp.float32) * scale * level
    return jnp.minimum(jnp.maximum(values, -bound), bound).astype(held_as)


def setup_inputs(seed: int = 0) -> dict:
    splits = jax.random.split(jax.random.key(seed), 19)
    tokens = scatter_about(splits[0], (REQUESTS, D), 1.0, 6.0, ((0, 32),))
    norm_gain = jnp.clip(1.0 + 0.1 * jax.random.normal(splits[1], (D,), jnp.float32), 0.5, 1.5)
    qkv_weight = scatter_about(splits[2], (D, 3 * ATTENTION_COUNT * DH), D ** -0.5, 0.1875, ((1, 4),))
    conv_weight = scatter_about(splits[3], (CONV, 3 * ATTENTION_COUNT * DH), 0.5, 3.0, ((1, 4),), jnp.float32)
    conv_state = scatter_about(splits[4], (REQUESTS, CONV - 1, 3 * ATTENTION_COUNT * DH), 1.0, 6.0, ((0, 8), (2, 4)))
    mesa_gates = scatter_about(splits[5], (D, 2 * ATTENTION_COUNT), D ** -0.5, 0.1875)
    mesa_bias = scatter_about(splits[6], (2 * ATTENTION_COUNT,), 1.0, 3.0, (), jnp.float32)
    ridge_term = jnp.clip(jnp.exp(jax.random.uniform(splits[7], (ATTENTION_COUNT,), jnp.float32, math.log(0.5), math.log(2.0))), 0.5, 2.0)
    key_cache = scatter_about(splits[8], (PAGES, PAGE, ATTENTION_COUNT * DH), (DH ** -0.5), 1.25, ((0, 32),))
    value_cache = scatter_about(splits[9], (PAGES, PAGE, ATTENTION_COUNT * DH), 1.0, 6.0, ((0, 32),))
    log_weight = draw_log_weight(jax.random.fold_in(splits[18], 71), 0)
    page_owner = draw_page_owner(jax.random.fold_in(splits[18], 71), 0)
    page_fill = draw_page_fill(jax.random.fold_in(splits[18], 71), 0)
    out_weight = scatter_about(splits[13], (ATTENTION_COUNT * DH, D), (ATTENTION_COUNT * DH) ** -0.5, 0.1875, ((0, 4),))
    mlp_gain = jnp.clip(1.0 + 0.1 * jax.random.normal(splits[14], (D,), jnp.float32), 0.5, 1.5)
    gate_weight = scatter_about(splits[15], (D, FF), D ** -0.5, 0.1875, ((1, 4),))
    up_weight = scatter_about(splits[16], (D, FF), D ** -0.5, 0.1875, ((1, 4),))
    down_weight = scatter_about(splits[17], (FF, D), FF ** -0.5, 0.109375, ((0, 4),))
    return dict(tokens=tokens, norm_gain=norm_gain, qkv_weight=qkv_weight, conv_weight=conv_weight, conv_state=conv_state, mesa_gates=mesa_gates, mesa_bias=mesa_bias, ridge_term=ridge_term, key_cache=key_cache, value_cache=value_cache, log_weight=log_weight, page_owner=page_owner, page_fill=page_fill, out_weight=out_weight, mlp_gain=mlp_gain, gate_weight=gate_weight, up_weight=up_weight, down_weight=down_weight)


precise = lax.Precision.HIGHEST

def scaled_norm(row_vals, gain_vec):
    wide_rows = row_vals.astype(jnp.float32)
    factor = lax.rsqrt(lax.optimization_barrier(jnp.mean(wide_rows * wide_rows, axis=-1, keepdims=True)) + 1e-05)
    return (wide_rows * factor * gain_vec).astype(jnp.bfloat16)

def unit_rows(vectors):
    return vectors * lax.rsqrt(lax.optimization_barrier(jnp.sum(vectors * vectors, axis=-1, keepdims=True)) + 1e-06)

def slot_weights(owner_hot, decay_rows, log_weight, page_fill):
    page_len = log_weight.shape[2]
    slot_decay = jnp.dot(owner_hot, decay_rows, precision=precise)
    live_mask = (jnp.arange(page_len)[None, :] < page_fill[:, None]).astype(jnp.float32)
    return slot_decay[:, :, None] * jnp.exp(log_weight.astype(jnp.float32)) * live_mask[:, None, :]

def slot_terms(key_rows, source_rows, owner_hot, slot_weight, directions):
    slot_count, page_len, width_all = key_rows.shape
    head_count = slot_weight.shape[1]
    head_size = width_all // head_count
    member_count = owner_hot.shape[1]
    slot_dir = jnp.dot(owner_hot, directions.reshape(member_count, width_all), precision=precise)
    slot_dir = slot_dir.reshape(slot_count, head_count, head_size)
    key_wide = key_rows.astype(jnp.float32).reshape(slot_count, page_len, head_count, head_size)
    scores = jnp.einsum('sthd,shd->sht', key_wide, slot_dir, precision=precise)
    source_wide = source_rows.astype(jnp.float32).reshape(slot_count, page_len, head_count, head_size)
    contribution = jnp.einsum('sht,sthd->shd', slot_weight * scores, source_wide, precision=precise)
    summed = jnp.dot(owner_hot.T, contribution.reshape(slot_count, width_all), precision=precise)
    return summed.reshape(member_count, head_count, head_size)

def new_term(vectors, source_rows, strength_rows, key_new):
    return strength_rows[:, :, None] * source_rows * lax.optimization_barrier(jnp.sum(key_new * vectors, axis=-1, keepdims=True))

def conjugate(query_rows, key_new, value_new, strength_rows, ridge_term, reduce_fn):
    solution = jnp.zeros_like(query_rows)
    residual = query_rows
    direction = query_rows
    res_norm = lax.optimization_barrier(jnp.sum(residual * residual, axis=-1))
    for iteration in range(ITERS):
        image_vec = reduce_fn(direction, False) + new_term(direction, key_new, strength_rows, key_new) + ridge_term[None, :, None] * direction
        step_size = res_norm / lax.optimization_barrier(jnp.sum(direction * image_vec, axis=-1))
        solution = solution + step_size[:, :, None] * direction
        residual = residual - step_size[:, :, None] * image_vec
        next_norm = lax.optimization_barrier(jnp.sum(residual * residual, axis=-1))
        direction = residual + (next_norm / res_norm)[:, :, None] * direction
        res_norm = next_norm
    return reduce_fn(solution, True) + new_term(solution, value_new, strength_rows, key_new)

def reference(tokens, norm_gain, qkv_weight, conv_weight, conv_state, mesa_gates, mesa_bias, ridge_term, key_cache, value_cache, log_weight, page_owner, page_fill, out_weight, mlp_gain, gate_weight, up_weight, down_weight):
    row_count = tokens.shape[0]
    normed = scaled_norm(tokens, norm_gain)
    fresh_proj = jnp.dot(normed, qkv_weight, preferred_element_type=jnp.float32)
    past_rows = conv_state.astype(jnp.float32)
    pre_conv = conv_weight[3] * fresh_proj + conv_weight[0] * past_rows[:, 0] + conv_weight[1] * past_rows[:, 1] + conv_weight[2] * past_rows[:, 2]
    mixed_rows = jax.nn.silu(pre_conv).astype(jnp.bfloat16)
    split_rows = mixed_rows.astype(jnp.float32).reshape(row_count, 3, ATTENTION_COUNT, DH)
    query_rows = unit_rows(split_rows[:, 0])
    key_new = unit_rows(split_rows[:, 1])
    value_new = split_rows[:, 2]
    gate_vals = jax.nn.sigmoid(jnp.dot(normed, mesa_gates, preferred_element_type=jnp.float32) + mesa_bias)
    decay_rows = gate_vals[:, :ATTENTION_COUNT]
    strength_rows = gate_vals[:, ATTENTION_COUNT:]
    couple_number = N_GROUP // 2

    def per_pair(block):
        query_pair, key_pair, value_pair, decay_pair, strength_pair, keys_pair, values_pair, logw_pair, owner_pair, fill_pair = block
        owner_hot = (owner_pair[:, None] == jnp.arange(COUPLED_QUERIES)[None, :]).astype(jnp.float32)
        weights_pair = slot_weights(owner_hot, decay_pair, logw_pair, fill_pair)

        def reduce_fn(vectors, with_values):
            source_rows = values_pair if with_values else keys_pair
            return slot_terms(keys_pair, source_rows, owner_hot, weights_pair, vectors)
        return conjugate(query_pair, key_pair, value_pair, strength_pair, ridge_term, reduce_fn)
    blocks = (query_rows.reshape(couple_number, COUPLED_QUERIES, ATTENTION_COUNT, DH), key_new.reshape(couple_number, COUPLED_QUERIES, ATTENTION_COUNT, DH), value_new.reshape(couple_number, COUPLED_QUERIES, ATTENTION_COUNT, DH), decay_rows.reshape(couple_number, COUPLED_QUERIES, ATTENTION_COUNT), strength_rows.reshape(couple_number, COUPLED_QUERIES, ATTENTION_COUNT), key_cache.reshape(couple_number, SLOTS_PAIR, PAGE, ATTENTION_COUNT * DH), value_cache.reshape(couple_number, SLOTS_PAIR, PAGE, ATTENTION_COUNT * DH), log_weight.reshape(couple_number, SLOTS_PAIR, ATTENTION_COUNT, PAGE), page_owner.reshape(couple_number, SLOTS_PAIR), page_fill.reshape(couple_number, SLOTS_PAIR))
    found = lax.map(per_pair, blocks)
    retrieved = found.reshape(row_count, ATTENTION_COUNT * DH).astype(jnp.bfloat16)
    attended = jnp.dot(retrieved, out_weight, preferred_element_type=jnp.float32)
    mid_rows = (tokens.astype(jnp.float32) + attended).astype(jnp.bfloat16)
    mlp_in = scaled_norm(mid_rows, mlp_gain)
    gate_part = jnp.dot(mlp_in, gate_weight, preferred_element_type=jnp.float32)
    up_part = jnp.dot(mlp_in, up_weight, preferred_element_type=jnp.float32)
    hidden_rows = (jax.nn.silu(gate_part) * up_part).astype(jnp.bfloat16)
    down_part = jnp.dot(hidden_rows, down_weight, preferred_element_type=jnp.float32)
    layer_out = (mid_rows.astype(jnp.float32) + down_part).astype(jnp.bfloat16)
    return (retrieved, layer_out)
```

```python
import functools

import jax
import jax.numpy as jnp
from jax import lax
from jax.experimental import pallas as pl
from jax.experimental.pallas import tpu as pltpu
from jax.sharding import Mesh
from jax.sharding import PartitionSpec as P

ITERS = 4


precise = lax.Precision.HIGHEST

VMEM = pl.BlockSpec(memory_space=pltpu.VMEM)
SMEM = pl.BlockSpec(memory_space=pltpu.SMEM)


def partner(value, axis, apart):
    mask = 2**apart
    pairs = [(source, source ^ mask) for source in range(lax.axis_size(axis))]
    return lax.ppermute(value, axis, pairs)


def scaled_norm(row_vals, gain_vec):
    wide_rows = row_vals.astype(jnp.float32)
    factor = lax.rsqrt(jnp.mean(wide_rows * wide_rows, axis=-1, keepdims=True) + 1e-05)
    return (wide_rows * factor * gain_vec).astype(jnp.bfloat16)


def unit_rows(vectors):
    return vectors * lax.rsqrt(jnp.sum(vectors * vectors, axis=-1, keepdims=True) + 1e-06)


def slot_weights(owner_hot, decay_rows, log_weight, page_fill):
    page_len = log_weight.shape[2]
    slot_decay = jnp.dot(owner_hot, decay_rows, precision=precise)
    live_mask = (jnp.arange(page_len)[None, :] < page_fill[:, None]).astype(jnp.float32)
    return slot_decay[:, :, None] * jnp.exp(log_weight.astype(jnp.float32)) * live_mask[:, None, :]


def slot_terms(key_rows, source_rows, owner_hot, slot_weight, directions):
    slot_count, page_len, width_all = key_rows.shape
    head_count = slot_weight.shape[1]
    head_size = width_all // head_count
    member_count = owner_hot.shape[1]
    slot_dir = jnp.dot(owner_hot, directions.reshape(member_count, width_all), precision=precise)
    slot_dir = slot_dir.reshape(slot_count, head_count, head_size)
    key_wide = key_rows.astype(jnp.float32).reshape(slot_count, page_len, head_count, head_size)
    scores = jnp.einsum("sthd,shd->sht", key_wide, slot_dir, precision=precise)
    source_wide = source_rows.astype(jnp.float32).reshape(
        slot_count, page_len, head_count, head_size
    )
    contribution = jnp.einsum("sht,sthd->shd", slot_weight * scores, source_wide, precision=precise)
    summed = jnp.dot(owner_hot.T, contribution.reshape(slot_count, width_all), precision=precise)
    return summed.reshape(member_count, head_count, head_size)


def new_term(vectors, source_rows, strength_rows, key_new):
    return (
        strength_rows[:, :, None] * source_rows * jnp.sum(key_new * vectors, axis=-1, keepdims=True)
    )


def conjugate(query_rows, key_new, value_new, strength_rows, ridge_term, reduce_fn):
    solution = jnp.zeros_like(query_rows)
    residual = query_rows
    direction = query_rows
    res_norm = jnp.sum(residual * residual, axis=-1)
    for iteration in range(ITERS):
        image_vec = (
            reduce_fn(direction, False)
            + new_term(direction, key_new, strength_rows, key_new)
            + ridge_term[None, :, None] * direction
        )
        step_size = res_norm / jnp.sum(direction * image_vec, axis=-1)
        solution = solution + step_size[:, :, None] * direction
        residual = residual - step_size[:, :, None] * image_vec
        next_norm = jnp.sum(residual * residual, axis=-1)
        direction = residual + (next_norm / res_norm)[:, :, None] * direction
        res_norm = next_norm
    return reduce_fn(solution, True) + new_term(solution, value_new, strength_rows, key_new)


def pair_order(mine, theirs, parity):
    first = jnp.where(parity == 0, mine, theirs)
    second = jnp.where(parity == 0, theirs, mine)
    return jnp.concatenate([first, second], axis=0)


def spread_body(
    tokens,
    norm_gain,
    qkv_weight,
    conv_weight,
    conv_state,
    mesa_gates,
    mesa_bias,
    ridge_term,
    key_cache,
    value_cache,
    log_weight,
    page_owner,
    page_fill,
    out_weight,
    mlp_gain,
    gate_weight,
    up_weight,
    down_weight,
):
    req_rows = tokens.shape[0]
    group_rows = req_rows * lax.axis_size("shard")
    head_count = ridge_term.shape[0]
    width_all = key_cache.shape[2]
    head_size = width_all // head_count
    parity = lax.axis_index("group") % 2
    normed = scaled_norm(tokens, norm_gain)
    fresh_proj = jnp.dot(
        lax.all_gather(normed, "shard", axis=0, tiled=True),
        qkv_weight,
        preferred_element_type=jnp.float32,
    )
    past_rows = conv_state.astype(jnp.float32)
    pre_conv = (
        conv_weight[3] * fresh_proj
        + conv_weight[0] * past_rows[:, 0]
        + conv_weight[1] * past_rows[:, 1]
        + conv_weight[2] * past_rows[:, 2]
    )
    mixed_cols = jax.nn.silu(pre_conv).astype(jnp.bfloat16)
    home_rows = lax.all_to_all(mixed_cols, "shard", split_axis=0, concat_axis=1, tiled=True)
    split_rows = home_rows.astype(jnp.float32).reshape(req_rows, 3, head_count, head_size)
    query_home = unit_rows(split_rows[:, 0])
    key_home = unit_rows(split_rows[:, 1])
    value_home = split_rows[:, 2]
    gate_vals = jax.nn.sigmoid(
        jnp.dot(normed, mesa_gates, preferred_element_type=jnp.float32) + mesa_bias
    )
    decay_home = gate_vals[:, :head_count]
    strength_home = gate_vals[:, head_count:]
    owner_hot = (page_owner[:, None] == jnp.arange(2 * group_rows)[None, :]).astype(jnp.float32)
    stored = {}

    def cache_pass(directions, decay_grp, with_values):
        far_dirs, far_decay = partner((directions, decay_grp), "group", 0)
        pair_dirs = pair_order(directions, far_dirs, parity)
        pair_decay = pair_order(decay_grp, far_decay, parity)
        if "weight" not in stored:
            stored["weight"] = slot_weights(owner_hot, pair_decay, log_weight, page_fill)
        source_rows = value_cache if with_values else key_cache
        summed = slot_terms(key_cache, source_rows, owner_hot, stored["weight"], pair_dirs)
        mine = jnp.where(parity == 0, summed[:group_rows], summed[group_rows:])
        theirs = jnp.where(parity == 0, summed[group_rows:], summed[:group_rows])
        returned = partner(theirs, "group", 0)
        return mine + returned

    def reduce_home(vectors, with_values):
        directions, decay_grp = (
            lax.all_gather(vectors, "shard", axis=0, tiled=True),
            lax.all_gather(decay_home, "shard", axis=0, tiled=True),
        )
        return lax.psum_scatter(
            cache_pass(directions, decay_grp, with_values), "shard", scatter_dimension=0, tiled=True
        )

    found = conjugate(query_home, key_home, value_home, strength_home, ridge_term, reduce_home)
    retrieved = found.reshape(req_rows, width_all).astype(jnp.bfloat16)
    columns = lax.all_to_all(retrieved, "shard", split_axis=1, concat_axis=0, tiled=True)
    attended = lax.psum_scatter(
        jnp.dot(columns, out_weight, preferred_element_type=jnp.float32),
        "shard",
        scatter_dimension=0,
        tiled=True,
    )
    mid_rows = (tokens.astype(jnp.float32) + attended).astype(jnp.bfloat16)
    mlp_in = scaled_norm(mid_rows, mlp_gain)
    piece_rows = lax.all_gather(mlp_in, "shard", axis=0, tiled=True)
    gate_part = jnp.dot(piece_rows, gate_weight, preferred_element_type=jnp.float32)
    up_part = jnp.dot(piece_rows, up_weight, preferred_element_type=jnp.float32)
    hidden_rows = (jax.nn.silu(gate_part) * up_part).astype(jnp.bfloat16)
    down_part = lax.psum_scatter(
        jnp.dot(hidden_rows, down_weight, preferred_element_type=jnp.float32),
        "shard",
        scatter_dimension=0,
        tiled=True,
    )
    layer_out = (mid_rows.astype(jnp.float32) + down_part).astype(jnp.bfloat16)
    return (retrieved, layer_out)


PACK = 8
MASKED = -1e38


def split_pair(value):
    high = value.astype(jnp.bfloat16)
    low = (value - high.astype(jnp.float32)).astype(jnp.bfloat16)
    return high, low


def hot(rows, columns, target_fn):
    row = lax.broadcasted_iota(jnp.int32, (rows, columns), 0)
    column = lax.broadcasted_iota(jnp.int32, (rows, columns), 1)
    return column == target_fn(row)


def project_kernel(
    shards,
    req_rows,
    slots,
    head_count,
    head_size,
    place_ref,
    pack_ref,
    gain_ref,
    qkv_ref,
    tap_ref,
    past_ref,
    gates_ref,
    bias_ref,
    mixed_ref,
    tokens_ref,
    weight_ref,
    strength_ref,
):
    shard = place_ref[0]
    member = place_ref[1]
    head = shard * 2 + member
    group_rows = shards * req_rows
    pair_rows = 2 * group_rows
    packed = 2 * shards * PACK

    def home_of(row):
        x = row // group_rows
        s = (row % group_rows) // req_rows
        return (s * 2 + x) * PACK + row % req_rows

    one = jnp.ones((), jnp.bfloat16)
    zero = jnp.zeros((), jnp.bfloat16)
    pick_pair = jnp.where(hot(pair_rows, packed, home_of), one, zero)
    pick_group = jnp.where(
        hot(group_rows, packed, lambda row: home_of(row + member * group_rows)), one, zero
    )
    pair_tokens = jnp.dot(pick_pair, pack_ref[...], preferred_element_type=jnp.float32)
    own_tokens = jnp.dot(pick_group, pack_ref[...], preferred_element_type=jnp.float32)
    tokens_ref[...] = own_tokens
    normed = scaled_norm(pair_tokens, gain_ref[...])
    own = scaled_norm(own_tokens, gain_ref[...])
    fresh = jnp.dot(own, qkv_ref[...], preferred_element_type=jnp.float32)
    before = tap_ref[3:4, :] * fresh + past_ref[...]
    mixed_ref[...] = (before / (1.0 + jnp.exp(-before))).astype(jnp.bfloat16)

    raw = jnp.dot(normed, gates_ref[...], preferred_element_type=jnp.float32) + bias_ref[...]
    gate_vals = 1.0 / (1.0 + jnp.exp(-raw))
    column = lax.broadcasted_iota(jnp.int32, gate_vals.shape, 1)
    decay = jnp.sum(jnp.where(column == head, gate_vals, 0.0), axis=1, keepdims=True)
    strength = jnp.sum(
        jnp.where(column == head + head_count, gate_vals, 0.0), axis=1, keepdims=True
    )
    strength_ref[...] = jnp.broadcast_to(strength, strength_ref.shape)

    all_slots = 2 * shards * slots
    mine = pack_ref[:, pl.ds(pl.multiple_of(head * head_size, head_size), head_size)]
    pick_slot = hot(
        all_slots, packed, lambda row: (row // slots) * PACK + req_rows + row % slots
    )
    logs = jnp.dot(jnp.where(pick_slot, one, zero), mine, preferred_element_type=jnp.float32)
    pick_owner = hot(all_slots, packed, lambda row: (row // slots) * PACK + req_rows + slots)
    owners = jnp.dot(jnp.where(pick_owner, one, zero), mine, preferred_element_type=jnp.float32)
    at_slot = hot(all_slots, head_size, lambda row: row % slots)
    owner = jnp.sum(jnp.where(at_slot, owners, 0.0), axis=1, keepdims=True).astype(jnp.int32)
    request = lax.broadcasted_iota(jnp.int32, (all_slots, pair_rows), 1)
    owner_hot = jnp.where(request == owner, 1.0, 0.0)
    wide_decay = jnp.broadcast_to(decay, (pair_rows, head_size))
    slot_decay = jnp.dot(
        owner_hot, wide_decay, precision=precise, preferred_element_type=jnp.float32
    )
    weight_ref[...] = slot_decay * jnp.exp(logs)


def solve_kernel(
    shards,
    head_count,
    place_ref,
    owner_ref,
    ridge_ref,
    mixed_ref,
    key_ref,
    weight_ref,
    strength_ref,
    high_ref,
    low_ref,
    term_ref,
    gram_ref,
):
    shard = place_ref[0]
    member = place_ref[1]
    head = shard * 2 + member
    all_slots, page, head_size = key_ref.shape
    pair_rows = strength_ref.shape[0]
    blocks = mixed_ref.shape[1] // head_size

    gram_ref[...] = jnp.zeros_like(gram_ref)
    for slot in range(all_slots):
        keys = key_ref[slot]
        turned = keys.T.astype(jnp.float32) * weight_ref[slot : slot + 1, :]
        high, low = split_pair(turned)
        piece = jnp.dot(high, keys, preferred_element_type=jnp.float32) + jnp.dot(
            low, keys, preferred_element_type=jnp.float32
        )
        owner = owner_ref[slot]
        gram_ref[owner] = gram_ref[owner] + piece

    def columns_of(block):
        source = block // blocks
        start = pl.multiple_of((block % blocks) * head_size, head_size)
        first = pl.multiple_of(source * pair_rows, pair_rows)
        return mixed_ref[pl.ds(first, pair_rows), pl.ds(start, head_size)].astype(jnp.float32)

    query = unit_rows(columns_of(head))
    key_new = unit_rows(columns_of(head + head_count))
    value_new = columns_of(head + 2 * head_count)
    strength = strength_ref[...]
    ridge = ridge_ref[head]

    def image_of(vectors):
        turned = vectors.T
        pieces = []
        for row in range(pair_rows):
            spread = jnp.broadcast_to(turned[:, row : row + 1], (head_size, head_size))
            pieces.append(jnp.sum(gram_ref[row] * spread, axis=0, keepdims=True))
        return jnp.concatenate(pieces, axis=0)

    found = jnp.zeros_like(query)
    residual = query
    direction = query
    res_norm = jnp.sum(residual * residual, axis=-1, keepdims=True)
    for iteration in range(ITERS):
        along = jnp.sum(key_new * direction, axis=-1, keepdims=True)
        image = image_of(direction) + strength * key_new * along + ridge * direction
        step = res_norm / jnp.sum(direction * image, axis=-1, keepdims=True)
        found = found + step * direction
        residual = residual - step * image
        next_norm = jnp.sum(residual * residual, axis=-1, keepdims=True)
        direction = residual + (next_norm / res_norm) * direction
        res_norm = next_norm

    term_ref[...] = strength * value_new * jnp.sum(key_new * found, axis=-1, keepdims=True)
    high, low = split_pair(found)
    third = (found - high.astype(jnp.float32) - low.astype(jnp.float32)).astype(jnp.bfloat16)
    stacked = jnp.concatenate([high, low, third], axis=0)
    request = lax.broadcasted_iota(jnp.int32, (pair_rows, page), 0)
    for slot in range(all_slots):
        scores = lax.dot_general(
            stacked, key_ref[slot], (((1,), (1,)), ((), ())), preferred_element_type=jnp.float32
        )
        scores = (
            scores[:pair_rows] + scores[pair_rows : 2 * pair_rows] + scores[2 * pair_rows :]
        )
        kept = jnp.where(request == owner_ref[slot], scores * weight_ref[slot : slot + 1, :], 0.0)
        high, low = split_pair(kept)
        high_ref[:, slot * page : (slot + 1) * page] = high
        low_ref[:, slot * page : (slot + 1) * page] = low


def read_kernel(place_ref, high_ref, low_ref, term_ref, value_ref, out_ref, send_ref):
    member = place_ref[1]
    head_size = term_ref.shape[1]
    width = out_ref.shape[1]
    both = jnp.concatenate([high_ref[...], low_ref[...]], axis=0)
    summed = jnp.dot(both, value_ref[...], preferred_element_type=jnp.float32)
    rows = term_ref.shape[0]
    retrieved = (summed[:rows] + summed[rows:] + term_ref[...]).astype(jnp.bfloat16)
    start = pl.multiple_of(member * head_size, head_size)
    part = jnp.dot(
        retrieved, out_ref[pl.ds(start, head_size), :], preferred_element_type=jnp.float32
    )
    send_ref[:, :width] = part.astype(jnp.bfloat16)
    send_ref[:, width:] = retrieved


def mlp_kernel(
    place_ref, part_ref, tokens_ref, gain_ref, gate_ref, up_ref, down_ref, mid_ref, send_ref
):
    member = place_ref[1]
    devices = part_ref.shape[0]
    group_rows, width = tokens_ref.shape
    first = pl.multiple_of(member * group_rows, group_rows)
    total = tokens_ref[...]
    attended = part_ref[0, pl.ds(first, group_rows), :width].astype(jnp.float32)
    for source in range(1, devices):
        attended += part_ref[source, pl.ds(first, group_rows), :width].astype(jnp.float32)
    mid_rows = (total + attended).astype(jnp.bfloat16)
    mid_ref[...] = mid_rows
    mlp_in = scaled_norm(mid_rows, gain_ref[...])
    gate_part = jnp.dot(mlp_in, gate_ref[...], preferred_element_type=jnp.float32)
    up_part = jnp.dot(mlp_in, up_ref[...], preferred_element_type=jnp.float32)
    hidden = (gate_part / (1.0 + jnp.exp(-gate_part)) * up_part).astype(jnp.bfloat16)
    send_ref[...] = jnp.dot(hidden, down_ref[...], preferred_element_type=jnp.float32)


def head_body(
    tokens,
    norm_gain,
    qkv_weight,
    conv_weight,
    conv_state,
    mesa_gates,
    mesa_bias,
    ridge_term,
    key_cache,
    value_cache,
    log_weight,
    page_owner,
    page_fill,
    out_weight,
    mlp_gain,
    gate_weight,
    up_weight,
    down_weight,
):
    pair = ("shard", "member")
    shards = lax.axis_size("shard")
    shard = lax.axis_index("shard")
    member = lax.axis_index("member")
    req_rows, width = tokens.shape
    slots, page, _ = key_cache.shape
    head_count = ridge_term.shape[0]
    head_size = width // head_count
    group_rows = shards * req_rows
    pair_rows = 2 * group_rows
    all_slots = 2 * shards * slots
    columns = qkv_weight.shape[1]
    place = jnp.stack([shard, member]).astype(jnp.int32)

    live = jnp.arange(page)[None, None, :] < page_fill[:, None, None]
    masked = jnp.where(live, log_weight, jnp.asarray(MASKED, jnp.bfloat16)).reshape(slots, width)
    owner_row = jnp.tile(
        jnp.pad(page_owner.astype(jnp.bfloat16), (0, head_size - slots)), head_count
    )
    pack = jnp.concatenate(
        [
            tokens,
            masked,
            owner_row[None, :],
            jnp.zeros((PACK - req_rows - slots - 1, width), jnp.bfloat16),
        ],
        axis=0,
    )
    packs = lax.all_gather(pack, pair, axis=0, tiled=True)
    keys = lax.all_to_all(key_cache, pair, split_axis=2, concat_axis=0, tiled=True)
    values = lax.all_to_all(value_cache, pair, split_axis=2, concat_axis=0, tiled=True)

    past = conv_state.astype(jnp.float32)
    past = conv_weight[0] * past[:, 0] + conv_weight[1] * past[:, 1] + conv_weight[2] * past[:, 2]

    mixed, own_tokens, weight, strength = pl.pallas_call(
        functools.partial(project_kernel, shards, req_rows, slots, head_count, head_size),
        out_shape=(
            jax.ShapeDtypeStruct((group_rows, columns), jnp.bfloat16),
            jax.ShapeDtypeStruct((group_rows, width), jnp.float32),
            jax.ShapeDtypeStruct((all_slots, page), jnp.float32),
            jax.ShapeDtypeStruct((pair_rows, head_size), jnp.float32),
        ),
        in_specs=[SMEM] + [VMEM] * 7,
        out_specs=(VMEM,) * 4,
        name="project",
    )(
        place,
        packs,
        norm_gain[None, :],
        qkv_weight,
        conv_weight,
        past,
        mesa_gates,
        mesa_bias[None, :],
    )
    all_mixed = lax.all_gather(mixed, pair, axis=0, tiled=True)
    owners = packs.reshape(2 * shards, PACK, width)[:, req_rows + slots, :slots]
    owners = owners.reshape(all_slots).astype(jnp.int32)

    high, low, term = pl.pallas_call(
        functools.partial(solve_kernel, shards, head_count),
        out_shape=(
            jax.ShapeDtypeStruct((pair_rows, all_slots * page), jnp.bfloat16),
            jax.ShapeDtypeStruct((pair_rows, all_slots * page), jnp.bfloat16),
            jax.ShapeDtypeStruct((pair_rows, head_size), jnp.float32),
        ),
        in_specs=[SMEM] * 3 + [VMEM] * 4,
        out_specs=(VMEM,) * 3,
        scratch_shapes=[pltpu.VMEM((pair_rows, head_size, head_size), jnp.float32)],
        name="solve",
    )(place, owners, ridge_term, all_mixed, keys, weight, strength)

    parts = pl.pallas_call(
        read_kernel,
        out_shape=jax.ShapeDtypeStruct((pair_rows, width + head_size), jnp.bfloat16),
        in_specs=[SMEM] + [VMEM] * 5,
        out_specs=VMEM,
        name="read",
    )(place, high, low, term, values.reshape(all_slots * page, head_size), out_weight)
    all_parts = lax.all_gather(parts, pair, axis=0, tiled=False)

    mid_rows, down_part = pl.pallas_call(
        mlp_kernel,
        out_shape=(
            jax.ShapeDtypeStruct((group_rows, width), jnp.bfloat16),
            jax.ShapeDtypeStruct((group_rows, width), jnp.float32),
        ),
        in_specs=[SMEM] + [VMEM] * 6,
        out_specs=(VMEM,) * 2,
        name="mlp",
    )(
        place,
        all_parts,
        own_tokens,
        mlp_gain[None, :],
        gate_weight,
        up_weight,
        down_weight,
    )
    arrived = lax.all_to_all(down_part, "shard", split_axis=0, concat_axis=0, tiled=True)
    total = jnp.sum(arrived.reshape(shards, req_rows, width), axis=0)
    mid_home = lax.dynamic_slice_in_dim(mid_rows, shard * req_rows, req_rows, axis=0)
    layer_out = (mid_home.astype(jnp.float32) + total).astype(jnp.bfloat16)

    first = member * group_rows + shard * req_rows
    heads = lax.dynamic_slice(
        all_parts, (0, first, width), (2 * shards, req_rows, head_size)
    )
    retrieved = jnp.transpose(heads, (1, 0, 2)).reshape(req_rows, width)
    return (retrieved, layer_out)


def specs(group):
    rows = P((*group, "shard"))
    return (
        (
            rows,
            P(),
            P(None, "shard"),
            P(None, "shard"),
            P(group, None, "shard"),
            P(),
            P(),
            P(),
            rows,
            rows,
            rows,
            rows,
            rows,
            P("shard", None),
            P(),
            P(None, "shard"),
            P(None, "shard"),
            P("shard", None),
        ),
        (rows, rows),
    )


def solution(mesh):
    groups, shards = mesh.devices.shape

    def run(*args):
        head_count = args[7].shape[0]
        if 2 * shards == head_count:
            axes = ("pair", "member", "shard")
            used = Mesh(mesh.devices.reshape(groups // 2, 2, shards), axes)
            body, group = head_body, ("pair", "member")
        else:
            used, body, group = mesh, spread_body, ("group",)
        in_specs, out_specs = specs(group)
        return jax.shard_map(
            body, mesh=used, in_specs=in_specs, out_specs=out_specs, check_vma=False
        )(*args)

    return run
```

```python
import functools

import jax
import jax.numpy as jnp
from jax import lax
from jax.experimental import pallas as pl
from jax.experimental.pallas import tpu as pltpu
from jax.sharding import Mesh
from jax.sharding import PartitionSpec as P

ITERS = 4


precise = lax.Precision.HIGHEST

VMEM = pl.BlockSpec(memory_space=pltpu.VMEM)
SMEM = pl.BlockSpec(memory_space=pltpu.SMEM)


def partner(value, axis, apart):
    mask = 2**apart
    pairs = [(source, source ^ mask) for source in range(lax.axis_size(axis))]
    return lax.ppermute(value, axis, pairs)


def scaled_norm(row_vals, gain_vec):
    wide_rows = row_vals.astype(jnp.float32)
    factor = lax.rsqrt(jnp.mean(wide_rows * wide_rows, axis=-1, keepdims=True) + 1e-05)
    return (wide_rows * factor * gain_vec).astype(jnp.bfloat16)


def unit_rows(vectors):
    return vectors * lax.rsqrt(jnp.sum(vectors * vectors, axis=-1, keepdims=True) + 1e-06)


def slot_weights(owner_hot, decay_rows, log_weight, page_fill):
    page_len = log_weight.shape[2]
    slot_decay = jnp.dot(owner_hot, decay_rows, precision=precise)
    live_mask = (jnp.arange(page_len)[None, :] < page_fill[:, None]).astype(jnp.float32)
    return slot_decay[:, :, None] * jnp.exp(log_weight.astype(jnp.float32)) * live_mask[:, None, :]


def slot_terms(key_rows, source_rows, owner_hot, slot_weight, directions):
    slot_count, page_len, width_all = key_rows.shape
    head_count = slot_weight.shape[1]
    head_size = width_all // head_count
    member_count = owner_hot.shape[1]
    slot_dir = jnp.dot(owner_hot, directions.reshape(member_count, width_all), precision=precise)
    slot_dir = slot_dir.reshape(slot_count, head_count, head_size)
    key_wide = key_rows.astype(jnp.float32).reshape(slot_count, page_len, head_count, head_size)
    scores = jnp.einsum("sthd,shd->sht", key_wide, slot_dir, precision=precise)
    source_wide = source_rows.astype(jnp.float32).reshape(
        slot_count, page_len, head_count, head_size
    )
    contribution = jnp.einsum("sht,sthd->shd", slot_weight * scores, source_wide, precision=precise)
    summed = jnp.dot(owner_hot.T, contribution.reshape(slot_count, width_all), precision=precise)
    return summed.reshape(member_count, head_count, head_size)


def new_term(vectors, source_rows, strength_rows, key_new):
    return (
        strength_rows[:, :, None] * source_rows * jnp.sum(key_new * vectors, axis=-1, keepdims=True)
    )


def conjugate(query_rows, key_new, value_new, strength_rows, ridge_term, reduce_fn):
    solution = jnp.zeros_like(query_rows)
    residual = query_rows
    direction = query_rows
    res_norm = jnp.sum(residual * residual, axis=-1)
    for iteration in range(ITERS):
        image_vec = (
            reduce_fn(direction, False)
            + new_term(direction, key_new, strength_rows, key_new)
            + ridge_term[None, :, None] * direction
        )
        step_size = res_norm / jnp.sum(direction * image_vec, axis=-1)
        solution = solution + step_size[:, :, None] * direction
        residual = residual - step_size[:, :, None] * image_vec
        next_norm = jnp.sum(residual * residual, axis=-1)
        direction = residual + (next_norm / res_norm)[:, :, None] * direction
        res_norm = next_norm
    return reduce_fn(solution, True) + new_term(solution, value_new, strength_rows, key_new)


def pair_order(mine, theirs, parity):
    first = jnp.where(parity == 0, mine, theirs)
    second = jnp.where(parity == 0, theirs, mine)
    return jnp.concatenate([first, second], axis=0)


def spread_body(
    tokens,
    norm_gain,
    qkv_weight,
    conv_weight,
    conv_state,
    mesa_gates,
    mesa_bias,
    ridge_term,
    key_cache,
    value_cache,
    log_weight,
    page_owner,
    page_fill,
    out_weight,
    mlp_gain,
    gate_weight,
    up_weight,
    down_weight,
):
    req_rows = tokens.shape[0]
    group_rows = req_rows * lax.axis_size("shard")
    head_count = ridge_term.shape[0]
    width_all = key_cache.shape[2]
    head_size = width_all // head_count
    parity = lax.axis_index("group") % 2
    normed = scaled_norm(tokens, norm_gain)
    fresh_proj = jnp.dot(
        lax.all_gather(normed, "shard", axis=0, tiled=True),
        qkv_weight,
        preferred_element_type=jnp.float32,
    )
    past_rows = conv_state.astype(jnp.float32)
    pre_conv = (
        conv_weight[3] * fresh_proj
        + conv_weight[0] * past_rows[:, 0]
        + conv_weight[1] * past_rows[:, 1]
        + conv_weight[2] * past_rows[:, 2]
    )
    mixed_cols = jax.nn.silu(pre_conv).astype(jnp.bfloat16)
    home_rows = lax.all_to_all(mixed_cols, "shard", split_axis=0, concat_axis=1, tiled=True)
    split_rows = home_rows.astype(jnp.float32).reshape(req_rows, 3, head_count, head_size)
    query_home = unit_rows(split_rows[:, 0])
    key_home = unit_rows(split_rows[:, 1])
    value_home = split_rows[:, 2]
    gate_vals = jax.nn.sigmoid(
        jnp.dot(normed, mesa_gates, preferred_element_type=jnp.float32) + mesa_bias
    )
    decay_home = gate_vals[:, :head_count]
    strength_home = gate_vals[:, head_count:]
    owner_hot = (page_owner[:, None] == jnp.arange(2 * group_rows)[None, :]).astype(jnp.float32)
    stored = {}

    def cache_pass(directions, decay_grp, with_values):
        far_dirs, far_decay = partner((directions, decay_grp), "group", 0)
        pair_dirs = pair_order(directions, far_dirs, parity)
        pair_decay = pair_order(decay_grp, far_decay, parity)
        if "weight" not in stored:
            stored["weight"] = slot_weights(owner_hot, pair_decay, log_weight, page_fill)
        source_rows = value_cache if with_values else key_cache
        summed = slot_terms(key_cache, source_rows, owner_hot, stored["weight"], pair_dirs)
        mine = jnp.where(parity == 0, summed[:group_rows], summed[group_rows:])
        theirs = jnp.where(parity == 0, summed[group_rows:], summed[:group_rows])
        returned = partner(theirs, "group", 0)
        return mine + returned

    def reduce_home(vectors, with_values):
        directions, decay_grp = (
            lax.all_gather(vectors, "shard", axis=0, tiled=True),
            lax.all_gather(decay_home, "shard", axis=0, tiled=True),
        )
        return lax.psum_scatter(
            cache_pass(directions, decay_grp, with_values), "shard", scatter_dimension=0, tiled=True
        )

    found = conjugate(query_home, key_home, value_home, strength_home, ridge_term, reduce_home)
    retrieved = found.reshape(req_rows, width_all).astype(jnp.bfloat16)
    columns = lax.all_to_all(retrieved, "shard", split_axis=1, concat_axis=0, tiled=True)
    attended = lax.psum_scatter(
        jnp.dot(columns, out_weight, preferred_element_type=jnp.float32),
        "shard",
        scatter_dimension=0,
        tiled=True,
    )
    mid_rows = (tokens.astype(jnp.float32) + attended).astype(jnp.bfloat16)
    mlp_in = scaled_norm(mid_rows, mlp_gain)
    piece_rows = lax.all_gather(mlp_in, "shard", axis=0, tiled=True)
    gate_part = jnp.dot(piece_rows, gate_weight, preferred_element_type=jnp.float32)
    up_part = jnp.dot(piece_rows, up_weight, preferred_element_type=jnp.float32)
    hidden_rows = (jax.nn.silu(gate_part) * up_part).astype(jnp.bfloat16)
    down_part = lax.psum_scatter(
        jnp.dot(hidden_rows, down_weight, preferred_element_type=jnp.float32),
        "shard",
        scatter_dimension=0,
        tiled=True,
    )
    layer_out = (mid_rows.astype(jnp.float32) + down_part).astype(jnp.bfloat16)
    return (retrieved, layer_out)


TILE = 8
MASKED = -1e38
PAIR = ("shard", "member")
PARAMS = pltpu.CompilerParams(vmem_limit_bytes=16 * 1024 * 1024)


def split_pair(value):
    high = value.astype(jnp.bfloat16)
    low = (value - high.astype(jnp.float32)).astype(jnp.bfloat16)
    return high, low


def hot(rows, columns, target_fn):
    row = lax.broadcasted_iota(jnp.int32, (rows, columns), 0)
    column = lax.broadcasted_iota(jnp.int32, (rows, columns), 1)
    return jnp.where(column == target_fn(row), 1.0, 0.0).astype(jnp.bfloat16)


def here():
    return lax.axis_index("shard") * 2 + lax.axis_index("member")


def silu(value):
    return value / (1.0 + jnp.exp(-value))


def pack_kernel(owner_ref, fill_ref, tokens_ref, logs_ref, send_ref):
    req_rows, width = tokens_ref.shape
    slots, head_count, page = logs_ref.shape
    tokens = tokens_ref[...].astype(jnp.float32)
    blank = jnp.zeros((TILE - req_rows, width), jnp.float32)
    tile = jnp.concatenate([tokens, blank], axis=0).astype(jnp.bfloat16)
    spot = lax.broadcasted_iota(jnp.int32, (head_count, page), 1)
    logs = []
    lane = lax.broadcasted_iota(jnp.int32, (1, page), 1)
    owners = jnp.zeros((1, page), jnp.float32)
    for slot in range(slots):
        rows = logs_ref[slot].astype(jnp.float32)
        logs.append(jnp.where(spot < fill_ref[slot], rows, MASKED))
        owners = jnp.where(lane == slot, owner_ref[slot].astype(jnp.float32), owners)
    rest = jnp.zeros((TILE - slots - 1, page), jnp.float32)
    for head in range(head_count):
        rows = [log[head : head + 1, :] for log in logs]
        side = jnp.concatenate([*rows, owners, rest], axis=0).astype(jnp.bfloat16)
        send_ref[head * TILE : (head + 1) * TILE, :width] = tile
        send_ref[head * TILE : (head + 1) * TILE, width:] = side


def spread_kernel(cache_ref, *refs):
    *outs, sems = refs
    head_size = outs[0].shape[2]
    me = here()
    copies = []
    for apart, out_ref in enumerate(outs):
        start = pl.multiple_of((me ^ apart) * head_size, head_size)
        copies.append(
            pltpu.make_async_copy(
                cache_ref.at[:, :, pl.ds(start, head_size)], out_ref, sems.at[apart]
            )
        )
    for copy in copies:
        copy.start()
    for copy in copies:
        copy.wait()


def project_kernel(
    shards,
    req_rows,
    slots,
    head_count,
    pack_ref,
    gain_ref,
    qkv_ref,
    tap_ref,
    past_ref,
    gates_ref,
    bias_ref,
    mixed_ref,
    tokens_ref,
    weight_ref,
    owner_ref,
    strength_ref,
):
    member = lax.axis_index("member")
    head = here()
    group_rows = shards * req_rows
    pair_rows = 2 * group_rows
    packed = 2 * shards * TILE
    width = gain_ref.shape[1]
    page = weight_ref.shape[1]

    def home_of(row):
        x = row // group_rows
        s = (row % group_rows) // req_rows
        return (s * 2 + x) * TILE + row % req_rows

    pick_pair = hot(pair_rows, packed, home_of)
    pick_group = hot(group_rows, packed, lambda row: home_of(row + member * group_rows))
    rows = pack_ref[:, :width]
    pair_tokens = jnp.dot(pick_pair, rows, preferred_element_type=jnp.float32)
    own_tokens = jnp.dot(pick_group, rows, preferred_element_type=jnp.float32)
    tokens_ref[...] = own_tokens
    own = scaled_norm(own_tokens, gain_ref[...])
    fresh = jnp.dot(own, qkv_ref[...], preferred_element_type=jnp.float32)
    before = tap_ref[3:4, :] * fresh
    for tap in range(3):
        before = before + tap_ref[tap : tap + 1, :] * past_ref[tap].astype(jnp.float32)
    mixed = silu(before).astype(jnp.bfloat16)
    for target in range(2 * shards):
        mixed_ref[target * group_rows : (target + 1) * group_rows, :] = mixed

    normed = scaled_norm(pair_tokens, gain_ref[...])
    raw = lax.dot_general(
        normed, gates_ref[...], (((1,), (1,)), ((), ())), preferred_element_type=jnp.float32
    )
    gate_vals = 1.0 / (1.0 + jnp.exp(-(raw + bias_ref[...])))
    column = lax.broadcasted_iota(jnp.int32, gate_vals.shape, 1)
    decay = jnp.sum(jnp.where(column == head, gate_vals, 0.0), axis=1, keepdims=True)
    strength = jnp.sum(
        jnp.where(column == head + head_count, gate_vals, 0.0), axis=1, keepdims=True
    )
    strength_ref[...] = jnp.broadcast_to(strength, strength_ref.shape)

    all_slots = 2 * shards * slots
    side = pack_ref[:, width:]
    pick_slot = hot(all_slots, packed, lambda row: (row // slots) * TILE + row % slots)
    logs = jnp.dot(pick_slot, side, preferred_element_type=jnp.float32)
    pick_owner = hot(all_slots, packed, lambda row: (row // slots) * TILE + slots)
    owners = jnp.dot(pick_owner, side, preferred_element_type=jnp.float32)
    at_slot = hot(all_slots, page, lambda row: row % slots).astype(jnp.float32)
    owner = jnp.sum(at_slot * owners, axis=1, keepdims=True).astype(jnp.int32)
    owner_ref[...] = jnp.broadcast_to(owner, owner_ref.shape)
    request = lax.broadcasted_iota(jnp.int32, (all_slots, pair_rows), 1)
    owner_hot = jnp.where(request == owner, 1.0, 0.0)
    wide_decay = jnp.broadcast_to(decay, (pair_rows, page))
    slot_decay = jnp.dot(
        owner_hot, wide_decay, precision=precise, preferred_element_type=jnp.float32
    )
    weight_ref[...] = slot_decay * jnp.exp(logs)


def solve_kernel(
    head_count,
    owner_ref,
    ridge_ref,
    mixed_ref,
    weight_ref,
    strength_ref,
    *refs,
):
    *key_refs, both_ref, term_ref, gram_ref = refs
    head = here()
    slots, page, head_size = key_refs[0].shape
    pair_rows = strength_ref.shape[0]
    blocks = mixed_ref.shape[1] // head_size

    gram_ref[...] = jnp.zeros_like(gram_ref)
    for apart, key_ref in enumerate(key_refs):
        for spot in range(slots):
            slot = (head ^ apart) * slots + spot
            keys = key_ref[spot]
            turned = keys.T.astype(jnp.float32) * weight_ref[pl.ds(slot, 1), :]
            high, low = split_pair(turned)
            piece = jnp.dot(high, keys, preferred_element_type=jnp.float32) + jnp.dot(
                low, keys, preferred_element_type=jnp.float32
            )
            owner = owner_ref[slot, 0]
            gram_ref[owner] = gram_ref[owner] + piece

    def columns_of(block):
        source = block // blocks
        start = pl.multiple_of((block % blocks) * head_size, head_size)
        first = pl.multiple_of(source * pair_rows, pair_rows)
        return mixed_ref[pl.ds(first, pair_rows), pl.ds(start, head_size)].astype(jnp.float32)

    query = unit_rows(columns_of(head))
    key_new = unit_rows(columns_of(head + head_count))
    value_new = columns_of(head + 2 * head_count)
    strength = strength_ref[...]
    ridge = ridge_ref[head]

    def image_of(vectors):
        turned = vectors.T
        pieces = []
        for row in range(pair_rows):
            spread = jnp.broadcast_to(turned[:, row : row + 1], (head_size, head_size))
            pieces.append(jnp.sum(gram_ref[row] * spread, axis=0, keepdims=True))
        return jnp.concatenate(pieces, axis=0)

    found = jnp.zeros_like(query)
    residual = query
    direction = query
    res_norm = jnp.sum(residual * residual, axis=-1, keepdims=True)
    for iteration in range(ITERS):
        along = jnp.sum(key_new * direction, axis=-1, keepdims=True)
        image = image_of(direction) + strength * key_new * along + ridge * direction
        step = res_norm / jnp.sum(direction * image, axis=-1, keepdims=True)
        found = found + step * direction
        residual = residual - step * image
        next_norm = jnp.sum(residual * residual, axis=-1, keepdims=True)
        direction = residual + (next_norm / res_norm) * direction
        res_norm = next_norm

    term_ref[...] = strength * value_new * jnp.sum(key_new * found, axis=-1, keepdims=True)
    high, low = split_pair(found)
    third = (found - high.astype(jnp.float32) - low.astype(jnp.float32)).astype(jnp.bfloat16)
    stacked = jnp.concatenate([high, low, third], axis=0)
    request = lax.broadcasted_iota(jnp.int32, (pair_rows, page), 0)
    for apart, key_ref in enumerate(key_refs):
        for spot in range(slots):
            slot = (head ^ apart) * slots + spot
            scores = lax.dot_general(
                stacked, key_ref[spot], (((1,), (1,)), ((), ())), preferred_element_type=jnp.float32
            )
            scores = (
                scores[:pair_rows] + scores[pair_rows : 2 * pair_rows] + scores[2 * pair_rows :]
            )
            kept = jnp.where(
                request == owner_ref[slot, 0], scores * weight_ref[pl.ds(slot, 1), :], 0.0
            )
            high, low = split_pair(kept)
            first = (apart * slots + spot) * page
            both_ref[:pair_rows, first : first + page] = high
            both_ref[pair_rows:, first : first + page] = low


def read_kernel(both_ref, term_ref, out_ref, *refs):
    *value_refs, send_ref = refs
    member = lax.axis_index("member")
    rows, head_size = term_ref.shape
    slots, page, _ = value_refs[0].shape
    width = out_ref.shape[1]
    found = term_ref[...]
    for apart, value_ref in enumerate(value_refs):
        span = slots * page
        summed = jnp.dot(
            both_ref[:, apart * span : (apart + 1) * span],
            value_ref[...].reshape(span, head_size),
            preferred_element_type=jnp.float32,
        )
        found = found + (summed[:rows] + summed[rows:])
    retrieved = found.astype(jnp.bfloat16)
    start = pl.multiple_of(member * head_size, head_size)
    part = jnp.dot(
        retrieved, out_ref[pl.ds(start, head_size), :], preferred_element_type=jnp.float32
    ).astype(jnp.bfloat16)
    targets = send_ref.shape[0] * 2 // rows
    half = rows // 2
    for target in range(targets):
        x = target % 2
        spot = slice(target * half, (target + 1) * half)
        send_ref[spot, :width] = part[x * half : (x + 1) * half]
        send_ref[spot, width:] = retrieved[x * half : (x + 1) * half]


def mlp_kernel(
    shards,
    part_ref,
    tokens_ref,
    gain_ref,
    gate_ref,
    up_ref,
    down_ref,
    mid_ref,
    retrieved_ref,
    send_ref,
):
    shard = lax.axis_index("shard")
    group_rows, width = tokens_ref.shape
    devices = 2 * shards
    req_rows = group_rows // shards
    attended = part_ref[:group_rows, :width].astype(jnp.float32)
    for source in range(1, devices):
        spot = slice(source * group_rows, (source + 1) * group_rows)
        attended += part_ref[spot, :width].astype(jnp.float32)
    mid_rows = (tokens_ref[...] + attended).astype(jnp.bfloat16)
    mlp_in = scaled_norm(mid_rows, gain_ref[...])
    contract = (((1,), (1,)), ((), ()))
    gate_part = lax.dot_general(
        mlp_in, gate_ref[...], contract, preferred_element_type=jnp.float32
    )
    up_part = lax.dot_general(mlp_in, up_ref[...], contract, preferred_element_type=jnp.float32)
    hidden = (silu(gate_part) * up_part).astype(jnp.bfloat16)
    down = jnp.dot(hidden, down_ref[...], preferred_element_type=jnp.float32)
    send_ref[...] = down.reshape(send_ref.shape)

    def home_rows(value):
        row = lax.broadcasted_iota(jnp.int32, value.shape, 0)
        picked = [
            jnp.sum(jnp.where(row == shard * req_rows + i, value, 0.0), axis=0, keepdims=True)
            for i in range(req_rows)
        ]
        return jnp.concatenate(picked, axis=0)

    mid_ref[...] = home_rows(mid_rows.astype(jnp.float32))
    heads = [
        home_rows(
            part_ref[source * group_rows : (source + 1) * group_rows, width:].astype(jnp.float32)
        )
        for source in range(devices)
    ]
    retrieved_ref[...] = jnp.concatenate(heads, axis=1).astype(jnp.bfloat16)


def finish_kernel(shards, down_ref, mid_ref, layer_ref):
    req_rows, width = mid_ref.shape
    rows = down_ref.shape[0] // shards
    total = down_ref[:rows]
    for source in range(1, shards):
        total = total + down_ref[source * rows : (source + 1) * rows]
    layer_ref[...] = (mid_ref[...] + total.reshape(req_rows, width)).astype(jnp.bfloat16)


def head_body(
    tokens,
    norm_gain,
    qkv_weight,
    conv_weight,
    conv_state,
    mesa_gates,
    mesa_bias,
    ridge_term,
    key_cache,
    value_cache,
    log_weight,
    page_owner,
    page_fill,
    out_weight,
    mlp_gain,
    gate_weight,
    up_weight,
    down_weight,
):
    shards = lax.axis_size("shard")
    devices = 2 * shards
    req_rows, width = tokens.shape
    slots, page, _ = key_cache.shape
    head_count = ridge_term.shape[0]
    head_size = width // head_count
    group_rows = shards * req_rows
    pair_rows = 2 * group_rows
    all_slots = devices * slots
    columns = qkv_weight.shape[1]
    shape = jax.ShapeDtypeStruct
    bf16, f32 = jnp.bfloat16, jnp.float32

    def exchange(value, axes):
        return lax.all_to_all(value, axes, split_axis=0, concat_axis=0, tiled=True)

    pack = pl.pallas_call(
        pack_kernel,
        out_shape=shape((devices * TILE, width + page), bf16),
        in_specs=[SMEM] * 2 + [VMEM] * 2,
        out_specs=VMEM,
        compiler_params=PARAMS,
        name="pack",
    )(page_owner, page_fill, tokens, log_weight)
    packs = exchange(pack, PAIR)

    def spot(number):
        return number % 2 * shards + number // 2

    def spread(cache, name):
        pieces = pl.pallas_call(
            spread_kernel,
            out_shape=(shape((slots, page, head_size), bf16),) * devices,
            in_specs=[pl.BlockSpec(memory_space=pl.ANY)],
            out_specs=(pl.BlockSpec(memory_space=pl.ANY),) * devices,
            scratch_shapes=[pltpu.SemaphoreType.DMA((devices,))],
            compiler_params=PARAMS,
            name=name,
        )(cache)
        moved = [pieces[0]]
        for apart in range(1, devices):
            pairs = [(spot(source), spot(source ^ apart)) for source in range(devices)]
            moved.append(lax.ppermute(pieces[apart], ("member", "shard"), pairs))
        return moved

    keys = spread(key_cache, "spread_keys")
    values = spread(value_cache, "spread_values")

    mixed, own_tokens, weight, owner, strength = pl.pallas_call(
        functools.partial(project_kernel, shards, req_rows, slots, head_count),
        out_shape=(
            shape((devices * group_rows, columns), bf16),
            shape((group_rows, width), f32),
            shape((all_slots, page), f32),
            shape((all_slots, page), jnp.int32),
            shape((pair_rows, head_size), f32),
        ),
        in_specs=[VMEM] * 7,
        out_specs=(VMEM,) * 5,
        compiler_params=PARAMS,
        name="project",
    )(
        packs,
        norm_gain[None, :],
        qkv_weight,
        conv_weight,
        jnp.transpose(conv_state, (1, 0, 2)),
        mesa_gates.T,
        mesa_bias[None, :],
    )
    all_mixed = exchange(mixed, PAIR)

    both, term = pl.pallas_call(
        functools.partial(solve_kernel, head_count),
        out_shape=(
            shape((2 * pair_rows, all_slots * page), bf16),
            shape((pair_rows, head_size), f32),
        ),
        in_specs=[SMEM] * 2 + [VMEM] * (3 + devices),
        out_specs=(VMEM,) * 2,
        scratch_shapes=[pltpu.VMEM((pair_rows, head_size, head_size), f32)],
        compiler_params=PARAMS,
        name="solve",
    )(owner, ridge_term, all_mixed, weight, strength, *keys)

    parts = pl.pallas_call(
        read_kernel,
        out_shape=shape((devices * group_rows, width + head_size), bf16),
        in_specs=[VMEM] * (3 + devices),
        out_specs=VMEM,
        compiler_params=PARAMS,
        name="read",
    )(both, term, out_weight, *values)
    all_parts = exchange(parts, PAIR)

    mid_home, retrieved, down = pl.pallas_call(
        functools.partial(mlp_kernel, shards),
        out_shape=(
            shape((req_rows, width), f32),
            shape((req_rows, width), bf16),
            shape((group_rows * head_count, head_size), f32),
        ),
        in_specs=[VMEM] * 6,
        out_specs=(VMEM,) * 3,
        compiler_params=PARAMS,
        name="mlp",
    )(
        all_parts,
        own_tokens,
        mlp_gain[None, :],
        gate_weight.T,
        up_weight.T,
        down_weight,
    )
    layer_out = pl.pallas_call(
        functools.partial(finish_kernel, shards),
        out_shape=shape((req_rows, width), bf16),
        in_specs=[VMEM] * 2,
        out_specs=VMEM,
        compiler_params=PARAMS,
        name="finish",
    )(exchange(down, "shard"), mid_home)
    return (retrieved, layer_out)


def specs(group):
    rows = P((*group, "shard"))
    return (
        (
            rows,
            P(),
            P(None, "shard"),
            P(None, "shard"),
            P(group, None, "shard"),
            P(),
            P(),
            P(),
            rows,
            rows,
            rows,
            rows,
            rows,
            P("shard", None),
            P(),
            P(None, "shard"),
            P(None, "shard"),
            P("shard", None),
        ),
        (rows, rows),
    )


def solution(mesh):
    groups, shards = mesh.devices.shape

    def run(*args):
        head_count = args[7].shape[0]
        if 2 * shards == head_count:
            axes = ("pair", "member", "shard")
            used = Mesh(mesh.devices.reshape(groups // 2, 2, shards), axes)
            body, group = head_body, ("pair", "member")
        else:
            used, body, group = mesh, spread_body, ("group",)
        in_specs, out_specs = specs(group)
        return jax.shard_map(
            body, mesh=used, in_specs=in_specs, out_specs=out_specs, check_vma=False
        )(*args)

    return run
```

```python
import functools

import jax
import jax.numpy as jnp
from jax import lax
from jax.experimental import pallas as pl
from jax.experimental.pallas import tpu as pltpu
from jax.sharding import Mesh
from jax.sharding import PartitionSpec as P

ITERS = 4


precise = lax.Precision.HIGHEST

VMEM = pl.BlockSpec(memory_space=pltpu.VMEM)
SMEM = pl.BlockSpec(memory_space=pltpu.SMEM)


def partner(value, axis, apart):
    mask = 2**apart
    pairs = [(source, source ^ mask) for source in range(lax.axis_size(axis))]
    return lax.ppermute(value, axis, pairs)


def scaled_norm(row_vals, gain_vec):
    wide_rows = row_vals.astype(jnp.float32)
    factor = lax.rsqrt(jnp.mean(wide_rows * wide_rows, axis=-1, keepdims=True) + 1e-05)
    return (wide_rows * factor * gain_vec).astype(jnp.bfloat16)


def unit_rows(vectors):
    return vectors * lax.rsqrt(jnp.sum(vectors * vectors, axis=-1, keepdims=True) + 1e-06)


def slot_weights(owner_hot, decay_rows, log_weight, page_fill):
    page_len = log_weight.shape[2]
    slot_decay = jnp.dot(owner_hot, decay_rows, precision=precise)
    live_mask = (jnp.arange(page_len)[None, :] < page_fill[:, None]).astype(jnp.float32)
    return slot_decay[:, :, None] * jnp.exp(log_weight.astype(jnp.float32)) * live_mask[:, None, :]


def slot_terms(key_rows, source_rows, owner_hot, slot_weight, directions):
    slot_count, page_len, width_all = key_rows.shape
    head_count = slot_weight.shape[1]
    head_size = width_all // head_count
    member_count = owner_hot.shape[1]
    slot_dir = jnp.dot(owner_hot, directions.reshape(member_count, width_all), precision=precise)
    slot_dir = slot_dir.reshape(slot_count, head_count, head_size)
    key_wide = key_rows.astype(jnp.float32).reshape(slot_count, page_len, head_count, head_size)
    scores = jnp.einsum("sthd,shd->sht", key_wide, slot_dir, precision=precise)
    source_wide = source_rows.astype(jnp.float32).reshape(
        slot_count, page_len, head_count, head_size
    )
    contribution = jnp.einsum("sht,sthd->shd", slot_weight * scores, source_wide, precision=precise)
    summed = jnp.dot(owner_hot.T, contribution.reshape(slot_count, width_all), precision=precise)
    return summed.reshape(member_count, head_count, head_size)


def new_term(vectors, source_rows, strength_rows, key_new):
    return (
        strength_rows[:, :, None] * source_rows * jnp.sum(key_new * vectors, axis=-1, keepdims=True)
    )


def conjugate(query_rows, key_new, value_new, strength_rows, ridge_term, reduce_fn):
    solution = jnp.zeros_like(query_rows)
    residual = query_rows
    direction = query_rows
    res_norm = jnp.sum(residual * residual, axis=-1)
    for iteration in range(ITERS):
        image_vec = (
            reduce_fn(direction, False)
            + new_term(direction, key_new, strength_rows, key_new)
            + ridge_term[None, :, None] * direction
        )
        step_size = res_norm / jnp.sum(direction * image_vec, axis=-1)
        solution = solution + step_size[:, :, None] * direction
        residual = residual - step_size[:, :, None] * image_vec
        next_norm = jnp.sum(residual * residual, axis=-1)
        direction = residual + (next_norm / res_norm)[:, :, None] * direction
        res_norm = next_norm
    return reduce_fn(solution, True) + new_term(solution, value_new, strength_rows, key_new)


def pair_order(mine, theirs, parity):
    first = jnp.where(parity == 0, mine, theirs)
    second = jnp.where(parity == 0, theirs, mine)
    return jnp.concatenate([first, second], axis=0)


def spread_body(
    tokens,
    norm_gain,
    qkv_weight,
    conv_weight,
    conv_state,
    mesa_gates,
    mesa_bias,
    ridge_term,
    key_cache,
    value_cache,
    log_weight,
    page_owner,
    page_fill,
    out_weight,
    mlp_gain,
    gate_weight,
    up_weight,
    down_weight,
):
    req_rows = tokens.shape[0]
    group_rows = req_rows * lax.axis_size("shard")
    head_count = ridge_term.shape[0]
    width_all = key_cache.shape[2]
    head_size = width_all // head_count
    parity = lax.axis_index("group") % 2
    normed = scaled_norm(tokens, norm_gain)
    fresh_proj = jnp.dot(
        lax.all_gather(normed, "shard", axis=0, tiled=True),
        qkv_weight,
        preferred_element_type=jnp.float32,
    )
    past_rows = conv_state.astype(jnp.float32)
    pre_conv = (
        conv_weight[3] * fresh_proj
        + conv_weight[0] * past_rows[:, 0]
        + conv_weight[1] * past_rows[:, 1]
        + conv_weight[2] * past_rows[:, 2]
    )
    mixed_cols = jax.nn.silu(pre_conv).astype(jnp.bfloat16)
    home_rows = lax.all_to_all(mixed_cols, "shard", split_axis=0, concat_axis=1, tiled=True)
    split_rows = home_rows.astype(jnp.float32).reshape(req_rows, 3, head_count, head_size)
    query_home = unit_rows(split_rows[:, 0])
    key_home = unit_rows(split_rows[:, 1])
    value_home = split_rows[:, 2]
    gate_vals = jax.nn.sigmoid(
        jnp.dot(normed, mesa_gates, preferred_element_type=jnp.float32) + mesa_bias
    )
    decay_home = gate_vals[:, :head_count]
    strength_home = gate_vals[:, head_count:]
    owner_hot = (page_owner[:, None] == jnp.arange(2 * group_rows)[None, :]).astype(jnp.float32)
    stored = {}

    def cache_pass(directions, decay_grp, with_values):
        far_dirs, far_decay = partner((directions, decay_grp), "group", 0)
        pair_dirs = pair_order(directions, far_dirs, parity)
        pair_decay = pair_order(decay_grp, far_decay, parity)
        if "weight" not in stored:
            stored["weight"] = slot_weights(owner_hot, pair_decay, log_weight, page_fill)
        source_rows = value_cache if with_values else key_cache
        summed = slot_terms(key_cache, source_rows, owner_hot, stored["weight"], pair_dirs)
        mine = jnp.where(parity == 0, summed[:group_rows], summed[group_rows:])
        theirs = jnp.where(parity == 0, summed[group_rows:], summed[:group_rows])
        returned = partner(theirs, "group", 0)
        return mine + returned

    def reduce_home(vectors, with_values):
        directions, decay_grp = (
            lax.all_gather(vectors, "shard", axis=0, tiled=True),
            lax.all_gather(decay_home, "shard", axis=0, tiled=True),
        )
        return lax.psum_scatter(
            cache_pass(directions, decay_grp, with_values), "shard", scatter_dimension=0, tiled=True
        )

    found = conjugate(query_home, key_home, value_home, strength_home, ridge_term, reduce_home)
    retrieved = found.reshape(req_rows, width_all).astype(jnp.bfloat16)
    columns = lax.all_to_all(retrieved, "shard", split_axis=1, concat_axis=0, tiled=True)
    attended = lax.psum_scatter(
        jnp.dot(columns, out_weight, preferred_element_type=jnp.float32),
        "shard",
        scatter_dimension=0,
        tiled=True,
    )
    mid_rows = (tokens.astype(jnp.float32) + attended).astype(jnp.bfloat16)
    mlp_in = scaled_norm(mid_rows, mlp_gain)
    piece_rows = lax.all_gather(mlp_in, "shard", axis=0, tiled=True)
    gate_part = jnp.dot(piece_rows, gate_weight, preferred_element_type=jnp.float32)
    up_part = jnp.dot(piece_rows, up_weight, preferred_element_type=jnp.float32)
    hidden_rows = (jax.nn.silu(gate_part) * up_part).astype(jnp.bfloat16)
    down_part = lax.psum_scatter(
        jnp.dot(hidden_rows, down_weight, preferred_element_type=jnp.float32),
        "shard",
        scatter_dimension=0,
        tiled=True,
    )
    layer_out = (mid_rows.astype(jnp.float32) + down_part).astype(jnp.bfloat16)
    return (retrieved, layer_out)


TILE = 8
MASKED = -1e38
PAIR = ("shard", "member")
PARAMS = pltpu.CompilerParams(vmem_limit_bytes=16 * 1024 * 1024)
PAST, TAP, GAIN, BIAS, RIDGE = slice(0, 8), slice(8, 9), slice(9, 10), slice(10, 11), slice(11, 12)
GATES = slice(16, 32)
WHOLE = pltpu.CompilerParams(vmem_limit_bytes=62 * 1024 * 1024)


def split_pair(value):
    high = value.astype(jnp.bfloat16)
    low = (value - high.astype(jnp.float32)).astype(jnp.bfloat16)
    return high, low


def hot(rows, columns, target_fn):
    row = lax.broadcasted_iota(jnp.int32, (rows, columns), 0)
    column = lax.broadcasted_iota(jnp.int32, (rows, columns), 1)
    return jnp.where(column == target_fn(row), 1.0, 0.0).astype(jnp.bfloat16)


def here():
    return lax.axis_index("shard") * 2 + lax.axis_index("member")


def silu(value):
    return value / (1.0 + jnp.exp(-value))


def prep_kernel(
    tokens_hbm,
    logs_hbm,
    owner_hbm,
    fill_hbm,
    key_hbm,
    value_hbm,
    past_hbm,
    tap_hbm,
    gain_hbm,
    gates_hbm,
    bias_hbm,
    ridge_hbm,
    send_ref,
    misc_ref,
    *refs,
):
    *piece_refs, tokens_ref, logs_ref, owner_ref, fill_ref, state_ref, gates_ref = refs[:-6]
    tap_ref, gain_ref, bias_ref, ridge_ref, small_sems, big_sems = refs[-6:]
    req_rows, width = tokens_ref.shape
    slots, head_count, page = logs_ref.shape
    head_size = piece_refs[0].shape[2]
    me = here()
    small = [
        pltpu.make_async_copy(source, target, small_sems.at[place])
        for place, (source, target) in enumerate(
            [
                (owner_hbm, owner_ref),
                (fill_hbm, fill_ref),
                (tokens_hbm, tokens_ref),
                (logs_hbm, logs_ref),
                (past_hbm, state_ref),
                (tap_hbm, tap_ref),
                (gain_hbm, gain_ref),
                (gates_hbm, gates_ref),
                (bias_hbm, bias_ref),
                (ridge_hbm, ridge_ref),
            ]
        )
    ]
    big = []
    for apart, piece_ref in enumerate(piece_refs):
        start = pl.multiple_of((me ^ apart) * head_size, head_size)
        for part, cache in enumerate((key_hbm, value_hbm)):
            big.append(
                pltpu.make_async_copy(
                    cache.at[:, :, pl.ds(start, head_size)],
                    piece_ref.at[pl.ds(part * slots, slots)],
                    big_sems.at[2 * apart + part],
                )
            )
    for copy in small:
        copy.start()
    for copy in big:
        copy.start()
    for copy in small:
        copy.wait()

    tokens = tokens_ref[...].astype(jnp.float32)
    blank = jnp.zeros((TILE - req_rows, width), jnp.float32)
    tile = jnp.concatenate([tokens, blank], axis=0).astype(jnp.bfloat16)
    spot = lax.broadcasted_iota(jnp.int32, (head_count, page), 1)
    logs = []
    lane = lax.broadcasted_iota(jnp.int32, (1, page), 1)
    owners = jnp.zeros((1, page), jnp.float32)
    for slot in range(slots):
        rows = logs_ref[slot].astype(jnp.float32)
        logs.append(jnp.where(spot < fill_ref[slot], rows, MASKED))
        owners = jnp.where(lane == slot, owner_ref[slot].astype(jnp.float32), owners)
    rest = jnp.zeros((TILE - slots - 1, page), jnp.float32)
    for head in range(head_count):
        rows = [log[head : head + 1, :] for log in logs]
        side = jnp.concatenate([*rows, owners, rest], axis=0).astype(jnp.bfloat16)
        send_ref[head * TILE : (head + 1) * TILE, :width] = tile
        send_ref[head * TILE : (head + 1) * TILE, width:] = side

    past = tap_ref[0:1, :] * state_ref[0].astype(jnp.float32)
    past = past + tap_ref[1:2, :] * state_ref[1].astype(jnp.float32)
    past = past + tap_ref[2:3, :] * state_ref[2].astype(jnp.float32)
    columns = past.shape[1]
    misc_ref[PAST, :columns] = past
    misc_ref[TAP, :columns] = tap_ref[3:4, :]
    misc_ref[GAIN, :] = gain_ref[...]
    misc_ref[BIAS, : 2 * head_count] = bias_ref[...]
    ridges = jnp.zeros((1, page), jnp.float32)
    for head in range(head_count):
        ridges = jnp.where(lane == head, ridge_ref[head], ridges)
    misc_ref[RIDGE, :page] = ridges
    misc_ref[GATES, :] = gates_ref[...].astype(jnp.float32)
    for copy in big:
        copy.wait()


def project_kernel(
    shards,
    req_rows,
    slots,
    head_count,
    pack_ref,
    misc_ref,
    qkv_ref,
    send_ref,
    tokens_ref,
    weight_ref,
    owner_ref,
    strength_ref,
    mixed_ref,
):
    shard = lax.axis_index("shard")
    member = lax.axis_index("member")
    head = here()
    group_rows = shards * req_rows
    pair_rows = 2 * group_rows
    packed = 2 * shards * TILE
    width = misc_ref.shape[1]
    columns = qkv_ref.shape[1]
    page = weight_ref.shape[1]
    head_size = send_ref.shape[1]
    blocks = columns // head_size

    def home_of(row):
        x = row // group_rows
        s = (row % group_rows) // req_rows
        return (s * 2 + x) * TILE + row % req_rows

    pick_pair = hot(pair_rows, packed, home_of)
    pick_group = hot(group_rows, packed, lambda row: home_of(row + member * group_rows))
    rows = pack_ref[:, :width]
    pair_tokens = jnp.dot(pick_pair, rows, preferred_element_type=jnp.float32)
    own_tokens = jnp.dot(pick_group, rows, preferred_element_type=jnp.float32)
    tokens_ref[...] = own_tokens
    own = scaled_norm(own_tokens, misc_ref[GAIN, :])
    fresh = jnp.dot(own, qkv_ref[...], preferred_element_type=jnp.float32)
    before = misc_ref[TAP, :columns] * fresh + misc_ref[PAST, :columns]
    mixed_ref[...] = silu(before)
    for target in range(head_count):
        place = jnp.int32(0)
        for part in range(3):
            local = target + part * head_count - shard * blocks
            place = jnp.where((local >= 0) & (local < blocks), local, place)
        start = pl.multiple_of(place * head_size, head_size)
        send_ref[target * group_rows : (target + 1) * group_rows, :] = mixed_ref[
            :, pl.ds(start, head_size)
        ].astype(jnp.bfloat16)

    normed = scaled_norm(pair_tokens, misc_ref[GAIN, :])
    raw = lax.dot_general(
        normed,
        misc_ref[GATES, :].astype(jnp.bfloat16),
        (((1,), (1,)), ((), ())),
        preferred_element_type=jnp.float32,
    )
    gate_vals = 1.0 / (1.0 + jnp.exp(-(raw + misc_ref[BIAS, : 2 * head_count])))
    column = lax.broadcasted_iota(jnp.int32, gate_vals.shape, 1)
    decay = jnp.sum(jnp.where(column == head, gate_vals, 0.0), axis=1, keepdims=True)
    strength = jnp.sum(
        jnp.where(column == head + head_count, gate_vals, 0.0), axis=1, keepdims=True
    )
    strength_ref[:pair_rows, :] = jnp.broadcast_to(strength, (pair_rows, head_size))
    ridges = misc_ref[RIDGE, :page]
    spot = lax.broadcasted_iota(jnp.int32, ridges.shape, 1)
    ridge = jnp.sum(jnp.where(spot == head, ridges, 0.0), axis=1, keepdims=True)
    strength_ref[pair_rows:, :] = jnp.broadcast_to(ridge, (TILE, head_size))

    all_slots = 2 * shards * slots
    side = pack_ref[:, width:]
    pick_slot = hot(all_slots, packed, lambda row: (row // slots) * TILE + row % slots)
    logs = jnp.dot(pick_slot, side, preferred_element_type=jnp.float32)
    pick_owner = hot(all_slots, packed, lambda row: (row // slots) * TILE + slots)
    owners = jnp.dot(pick_owner, side, preferred_element_type=jnp.float32)
    at_slot = hot(all_slots, page, lambda row: row % slots).astype(jnp.float32)
    owner = jnp.sum(at_slot * owners, axis=1, keepdims=True).astype(jnp.int32)
    owner_ref[...] = jnp.broadcast_to(owner, owner_ref.shape)
    request = lax.broadcasted_iota(jnp.int32, (all_slots, pair_rows), 1)
    owner_hot = jnp.where(request == owner, 1.0, 0.0)
    wide_decay = jnp.broadcast_to(decay, (pair_rows, page))
    slot_decay = jnp.dot(
        owner_hot, wide_decay, precision=precise, preferred_element_type=jnp.float32
    )
    weight_ref[...] = slot_decay * jnp.exp(logs)


def gram_kernel(owner_ref, weight_ref, *refs):
    *piece_refs, gram_ref = refs
    head = here()
    slots = piece_refs[0].shape[0] // 2
    gram_ref[...] = jnp.zeros_like(gram_ref)
    for apart, piece_ref in enumerate(piece_refs):
        for spot in range(slots):
            slot = (head ^ apart) * slots + spot
            keys = piece_ref[spot]
            both = jnp.concatenate([keys, piece_ref[slots + spot]], axis=1)
            turned = keys.T.astype(jnp.float32) * weight_ref[pl.ds(slot, 1), :]
            high, low = split_pair(turned)
            piece = jnp.dot(high, both, preferred_element_type=jnp.float32) + jnp.dot(
                low, both, preferred_element_type=jnp.float32
            )
            owner = owner_ref[slot, 0]
            gram_ref[owner] = gram_ref[owner] + piece


def solve_kernel(
    head_count, blocks, mixed_ref, strength_ref, gram_ref, out_ref, send_ref
):
    head = here()
    member = lax.axis_index("member")
    pair_rows, head_size, _ = gram_ref.shape
    width = out_ref.shape[1]

    def columns_of(block):
        first = pl.multiple_of(block // blocks * pair_rows, pair_rows)
        return mixed_ref[pl.ds(first, pair_rows), :].astype(jnp.float32)

    query = unit_rows(columns_of(head))
    key_new = unit_rows(columns_of(head + head_count))
    value_new = columns_of(head + 2 * head_count)
    strength = strength_ref[:pair_rows, :]
    ridge = strength_ref[pair_rows : pair_rows + 1, :]

    def image_of(vectors, columns):
        turned = vectors.T
        pieces = []
        for row in range(pair_rows):
            spread = jnp.broadcast_to(turned[:, row : row + 1], (head_size, head_size))
            pieces.append(jnp.sum(gram_ref[row, :, columns] * spread, axis=0, keepdims=True))
        return jnp.concatenate(pieces, axis=0)

    found = jnp.zeros_like(query)
    residual = query
    direction = query
    res_norm = jnp.sum(residual * residual, axis=-1, keepdims=True)
    for iteration in range(ITERS):
        along = jnp.sum(key_new * direction, axis=-1, keepdims=True)
        image = image_of(direction, slice(0, head_size))
        image = image + strength * key_new * along + ridge * direction
        step = res_norm / jnp.sum(direction * image, axis=-1, keepdims=True)
        found = found + step * direction
        residual = residual - step * image
        next_norm = jnp.sum(residual * residual, axis=-1, keepdims=True)
        direction = residual + (next_norm / res_norm) * direction
        res_norm = next_norm

    total = image_of(found, slice(head_size, 2 * head_size))
    total = total + strength * value_new * jnp.sum(key_new * found, axis=-1, keepdims=True)
    retrieved = total.astype(jnp.bfloat16)
    start = pl.multiple_of(member * head_size, head_size)
    part = jnp.dot(
        retrieved, out_ref[pl.ds(start, head_size), :], preferred_element_type=jnp.float32
    ).astype(jnp.bfloat16)
    half = pair_rows // 2
    for target in range(head_count):
        x = target % 2
        spot = slice(target * half, (target + 1) * half)
        send_ref[spot, :width] = part[x * half : (x + 1) * half]
        send_ref[spot, width:] = retrieved[x * half : (x + 1) * half]


def mlp_kernel(
    shards,
    part_ref,
    tokens_ref,
    gain_ref,
    gate_ref,
    up_ref,
    down_ref,
    mid_ref,
    retrieved_ref,
    send_ref,
):
    shard = lax.axis_index("shard")
    group_rows, width = tokens_ref.shape
    devices = 2 * shards
    req_rows = group_rows // shards
    attended = part_ref[:group_rows, :width].astype(jnp.float32)
    for source in range(1, devices):
        spot = slice(source * group_rows, (source + 1) * group_rows)
        attended += part_ref[spot, :width].astype(jnp.float32)
    mid_rows = (tokens_ref[...] + attended).astype(jnp.bfloat16)
    mlp_in = scaled_norm(mid_rows, gain_ref[...])
    contract = (((1,), (1,)), ((), ()))
    gate_part = lax.dot_general(
        mlp_in, gate_ref[...], contract, preferred_element_type=jnp.float32
    )
    up_part = lax.dot_general(mlp_in, up_ref[...], contract, preferred_element_type=jnp.float32)
    hidden = (silu(gate_part) * up_part).astype(jnp.bfloat16)
    down = jnp.dot(hidden, down_ref[...], preferred_element_type=jnp.float32)
    send_ref[...] = down.reshape(send_ref.shape)

    def home_rows(value):
        row = lax.broadcasted_iota(jnp.int32, value.shape, 0)
        picked = [
            jnp.sum(jnp.where(row == shard * req_rows + i, value, 0.0), axis=0, keepdims=True)
            for i in range(req_rows)
        ]
        return jnp.concatenate(picked, axis=0)

    mid_ref[...] = home_rows(mid_rows.astype(jnp.float32))
    heads = [
        home_rows(
            part_ref[source * group_rows : (source + 1) * group_rows, width:].astype(jnp.float32)
        )
        for source in range(devices)
    ]
    retrieved_ref[...] = jnp.concatenate(heads, axis=1).astype(jnp.bfloat16)


def finish_kernel(shards, down_ref, mid_ref, layer_ref):
    req_rows, width = mid_ref.shape
    rows = down_ref.shape[0] // shards
    total = down_ref[:rows]
    for source in range(1, shards):
        total = total + down_ref[source * rows : (source + 1) * rows]
    layer_ref[...] = (mid_ref[...] + total.reshape(req_rows, width)).astype(jnp.bfloat16)


def head_body(
    tokens,
    norm_gain,
    qkv_weight,
    conv_weight,
    conv_state,
    mesa_gates,
    mesa_bias,
    ridge_term,
    key_cache,
    value_cache,
    log_weight,
    page_owner,
    page_fill,
    out_weight,
    mlp_gain,
    gate_weight,
    up_weight,
    down_weight,
):
    shards = lax.axis_size("shard")
    devices = 2 * shards
    req_rows, width = tokens.shape
    slots, page, _ = key_cache.shape
    head_count = ridge_term.shape[0]
    head_size = width // head_count
    group_rows = shards * req_rows
    pair_rows = 2 * group_rows
    all_slots = devices * slots
    columns = qkv_weight.shape[1]
    shape = jax.ShapeDtypeStruct
    bf16, f32 = jnp.bfloat16, jnp.float32

    def exchange(value, axes):
        return lax.all_to_all(value, axes, split_axis=0, concat_axis=0, tiled=True)

    def spot(number):
        return number % 2 * shards + number // 2

    any_space = pl.BlockSpec(memory_space=pl.ANY)
    hbm = pl.BlockSpec(memory_space=pltpu.HBM)
    past_rows = jnp.transpose(conv_state, (1, 0, 2))
    gates = mesa_gates.T
    pack, misc, *pieces = pl.pallas_call(
        prep_kernel,
        out_shape=(
            shape((devices * TILE, width + page), bf16),
            shape((GATES.stop, width), f32),
        )
        + (shape((2 * slots, page, head_size), bf16),) * devices,
        in_specs=[hbm] * 12,
        out_specs=(VMEM,) * 2 + (any_space,) * devices,
        scratch_shapes=[
            pltpu.VMEM(tokens.shape, bf16),
            pltpu.VMEM(log_weight.shape, bf16),
            pltpu.SMEM(page_owner.shape, jnp.int32),
            pltpu.SMEM(page_fill.shape, jnp.int32),
            pltpu.VMEM(past_rows.shape, bf16),
            pltpu.VMEM(gates.shape, bf16),
            pltpu.VMEM(conv_weight.shape, f32),
            pltpu.VMEM((1, width), f32),
            pltpu.VMEM((1, 2 * head_count), f32),
            pltpu.SMEM(ridge_term.shape, f32),
            pltpu.SemaphoreType.DMA((10,)),
            pltpu.SemaphoreType.DMA((2 * devices,)),
        ],
        compiler_params=WHOLE,
        name="prep",
    )(
        tokens,
        log_weight,
        page_owner,
        page_fill,
        key_cache,
        value_cache,
        past_rows,
        conv_weight,
        norm_gain[None, :],
        gates,
        mesa_bias[None, :],
        ridge_term,
    )
    packs = exchange(pack, PAIR)
    moved = [pieces[0]]
    for apart in range(1, devices):
        pairs = [(spot(source), spot(source ^ apart)) for source in range(devices)]
        moved.append(lax.ppermute(pieces[apart], ("member", "shard"), pairs))

    mixed, own_tokens, weight, owner, strength = pl.pallas_call(
        functools.partial(project_kernel, shards, req_rows, slots, head_count),
        out_shape=(
            shape((devices * group_rows, head_size), bf16),
            shape((group_rows, width), f32),
            shape((all_slots, page), f32),
            shape((all_slots, page), jnp.int32),
            shape((pair_rows + TILE, head_size), f32),
        ),
        in_specs=[VMEM] * 3,
        out_specs=(VMEM,) * 5,
        scratch_shapes=[pltpu.VMEM((group_rows, columns), f32)],
        compiler_params=PARAMS,
        name="project",
    )(packs, misc, qkv_weight)
    all_mixed = exchange(mixed, PAIR)

    gram = pl.pallas_call(
        gram_kernel,
        out_shape=shape((pair_rows, head_size, 2 * head_size), f32),
        in_specs=[SMEM] + [VMEM] * (1 + devices),
        out_specs=VMEM,
        compiler_params=PARAMS,
        name="gram",
    )(owner, weight, *moved)

    parts = pl.pallas_call(
        functools.partial(solve_kernel, head_count, columns // head_size),
        out_shape=shape((devices * group_rows, width + head_size), bf16),
        in_specs=[VMEM] * 4,
        out_specs=VMEM,
        compiler_params=PARAMS,
        name="solve",
    )(all_mixed, strength, gram, out_weight)
    all_parts = exchange(parts, PAIR)

    mid_home, retrieved, down = pl.pallas_call(
        functools.partial(mlp_kernel, shards),
        out_shape=(
            shape((req_rows, width), f32),
            shape((req_rows, width), bf16),
            shape((group_rows * head_count, head_size), f32),
        ),
        in_specs=[VMEM] * 6,
        out_specs=(VMEM,) * 3,
        compiler_params=PARAMS,
        name="mlp",
    )(
        all_parts,
        own_tokens,
        mlp_gain[None, :],
        gate_weight.T,
        up_weight.T,
        down_weight,
    )
    layer_out = pl.pallas_call(
        functools.partial(finish_kernel, shards),
        out_shape=shape((req_rows, width), bf16),
        in_specs=[VMEM] * 2,
        out_specs=VMEM,
        compiler_params=PARAMS,
        name="finish",
    )(exchange(down, "shard"), mid_home)
    return (retrieved, layer_out)


def specs(group):
    rows = P((*group, "shard"))
    return (
        (
            rows,
            P(),
            P(None, "shard"),
            P(None, "shard"),
            P(group, None, "shard"),
            P(),
            P(),
            P(),
            rows,
            rows,
            rows,
            rows,
            rows,
            P("shard", None),
            P(),
            P(None, "shard"),
            P(None, "shard"),
            P("shard", None),
        ),
        (rows, rows),
    )


def solution(mesh):
    groups, shards = mesh.devices.shape

    def run(*args):
        head_count = args[7].shape[0]
        spread = 2 * shards == head_count and args[2].shape[1] // shards <= args[0].shape[1]
        if spread:
            axes = ("pair", "member", "shard")
            used = Mesh(mesh.devices.reshape(groups // 2, 2, shards), axes)
            body, group = head_body, ("pair", "member")
        else:
            used, body, group = mesh, spread_body, ("group",)
        in_specs, out_specs = specs(group)
        return jax.shard_map(
            body, mesh=used, in_specs=in_specs, out_specs=out_specs, check_vma=False
        )(*args)

    return run
```

```python
import functools

import jax
import jax.numpy as jnp
from jax import lax
from jax.experimental import pallas as pl
from jax.experimental.pallas import tpu as pltpu
from jax.sharding import Mesh
from jax.sharding import PartitionSpec as P

ITERS = 4


precise = lax.Precision.HIGHEST

VMEM = pl.BlockSpec(memory_space=pltpu.VMEM)
SMEM = pl.BlockSpec(memory_space=pltpu.SMEM)


def partner(value, axis, apart):
    mask = 2**apart
    pairs = [(source, source ^ mask) for source in range(lax.axis_size(axis))]
    return lax.ppermute(value, axis, pairs)


def scaled_norm(row_vals, gain_vec):
    wide_rows = row_vals.astype(jnp.float32)
    factor = lax.rsqrt(jnp.mean(wide_rows * wide_rows, axis=-1, keepdims=True) + 1e-05)
    return (wide_rows * factor * gain_vec).astype(jnp.bfloat16)


def unit_rows(vectors):
    return vectors * lax.rsqrt(jnp.sum(vectors * vectors, axis=-1, keepdims=True) + 1e-06)


def slot_weights(owner_hot, decay_rows, log_weight, page_fill):
    page_len = log_weight.shape[2]
    slot_decay = jnp.dot(owner_hot, decay_rows, precision=precise)
    live_mask = (jnp.arange(page_len)[None, :] < page_fill[:, None]).astype(jnp.float32)
    return slot_decay[:, :, None] * jnp.exp(log_weight.astype(jnp.float32)) * live_mask[:, None, :]


def slot_terms(key_rows, source_rows, owner_hot, slot_weight, directions):
    slot_count, page_len, width_all = key_rows.shape
    head_count = slot_weight.shape[1]
    head_size = width_all // head_count
    member_count = owner_hot.shape[1]
    slot_dir = jnp.dot(owner_hot, directions.reshape(member_count, width_all), precision=precise)
    slot_dir = slot_dir.reshape(slot_count, head_count, head_size)
    key_wide = key_rows.astype(jnp.float32).reshape(slot_count, page_len, head_count, head_size)
    scores = jnp.einsum("sthd,shd->sht", key_wide, slot_dir, precision=precise)
    source_wide = source_rows.astype(jnp.float32).reshape(
        slot_count, page_len, head_count, head_size
    )
    contribution = jnp.einsum("sht,sthd->shd", slot_weight * scores, source_wide, precision=precise)
    summed = jnp.dot(owner_hot.T, contribution.reshape(slot_count, width_all), precision=precise)
    return summed.reshape(member_count, head_count, head_size)


def new_term(vectors, source_rows, strength_rows, key_new):
    return (
        strength_rows[:, :, None] * source_rows * jnp.sum(key_new * vectors, axis=-1, keepdims=True)
    )


def conjugate(query_rows, key_new, value_new, strength_rows, ridge_term, reduce_fn):
    solution = jnp.zeros_like(query_rows)
    residual = query_rows
    direction = query_rows
    res_norm = jnp.sum(residual * residual, axis=-1)
    for iteration in range(ITERS):
        image_vec = (
            reduce_fn(direction, False)
            + new_term(direction, key_new, strength_rows, key_new)
            + ridge_term[None, :, None] * direction
        )
        step_size = res_norm / jnp.sum(direction * image_vec, axis=-1)
        solution = solution + step_size[:, :, None] * direction
        residual = residual - step_size[:, :, None] * image_vec
        next_norm = jnp.sum(residual * residual, axis=-1)
        direction = residual + (next_norm / res_norm)[:, :, None] * direction
        res_norm = next_norm
    return reduce_fn(solution, True) + new_term(solution, value_new, strength_rows, key_new)


def pair_order(mine, theirs, parity):
    first = jnp.where(parity == 0, mine, theirs)
    second = jnp.where(parity == 0, theirs, mine)
    return jnp.concatenate([first, second], axis=0)


def spread_body(
    tokens,
    norm_gain,
    qkv_weight,
    conv_weight,
    conv_state,
    mesa_gates,
    mesa_bias,
    ridge_term,
    key_cache,
    value_cache,
    log_weight,
    page_owner,
    page_fill,
    out_weight,
    mlp_gain,
    gate_weight,
    up_weight,
    down_weight,
):
    req_rows = tokens.shape[0]
    group_rows = req_rows * lax.axis_size("shard")
    head_count = ridge_term.shape[0]
    width_all = key_cache.shape[2]
    head_size = width_all // head_count
    parity = lax.axis_index("group") % 2
    normed = scaled_norm(tokens, norm_gain)
    fresh_proj = jnp.dot(
        lax.all_gather(normed, "shard", axis=0, tiled=True),
        qkv_weight,
        preferred_element_type=jnp.float32,
    )
    past_rows = conv_state.astype(jnp.float32)
    pre_conv = (
        conv_weight[3] * fresh_proj
        + conv_weight[0] * past_rows[:, 0]
        + conv_weight[1] * past_rows[:, 1]
        + conv_weight[2] * past_rows[:, 2]
    )
    mixed_cols = jax.nn.silu(pre_conv).astype(jnp.bfloat16)
    home_rows = lax.all_to_all(mixed_cols, "shard", split_axis=0, concat_axis=1, tiled=True)
    split_rows = home_rows.astype(jnp.float32).reshape(req_rows, 3, head_count, head_size)
    query_home = unit_rows(split_rows[:, 0])
    key_home = unit_rows(split_rows[:, 1])
    value_home = split_rows[:, 2]
    gate_vals = jax.nn.sigmoid(
        jnp.dot(normed, mesa_gates, preferred_element_type=jnp.float32) + mesa_bias
    )
    decay_home = gate_vals[:, :head_count]
    strength_home = gate_vals[:, head_count:]
    owner_hot = (page_owner[:, None] == jnp.arange(2 * group_rows)[None, :]).astype(jnp.float32)
    stored = {}

    def cache_pass(directions, decay_grp, with_values):
        far_dirs, far_decay = partner((directions, decay_grp), "group", 0)
        pair_dirs = pair_order(directions, far_dirs, parity)
        pair_decay = pair_order(decay_grp, far_decay, parity)
        if "weight" not in stored:
            stored["weight"] = slot_weights(owner_hot, pair_decay, log_weight, page_fill)
        source_rows = value_cache if with_values else key_cache
        summed = slot_terms(key_cache, source_rows, owner_hot, stored["weight"], pair_dirs)
        mine = jnp.where(parity == 0, summed[:group_rows], summed[group_rows:])
        theirs = jnp.where(parity == 0, summed[group_rows:], summed[:group_rows])
        returned = partner(theirs, "group", 0)
        return mine + returned

    def reduce_home(vectors, with_values):
        directions, decay_grp = (
            lax.all_gather(vectors, "shard", axis=0, tiled=True),
            lax.all_gather(decay_home, "shard", axis=0, tiled=True),
        )
        return lax.psum_scatter(
            cache_pass(directions, decay_grp, with_values), "shard", scatter_dimension=0, tiled=True
        )

    found = conjugate(query_home, key_home, value_home, strength_home, ridge_term, reduce_home)
    retrieved = found.reshape(req_rows, width_all).astype(jnp.bfloat16)
    columns = lax.all_to_all(retrieved, "shard", split_axis=1, concat_axis=0, tiled=True)
    attended = lax.psum_scatter(
        jnp.dot(columns, out_weight, preferred_element_type=jnp.float32),
        "shard",
        scatter_dimension=0,
        tiled=True,
    )
    mid_rows = (tokens.astype(jnp.float32) + attended).astype(jnp.bfloat16)
    mlp_in = scaled_norm(mid_rows, mlp_gain)
    piece_rows = lax.all_gather(mlp_in, "shard", axis=0, tiled=True)
    gate_part = jnp.dot(piece_rows, gate_weight, preferred_element_type=jnp.float32)
    up_part = jnp.dot(piece_rows, up_weight, preferred_element_type=jnp.float32)
    hidden_rows = (jax.nn.silu(gate_part) * up_part).astype(jnp.bfloat16)
    down_part = lax.psum_scatter(
        jnp.dot(hidden_rows, down_weight, preferred_element_type=jnp.float32),
        "shard",
        scatter_dimension=0,
        tiled=True,
    )
    layer_out = (mid_rows.astype(jnp.float32) + down_part).astype(jnp.bfloat16)
    return (retrieved, layer_out)


TILE = 8
MASKED = -1e38
PAIR = ("shard", "member")
PARAMS = pltpu.CompilerParams(vmem_limit_bytes=16 * 1024 * 1024)
PAST, TAP, GAIN, BIAS, RIDGE = slice(0, 8), slice(8, 9), slice(9, 10), slice(10, 11), slice(11, 12)
GATES = slice(16, 32)
WHOLE = pltpu.CompilerParams(vmem_limit_bytes=62 * 1024 * 1024)


def split_pair(value):
    high = value.astype(jnp.bfloat16)
    low = (value - high.astype(jnp.float32)).astype(jnp.bfloat16)
    return high, low


def hot(rows, columns, target_fn):
    row = lax.broadcasted_iota(jnp.int32, (rows, columns), 0)
    column = lax.broadcasted_iota(jnp.int32, (rows, columns), 1)
    return jnp.where(column == target_fn(row), 1.0, 0.0).astype(jnp.bfloat16)


def here():
    return lax.axis_index("shard") * 2 + lax.axis_index("member")


def silu(value):
    return value / (1.0 + jnp.exp(-value))


def prep_kernel(
    tokens_hbm,
    logs_hbm,
    owner_hbm,
    fill_hbm,
    past_hbm,
    tap_hbm,
    gain_hbm,
    gates_hbm,
    bias_hbm,
    ridge_hbm,
    send_ref,
    misc_ref,
    tokens_ref,
    logs_ref,
    owner_ref,
    fill_ref,
    state_ref,
    gates_ref,
    tap_ref,
    gain_ref,
    bias_ref,
    ridge_ref,
    sems,
):
    req_rows, width = tokens_ref.shape
    slots, head_count, page = logs_ref.shape
    copies = [
        pltpu.make_async_copy(source, target, sems.at[place])
        for place, (source, target) in enumerate(
            [
                (owner_hbm, owner_ref),
                (fill_hbm, fill_ref),
                (tokens_hbm, tokens_ref),
                (logs_hbm, logs_ref),
                (past_hbm, state_ref),
                (tap_hbm, tap_ref),
                (gain_hbm, gain_ref),
                (gates_hbm, gates_ref),
                (bias_hbm, bias_ref),
                (ridge_hbm, ridge_ref),
            ]
        )
    ]
    for copy in copies:
        copy.start()
    for copy in copies:
        copy.wait()

    tokens = tokens_ref[...].astype(jnp.float32)
    blank = jnp.zeros((TILE - req_rows, width), jnp.float32)
    tile = jnp.concatenate([tokens, blank], axis=0).astype(jnp.bfloat16)
    spot = lax.broadcasted_iota(jnp.int32, (head_count, page), 1)
    logs = []
    lane = lax.broadcasted_iota(jnp.int32, (1, page), 1)
    owners = jnp.zeros((1, page), jnp.float32)
    for slot in range(slots):
        rows = logs_ref[slot].astype(jnp.float32)
        logs.append(jnp.where(spot < fill_ref[slot], rows, MASKED))
        owners = jnp.where(lane == slot, owner_ref[slot].astype(jnp.float32), owners)
    rest = jnp.zeros((TILE - slots - 1, page), jnp.float32)
    for head in range(head_count):
        rows = [log[head : head + 1, :] for log in logs]
        side = jnp.concatenate([*rows, owners, rest], axis=0).astype(jnp.bfloat16)
        send_ref[head * TILE : (head + 1) * TILE, :width] = tile
        send_ref[head * TILE : (head + 1) * TILE, width:] = side

    past = tap_ref[0:1, :] * state_ref[0].astype(jnp.float32)
    past = past + tap_ref[1:2, :] * state_ref[1].astype(jnp.float32)
    past = past + tap_ref[2:3, :] * state_ref[2].astype(jnp.float32)
    columns = past.shape[1]
    misc_ref[PAST, :columns] = past
    misc_ref[TAP, :columns] = tap_ref[3:4, :]
    misc_ref[GAIN, :] = gain_ref[...]
    misc_ref[BIAS, : 2 * head_count] = bias_ref[...]
    ridges = jnp.zeros((1, page), jnp.float32)
    for head in range(head_count):
        ridges = jnp.where(lane == head, ridge_ref[head], ridges)
    misc_ref[RIDGE, :page] = ridges
    misc_ref[GATES, :] = gates_ref[...].astype(jnp.float32)


def spread_kernel(key_ref, value_ref, *refs):
    *piece_refs, sems = refs
    slots = key_ref.shape[0]
    head_size = piece_refs[0].shape[2]
    me = here()
    copies = []
    for apart, piece_ref in enumerate(piece_refs):
        start = pl.multiple_of((me ^ apart) * head_size, head_size)
        for part, cache in enumerate((key_ref, value_ref)):
            copies.append(
                pltpu.make_async_copy(
                    cache.at[:, :, pl.ds(start, head_size)],
                    piece_ref.at[pl.ds(part * slots, slots)],
                    sems.at[2 * apart + part],
                )
            )
    for copy in copies:
        copy.start()
    for copy in copies:
        copy.wait()


def project_kernel(
    shards,
    req_rows,
    slots,
    head_count,
    pack_ref,
    misc_ref,
    qkv_ref,
    send_ref,
    tokens_ref,
    weight_ref,
    owner_ref,
    strength_ref,
    mixed_ref,
):
    shard = lax.axis_index("shard")
    member = lax.axis_index("member")
    head = here()
    group_rows = shards * req_rows
    pair_rows = 2 * group_rows
    packed = 2 * shards * TILE
    width = misc_ref.shape[1]
    columns = qkv_ref.shape[1]
    page = weight_ref.shape[1]
    head_size = send_ref.shape[1]
    blocks = columns // head_size

    def home_of(row):
        x = row // group_rows
        s = (row % group_rows) // req_rows
        return (s * 2 + x) * TILE + row % req_rows

    pick_pair = hot(pair_rows, packed, home_of)
    pick_group = hot(group_rows, packed, lambda row: home_of(row + member * group_rows))
    rows = pack_ref[:, :width]
    pair_tokens = jnp.dot(pick_pair, rows, preferred_element_type=jnp.float32)
    own_tokens = jnp.dot(pick_group, rows, preferred_element_type=jnp.float32)
    tokens_ref[...] = own_tokens
    own = scaled_norm(own_tokens, misc_ref[GAIN, :])
    fresh = jnp.dot(own, qkv_ref[...], preferred_element_type=jnp.float32)
    before = misc_ref[TAP, :columns] * fresh + misc_ref[PAST, :columns]
    mixed_ref[...] = silu(before)
    for target in range(head_count):
        place = jnp.int32(0)
        for part in range(3):
            local = target + part * head_count - shard * blocks
            place = jnp.where((local >= 0) & (local < blocks), local, place)
        start = pl.multiple_of(place * head_size, head_size)
        send_ref[target * group_rows : (target + 1) * group_rows, :] = mixed_ref[
            :, pl.ds(start, head_size)
        ].astype(jnp.bfloat16)

    normed = scaled_norm(pair_tokens, misc_ref[GAIN, :])
    raw = lax.dot_general(
        normed,
        misc_ref[GATES, :].astype(jnp.bfloat16),
        (((1,), (1,)), ((), ())),
        preferred_element_type=jnp.float32,
    )
    gate_vals = 1.0 / (1.0 + jnp.exp(-(raw + misc_ref[BIAS, : 2 * head_count])))
    column = lax.broadcasted_iota(jnp.int32, gate_vals.shape, 1)
    decay = jnp.sum(jnp.where(column == head, gate_vals, 0.0), axis=1, keepdims=True)
    strength = jnp.sum(
        jnp.where(column == head + head_count, gate_vals, 0.0), axis=1, keepdims=True
    )
    strength_ref[:pair_rows, :] = jnp.broadcast_to(strength, (pair_rows, head_size))
    ridges = misc_ref[RIDGE, :page]
    spot = lax.broadcasted_iota(jnp.int32, ridges.shape, 1)
    ridge = jnp.sum(jnp.where(spot == head, ridges, 0.0), axis=1, keepdims=True)
    strength_ref[pair_rows:, :] = jnp.broadcast_to(ridge, (TILE, head_size))

    all_slots = 2 * shards * slots
    side = pack_ref[:, width:]
    pick_slot = hot(all_slots, packed, lambda row: (row // slots) * TILE + row % slots)
    logs = jnp.dot(pick_slot, side, preferred_element_type=jnp.float32)
    pick_owner = hot(all_slots, packed, lambda row: (row // slots) * TILE + slots)
    owners = jnp.dot(pick_owner, side, preferred_element_type=jnp.float32)
    at_slot = hot(all_slots, page, lambda row: row % slots).astype(jnp.float32)
    owner = jnp.sum(at_slot * owners, axis=1, keepdims=True).astype(jnp.int32)
    owner_ref[...] = jnp.broadcast_to(owner, owner_ref.shape)
    request = lax.broadcasted_iota(jnp.int32, (all_slots, pair_rows), 1)
    owner_hot = jnp.where(request == owner, 1.0, 0.0)
    wide_decay = jnp.broadcast_to(decay, (pair_rows, page))
    slot_decay = jnp.dot(
        owner_hot, wide_decay, precision=precise, preferred_element_type=jnp.float32
    )
    weight_ref[...] = slot_decay * jnp.exp(logs)


def gram_kernel(owner_ref, weight_ref, *refs):
    *piece_refs, gram_ref = refs
    head = here()
    slots = piece_refs[0].shape[0] // 2
    gram_ref[...] = jnp.zeros_like(gram_ref)
    for apart, piece_ref in enumerate(piece_refs):
        for spot in range(slots):
            slot = (head ^ apart) * slots + spot
            keys = piece_ref[spot]
            both = jnp.concatenate([keys, piece_ref[slots + spot]], axis=1)
            turned = keys.T.astype(jnp.float32) * weight_ref[pl.ds(slot, 1), :]
            high, low = split_pair(turned)
            piece = jnp.dot(high, both, preferred_element_type=jnp.float32) + jnp.dot(
                low, both, preferred_element_type=jnp.float32
            )
            owner = owner_ref[slot, 0]
            gram_ref[owner] = gram_ref[owner] + piece


def solve_kernel(
    head_count, blocks, mixed_ref, strength_ref, gram_ref, out_ref, send_ref
):
    head = here()
    member = lax.axis_index("member")
    pair_rows, head_size, _ = gram_ref.shape
    width = out_ref.shape[1]

    def columns_of(block):
        first = pl.multiple_of(block // blocks * pair_rows, pair_rows)
        return mixed_ref[pl.ds(first, pair_rows), :].astype(jnp.float32)

    query = unit_rows(columns_of(head))
    key_new = unit_rows(columns_of(head + head_count))
    value_new = columns_of(head + 2 * head_count)
    strength = strength_ref[:pair_rows, :]
    ridge = strength_ref[pair_rows : pair_rows + 1, :]

    def image_of(vectors, columns):
        turned = vectors.T
        pieces = []
        for row in range(pair_rows):
            spread = jnp.broadcast_to(turned[:, row : row + 1], (head_size, head_size))
            pieces.append(jnp.sum(gram_ref[row, :, columns] * spread, axis=0, keepdims=True))
        return jnp.concatenate(pieces, axis=0)

    found = jnp.zeros_like(query)
    residual = query
    direction = query
    res_norm = jnp.sum(residual * residual, axis=-1, keepdims=True)
    for iteration in range(ITERS):
        along = jnp.sum(key_new * direction, axis=-1, keepdims=True)
        image = image_of(direction, slice(0, head_size))
        image = image + strength * key_new * along + ridge * direction
        step = res_norm / jnp.sum(direction * image, axis=-1, keepdims=True)
        found = found + step * direction
        residual = residual - step * image
        next_norm = jnp.sum(residual * residual, axis=-1, keepdims=True)
        direction = residual + (next_norm / res_norm) * direction
        res_norm = next_norm

    total = image_of(found, slice(head_size, 2 * head_size))
    total = total + strength * value_new * jnp.sum(key_new * found, axis=-1, keepdims=True)
    retrieved = total.astype(jnp.bfloat16)
    start = pl.multiple_of(member * head_size, head_size)
    part = jnp.dot(
        retrieved, out_ref[pl.ds(start, head_size), :], preferred_element_type=jnp.float32
    ).astype(jnp.bfloat16)
    half = pair_rows // 2
    for target in range(head_count):
        x = target % 2
        spot = slice(target * half, (target + 1) * half)
        send_ref[spot, :width] = part[x * half : (x + 1) * half]
        send_ref[spot, width:] = retrieved[x * half : (x + 1) * half]


def mlp_kernel(
    shards,
    part_ref,
    tokens_ref,
    gain_ref,
    gate_ref,
    up_ref,
    down_ref,
    mid_ref,
    retrieved_ref,
    send_ref,
):
    shard = lax.axis_index("shard")
    group_rows, width = tokens_ref.shape
    devices = 2 * shards
    req_rows = group_rows // shards
    attended = part_ref[:group_rows, :width].astype(jnp.float32)
    for source in range(1, devices):
        spot = slice(source * group_rows, (source + 1) * group_rows)
        attended += part_ref[spot, :width].astype(jnp.float32)
    mid_rows = (tokens_ref[...] + attended).astype(jnp.bfloat16)
    mlp_in = scaled_norm(mid_rows, gain_ref[...])
    contract = (((1,), (1,)), ((), ()))
    gate_part = lax.dot_general(
        mlp_in, gate_ref[...], contract, preferred_element_type=jnp.float32
    )
    up_part = lax.dot_general(mlp_in, up_ref[...], contract, preferred_element_type=jnp.float32)
    hidden = (silu(gate_part) * up_part).astype(jnp.bfloat16)
    down = jnp.dot(hidden, down_ref[...], preferred_element_type=jnp.float32)
    send_ref[...] = down.reshape(send_ref.shape)

    def home_rows(value):
        row = lax.broadcasted_iota(jnp.int32, value.shape, 0)
        picked = [
            jnp.sum(jnp.where(row == shard * req_rows + i, value, 0.0), axis=0, keepdims=True)
            for i in range(req_rows)
        ]
        return jnp.concatenate(picked, axis=0)

    mid_ref[...] = home_rows(mid_rows.astype(jnp.float32))
    heads = [
        home_rows(
            part_ref[source * group_rows : (source + 1) * group_rows, width:].astype(jnp.float32)
        )
        for source in range(devices)
    ]
    retrieved_ref[...] = jnp.concatenate(heads, axis=1).astype(jnp.bfloat16)


def finish_kernel(shards, down_ref, mid_ref, layer_ref):
    req_rows, width = mid_ref.shape
    rows = down_ref.shape[0] // shards
    total = down_ref[:rows]
    for source in range(1, shards):
        total = total + down_ref[source * rows : (source + 1) * rows]
    layer_ref[...] = (mid_ref[...] + total.reshape(req_rows, width)).astype(jnp.bfloat16)


def far_first(apart):
    return (-bin(apart & ~2).count("1"), apart & 2, apart)


def head_body(
    tokens,
    norm_gain,
    qkv_weight,
    conv_weight,
    conv_state,
    mesa_gates,
    mesa_bias,
    ridge_term,
    key_cache,
    value_cache,
    log_weight,
    page_owner,
    page_fill,
    out_weight,
    mlp_gain,
    gate_weight,
    up_weight,
    down_weight,
):
    shards = lax.axis_size("shard")
    devices = 2 * shards
    req_rows, width = tokens.shape
    slots, page, _ = key_cache.shape
    head_count = ridge_term.shape[0]
    head_size = width // head_count
    group_rows = shards * req_rows
    pair_rows = 2 * group_rows
    all_slots = devices * slots
    columns = qkv_weight.shape[1]
    shape = jax.ShapeDtypeStruct
    bf16, f32 = jnp.bfloat16, jnp.float32

    def exchange(value, axes):
        return lax.all_to_all(value, axes, split_axis=0, concat_axis=0, tiled=True)

    def spot(number):
        return number % 2 * shards + number // 2

    any_space = pl.BlockSpec(memory_space=pl.ANY)
    hbm = pl.BlockSpec(memory_space=pltpu.HBM)
    past_rows = jnp.transpose(conv_state, (1, 0, 2))
    gates = mesa_gates.T
    pack, misc = pl.pallas_call(
        prep_kernel,
        out_shape=(
            shape((devices * TILE, width + page), bf16),
            shape((GATES.stop, width), f32),
        ),
        in_specs=[hbm] * 10,
        out_specs=(VMEM,) * 2,
        scratch_shapes=[
            pltpu.VMEM(tokens.shape, bf16),
            pltpu.VMEM(log_weight.shape, bf16),
            pltpu.SMEM(page_owner.shape, jnp.int32),
            pltpu.SMEM(page_fill.shape, jnp.int32),
            pltpu.VMEM(past_rows.shape, bf16),
            pltpu.VMEM(gates.shape, bf16),
            pltpu.VMEM(conv_weight.shape, f32),
            pltpu.VMEM((1, width), f32),
            pltpu.VMEM((1, 2 * head_count), f32),
            pltpu.SMEM(ridge_term.shape, f32),
            pltpu.SemaphoreType.DMA((10,)),
        ],
        compiler_params=WHOLE,
        name="prep",
    )(
        tokens,
        log_weight,
        page_owner,
        page_fill,
        past_rows,
        conv_weight,
        norm_gain[None, :],
        gates,
        mesa_bias[None, :],
        ridge_term,
    )
    packs = exchange(pack, PAIR)
    pieces = pl.pallas_call(
        spread_kernel,
        out_shape=(shape((2 * slots, page, head_size), bf16),) * devices,
        in_specs=[any_space] * 2,
        out_specs=(any_space,) * devices,
        scratch_shapes=[pltpu.SemaphoreType.DMA((2 * devices,))],
        compiler_params=PARAMS,
        name="spread",
    )(key_cache, value_cache)
    pieces, packs = lax.optimization_barrier((pieces, packs))
    moved = list(pieces)
    for apart in sorted(range(1, devices), key=far_first):
        pairs = [(spot(source), spot(source ^ apart)) for source in range(devices)]
        moved[apart] = lax.ppermute(pieces[apart], ("member", "shard"), pairs)

    mixed, own_tokens, weight, owner, strength = pl.pallas_call(
        functools.partial(project_kernel, shards, req_rows, slots, head_count),
        out_shape=(
            shape((devices * group_rows, head_size), bf16),
            shape((group_rows, width), f32),
            shape((all_slots, page), f32),
            shape((all_slots, page), jnp.int32),
            shape((pair_rows + TILE, head_size), f32),
        ),
        in_specs=[VMEM] * 3,
        out_specs=(VMEM,) * 5,
        scratch_shapes=[pltpu.VMEM((group_rows, columns), f32)],
        compiler_params=PARAMS,
        name="project",
    )(packs, misc, qkv_weight)
    all_mixed = exchange(mixed, PAIR)

    gram = pl.pallas_call(
        gram_kernel,
        out_shape=shape((pair_rows, head_size, 2 * head_size), f32),
        in_specs=[SMEM] + [VMEM] * (1 + devices),
        out_specs=VMEM,
        compiler_params=PARAMS,
        name="gram",
    )(owner, weight, *moved)

    parts = pl.pallas_call(
        functools.partial(solve_kernel, head_count, columns // head_size),
        out_shape=shape((devices * group_rows, width + head_size), bf16),
        in_specs=[VMEM] * 4,
        out_specs=VMEM,
        compiler_params=PARAMS,
        name="solve",
    )(all_mixed, strength, gram, out_weight)
    all_parts = exchange(parts, PAIR)

    mid_home, retrieved, down = pl.pallas_call(
        functools.partial(mlp_kernel, shards),
        out_shape=(
            shape((req_rows, width), f32),
            shape((req_rows, width), bf16),
            shape((group_rows * head_count, head_size), f32),
        ),
        in_specs=[VMEM] * 6,
        out_specs=(VMEM,) * 3,
        compiler_params=PARAMS,
        name="mlp",
    )(
        all_parts,
        own_tokens,
        mlp_gain[None, :],
        gate_weight.T,
        up_weight.T,
        down_weight,
    )
    layer_out = pl.pallas_call(
        functools.partial(finish_kernel, shards),
        out_shape=shape((req_rows, width), bf16),
        in_specs=[VMEM] * 2,
        out_specs=VMEM,
        compiler_params=PARAMS,
        name="finish",
    )(exchange(down, "shard"), mid_home)
    return (retrieved, layer_out)


def specs(group):
    rows = P((*group, "shard"))
    return (
        (
            rows,
            P(),
            P(None, "shard"),
            P(None, "shard"),
            P(group, None, "shard"),
            P(),
            P(),
            P(),
            rows,
            rows,
            rows,
            rows,
            rows,
            P("shard", None),
            P(),
            P(None, "shard"),
            P(None, "shard"),
            P("shard", None),
        ),
        (rows, rows),
    )


def solution(mesh):
    groups, shards = mesh.devices.shape

    def run(*args):
        head_count = args[7].shape[0]
        spread = 2 * shards == head_count and args[2].shape[1] // shards <= args[0].shape[1]
        if spread:
            axes = ("pair", "member", "shard")
            used = Mesh(mesh.devices.reshape(groups // 2, 2, shards), axes)
            body, group = head_body, ("pair", "member")
        else:
            used, body, group = mesh, spread_body, ("group",)
        in_specs, out_specs = specs(group)
        return jax.shard_map(
            body, mesh=used, in_specs=in_specs, out_specs=out_specs, check_vma=False
        )(*args)

    return run
```

```python
import functools

import jax
import jax.numpy as jnp
from jax import lax
from jax.experimental import pallas as pl
from jax.experimental.pallas import tpu as pltpu
from jax.sharding import Mesh
from jax.sharding import PartitionSpec as P

ITERS = 4


precise = lax.Precision.HIGHEST

VMEM = pl.BlockSpec(memory_space=pltpu.VMEM)
SMEM = pl.BlockSpec(memory_space=pltpu.SMEM)


def partner(value, axis, apart):
    mask = 2**apart
    pairs = [(source, source ^ mask) for source in range(lax.axis_size(axis))]
    return lax.ppermute(value, axis, pairs)


def scaled_norm(row_vals, gain_vec):
    wide_rows = row_vals.astype(jnp.float32)
    factor = lax.rsqrt(jnp.mean(wide_rows * wide_rows, axis=-1, keepdims=True) + 1e-05)
    return (wide_rows * factor * gain_vec).astype(jnp.bfloat16)


def unit_rows(vectors):
    return vectors * lax.rsqrt(jnp.sum(vectors * vectors, axis=-1, keepdims=True) + 1e-06)


def slot_weights(owner_hot, decay_rows, log_weight, page_fill):
    page_len = log_weight.shape[2]
    slot_decay = jnp.dot(owner_hot, decay_rows, precision=precise)
    live_mask = (jnp.arange(page_len)[None, :] < page_fill[:, None]).astype(jnp.float32)
    return slot_decay[:, :, None] * jnp.exp(log_weight.astype(jnp.float32)) * live_mask[:, None, :]


def slot_terms(key_rows, source_rows, owner_hot, slot_weight, directions):
    slot_count, page_len, width_all = key_rows.shape
    head_count = slot_weight.shape[1]
    head_size = width_all // head_count
    member_count = owner_hot.shape[1]
    slot_dir = jnp.dot(owner_hot, directions.reshape(member_count, width_all), precision=precise)
    slot_dir = slot_dir.reshape(slot_count, head_count, head_size)
    key_wide = key_rows.astype(jnp.float32).reshape(slot_count, page_len, head_count, head_size)
    scores = jnp.einsum("sthd,shd->sht", key_wide, slot_dir, precision=precise)
    source_wide = source_rows.astype(jnp.float32).reshape(
        slot_count, page_len, head_count, head_size
    )
    contribution = jnp.einsum("sht,sthd->shd", slot_weight * scores, source_wide, precision=precise)
    summed = jnp.dot(owner_hot.T, contribution.reshape(slot_count, width_all), precision=precise)
    return summed.reshape(member_count, head_count, head_size)


def new_term(vectors, source_rows, strength_rows, key_new):
    return (
        strength_rows[:, :, None] * source_rows * jnp.sum(key_new * vectors, axis=-1, keepdims=True)
    )


def conjugate(query_rows, key_new, value_new, strength_rows, ridge_term, reduce_fn):
    solution = jnp.zeros_like(query_rows)
    residual = query_rows
    direction = query_rows
    res_norm = jnp.sum(residual * residual, axis=-1)
    for iteration in range(ITERS):
        image_vec = (
            reduce_fn(direction, False)
            + new_term(direction, key_new, strength_rows, key_new)
            + ridge_term[None, :, None] * direction
        )
        step_size = res_norm / jnp.sum(direction * image_vec, axis=-1)
        solution = solution + step_size[:, :, None] * direction
        residual = residual - step_size[:, :, None] * image_vec
        next_norm = jnp.sum(residual * residual, axis=-1)
        direction = residual + (next_norm / res_norm)[:, :, None] * direction
        res_norm = next_norm
    return reduce_fn(solution, True) + new_term(solution, value_new, strength_rows, key_new)


def pair_order(mine, theirs, parity):
    first = jnp.where(parity == 0, mine, theirs)
    second = jnp.where(parity == 0, theirs, mine)
    return jnp.concatenate([first, second], axis=0)


def spread_body(
    tokens,
    norm_gain,
    qkv_weight,
    conv_weight,
    conv_state,
    mesa_gates,
    mesa_bias,
    ridge_term,
    key_cache,
    value_cache,
    log_weight,
    page_owner,
    page_fill,
    out_weight,
    mlp_gain,
    gate_weight,
    up_weight,
    down_weight,
):
    req_rows = tokens.shape[0]
    group_rows = req_rows * lax.axis_size("shard")
    head_count = ridge_term.shape[0]
    width_all = key_cache.shape[2]
    head_size = width_all // head_count
    parity = lax.axis_index("group") % 2
    normed = scaled_norm(tokens, norm_gain)
    fresh_proj = jnp.dot(
        lax.all_gather(normed, "shard", axis=0, tiled=True),
        qkv_weight,
        preferred_element_type=jnp.float32,
    )
    past_rows = conv_state.astype(jnp.float32)
    pre_conv = (
        conv_weight[3] * fresh_proj
        + conv_weight[0] * past_rows[:, 0]
        + conv_weight[1] * past_rows[:, 1]
        + conv_weight[2] * past_rows[:, 2]
    )
    mixed_cols = jax.nn.silu(pre_conv).astype(jnp.bfloat16)
    home_rows = lax.all_to_all(mixed_cols, "shard", split_axis=0, concat_axis=1, tiled=True)
    split_rows = home_rows.astype(jnp.float32).reshape(req_rows, 3, head_count, head_size)
    query_home = unit_rows(split_rows[:, 0])
    key_home = unit_rows(split_rows[:, 1])
    value_home = split_rows[:, 2]
    gate_vals = jax.nn.sigmoid(
        jnp.dot(normed, mesa_gates, preferred_element_type=jnp.float32) + mesa_bias
    )
    decay_home = gate_vals[:, :head_count]
    strength_home = gate_vals[:, head_count:]
    owner_hot = (page_owner[:, None] == jnp.arange(2 * group_rows)[None, :]).astype(jnp.float32)
    stored = {}

    def cache_pass(directions, decay_grp, with_values):
        far_dirs, far_decay = partner((directions, decay_grp), "group", 0)
        pair_dirs = pair_order(directions, far_dirs, parity)
        pair_decay = pair_order(decay_grp, far_decay, parity)
        if "weight" not in stored:
            stored["weight"] = slot_weights(owner_hot, pair_decay, log_weight, page_fill)
        source_rows = value_cache if with_values else key_cache
        summed = slot_terms(key_cache, source_rows, owner_hot, stored["weight"], pair_dirs)
        mine = jnp.where(parity == 0, summed[:group_rows], summed[group_rows:])
        theirs = jnp.where(parity == 0, summed[group_rows:], summed[:group_rows])
        returned = partner(theirs, "group", 0)
        return mine + returned

    def reduce_home(vectors, with_values):
        directions, decay_grp = (
            lax.all_gather(vectors, "shard", axis=0, tiled=True),
            lax.all_gather(decay_home, "shard", axis=0, tiled=True),
        )
        return lax.psum_scatter(
            cache_pass(directions, decay_grp, with_values), "shard", scatter_dimension=0, tiled=True
        )

    found = conjugate(query_home, key_home, value_home, strength_home, ridge_term, reduce_home)
    retrieved = found.reshape(req_rows, width_all).astype(jnp.bfloat16)
    columns = lax.all_to_all(retrieved, "shard", split_axis=1, concat_axis=0, tiled=True)
    attended = lax.psum_scatter(
        jnp.dot(columns, out_weight, preferred_element_type=jnp.float32),
        "shard",
        scatter_dimension=0,
        tiled=True,
    )
    mid_rows = (tokens.astype(jnp.float32) + attended).astype(jnp.bfloat16)
    mlp_in = scaled_norm(mid_rows, mlp_gain)
    piece_rows = lax.all_gather(mlp_in, "shard", axis=0, tiled=True)
    gate_part = jnp.dot(piece_rows, gate_weight, preferred_element_type=jnp.float32)
    up_part = jnp.dot(piece_rows, up_weight, preferred_element_type=jnp.float32)
    hidden_rows = (jax.nn.silu(gate_part) * up_part).astype(jnp.bfloat16)
    down_part = lax.psum_scatter(
        jnp.dot(hidden_rows, down_weight, preferred_element_type=jnp.float32),
        "shard",
        scatter_dimension=0,
        tiled=True,
    )
    layer_out = (mid_rows.astype(jnp.float32) + down_part).astype(jnp.bfloat16)
    return (retrieved, layer_out)


TILE = 8
MASKED = -1e38
PAIR = ("shard", "member")
PARAMS = pltpu.CompilerParams(vmem_limit_bytes=16 * 1024 * 1024)
PAST, TAP, GAIN, BIAS, RIDGE = slice(0, 8), slice(8, 9), slice(9, 10), slice(10, 11), slice(11, 12)
GATES = slice(16, 32)

SEND = ((0, 0), (1, 4), (4, 1), (3, 6), (6, 3), (5, 5), (7, 7), (2, 2))
FROM = tuple((b, a) if a & 2 else (a, b) for a, b in SEND)
EARLY = 2
FIRST = 5


def split_pair(value):
    high = value.astype(jnp.bfloat16)
    low = (value - high.astype(jnp.float32)).astype(jnp.bfloat16)
    return high, low


def hot(rows, columns, target_fn):
    row = lax.broadcasted_iota(jnp.int32, (rows, columns), 0)
    column = lax.broadcasted_iota(jnp.int32, (rows, columns), 1)
    return jnp.where(column == target_fn(row), 1.0, 0.0).astype(jnp.bfloat16)


def here():
    return lax.axis_index("shard") * 2 + lax.axis_index("member")


def at_step(table, step, me):
    return me ^ jnp.where((me & 2) == 0, table[step][0], table[step][1])


def silu(value):
    return value / (1.0 + jnp.exp(-value))


def prep_kernel(
    tokens_hbm,
    logs_hbm,
    owner_hbm,
    fill_hbm,
    key_hbm,
    value_hbm,
    past_hbm,
    tap_hbm,
    gain_hbm,
    gates_hbm,
    bias_hbm,
    ridge_hbm,
    send_ref,
    misc_ref,
    *refs,
):
    *piece_refs, tokens_ref, logs_ref, owner_ref, fill_ref, state_ref, gates_ref = refs[:-9]
    tap_ref, gain_ref, bias_ref, ridge_ref, keys_ref, values_ref, sems, load_sems, cut_sems = refs[-9:]
    me = here()
    req_rows, width = tokens_ref.shape
    slots, head_count, page = logs_ref.shape
    head_size = piece_refs[0].shape[2]
    copies = [
        pltpu.make_async_copy(source, target, sems.at[place])
        for place, (source, target) in enumerate(
            [
                (owner_hbm, owner_ref),
                (fill_hbm, fill_ref),
                (tokens_hbm, tokens_ref),
                (logs_hbm, logs_ref),
                (past_hbm, state_ref),
                (tap_hbm, tap_ref),
                (gain_hbm, gain_ref),
                (gates_hbm, gates_ref),
                (bias_hbm, bias_ref),
                (ridge_hbm, ridge_ref),
            ]
        )
    ]
    loads = [
        [
            pltpu.make_async_copy(
                source.at[slot], target.at[slot], load_sems.at[part * source.shape[0] + slot]
            )
            for slot in range(source.shape[0])
        ]
        for part, (source, target) in enumerate(((key_hbm, keys_ref), (value_hbm, values_ref)))
    ]
    for copy in [*copies, *loads[0], *loads[1]]:
        copy.start()
    cuts = []
    for part, cache in enumerate((keys_ref, values_ref)):
        for copy in loads[part]:
            copy.wait()
        for step, piece_ref in enumerate(piece_refs):
            start = pl.multiple_of(at_step(SEND, step, me) * head_size, head_size)
            cut = pltpu.make_async_copy(
                cache.at[:, :, pl.ds(start, head_size)],
                piece_ref.at[pl.ds(part * cache.shape[0], cache.shape[0])],
                cut_sems.at[2 * step + part],
            )
            cut.start()
            cuts.append(cut)
    for copy in copies:
        copy.wait()

    tokens = tokens_ref[...].astype(jnp.float32)
    blank = jnp.zeros((TILE - req_rows, width), jnp.float32)
    tile = jnp.concatenate([tokens, blank], axis=0).astype(jnp.bfloat16)
    spot = lax.broadcasted_iota(jnp.int32, (head_count, page), 1)
    logs = []
    lane = lax.broadcasted_iota(jnp.int32, (1, page), 1)
    owners = jnp.zeros((1, page), jnp.float32)
    for slot in range(slots):
        rows = logs_ref[slot].astype(jnp.float32)
        logs.append(jnp.where(spot < fill_ref[slot], rows, MASKED))
        owners = jnp.where(lane == slot, owner_ref[slot].astype(jnp.float32), owners)
    rest = jnp.zeros((TILE - slots - 1, page), jnp.float32)
    for head in range(head_count):
        rows = [log[head : head + 1, :] for log in logs]
        side = jnp.concatenate([*rows, owners, rest], axis=0).astype(jnp.bfloat16)
        send_ref[head * TILE : (head + 1) * TILE, :width] = tile
        send_ref[head * TILE : (head + 1) * TILE, width:] = side

    past = tap_ref[0:1, :] * state_ref[0].astype(jnp.float32)
    past = past + tap_ref[1:2, :] * state_ref[1].astype(jnp.float32)
    past = past + tap_ref[2:3, :] * state_ref[2].astype(jnp.float32)
    columns = past.shape[1]
    misc_ref[PAST, :columns] = past
    misc_ref[TAP, :columns] = tap_ref[3:4, :]
    misc_ref[GAIN, :] = gain_ref[...]
    misc_ref[BIAS, : 2 * head_count] = bias_ref[...]
    ridges = jnp.zeros((1, page), jnp.float32)
    for head in range(head_count):
        ridges = jnp.where(lane == head, ridge_ref[head], ridges)
    misc_ref[RIDGE, :page] = ridges
    misc_ref[GATES, :] = gates_ref[...].astype(jnp.float32)
    for cut in cuts:
        cut.wait()


def project_kernel(
    shards,
    req_rows,
    slots,
    head_count,
    pack_ref,
    misc_ref,
    qkv_ref,
    send_ref,
    tokens_ref,
    weight_ref,
    owner_ref,
    strength_ref,
    mixed_ref,
):
    shard = lax.axis_index("shard")
    member = lax.axis_index("member")
    head = here()
    group_rows = shards * req_rows
    pair_rows = 2 * group_rows
    packed = 2 * shards * TILE
    width = misc_ref.shape[1]
    columns = qkv_ref.shape[1]
    page = weight_ref.shape[1]
    head_size = send_ref.shape[1]
    blocks = columns // head_size

    def home_of(row):
        x = row // group_rows
        s = (row % group_rows) // req_rows
        return (s * 2 + x) * TILE + row % req_rows

    pick_pair = hot(pair_rows, packed, home_of)
    pick_group = hot(group_rows, packed, lambda row: home_of(row + member * group_rows))
    rows = pack_ref[:, :width]
    pair_tokens = jnp.dot(pick_pair, rows, preferred_element_type=jnp.float32)
    own_tokens = jnp.dot(pick_group, rows, preferred_element_type=jnp.float32)
    tokens_ref[...] = own_tokens
    own = scaled_norm(own_tokens, misc_ref[GAIN, :])
    fresh = jnp.dot(own, qkv_ref[...], preferred_element_type=jnp.float32)
    before = misc_ref[TAP, :columns] * fresh + misc_ref[PAST, :columns]
    mixed_ref[...] = silu(before)
    for target in range(head_count):
        place = jnp.int32(0)
        for part in range(3):
            local = target + part * head_count - shard * blocks
            place = jnp.where((local >= 0) & (local < blocks), local, place)
        start = pl.multiple_of(place * head_size, head_size)
        send_ref[target * group_rows : (target + 1) * group_rows, :] = mixed_ref[
            :, pl.ds(start, head_size)
        ].astype(jnp.bfloat16)

    normed = scaled_norm(pair_tokens, misc_ref[GAIN, :])
    raw = lax.dot_general(
        normed,
        misc_ref[GATES, :].astype(jnp.bfloat16),
        (((1,), (1,)), ((), ())),
        preferred_element_type=jnp.float32,
    )
    gate_vals = 1.0 / (1.0 + jnp.exp(-(raw + misc_ref[BIAS, : 2 * head_count])))
    column = lax.broadcasted_iota(jnp.int32, gate_vals.shape, 1)
    decay = jnp.sum(jnp.where(column == head, gate_vals, 0.0), axis=1, keepdims=True)
    strength = jnp.sum(
        jnp.where(column == head + head_count, gate_vals, 0.0), axis=1, keepdims=True
    )
    strength_ref[:pair_rows, :] = jnp.broadcast_to(strength, (pair_rows, head_size))
    ridges = misc_ref[RIDGE, :page]
    spot = lax.broadcasted_iota(jnp.int32, ridges.shape, 1)
    ridge = jnp.sum(jnp.where(spot == head, ridges, 0.0), axis=1, keepdims=True)
    strength_ref[pair_rows:, :] = jnp.broadcast_to(ridge, (TILE, head_size))

    all_slots = 2 * shards * slots
    side = pack_ref[:, width:]
    pick_slot = hot(all_slots, packed, lambda row: (row // slots) * TILE + row % slots)
    logs = jnp.dot(pick_slot, side, preferred_element_type=jnp.float32)
    pick_owner = hot(all_slots, packed, lambda row: (row // slots) * TILE + slots)
    owners = jnp.dot(pick_owner, side, preferred_element_type=jnp.float32)
    at_slot = hot(all_slots, page, lambda row: row % slots).astype(jnp.float32)
    owner = jnp.sum(at_slot * owners, axis=1, keepdims=True).astype(jnp.int32)
    owner_ref[...] = jnp.broadcast_to(owner, owner_ref.shape)
    request = lax.broadcasted_iota(jnp.int32, (all_slots, pair_rows), 1)
    owner_hot = jnp.where(request == owner, 1.0, 0.0)
    wide_decay = jnp.broadcast_to(decay, (pair_rows, page))
    slot_decay = jnp.dot(
        owner_hot, wide_decay, precision=precise, preferred_element_type=jnp.float32
    )
    weight_ref[...] = slot_decay * jnp.exp(logs)


def gram_kernel(first, owner_ref, weight_ref, *refs):
    if first:
        *piece_refs, before_ref, gram_ref = refs
    else:
        *piece_refs, gram_ref = refs
        gram_ref[...] = jnp.zeros_like(gram_ref)
    me = here()
    slots = piece_refs[0].shape[0] // 2
    for step, piece_ref in enumerate(piece_refs, first):
        for spot in range(slots):
            slot = at_step(FROM, step, me) * slots + spot
            keys = piece_ref[spot]
            both = jnp.concatenate([keys, piece_ref[slots + spot]], axis=1)
            turned = keys.T.astype(jnp.float32) * weight_ref[pl.ds(slot, 1), :]
            high, low = split_pair(turned)
            piece = jnp.dot(high, both, preferred_element_type=jnp.float32) + jnp.dot(
                low, both, preferred_element_type=jnp.float32
            )
            owner = owner_ref[slot, 0]
            gram_ref[owner] = gram_ref[owner] + piece


def solve_kernel(
    head_count, blocks, mixed_ref, strength_ref, gram_ref, out_ref, send_ref
):
    head = here()
    member = lax.axis_index("member")
    pair_rows, head_size, _ = gram_ref.shape
    width = out_ref.shape[1]

    def columns_of(block):
        first = pl.multiple_of(block // blocks * pair_rows, pair_rows)
        return mixed_ref[pl.ds(first, pair_rows), :].astype(jnp.float32)

    query = unit_rows(columns_of(head))
    key_new = unit_rows(columns_of(head + head_count))
    value_new = columns_of(head + 2 * head_count)
    strength = strength_ref[:pair_rows, :]
    ridge = strength_ref[pair_rows : pair_rows + 1, :]

    def image_of(vectors, columns):
        turned = vectors.T
        pieces = []
        for row in range(pair_rows):
            spread = jnp.broadcast_to(turned[:, row : row + 1], (head_size, head_size))
            pieces.append(jnp.sum(gram_ref[row, :, columns] * spread, axis=0, keepdims=True))
        return jnp.concatenate(pieces, axis=0)

    found = jnp.zeros_like(query)
    residual = query
    direction = query
    res_norm = jnp.sum(residual * residual, axis=-1, keepdims=True)
    for iteration in range(ITERS):
        along = jnp.sum(key_new * direction, axis=-1, keepdims=True)
        image = image_of(direction, slice(0, head_size))
        image = image + strength * key_new * along + ridge * direction
        step = res_norm / jnp.sum(direction * image, axis=-1, keepdims=True)
        found = found + step * direction
        residual = residual - step * image
        next_norm = jnp.sum(residual * residual, axis=-1, keepdims=True)
        direction = residual + (next_norm / res_norm) * direction
        res_norm = next_norm

    total = image_of(found, slice(head_size, 2 * head_size))
    total = total + strength * value_new * jnp.sum(key_new * found, axis=-1, keepdims=True)
    retrieved = total.astype(jnp.bfloat16)
    start = pl.multiple_of(member * head_size, head_size)
    part = jnp.dot(
        retrieved, out_ref[pl.ds(start, head_size), :], preferred_element_type=jnp.float32
    ).astype(jnp.bfloat16)
    half = pair_rows // 2
    for target in range(head_count):
        x = target % 2
        spot = slice(target * half, (target + 1) * half)
        send_ref[spot, :width] = part[x * half : (x + 1) * half]
        send_ref[spot, width:] = retrieved[x * half : (x + 1) * half]


def mlp_kernel(
    shards,
    part_ref,
    tokens_ref,
    gain_ref,
    gate_ref,
    up_ref,
    down_ref,
    mid_ref,
    retrieved_ref,
    send_ref,
):
    shard = lax.axis_index("shard")
    group_rows, width = tokens_ref.shape
    devices = 2 * shards
    req_rows = group_rows // shards
    attended = part_ref[:group_rows, :width].astype(jnp.float32)
    for source in range(1, devices):
        spot = slice(source * group_rows, (source + 1) * group_rows)
        attended += part_ref[spot, :width].astype(jnp.float32)
    mid_rows = (tokens_ref[...] + attended).astype(jnp.bfloat16)
    mlp_in = scaled_norm(mid_rows, gain_ref[...])
    contract = (((1,), (1,)), ((), ()))
    gate_part = lax.dot_general(
        mlp_in, gate_ref[...], contract, preferred_element_type=jnp.float32
    )
    up_part = lax.dot_general(mlp_in, up_ref[...], contract, preferred_element_type=jnp.float32)
    hidden = (silu(gate_part) * up_part).astype(jnp.bfloat16)
    down = jnp.dot(hidden, down_ref[...], preferred_element_type=jnp.float32)
    send_ref[...] = down.reshape(send_ref.shape)

    def home_rows(value):
        row = lax.broadcasted_iota(jnp.int32, value.shape, 0)
        picked = [
            jnp.sum(jnp.where(row == shard * req_rows + i, value, 0.0), axis=0, keepdims=True)
            for i in range(req_rows)
        ]
        return jnp.concatenate(picked, axis=0)

    mid_ref[...] = home_rows(mid_rows.astype(jnp.float32))
    heads = [
        home_rows(
            part_ref[source * group_rows : (source + 1) * group_rows, width:].astype(jnp.float32)
        )
        for source in range(devices)
    ]
    retrieved_ref[...] = jnp.concatenate(heads, axis=1).astype(jnp.bfloat16)


def finish_kernel(shards, down_ref, mid_ref, layer_ref):
    req_rows, width = mid_ref.shape
    rows = down_ref.shape[0] // shards
    total = down_ref[:rows]
    for source in range(1, shards):
        total = total + down_ref[source * rows : (source + 1) * rows]
    layer_ref[...] = (mid_ref[...] + total.reshape(req_rows, width)).astype(jnp.bfloat16)


def head_body(
    tokens,
    norm_gain,
    qkv_weight,
    conv_weight,
    conv_state,
    mesa_gates,
    mesa_bias,
    ridge_term,
    key_cache,
    value_cache,
    log_weight,
    page_owner,
    page_fill,
    out_weight,
    mlp_gain,
    gate_weight,
    up_weight,
    down_weight,
):
    shards = lax.axis_size("shard")
    devices = 2 * shards
    req_rows, width = tokens.shape
    slots, page, _ = key_cache.shape
    head_count = ridge_term.shape[0]
    head_size = width // head_count
    group_rows = shards * req_rows
    pair_rows = 2 * group_rows
    all_slots = devices * slots
    columns = qkv_weight.shape[1]
    shape = jax.ShapeDtypeStruct
    bf16, f32 = jnp.bfloat16, jnp.float32

    def exchange(value, axes):
        return lax.all_to_all(value, axes, split_axis=0, concat_axis=0, tiled=True)

    def spot(number):
        return number % 2 * shards + number // 2

    any_space = pl.BlockSpec(memory_space=pl.ANY)
    hbm = pl.BlockSpec(memory_space=pltpu.HBM)
    past_rows = jnp.transpose(conv_state, (1, 0, 2))
    gates = mesa_gates.T
    pack, misc, *pieces = pl.pallas_call(
        prep_kernel,
        out_shape=(
            shape((devices * TILE, width + page), bf16),
            shape((GATES.stop, width), f32),
        )
        + (shape((2 * slots, page, head_size), bf16),) * devices,
        in_specs=[hbm] * 12,
        out_specs=(VMEM,) * 2 + (any_space,) * devices,
        scratch_shapes=[
            pltpu.VMEM(tokens.shape, bf16),
            pltpu.VMEM(log_weight.shape, bf16),
            pltpu.SMEM(page_owner.shape, jnp.int32),
            pltpu.SMEM(page_fill.shape, jnp.int32),
            pltpu.VMEM(past_rows.shape, bf16),
            pltpu.VMEM(gates.shape, bf16),
            pltpu.VMEM(conv_weight.shape, f32),
            pltpu.VMEM((1, width), f32),
            pltpu.VMEM((1, 2 * head_count), f32),
            pltpu.SMEM(ridge_term.shape, f32),
            pltpu.VMEM(key_cache.shape, bf16),
            pltpu.VMEM(value_cache.shape, bf16),
            pltpu.SemaphoreType.DMA((10,)),
            pltpu.SemaphoreType.DMA((2 * slots,)),
            pltpu.SemaphoreType.DMA((2 * devices,)),
        ],
        compiler_params=PARAMS,
        name="prep",
    )(
        *(
            pltpu.with_memory_space_constraint(value, pltpu.HBM)
            for value in (
                tokens,
                log_weight,
                page_owner,
                page_fill,
                key_cache,
                value_cache,
                past_rows,
                conv_weight,
                norm_gain[None, :],
                gates,
                mesa_bias[None, :],
                ridge_term,
            )
        )
    )
    packs = exchange(pack, PAIR)

    def move(step):
        pairs = [
            (spot(source), spot(source ^ SEND[step][source >> 1 & 1])) for source in range(devices)
        ]
        return lax.ppermute(pieces[step], ("member", "shard"), pairs)

    moved = [pieces[0]] + [move(step) for step in range(1, 1 + EARLY)]
    pieces, packs = lax.optimization_barrier((pieces, packs))
    moved += [move(step) for step in range(1 + EARLY, devices)]

    mixed, own_tokens, weight, owner, strength = pl.pallas_call(
        functools.partial(project_kernel, shards, req_rows, slots, head_count),
        out_shape=(
            shape((devices * group_rows, head_size), bf16),
            shape((group_rows, width), f32),
            shape((all_slots, page), f32),
            shape((all_slots, page), jnp.int32),
            shape((pair_rows + TILE, head_size), f32),
        ),
        in_specs=[VMEM] * 3,
        out_specs=(VMEM,) * 5,
        scratch_shapes=[pltpu.VMEM((group_rows, columns), f32)],
        compiler_params=PARAMS,
        name="project",
    )(packs, misc, qkv_weight)
    all_mixed = exchange(mixed, PAIR)

    def add_up(first, last, before):
        known = [] if before is None else [before]
        count = last - first + len(known)
        return pl.pallas_call(
            functools.partial(gram_kernel, first),
            out_shape=shape((pair_rows, head_size, 2 * head_size), f32),
            in_specs=[SMEM] + [VMEM] * (1 + count),
            out_specs=VMEM,
            input_output_aliases={1 + count: 0} if known else {},
            compiler_params=PARAMS,
            name="gram",
        )(owner, weight, *moved[first:last], *known)

    gram = add_up(FIRST, devices, add_up(0, FIRST, None))

    parts = pl.pallas_call(
        functools.partial(solve_kernel, head_count, columns // head_size),
        out_shape=shape((devices * group_rows, width + head_size), bf16),
        in_specs=[VMEM] * 4,
        out_specs=VMEM,
        compiler_params=PARAMS,
        name="solve",
    )(all_mixed, strength, gram, out_weight)
    all_parts = exchange(parts, PAIR)

    mid_home, retrieved, down = pl.pallas_call(
        functools.partial(mlp_kernel, shards),
        out_shape=(
            shape((req_rows, width), f32),
            shape((req_rows, width), bf16),
            shape((group_rows * head_count, head_size), f32),
        ),
        in_specs=[VMEM] * 6,
        out_specs=(VMEM,) * 3,
        compiler_params=PARAMS,
        name="mlp",
    )(
        all_parts,
        own_tokens,
        mlp_gain[None, :],
        gate_weight.T,
        up_weight.T,
        down_weight,
    )
    layer_out = pl.pallas_call(
        functools.partial(finish_kernel, shards),
        out_shape=shape((req_rows, width), bf16),
        in_specs=[VMEM] * 2,
        out_specs=VMEM,
        compiler_params=PARAMS,
        name="finish",
    )(exchange(down, "shard"), mid_home)
    return (retrieved, layer_out)


def specs(group):
    rows = P((*group, "shard"))
    return (
        (
            rows,
            P(),
            P(None, "shard"),
            P(None, "shard"),
            P(group, None, "shard"),
            P(),
            P(),
            P(),
            rows,
            rows,
            rows,
            rows,
            rows,
            P("shard", None),
            P(),
            P(None, "shard"),
            P(None, "shard"),
            P("shard", None),
        ),
        (rows, rows),
    )


def solution(mesh):
    groups, shards = mesh.devices.shape

    def run(*args):
        head_count = args[7].shape[0]
        if 2 * shards == head_count == len(SEND):
            axes = ("pair", "member", "shard")
            used = Mesh(mesh.devices.reshape(groups // 2, 2, shards), axes)
            body, group = head_body, ("pair", "member")
        else:
            used, body, group = mesh, spread_body, ("group",)
        in_specs, out_specs = specs(group)
        return jax.shard_map(
            body, mesh=used, in_specs=in_specs, out_specs=out_specs, check_vma=False
        )(*args)

    return run
```

```python
import functools

import jax
import jax.numpy as jnp
from jax import lax
from jax.experimental import pallas as pl
from jax.experimental.pallas import tpu as pltpu
from jax.sharding import Mesh
from jax.sharding import PartitionSpec as P

ITERS = 4


precise = lax.Precision.HIGHEST

VMEM = pl.BlockSpec(memory_space=pltpu.VMEM)
SMEM = pl.BlockSpec(memory_space=pltpu.SMEM)


def partner(value, axis, apart):
    mask = 2**apart
    pairs = [(source, source ^ mask) for source in range(lax.axis_size(axis))]
    return lax.ppermute(value, axis, pairs)


def scaled_norm(row_vals, gain_vec):
    wide_rows = row_vals.astype(jnp.float32)
    factor = lax.rsqrt(jnp.mean(wide_rows * wide_rows, axis=-1, keepdims=True) + 1e-05)
    return (wide_rows * factor * gain_vec).astype(jnp.bfloat16)


def unit_rows(vectors):
    return vectors * lax.rsqrt(jnp.sum(vectors * vectors, axis=-1, keepdims=True) + 1e-06)


def slot_weights(owner_hot, decay_rows, log_weight, page_fill):
    page_len = log_weight.shape[2]
    slot_decay = jnp.dot(owner_hot, decay_rows, precision=precise)
    live_mask = (jnp.arange(page_len)[None, :] < page_fill[:, None]).astype(jnp.float32)
    return slot_decay[:, :, None] * jnp.exp(log_weight.astype(jnp.float32)) * live_mask[:, None, :]


def slot_terms(key_rows, source_rows, owner_hot, slot_weight, directions):
    slot_count, page_len, width_all = key_rows.shape
    head_count = slot_weight.shape[1]
    head_size = width_all // head_count
    member_count = owner_hot.shape[1]
    slot_dir = jnp.dot(owner_hot, directions.reshape(member_count, width_all), precision=precise)
    slot_dir = slot_dir.reshape(slot_count, head_count, head_size)
    key_wide = key_rows.astype(jnp.float32).reshape(slot_count, page_len, head_count, head_size)
    scores = jnp.einsum("sthd,shd->sht", key_wide, slot_dir, precision=precise)
    source_wide = source_rows.astype(jnp.float32).reshape(
        slot_count, page_len, head_count, head_size
    )
    contribution = jnp.einsum("sht,sthd->shd", slot_weight * scores, source_wide, precision=precise)
    summed = jnp.dot(owner_hot.T, contribution.reshape(slot_count, width_all), precision=precise)
    return summed.reshape(member_count, head_count, head_size)


def new_term(vectors, source_rows, strength_rows, key_new):
    return (
        strength_rows[:, :, None] * source_rows * jnp.sum(key_new * vectors, axis=-1, keepdims=True)
    )


def conjugate(query_rows, key_new, value_new, strength_rows, ridge_term, reduce_fn):
    solution = jnp.zeros_like(query_rows)
    residual = query_rows
    direction = query_rows
    res_norm = jnp.sum(residual * residual, axis=-1)
    for iteration in range(ITERS):
        image_vec = (
            reduce_fn(direction, False)
            + new_term(direction, key_new, strength_rows, key_new)
            + ridge_term[None, :, None] * direction
        )
        step_size = res_norm / jnp.sum(direction * image_vec, axis=-1)
        solution = solution + step_size[:, :, None] * direction
        residual = residual - step_size[:, :, None] * image_vec
        next_norm = jnp.sum(residual * residual, axis=-1)
        direction = residual + (next_norm / res_norm)[:, :, None] * direction
        res_norm = next_norm
    return reduce_fn(solution, True) + new_term(solution, value_new, strength_rows, key_new)


def pair_order(mine, theirs, parity):
    first = jnp.where(parity == 0, mine, theirs)
    second = jnp.where(parity == 0, theirs, mine)
    return jnp.concatenate([first, second], axis=0)


def spread_body(
    tokens,
    norm_gain,
    qkv_weight,
    conv_weight,
    conv_state,
    mesa_gates,
    mesa_bias,
    ridge_term,
    key_cache,
    value_cache,
    log_weight,
    page_owner,
    page_fill,
    out_weight,
    mlp_gain,
    gate_weight,
    up_weight,
    down_weight,
):
    req_rows = tokens.shape[0]
    group_rows = req_rows * lax.axis_size("shard")
    head_count = ridge_term.shape[0]
    width_all = key_cache.shape[2]
    head_size = width_all // head_count
    parity = lax.axis_index("group") % 2
    normed = scaled_norm(tokens, norm_gain)
    fresh_proj = jnp.dot(
        lax.all_gather(normed, "shard", axis=0, tiled=True),
        qkv_weight,
        preferred_element_type=jnp.float32,
    )
    past_rows = conv_state.astype(jnp.float32)
    pre_conv = (
        conv_weight[3] * fresh_proj
        + conv_weight[0] * past_rows[:, 0]
        + conv_weight[1] * past_rows[:, 1]
        + conv_weight[2] * past_rows[:, 2]
    )
    mixed_cols = jax.nn.silu(pre_conv).astype(jnp.bfloat16)
    home_rows = lax.all_to_all(mixed_cols, "shard", split_axis=0, concat_axis=1, tiled=True)
    split_rows = home_rows.astype(jnp.float32).reshape(req_rows, 3, head_count, head_size)
    query_home = unit_rows(split_rows[:, 0])
    key_home = unit_rows(split_rows[:, 1])
    value_home = split_rows[:, 2]
    gate_vals = jax.nn.sigmoid(
        jnp.dot(normed, mesa_gates, preferred_element_type=jnp.float32) + mesa_bias
    )
    decay_home = gate_vals[:, :head_count]
    strength_home = gate_vals[:, head_count:]
    owner_hot = (page_owner[:, None] == jnp.arange(2 * group_rows)[None, :]).astype(jnp.float32)
    stored = {}

    def cache_pass(directions, decay_grp, with_values):
        far_dirs, far_decay = partner((directions, decay_grp), "group", 0)
        pair_dirs = pair_order(directions, far_dirs, parity)
        pair_decay = pair_order(decay_grp, far_decay, parity)
        if "weight" not in stored:
            stored["weight"] = slot_weights(owner_hot, pair_decay, log_weight, page_fill)
        source_rows = value_cache if with_values else key_cache
        summed = slot_terms(key_cache, source_rows, owner_hot, stored["weight"], pair_dirs)
        mine = jnp.where(parity == 0, summed[:group_rows], summed[group_rows:])
        theirs = jnp.where(parity == 0, summed[group_rows:], summed[:group_rows])
        returned = partner(theirs, "group", 0)
        return mine + returned

    def reduce_home(vectors, with_values):
        directions, decay_grp = (
            lax.all_gather(vectors, "shard", axis=0, tiled=True),
            lax.all_gather(decay_home, "shard", axis=0, tiled=True),
        )
        return lax.psum_scatter(
            cache_pass(directions, decay_grp, with_values), "shard", scatter_dimension=0, tiled=True
        )

    found = conjugate(query_home, key_home, value_home, strength_home, ridge_term, reduce_home)
    retrieved = found.reshape(req_rows, width_all).astype(jnp.bfloat16)
    columns = lax.all_to_all(retrieved, "shard", split_axis=1, concat_axis=0, tiled=True)
    attended = lax.psum_scatter(
        jnp.dot(columns, out_weight, preferred_element_type=jnp.float32),
        "shard",
        scatter_dimension=0,
        tiled=True,
    )
    mid_rows = (tokens.astype(jnp.float32) + attended).astype(jnp.bfloat16)
    mlp_in = scaled_norm(mid_rows, mlp_gain)
    piece_rows = lax.all_gather(mlp_in, "shard", axis=0, tiled=True)
    gate_part = jnp.dot(piece_rows, gate_weight, preferred_element_type=jnp.float32)
    up_part = jnp.dot(piece_rows, up_weight, preferred_element_type=jnp.float32)
    hidden_rows = (jax.nn.silu(gate_part) * up_part).astype(jnp.bfloat16)
    down_part = lax.psum_scatter(
        jnp.dot(hidden_rows, down_weight, preferred_element_type=jnp.float32),
        "shard",
        scatter_dimension=0,
        tiled=True,
    )
    layer_out = (mid_rows.astype(jnp.float32) + down_part).astype(jnp.bfloat16)
    return (retrieved, layer_out)


TILE = 8
MASKED = -1e38
PAIR = ("shard", "member")
PARAMS = pltpu.CompilerParams(vmem_limit_bytes=16 * 1024 * 1024)
PAST, TAP, GAIN, BIAS, RIDGE = slice(0, 8), slice(8, 9), slice(9, 10), slice(10, 11), slice(11, 12)
GATES = slice(16, 32)

SEND = ((0, 0), (1, 4), (4, 1), (3, 6), (6, 3), (5, 5), (7, 7), (2, 2))
FROM = tuple((b, a) if a & 2 else (a, b) for a, b in SEND)
EARLY = 4


def split_pair(value):
    high = value.astype(jnp.bfloat16)
    low = (value - high.astype(jnp.float32)).astype(jnp.bfloat16)
    return high, low


def hot(rows, columns, target_fn):
    row = lax.broadcasted_iota(jnp.int32, (rows, columns), 0)
    column = lax.broadcasted_iota(jnp.int32, (rows, columns), 1)
    return jnp.where(column == target_fn(row), 1.0, 0.0).astype(jnp.bfloat16)


def here():
    return lax.axis_index("shard") * 2 + lax.axis_index("member")


def at_step(table, step, me):
    return me ^ jnp.where((me & 2) == 0, table[step][0], table[step][1])


def silu(value):
    return value / (1.0 + jnp.exp(-value))


def prep_kernel(
    tokens_hbm,
    logs_hbm,
    owner_hbm,
    fill_hbm,
    key_hbm,
    value_hbm,
    past_hbm,
    tap_hbm,
    gain_hbm,
    gates_hbm,
    bias_hbm,
    ridge_hbm,
    send_ref,
    misc_ref,
    *refs,
):
    *piece_refs, tokens_ref, logs_ref, owner_ref, fill_ref, state_ref, gates_ref = refs[:-9]
    tap_ref, gain_ref, bias_ref, ridge_ref, keys_ref, values_ref, sems, load_sems, cut_sems = refs[-9:]
    me = here()
    req_rows, width = tokens_ref.shape
    slots, head_count, page = logs_ref.shape
    head_size = piece_refs[0].shape[2]
    copies = [
        pltpu.make_async_copy(source, target, sems.at[place])
        for place, (source, target) in enumerate(
            [
                (owner_hbm, owner_ref),
                (fill_hbm, fill_ref),
                (tokens_hbm, tokens_ref),
                (logs_hbm, logs_ref),
                (past_hbm, state_ref),
                (tap_hbm, tap_ref),
                (gain_hbm, gain_ref),
                (gates_hbm, gates_ref),
                (bias_hbm, bias_ref),
                (ridge_hbm, ridge_ref),
            ]
        )
    ]
    loads = [
        [
            pltpu.make_async_copy(
                source.at[slot], target.at[slot], load_sems.at[part * source.shape[0] + slot]
            )
            for slot in range(source.shape[0])
        ]
        for part, (source, target) in enumerate(((key_hbm, keys_ref), (value_hbm, values_ref)))
    ]
    for copy in [*copies, *loads[0], *loads[1]]:
        copy.start()
    cuts = []
    for part, cache in enumerate((keys_ref, values_ref)):
        for copy in loads[part]:
            copy.wait()
        for step, piece_ref in enumerate(piece_refs):
            start = pl.multiple_of(at_step(SEND, step, me) * head_size, head_size)
            cut = pltpu.make_async_copy(
                cache.at[:, :, pl.ds(start, head_size)],
                piece_ref.at[pl.ds(part * cache.shape[0], cache.shape[0])],
                cut_sems.at[2 * step + part],
            )
            cut.start()
            cuts.append(cut)
    for copy in copies:
        copy.wait()

    tokens = tokens_ref[...].astype(jnp.float32)
    blank = jnp.zeros((TILE - req_rows, width), jnp.float32)
    tile = jnp.concatenate([tokens, blank], axis=0).astype(jnp.bfloat16)
    spot = lax.broadcasted_iota(jnp.int32, (head_count, page), 1)
    logs = []
    lane = lax.broadcasted_iota(jnp.int32, (1, page), 1)
    owners = jnp.zeros((1, page), jnp.float32)
    for slot in range(slots):
        rows = logs_ref[slot].astype(jnp.float32)
        logs.append(jnp.where(spot < fill_ref[slot], rows, MASKED))
        owners = jnp.where(lane == slot, owner_ref[slot].astype(jnp.float32), owners)
    rest = jnp.zeros((TILE - slots - 1, page), jnp.float32)
    for head in range(head_count):
        rows = [log[head : head + 1, :] for log in logs]
        side = jnp.concatenate([*rows, owners, rest], axis=0).astype(jnp.bfloat16)
        send_ref[head * TILE : (head + 1) * TILE, :width] = tile
        send_ref[head * TILE : (head + 1) * TILE, width:] = side

    past = tap_ref[0:1, :] * state_ref[0].astype(jnp.float32)
    past = past + tap_ref[1:2, :] * state_ref[1].astype(jnp.float32)
    past = past + tap_ref[2:3, :] * state_ref[2].astype(jnp.float32)
    columns = past.shape[1]
    misc_ref[PAST, :columns] = past
    misc_ref[TAP, :columns] = tap_ref[3:4, :]
    misc_ref[GAIN, :] = gain_ref[...]
    misc_ref[BIAS, : 2 * head_count] = bias_ref[...]
    ridges = jnp.zeros((1, page), jnp.float32)
    for head in range(head_count):
        ridges = jnp.where(lane == head, ridge_ref[head], ridges)
    misc_ref[RIDGE, :page] = ridges
    misc_ref[GATES, :] = gates_ref[...].astype(jnp.float32)
    for cut in cuts:
        cut.wait()


def project_kernel(
    shards,
    req_rows,
    slots,
    head_count,
    pack_ref,
    misc_ref,
    qkv_ref,
    send_ref,
    tokens_ref,
    weight_ref,
    owner_ref,
    strength_ref,
    mixed_ref,
):
    shard = lax.axis_index("shard")
    member = lax.axis_index("member")
    head = here()
    group_rows = shards * req_rows
    pair_rows = 2 * group_rows
    packed = 2 * shards * TILE
    width = misc_ref.shape[1]
    columns = qkv_ref.shape[1]
    page = weight_ref.shape[1]
    head_size = send_ref.shape[1]
    blocks = columns // head_size

    def home_of(row):
        x = row // group_rows
        s = (row % group_rows) // req_rows
        return (s * 2 + x) * TILE + row % req_rows

    pick_pair = hot(pair_rows, packed, home_of)
    pick_group = hot(group_rows, packed, lambda row: home_of(row + member * group_rows))
    rows = pack_ref[:, :width]
    pair_tokens = jnp.dot(pick_pair, rows, preferred_element_type=jnp.float32)
    own_tokens = jnp.dot(pick_group, rows, preferred_element_type=jnp.float32)
    tokens_ref[...] = own_tokens
    own = scaled_norm(own_tokens, misc_ref[GAIN, :])
    fresh = jnp.dot(own, qkv_ref[...], preferred_element_type=jnp.float32)
    before = misc_ref[TAP, :columns] * fresh + misc_ref[PAST, :columns]
    mixed_ref[...] = silu(before)
    for target in range(head_count):
        place = jnp.int32(0)
        for part in range(3):
            local = target + part * head_count - shard * blocks
            place = jnp.where((local >= 0) & (local < blocks), local, place)
        start = pl.multiple_of(place * head_size, head_size)
        send_ref[target * group_rows : (target + 1) * group_rows, :] = mixed_ref[
            :, pl.ds(start, head_size)
        ].astype(jnp.bfloat16)

    normed = scaled_norm(pair_tokens, misc_ref[GAIN, :])
    raw = lax.dot_general(
        normed,
        misc_ref[GATES, :].astype(jnp.bfloat16),
        (((1,), (1,)), ((), ())),
        preferred_element_type=jnp.float32,
    )
    gate_vals = 1.0 / (1.0 + jnp.exp(-(raw + misc_ref[BIAS, : 2 * head_count])))
    column = lax.broadcasted_iota(jnp.int32, gate_vals.shape, 1)
    decay = jnp.sum(jnp.where(column == head, gate_vals, 0.0), axis=1, keepdims=True)
    strength = jnp.sum(
        jnp.where(column == head + head_count, gate_vals, 0.0), axis=1, keepdims=True
    )
    strength_ref[:pair_rows, :] = jnp.broadcast_to(strength, (pair_rows, head_size))
    ridges = misc_ref[RIDGE, :page]
    spot = lax.broadcasted_iota(jnp.int32, ridges.shape, 1)
    ridge = jnp.sum(jnp.where(spot == head, ridges, 0.0), axis=1, keepdims=True)
    strength_ref[pair_rows:, :] = jnp.broadcast_to(ridge, (TILE, head_size))

    all_slots = 2 * shards * slots
    side = pack_ref[:, width:]
    pick_slot = hot(all_slots, packed, lambda row: (row // slots) * TILE + row % slots)
    logs = jnp.dot(pick_slot, side, preferred_element_type=jnp.float32)
    pick_owner = hot(all_slots, packed, lambda row: (row // slots) * TILE + slots)
    owners = jnp.dot(pick_owner, side, preferred_element_type=jnp.float32)
    at_slot = hot(all_slots, page, lambda row: row % slots).astype(jnp.float32)
    owner = jnp.sum(at_slot * owners, axis=1, keepdims=True).astype(jnp.int32)
    owner_ref[...] = jnp.broadcast_to(owner, owner_ref.shape)
    request = lax.broadcasted_iota(jnp.int32, (all_slots, pair_rows), 1)
    owner_hot = jnp.where(request == owner, 1.0, 0.0)
    wide_decay = jnp.broadcast_to(decay, (pair_rows, page))
    slot_decay = jnp.dot(
        owner_hot, wide_decay, precision=precise, preferred_element_type=jnp.float32
    )
    weight_ref[...] = slot_decay * jnp.exp(logs)


def gram_kernel(owner_ref, weight_ref, *refs):
    *piece_refs, gram_ref = refs
    me = here()
    slots = piece_refs[0].shape[0] // 2
    gram_ref[...] = jnp.zeros_like(gram_ref)
    for step, piece_ref in enumerate(piece_refs):
        for spot in range(slots):
            slot = at_step(FROM, step, me) * slots + spot
            keys = piece_ref[spot]
            both = jnp.concatenate([keys, piece_ref[slots + spot]], axis=1)
            turned = keys.T.astype(jnp.float32) * weight_ref[pl.ds(slot, 1), :]
            high, low = split_pair(turned)
            piece = jnp.dot(high, both, preferred_element_type=jnp.float32) + jnp.dot(
                low, both, preferred_element_type=jnp.float32
            )
            owner = owner_ref[slot, 0]
            gram_ref[owner] = gram_ref[owner] + piece


def solve_kernel(
    head_count, blocks, mixed_ref, strength_ref, gram_ref, out_ref, send_ref
):
    head = here()
    member = lax.axis_index("member")
    pair_rows, head_size, _ = gram_ref.shape
    width = out_ref.shape[1]

    def columns_of(block):
        first = pl.multiple_of(block // blocks * pair_rows, pair_rows)
        return mixed_ref[pl.ds(first, pair_rows), :].astype(jnp.float32)

    query = unit_rows(columns_of(head))
    key_new = unit_rows(columns_of(head + head_count))
    value_new = columns_of(head + 2 * head_count)
    strength = strength_ref[:pair_rows, :]
    ridge = strength_ref[pair_rows : pair_rows + 1, :]

    def image_of(vectors, columns):
        turned = vectors.T
        pieces = []
        for row in range(pair_rows):
            spread = jnp.broadcast_to(turned[:, row : row + 1], (head_size, head_size))
            pieces.append(jnp.sum(gram_ref[row, :, columns] * spread, axis=0, keepdims=True))
        return jnp.concatenate(pieces, axis=0)

    found = jnp.zeros_like(query)
    residual = query
    direction = query
    res_norm = jnp.sum(residual * residual, axis=-1, keepdims=True)
    for iteration in range(ITERS):
        along = jnp.sum(key_new * direction, axis=-1, keepdims=True)
        image = image_of(direction, slice(0, head_size))
        image = image + strength * key_new * along + ridge * direction
        step = res_norm / jnp.sum(direction * image, axis=-1, keepdims=True)
        found = found + step * direction
        residual = residual - step * image
        next_norm = jnp.sum(residual * residual, axis=-1, keepdims=True)
        direction = residual + (next_norm / res_norm) * direction
        res_norm = next_norm

    total = image_of(found, slice(head_size, 2 * head_size))
    total = total + strength * value_new * jnp.sum(key_new * found, axis=-1, keepdims=True)
    retrieved = total.astype(jnp.bfloat16)
    start = pl.multiple_of(member * head_size, head_size)
    part = jnp.dot(
        retrieved, out_ref[pl.ds(start, head_size), :], preferred_element_type=jnp.float32
    ).astype(jnp.bfloat16)
    half = pair_rows // 2
    for target in range(head_count):
        x = target % 2
        spot = slice(target * half, (target + 1) * half)
        send_ref[spot, :width] = part[x * half : (x + 1) * half]
        send_ref[spot, width:] = retrieved[x * half : (x + 1) * half]


def mlp_kernel(
    shards,
    part_ref,
    tokens_ref,
    gain_ref,
    gate_ref,
    up_ref,
    down_ref,
    mid_ref,
    retrieved_ref,
    send_ref,
):
    shard = lax.axis_index("shard")
    group_rows, width = tokens_ref.shape
    devices = 2 * shards
    req_rows = group_rows // shards
    attended = part_ref[:group_rows, :width].astype(jnp.float32)
    for source in range(1, devices):
        spot = slice(source * group_rows, (source + 1) * group_rows)
        attended += part_ref[spot, :width].astype(jnp.float32)
    mid_rows = (tokens_ref[...] + attended).astype(jnp.bfloat16)
    mlp_in = scaled_norm(mid_rows, gain_ref[...])
    contract = (((1,), (1,)), ((), ()))
    gate_part = lax.dot_general(
        mlp_in, gate_ref[...], contract, preferred_element_type=jnp.float32
    )
    up_part = lax.dot_general(mlp_in, up_ref[...], contract, preferred_element_type=jnp.float32)
    hidden = (silu(gate_part) * up_part).astype(jnp.bfloat16)
    down = jnp.dot(hidden, down_ref[...], preferred_element_type=jnp.float32)
    send_ref[...] = down.reshape(send_ref.shape)

    def home_rows(value):
        row = lax.broadcasted_iota(jnp.int32, value.shape, 0)
        picked = [
            jnp.sum(jnp.where(row == shard * req_rows + i, value, 0.0), axis=0, keepdims=True)
            for i in range(req_rows)
        ]
        return jnp.concatenate(picked, axis=0)

    mid_ref[...] = home_rows(mid_rows.astype(jnp.float32))
    heads = [
        home_rows(
            part_ref[source * group_rows : (source + 1) * group_rows, width:].astype(jnp.float32)
        )
        for source in range(devices)
    ]
    retrieved_ref[...] = jnp.concatenate(heads, axis=1).astype(jnp.bfloat16)


def finish_kernel(shards, down_ref, mid_ref, layer_ref):
    req_rows, width = mid_ref.shape
    rows = down_ref.shape[0] // shards
    total = down_ref[:rows]
    for source in range(1, shards):
        total = total + down_ref[source * rows : (source + 1) * rows]
    layer_ref[...] = (mid_ref[...] + total.reshape(req_rows, width)).astype(jnp.bfloat16)


def head_body(
    tokens,
    norm_gain,
    qkv_weight,
    conv_weight,
    conv_state,
    mesa_gates,
    mesa_bias,
    ridge_term,
    key_cache,
    value_cache,
    log_weight,
    page_owner,
    page_fill,
    out_weight,
    mlp_gain,
    gate_weight,
    up_weight,
    down_weight,
):
    shards = lax.axis_size("shard")
    devices = 2 * shards
    req_rows, width = tokens.shape
    slots, page, _ = key_cache.shape
    head_count = ridge_term.shape[0]
    head_size = width // head_count
    group_rows = shards * req_rows
    pair_rows = 2 * group_rows
    all_slots = devices * slots
    columns = qkv_weight.shape[1]
    shape = jax.ShapeDtypeStruct
    bf16, f32 = jnp.bfloat16, jnp.float32

    def exchange(value, axes):
        return lax.all_to_all(value, axes, split_axis=0, concat_axis=0, tiled=True)

    def spot(number):
        return number % 2 * shards + number // 2

    any_space = pl.BlockSpec(memory_space=pl.ANY)
    hbm = pl.BlockSpec(memory_space=pltpu.HBM)
    past_rows = jnp.transpose(conv_state, (1, 0, 2))
    gates = mesa_gates.T
    pack, misc, *pieces = pl.pallas_call(
        prep_kernel,
        out_shape=(
            shape((devices * TILE, width + page), bf16),
            shape((GATES.stop, width), f32),
        )
        + (shape((2 * slots, page, head_size), bf16),) * devices,
        in_specs=[hbm] * 12,
        out_specs=(VMEM,) * 2 + (any_space,) * devices,
        scratch_shapes=[
            pltpu.VMEM(tokens.shape, bf16),
            pltpu.VMEM(log_weight.shape, bf16),
            pltpu.SMEM(page_owner.shape, jnp.int32),
            pltpu.SMEM(page_fill.shape, jnp.int32),
            pltpu.VMEM(past_rows.shape, bf16),
            pltpu.VMEM(gates.shape, bf16),
            pltpu.VMEM(conv_weight.shape, f32),
            pltpu.VMEM((1, width), f32),
            pltpu.VMEM((1, 2 * head_count), f32),
            pltpu.SMEM(ridge_term.shape, f32),
            pltpu.VMEM(key_cache.shape, bf16),
            pltpu.VMEM(value_cache.shape, bf16),
            pltpu.SemaphoreType.DMA((10,)),
            pltpu.SemaphoreType.DMA((2 * slots,)),
            pltpu.SemaphoreType.DMA((2 * devices,)),
        ],
        compiler_params=PARAMS,
        name="prep",
    )(
        *(
            pltpu.with_memory_space_constraint(value, pltpu.HBM)
            for value in (
                tokens,
                log_weight,
                page_owner,
                page_fill,
                key_cache,
                value_cache,
                past_rows,
                conv_weight,
                norm_gain[None, :],
                gates,
                mesa_bias[None, :],
                ridge_term,
            )
        )
    )
    packs = exchange(pack, PAIR)

    def move(step):
        pairs = [
            (spot(source), spot(source ^ SEND[step][source >> 1 & 1])) for source in range(devices)
        ]
        return lax.ppermute(pieces[step], ("member", "shard"), pairs)

    moved = [pieces[0]] + [move(step) for step in range(1, 1 + EARLY)]
    pieces, packs = lax.optimization_barrier((pieces, packs))
    moved += [move(step) for step in range(1 + EARLY, devices)]

    mixed, own_tokens, weight, owner, strength = pl.pallas_call(
        functools.partial(project_kernel, shards, req_rows, slots, head_count),
        out_shape=(
            shape((devices * group_rows, head_size), bf16),
            shape((group_rows, width), f32),
            shape((all_slots, page), f32),
            shape((all_slots, page), jnp.int32),
            shape((pair_rows + TILE, head_size), f32),
        ),
        in_specs=[VMEM] * 3,
        out_specs=(VMEM,) * 5,
        scratch_shapes=[pltpu.VMEM((group_rows, columns), f32)],
        compiler_params=PARAMS,
        name="project",
    )(packs, misc, qkv_weight)
    all_mixed = exchange(mixed, PAIR)

    all_mixed, owner, weight = lax.optimization_barrier((all_mixed, owner, weight))
    gram = pl.pallas_call(
        gram_kernel,
        out_shape=shape((pair_rows, head_size, 2 * head_size), f32),
        in_specs=[SMEM] + [VMEM] * (1 + devices),
        out_specs=VMEM,
        compiler_params=PARAMS,
        name="gram",
    )(owner, weight, *moved)

    parts = pl.pallas_call(
        functools.partial(solve_kernel, head_count, columns // head_size),
        out_shape=shape((devices * group_rows, width + head_size), bf16),
        in_specs=[VMEM] * 4,
        out_specs=VMEM,
        compiler_params=PARAMS,
        name="solve",
    )(all_mixed, strength, gram, out_weight)
    all_parts = exchange(parts, PAIR)

    mid_home, retrieved, down = pl.pallas_call(
        functools.partial(mlp_kernel, shards),
        out_shape=(
            shape((req_rows, width), f32),
            shape((req_rows, width), bf16),
            shape((group_rows * head_count, head_size), f32),
        ),
        in_specs=[VMEM] * 6,
        out_specs=(VMEM,) * 3,
        compiler_params=PARAMS,
        name="mlp",
    )(
        all_parts,
        own_tokens,
        mlp_gain[None, :],
        gate_weight.T,
        up_weight.T,
        down_weight,
    )
    layer_out = pl.pallas_call(
        functools.partial(finish_kernel, shards),
        out_shape=shape((req_rows, width), bf16),
        in_specs=[VMEM] * 2,
        out_specs=VMEM,
        compiler_params=PARAMS,
        name="finish",
    )(exchange(down, "shard"), mid_home)
    return (retrieved, layer_out)


def specs(group):
    rows = P((*group, "shard"))
    return (
        (
            rows,
            P(),
            P(None, "shard"),
            P(None, "shard"),
            P(group, None, "shard"),
            P(),
            P(),
            P(),
            rows,
            rows,
            rows,
            rows,
            rows,
            P("shard", None),
            P(),
            P(None, "shard"),
            P(None, "shard"),
            P("shard", None),
        ),
        (rows, rows),
    )


def solution(mesh):
    groups, shards = mesh.devices.shape

    def run(*args):
        head_count = args[7].shape[0]
        if 2 * shards == head_count == len(SEND):
            axes = ("pair", "member", "shard")
            used = Mesh(mesh.devices.reshape(groups // 2, 2, shards), axes)
            body, group = head_body, ("pair", "member")
        else:
            used, body, group = mesh, spread_body, ("group",)
        in_specs, out_specs = specs(group)
        return jax.shard_map(
            body, mesh=used, in_specs=in_specs, out_specs=out_specs, check_vma=False
        )(*args)

    return run
```

```python
import functools

import jax
import jax.numpy as jnp
from jax import lax
from jax.experimental import pallas as pl
from jax.experimental.pallas import tpu as pltpu
from jax.sharding import Mesh
from jax.sharding import PartitionSpec as P

ITERS = 4


precise = lax.Precision.HIGHEST

VMEM = pl.BlockSpec(memory_space=pltpu.VMEM)
SMEM = pl.BlockSpec(memory_space=pltpu.SMEM)


def partner(value, axis, apart):
    mask = 2**apart
    pairs = [(source, source ^ mask) for source in range(lax.axis_size(axis))]
    return lax.ppermute(value, axis, pairs)


def scaled_norm(row_vals, gain_vec):
    wide_rows = row_vals.astype(jnp.float32)
    factor = lax.rsqrt(jnp.mean(wide_rows * wide_rows, axis=-1, keepdims=True) + 1e-05)
    return (wide_rows * factor * gain_vec).astype(jnp.bfloat16)


def unit_rows(vectors):
    return vectors * lax.rsqrt(jnp.sum(vectors * vectors, axis=-1, keepdims=True) + 1e-06)


def slot_weights(owner_hot, decay_rows, log_weight, page_fill):
    page_len = log_weight.shape[2]
    slot_decay = jnp.dot(owner_hot, decay_rows, precision=precise)
    live_mask = (jnp.arange(page_len)[None, :] < page_fill[:, None]).astype(jnp.float32)
    return slot_decay[:, :, None] * jnp.exp(log_weight.astype(jnp.float32)) * live_mask[:, None, :]


def slot_terms(key_rows, source_rows, owner_hot, slot_weight, directions):
    slot_count, page_len, width_all = key_rows.shape
    head_count = slot_weight.shape[1]
    head_size = width_all // head_count
    member_count = owner_hot.shape[1]
    slot_dir = jnp.dot(owner_hot, directions.reshape(member_count, width_all), precision=precise)
    slot_dir = slot_dir.reshape(slot_count, head_count, head_size)
    key_wide = key_rows.astype(jnp.float32).reshape(slot_count, page_len, head_count, head_size)
    scores = jnp.einsum("sthd,shd->sht", key_wide, slot_dir, precision=precise)
    source_wide = source_rows.astype(jnp.float32).reshape(
        slot_count, page_len, head_count, head_size
    )
    contribution = jnp.einsum("sht,sthd->shd", slot_weight * scores, source_wide, precision=precise)
    summed = jnp.dot(owner_hot.T, contribution.reshape(slot_count, width_all), precision=precise)
    return summed.reshape(member_count, head_count, head_size)


def new_term(vectors, source_rows, strength_rows, key_new):
    return (
        strength_rows[:, :, None] * source_rows * jnp.sum(key_new * vectors, axis=-1, keepdims=True)
    )


def conjugate(query_rows, key_new, value_new, strength_rows, ridge_term, reduce_fn):
    solution = jnp.zeros_like(query_rows)
    residual = query_rows
    direction = query_rows
    res_norm = jnp.sum(residual * residual, axis=-1)
    for iteration in range(ITERS):
        image_vec = (
            reduce_fn(direction, False)
            + new_term(direction, key_new, strength_rows, key_new)
            + ridge_term[None, :, None] * direction
        )
        step_size = res_norm / jnp.sum(direction * image_vec, axis=-1)
        solution = solution + step_size[:, :, None] * direction
        residual = residual - step_size[:, :, None] * image_vec
        next_norm = jnp.sum(residual * residual, axis=-1)
        direction = residual + (next_norm / res_norm)[:, :, None] * direction
        res_norm = next_norm
    return reduce_fn(solution, True) + new_term(solution, value_new, strength_rows, key_new)


def pair_order(mine, theirs, parity):
    first = jnp.where(parity == 0, mine, theirs)
    second = jnp.where(parity == 0, theirs, mine)
    return jnp.concatenate([first, second], axis=0)


def spread_body(
    tokens,
    norm_gain,
    qkv_weight,
    conv_weight,
    conv_state,
    mesa_gates,
    mesa_bias,
    ridge_term,
    key_cache,
    value_cache,
    log_weight,
    page_owner,
    page_fill,
    out_weight,
    mlp_gain,
    gate_weight,
    up_weight,
    down_weight,
):
    req_rows = tokens.shape[0]
    group_rows = req_rows * lax.axis_size("shard")
    head_count = ridge_term.shape[0]
    width_all = key_cache.shape[2]
    head_size = width_all // head_count
    parity = lax.axis_index("group") % 2
    normed = scaled_norm(tokens, norm_gain)
    fresh_proj = jnp.dot(
        lax.all_gather(normed, "shard", axis=0, tiled=True),
        qkv_weight,
        preferred_element_type=jnp.float32,
    )
    past_rows = conv_state.astype(jnp.float32)
    pre_conv = (
        conv_weight[3] * fresh_proj
        + conv_weight[0] * past_rows[:, 0]
        + conv_weight[1] * past_rows[:, 1]
        + conv_weight[2] * past_rows[:, 2]
    )
    mixed_cols = jax.nn.silu(pre_conv).astype(jnp.bfloat16)
    home_rows = lax.all_to_all(mixed_cols, "shard", split_axis=0, concat_axis=1, tiled=True)
    split_rows = home_rows.astype(jnp.float32).reshape(req_rows, 3, head_count, head_size)
    query_home = unit_rows(split_rows[:, 0])
    key_home = unit_rows(split_rows[:, 1])
    value_home = split_rows[:, 2]
    gate_vals = jax.nn.sigmoid(
        jnp.dot(normed, mesa_gates, preferred_element_type=jnp.float32) + mesa_bias
    )
    decay_home = gate_vals[:, :head_count]
    strength_home = gate_vals[:, head_count:]
    owner_hot = (page_owner[:, None] == jnp.arange(2 * group_rows)[None, :]).astype(jnp.float32)
    stored = {}

    def cache_pass(directions, decay_grp, with_values):
        far_dirs, far_decay = partner((directions, decay_grp), "group", 0)
        pair_dirs = pair_order(directions, far_dirs, parity)
        pair_decay = pair_order(decay_grp, far_decay, parity)
        if "weight" not in stored:
            stored["weight"] = slot_weights(owner_hot, pair_decay, log_weight, page_fill)
        source_rows = value_cache if with_values else key_cache
        summed = slot_terms(key_cache, source_rows, owner_hot, stored["weight"], pair_dirs)
        mine = jnp.where(parity == 0, summed[:group_rows], summed[group_rows:])
        theirs = jnp.where(parity == 0, summed[group_rows:], summed[:group_rows])
        returned = partner(theirs, "group", 0)
        return mine + returned

    def reduce_home(vectors, with_values):
        directions, decay_grp = (
            lax.all_gather(vectors, "shard", axis=0, tiled=True),
            lax.all_gather(decay_home, "shard", axis=0, tiled=True),
        )
        return lax.psum_scatter(
            cache_pass(directions, decay_grp, with_values), "shard", scatter_dimension=0, tiled=True
        )

    found = conjugate(query_home, key_home, value_home, strength_home, ridge_term, reduce_home)
    retrieved = found.reshape(req_rows, width_all).astype(jnp.bfloat16)
    columns = lax.all_to_all(retrieved, "shard", split_axis=1, concat_axis=0, tiled=True)
    attended = lax.psum_scatter(
        jnp.dot(columns, out_weight, preferred_element_type=jnp.float32),
        "shard",
        scatter_dimension=0,
        tiled=True,
    )
    mid_rows = (tokens.astype(jnp.float32) + attended).astype(jnp.bfloat16)
    mlp_in = scaled_norm(mid_rows, mlp_gain)
    piece_rows = lax.all_gather(mlp_in, "shard", axis=0, tiled=True)
    gate_part = jnp.dot(piece_rows, gate_weight, preferred_element_type=jnp.float32)
    up_part = jnp.dot(piece_rows, up_weight, preferred_element_type=jnp.float32)
    hidden_rows = (jax.nn.silu(gate_part) * up_part).astype(jnp.bfloat16)
    down_part = lax.psum_scatter(
        jnp.dot(hidden_rows, down_weight, preferred_element_type=jnp.float32),
        "shard",
        scatter_dimension=0,
        tiled=True,
    )
    layer_out = (mid_rows.astype(jnp.float32) + down_part).astype(jnp.bfloat16)
    return (retrieved, layer_out)


TILE = 8
MASKED = -1e38
PAIR = ("shard", "member")
PARAMS = pltpu.CompilerParams(vmem_limit_bytes=16 * 1024 * 1024)
PAST, TAP, GAIN, BIAS, RIDGE = slice(0, 8), slice(8, 9), slice(9, 10), slice(10, 11), slice(11, 12)
GATES = slice(16, 32)

SEND = ((0, 0), (1, 4), (4, 1), (3, 6), (6, 3), (5, 5), (7, 7), (2, 2))
FROM = tuple((b, a) if a & 2 else (a, b) for a, b in SEND)
EARLY = 4


def split_pair(value):
    high = value.astype(jnp.bfloat16)
    low = (value - high.astype(jnp.float32)).astype(jnp.bfloat16)
    return high, low


def hot(rows, columns, target_fn):
    row = lax.broadcasted_iota(jnp.int32, (rows, columns), 0)
    column = lax.broadcasted_iota(jnp.int32, (rows, columns), 1)
    return jnp.where(column == target_fn(row), 1.0, 0.0).astype(jnp.bfloat16)


def here():
    return lax.axis_index("shard") * 2 + lax.axis_index("member")


def at_step(table, step, me):
    return me ^ jnp.where((me & 2) == 0, table[step][0], table[step][1])


def silu(value):
    return value / (1.0 + jnp.exp(-value))


def prep_kernel(
    tokens_hbm,
    logs_hbm,
    owner_hbm,
    fill_hbm,
    key_hbm,
    value_hbm,
    past_hbm,
    tap_hbm,
    gain_hbm,
    gates_hbm,
    bias_hbm,
    ridge_hbm,
    send_ref,
    misc_ref,
    *refs,
):
    *piece_refs, tokens_ref, logs_ref, owner_ref, fill_ref, state_ref, gates_ref = refs[:-9]
    tap_ref, gain_ref, bias_ref, ridge_ref, keys_ref, values_ref, sems, load_sems, cut_sems = refs[-9:]
    me = here()
    req_rows, width = tokens_ref.shape
    slots, head_count, page = logs_ref.shape
    head_size = piece_refs[0].shape[2]
    copies = [
        pltpu.make_async_copy(source, target, sems.at[place])
        for place, (source, target) in enumerate(
            [
                (owner_hbm, owner_ref),
                (fill_hbm, fill_ref),
                (tokens_hbm, tokens_ref),
                (logs_hbm, logs_ref),
                (past_hbm, state_ref),
                (tap_hbm, tap_ref),
                (gain_hbm, gain_ref),
                (gates_hbm, gates_ref),
                (bias_hbm, bias_ref),
                (ridge_hbm, ridge_ref),
            ]
        )
    ]
    loads = [
        [
            pltpu.make_async_copy(
                source.at[slot], target.at[slot], load_sems.at[part * source.shape[0] + slot]
            )
            for slot in range(source.shape[0])
        ]
        for part, (source, target) in enumerate(((key_hbm, keys_ref), (value_hbm, values_ref)))
    ]
    for copy in [*copies, *loads[0], *loads[1]]:
        copy.start()
    for copy in copies:
        copy.wait()

    tokens = tokens_ref[...].astype(jnp.float32)
    rows = [
        tokens[row : row + 1, first : first + page]
        for row in range(req_rows)
        for first in range(0, width, page)
    ]
    tile = jnp.concatenate(rows, axis=0).astype(jnp.bfloat16)
    packed = tile.shape[0] + TILE
    spot = lax.broadcasted_iota(jnp.int32, (head_count, page), 1)
    logs = []
    lane = lax.broadcasted_iota(jnp.int32, (1, page), 1)
    owners = jnp.zeros((1, page), jnp.float32)
    for slot in range(slots):
        rows = logs_ref[slot].astype(jnp.float32)
        logs.append(jnp.where(spot < fill_ref[slot], rows, MASKED))
        owners = jnp.where(lane == slot, owner_ref[slot].astype(jnp.float32), owners)
    rest = jnp.zeros((TILE - slots - 1, page), jnp.float32)
    for head in range(head_count):
        rows = [log[head : head + 1, :] for log in logs]
        side = jnp.concatenate([*rows, owners, rest], axis=0).astype(jnp.bfloat16)
        send_ref[head * packed : head * packed + tile.shape[0], :] = tile
        send_ref[head * packed + tile.shape[0] : (head + 1) * packed, :] = side

    past = tap_ref[0:1, :] * state_ref[0].astype(jnp.float32)
    past = past + tap_ref[1:2, :] * state_ref[1].astype(jnp.float32)
    past = past + tap_ref[2:3, :] * state_ref[2].astype(jnp.float32)
    columns = past.shape[1]
    misc_ref[PAST, :columns] = past
    misc_ref[TAP, :columns] = tap_ref[3:4, :]
    misc_ref[GAIN, :] = gain_ref[...]
    misc_ref[BIAS, : 2 * head_count] = bias_ref[...]
    ridges = jnp.zeros((1, page), jnp.float32)
    for head in range(head_count):
        ridges = jnp.where(lane == head, ridge_ref[head], ridges)
    misc_ref[RIDGE, :page] = ridges
    misc_ref[GATES, :] = gates_ref[...].astype(jnp.float32)
    cuts = []
    for part, cache in enumerate((keys_ref, values_ref)):
        for copy in loads[part]:
            copy.wait()
        for step, piece_ref in enumerate(piece_refs):
            start = pl.multiple_of(at_step(SEND, step, me) * head_size, head_size)
            cut = pltpu.make_async_copy(
                cache.at[:, :, pl.ds(start, head_size)],
                piece_ref.at[pl.ds(part * cache.shape[0], cache.shape[0])],
                cut_sems.at[2 * step + part],
            )
            cut.start()
            cuts.append(cut)
    for cut in cuts:
        cut.wait()


def project_kernel(
    shards,
    req_rows,
    slots,
    head_count,
    pack_ref,
    misc_ref,
    qkv_ref,
    send_ref,
    tokens_ref,
    weight_ref,
    owner_ref,
    strength_ref,
    mixed_ref,
):
    shard = lax.axis_index("shard")
    member = lax.axis_index("member")
    head = here()
    group_rows = shards * req_rows
    pair_rows = 2 * group_rows
    width = misc_ref.shape[1]
    columns = qkv_ref.shape[1]
    page = weight_ref.shape[1]
    head_size = send_ref.shape[1]
    blocks = columns // head_size
    parts = width // page
    packed = pack_ref.shape[0]
    tall = packed // (2 * shards)

    def rows_of(first, count):
        def home_of(row):
            request = row % count + first
            x = request // group_rows
            s = (request % group_rows) // req_rows
            return (s * 2 + x) * tall + request % req_rows * parts + row // count

        picked = jnp.dot(
            hot(count * parts, packed, home_of), pack_ref[...], preferred_element_type=jnp.float32
        )
        return jnp.concatenate(
            [picked[part * count : (part + 1) * count] for part in range(parts)], axis=1
        )

    own_tokens = rows_of(member * group_rows, group_rows)
    tokens_ref[...] = own_tokens
    own = scaled_norm(own_tokens, misc_ref[GAIN, :])
    fresh = jnp.dot(own, qkv_ref[...], preferred_element_type=jnp.float32)
    before = misc_ref[TAP, :columns] * fresh + misc_ref[PAST, :columns]
    mixed_ref[...] = silu(before)
    for target in range(head_count):
        place = jnp.int32(0)
        for part in range(3):
            local = target + part * head_count - shard * blocks
            place = jnp.where((local >= 0) & (local < blocks), local, place)
        start = pl.multiple_of(place * head_size, head_size)
        send_ref[target * group_rows : (target + 1) * group_rows, :] = mixed_ref[
            :, pl.ds(start, head_size)
        ].astype(jnp.bfloat16)

    normed = scaled_norm(rows_of(0, pair_rows), misc_ref[GAIN, :])
    raw = lax.dot_general(
        normed,
        misc_ref[GATES, :].astype(jnp.bfloat16),
        (((1,), (1,)), ((), ())),
        preferred_element_type=jnp.float32,
    )
    gate_vals = 1.0 / (1.0 + jnp.exp(-(raw + misc_ref[BIAS, : 2 * head_count])))
    column = lax.broadcasted_iota(jnp.int32, gate_vals.shape, 1)
    decay = jnp.sum(jnp.where(column == head, gate_vals, 0.0), axis=1, keepdims=True)
    strength = jnp.sum(
        jnp.where(column == head + head_count, gate_vals, 0.0), axis=1, keepdims=True
    )
    strength_ref[:pair_rows, :] = jnp.broadcast_to(strength, (pair_rows, head_size))
    ridges = misc_ref[RIDGE, :page]
    spot = lax.broadcasted_iota(jnp.int32, ridges.shape, 1)
    ridge = jnp.sum(jnp.where(spot == head, ridges, 0.0), axis=1, keepdims=True)
    strength_ref[pair_rows:, :] = jnp.broadcast_to(ridge, (TILE, head_size))

    all_slots = 2 * shards * slots
    side = tall - TILE
    pick_slot = hot(all_slots, packed, lambda row: (row // slots) * tall + side + row % slots)
    logs = jnp.dot(pick_slot, pack_ref[...], preferred_element_type=jnp.float32)
    pick_owner = hot(all_slots, packed, lambda row: (row // slots) * tall + side + slots)
    owners = jnp.dot(pick_owner, pack_ref[...], preferred_element_type=jnp.float32)
    at_slot = hot(all_slots, page, lambda row: row % slots).astype(jnp.float32)
    owner = jnp.sum(at_slot * owners, axis=1, keepdims=True).astype(jnp.int32)
    owner_ref[...] = jnp.broadcast_to(owner, owner_ref.shape)
    request = lax.broadcasted_iota(jnp.int32, (all_slots, pair_rows), 1)
    owner_hot = jnp.where(request == owner, 1.0, 0.0)
    wide_decay = jnp.broadcast_to(decay, (pair_rows, page))
    slot_decay = jnp.dot(
        owner_hot, wide_decay, precision=precise, preferred_element_type=jnp.float32
    )
    weight_ref[...] = slot_decay * jnp.exp(logs)


def gram_kernel(first, owner_ref, weight_ref, *refs):
    if first:
        *piece_refs, before_ref, gram_ref = refs
    else:
        *piece_refs, gram_ref = refs
        gram_ref[...] = jnp.zeros_like(gram_ref)
    me = here()
    slots = piece_refs[0].shape[0] // 2
    for step, piece_ref in enumerate(piece_refs, first):
        for spot in range(slots):
            slot = at_step(FROM, step, me) * slots + spot
            keys = piece_ref[spot]
            both = jnp.concatenate([keys, piece_ref[slots + spot]], axis=1)
            turned = keys.T.astype(jnp.float32) * weight_ref[pl.ds(slot, 1), :]
            high, low = split_pair(turned)
            piece = jnp.dot(high, both, preferred_element_type=jnp.float32) + jnp.dot(
                low, both, preferred_element_type=jnp.float32
            )
            owner = owner_ref[slot, 0]
            gram_ref[owner] = gram_ref[owner] + piece


def solve_kernel(
    head_count, blocks, mixed_ref, strength_ref, gram_ref, out_ref, send_ref
):
    head = here()
    member = lax.axis_index("member")
    pair_rows, head_size, _ = gram_ref.shape
    width = out_ref.shape[1]

    def columns_of(block):
        first = pl.multiple_of(block // blocks * pair_rows, pair_rows)
        return mixed_ref[pl.ds(first, pair_rows), :].astype(jnp.float32)

    query = unit_rows(columns_of(head))
    key_new = unit_rows(columns_of(head + head_count))
    value_new = columns_of(head + 2 * head_count)
    strength = strength_ref[:pair_rows, :]
    ridge = strength_ref[pair_rows : pair_rows + 1, :]

    def image_of(vectors, columns):
        turned = vectors.T
        pieces = []
        for row in range(pair_rows):
            spread = jnp.broadcast_to(turned[:, row : row + 1], (head_size, head_size))
            pieces.append(jnp.sum(gram_ref[row, :, columns] * spread, axis=0, keepdims=True))
        return jnp.concatenate(pieces, axis=0)

    found = jnp.zeros_like(query)
    residual = query
    direction = query
    res_norm = jnp.sum(residual * residual, axis=-1, keepdims=True)
    for iteration in range(ITERS):
        along = jnp.sum(key_new * direction, axis=-1, keepdims=True)
        image = image_of(direction, slice(0, head_size))
        image = image + strength * key_new * along + ridge * direction
        step = res_norm / jnp.sum(direction * image, axis=-1, keepdims=True)
        found = found + step * direction
        residual = residual - step * image
        next_norm = jnp.sum(residual * residual, axis=-1, keepdims=True)
        direction = residual + (next_norm / res_norm) * direction
        res_norm = next_norm

    total = image_of(found, slice(head_size, 2 * head_size))
    total = total + strength * value_new * jnp.sum(key_new * found, axis=-1, keepdims=True)
    retrieved = total.astype(jnp.bfloat16)
    start = pl.multiple_of(member * head_size, head_size)
    part = jnp.dot(
        retrieved, out_ref[pl.ds(start, head_size), :], preferred_element_type=jnp.float32
    ).astype(jnp.bfloat16)
    half = pair_rows // 2
    for target in range(head_count):
        x = target % 2
        spot = slice(target * half, (target + 1) * half)
        send_ref[spot, :width] = part[x * half : (x + 1) * half]
        send_ref[spot, width:] = retrieved[x * half : (x + 1) * half]


def home_rows(value, req_rows):
    first = lax.axis_index("shard") * req_rows
    row = lax.broadcasted_iota(jnp.int32, value.shape, 0)
    picked = [
        jnp.sum(jnp.where(row == first + i, value, 0.0), axis=0, keepdims=True)
        for i in range(req_rows)
    ]
    return jnp.concatenate(picked, axis=0)


def mlp_kernel(
    shards,
    part_ref,
    tokens_ref,
    gain_ref,
    gate_ref,
    up_ref,
    down_ref,
    mid_ref,
    retrieved_ref,
    send_ref,
):
    group_rows, width = tokens_ref.shape
    devices = 2 * shards
    req_rows = group_rows // shards
    attended = part_ref[:group_rows, :width].astype(jnp.float32)
    for source in range(1, devices):
        spot = slice(source * group_rows, (source + 1) * group_rows)
        attended += part_ref[spot, :width].astype(jnp.float32)
    mid_rows = (tokens_ref[...] + attended).astype(jnp.bfloat16)
    mlp_in = scaled_norm(mid_rows, gain_ref[...])
    contract = (((1,), (1,)), ((), ()))
    gate_part = lax.dot_general(
        mlp_in, gate_ref[...], contract, preferred_element_type=jnp.float32
    )
    up_part = lax.dot_general(mlp_in, up_ref[...], contract, preferred_element_type=jnp.float32)
    hidden = (silu(gate_part) * up_part).astype(jnp.bfloat16)
    down = jnp.dot(hidden, down_ref[...], preferred_element_type=jnp.float32)
    send_ref[...] = down.reshape(send_ref.shape)
    mid_ref[...] = home_rows(mid_rows.astype(jnp.float32), mid_ref.shape[0])
    heads = [
        home_rows(
            part_ref[source * group_rows : (source + 1) * group_rows, width:].astype(jnp.float32),
            req_rows,
        )
        for source in range(devices)
    ]
    retrieved_ref[...] = jnp.concatenate(heads, axis=1).astype(jnp.bfloat16)


def finish_kernel(shards, down_ref, mid_ref, layer_ref):
    req_rows, width = mid_ref.shape
    rows = down_ref.shape[0] // shards
    total = down_ref[:rows]
    for source in range(1, shards):
        total = total + down_ref[source * rows : (source + 1) * rows]
    layer_ref[...] = (mid_ref[...] + total.reshape(req_rows, width)).astype(jnp.bfloat16)


def head_body(
    tokens,
    norm_gain,
    qkv_weight,
    conv_weight,
    conv_state,
    mesa_gates,
    mesa_bias,
    ridge_term,
    key_cache,
    value_cache,
    log_weight,
    page_owner,
    page_fill,
    out_weight,
    mlp_gain,
    gate_weight,
    up_weight,
    down_weight,
):
    shards = lax.axis_size("shard")
    devices = 2 * shards
    req_rows, width = tokens.shape
    slots, page, _ = key_cache.shape
    head_count = ridge_term.shape[0]
    head_size = width // head_count
    group_rows = shards * req_rows
    pair_rows = 2 * group_rows
    all_slots = devices * slots
    columns = qkv_weight.shape[1]
    shape = jax.ShapeDtypeStruct
    bf16, f32 = jnp.bfloat16, jnp.float32

    def exchange(value, axes):
        return lax.all_to_all(value, axes, split_axis=0, concat_axis=0, tiled=True)

    def spot(number):
        return number % 2 * shards + number // 2

    any_space = pl.BlockSpec(memory_space=pl.ANY)
    hbm = pl.BlockSpec(memory_space=pltpu.HBM)
    past_rows = jnp.transpose(conv_state, (1, 0, 2))
    gates = mesa_gates.T
    pack, misc, *pieces = pl.pallas_call(
        prep_kernel,
        out_shape=(
            shape((devices * (req_rows * width // page + TILE), page), bf16),
            shape((GATES.stop, width), f32),
        )
        + (shape((2 * slots, page, head_size), bf16),) * devices,
        in_specs=[hbm] * 12,
        out_specs=(VMEM,) * 2 + (any_space,) * devices,
        scratch_shapes=[
            pltpu.VMEM(tokens.shape, bf16),
            pltpu.VMEM(log_weight.shape, bf16),
            pltpu.SMEM(page_owner.shape, jnp.int32),
            pltpu.SMEM(page_fill.shape, jnp.int32),
            pltpu.VMEM(past_rows.shape, bf16),
            pltpu.VMEM(gates.shape, bf16),
            pltpu.VMEM(conv_weight.shape, f32),
            pltpu.VMEM((1, width), f32),
            pltpu.VMEM((1, 2 * head_count), f32),
            pltpu.SMEM(ridge_term.shape, f32),
            pltpu.VMEM(key_cache.shape, bf16),
            pltpu.VMEM(value_cache.shape, bf16),
            pltpu.SemaphoreType.DMA((10,)),
            pltpu.SemaphoreType.DMA((2 * slots,)),
            pltpu.SemaphoreType.DMA((2 * devices,)),
        ],
        compiler_params=PARAMS,
        name="prep",
    )(
        *(
            pltpu.with_memory_space_constraint(value, pltpu.HBM)
            for value in (
                tokens,
                log_weight,
                page_owner,
                page_fill,
                key_cache,
                value_cache,
                past_rows,
                conv_weight,
                norm_gain[None, :],
                gates,
                mesa_bias[None, :],
                ridge_term,
            )
        )
    )
    packs = exchange(pack, PAIR)

    def move(step):
        pairs = [
            (spot(source), spot(source ^ SEND[step][source >> 1 & 1])) for source in range(devices)
        ]
        return lax.ppermute(pieces[step], ("member", "shard"), pairs)

    moved = [pieces[0]] + [move(step) for step in range(1, 1 + EARLY)]
    pieces, packs = lax.optimization_barrier((pieces, packs))
    moved += [move(step) for step in range(1 + EARLY, devices)]

    mixed, own_tokens, weight, owner, strength = pl.pallas_call(
        functools.partial(project_kernel, shards, req_rows, slots, head_count),
        out_shape=(
            shape((devices * group_rows, head_size), bf16),
            shape((group_rows, width), f32),
            shape((all_slots, page), f32),
            shape((all_slots, page), jnp.int32),
            shape((pair_rows + TILE, head_size), f32),
        ),
        in_specs=[VMEM] * 3,
        out_specs=(VMEM,) * 5,
        scratch_shapes=[pltpu.VMEM((group_rows, columns), f32)],
        compiler_params=PARAMS,
        name="project",
    )(packs, misc, qkv_weight)

    def add_up(first, last, before, owner, weight):
        known = [] if before is None else [before]
        count = last - first + len(known)
        return pl.pallas_call(
            functools.partial(gram_kernel, first),
            out_shape=shape((pair_rows, head_size, 2 * head_size), f32),
            in_specs=[SMEM] + [VMEM] * (1 + count),
            out_specs=VMEM,
            input_output_aliases={1 + count: 0} if known else {},
            compiler_params=PARAMS,
            name="gram",
        )(owner, weight, *moved[first:last], *known)

    gram = add_up(0, 1 + EARLY, None, owner, weight)
    mixed, gram = lax.optimization_barrier((mixed, gram))
    all_mixed = exchange(mixed, PAIR)
    all_mixed, owner, weight, gram = lax.optimization_barrier((all_mixed, owner, weight, gram))
    gram = add_up(1 + EARLY, devices, gram, owner, weight)

    parts = pl.pallas_call(
        functools.partial(solve_kernel, head_count, columns // head_size),
        out_shape=shape((devices * group_rows, width + head_size), bf16),
        in_specs=[VMEM] * 4,
        out_specs=VMEM,
        compiler_params=PARAMS,
        name="solve",
    )(all_mixed, strength, gram, out_weight)
    all_parts = exchange(parts, PAIR)

    mid_home, retrieved, down = pl.pallas_call(
        functools.partial(mlp_kernel, shards),
        out_shape=(
            shape((req_rows, width), f32),
            shape((req_rows, width), bf16),
            shape((group_rows * head_count, head_size), f32),
        ),
        in_specs=[VMEM] * 6,
        out_specs=(VMEM,) * 3,
        compiler_params=PARAMS,
        name="mlp",
    )(
        all_parts,
        own_tokens,
        mlp_gain[None, :],
        gate_weight.T,
        up_weight.T,
        down_weight,
    )
    layer_out = pl.pallas_call(
        functools.partial(finish_kernel, shards),
        out_shape=shape((req_rows, width), bf16),
        in_specs=[VMEM] * 2,
        out_specs=VMEM,
        compiler_params=PARAMS,
        name="finish",
    )(exchange(down, "shard"), mid_home)
    return (retrieved, layer_out)


def specs(group):
    rows = P((*group, "shard"))
    return (
        (
            rows,
            P(),
            P(None, "shard"),
            P(None, "shard"),
            P(group, None, "shard"),
            P(),
            P(),
            P(),
            rows,
            rows,
            rows,
            rows,
            rows,
            P("shard", None),
            P(),
            P(None, "shard"),
            P(None, "shard"),
            P("shard", None),
        ),
        (rows, rows),
    )


def solution(mesh):
    groups, shards = mesh.devices.shape

    def run(*args):
        head_count = args[7].shape[0]
        if 2 * shards == head_count == len(SEND):
            axes = ("pair", "member", "shard")
            used = Mesh(mesh.devices.reshape(groups // 2, 2, shards), axes)
            body, group = head_body, ("pair", "member")
        else:
            used, body, group = mesh, spread_body, ("group",)
        in_specs, out_specs = specs(group)
        return jax.shard_map(
            body, mesh=used, in_specs=in_specs, out_specs=out_specs, check_vma=False
        )(*args)

    return run
```

```python
import functools

import jax
import jax.numpy as jnp
from jax import lax
from jax.experimental import pallas as pl
from jax.experimental.pallas import tpu as pltpu
from jax.sharding import Mesh
from jax.sharding import PartitionSpec as P

ITERS = 4


precise = lax.Precision.HIGHEST

VMEM = pl.BlockSpec(memory_space=pltpu.VMEM)
SMEM = pl.BlockSpec(memory_space=pltpu.SMEM)


def partner(value, axis, apart):
    mask = 2**apart
    pairs = [(source, source ^ mask) for source in range(lax.axis_size(axis))]
    return lax.ppermute(value, axis, pairs)


def scaled_norm(row_vals, gain_vec):
    wide_rows = row_vals.astype(jnp.float32)
    factor = lax.rsqrt(jnp.mean(wide_rows * wide_rows, axis=-1, keepdims=True) + 1e-05)
    return (wide_rows * factor * gain_vec).astype(jnp.bfloat16)


def unit_rows(vectors):
    return vectors * lax.rsqrt(jnp.sum(vectors * vectors, axis=-1, keepdims=True) + 1e-06)


def slot_weights(owner_hot, decay_rows, log_weight, page_fill):
    page_len = log_weight.shape[2]
    slot_decay = jnp.dot(owner_hot, decay_rows, precision=precise)
    live_mask = (jnp.arange(page_len)[None, :] < page_fill[:, None]).astype(jnp.float32)
    return slot_decay[:, :, None] * jnp.exp(log_weight.astype(jnp.float32)) * live_mask[:, None, :]


def slot_terms(key_rows, source_rows, owner_hot, slot_weight, directions):
    slot_count, page_len, width_all = key_rows.shape
    head_count = slot_weight.shape[1]
    head_size = width_all // head_count
    member_count = owner_hot.shape[1]
    slot_dir = jnp.dot(owner_hot, directions.reshape(member_count, width_all), precision=precise)
    slot_dir = slot_dir.reshape(slot_count, head_count, head_size)
    key_wide = key_rows.astype(jnp.float32).reshape(slot_count, page_len, head_count, head_size)
    scores = jnp.einsum("sthd,shd->sht", key_wide, slot_dir, precision=precise)
    source_wide = source_rows.astype(jnp.float32).reshape(
        slot_count, page_len, head_count, head_size
    )
    contribution = jnp.einsum("sht,sthd->shd", slot_weight * scores, source_wide, precision=precise)
    summed = jnp.dot(owner_hot.T, contribution.reshape(slot_count, width_all), precision=precise)
    return summed.reshape(member_count, head_count, head_size)


def new_term(vectors, source_rows, strength_rows, key_new):
    return (
        strength_rows[:, :, None] * source_rows * jnp.sum(key_new * vectors, axis=-1, keepdims=True)
    )


def conjugate(query_rows, key_new, value_new, strength_rows, ridge_term, reduce_fn):
    solution = jnp.zeros_like(query_rows)
    residual = query_rows
    direction = query_rows
    res_norm = jnp.sum(residual * residual, axis=-1)
    for iteration in range(ITERS):
        image_vec = (
            reduce_fn(direction, False)
            + new_term(direction, key_new, strength_rows, key_new)
            + ridge_term[None, :, None] * direction
        )
        step_size = res_norm / jnp.sum(direction * image_vec, axis=-1)
        solution = solution + step_size[:, :, None] * direction
        residual = residual - step_size[:, :, None] * image_vec
        next_norm = jnp.sum(residual * residual, axis=-1)
        direction = residual + (next_norm / res_norm)[:, :, None] * direction
        res_norm = next_norm
    return reduce_fn(solution, True) + new_term(solution, value_new, strength_rows, key_new)


def pair_order(mine, theirs, parity):
    first = jnp.where(parity == 0, mine, theirs)
    second = jnp.where(parity == 0, theirs, mine)
    return jnp.concatenate([first, second], axis=0)


def spread_body(
    tokens,
    norm_gain,
    qkv_weight,
    conv_weight,
    conv_state,
    mesa_gates,
    mesa_bias,
    ridge_term,
    key_cache,
    value_cache,
    log_weight,
    page_owner,
    page_fill,
    out_weight,
    mlp_gain,
    gate_weight,
    up_weight,
    down_weight,
):
    req_rows = tokens.shape[0]
    group_rows = req_rows * lax.axis_size("shard")
    head_count = ridge_term.shape[0]
    width_all = key_cache.shape[2]
    head_size = width_all // head_count
    parity = lax.axis_index("group") % 2
    normed = scaled_norm(tokens, norm_gain)
    fresh_proj = jnp.dot(
        lax.all_gather(normed, "shard", axis=0, tiled=True),
        qkv_weight,
        preferred_element_type=jnp.float32,
    )
    past_rows = conv_state.astype(jnp.float32)
    pre_conv = (
        conv_weight[3] * fresh_proj
        + conv_weight[0] * past_rows[:, 0]
        + conv_weight[1] * past_rows[:, 1]
        + conv_weight[2] * past_rows[:, 2]
    )
    mixed_cols = jax.nn.silu(pre_conv).astype(jnp.bfloat16)
    home_rows = lax.all_to_all(mixed_cols, "shard", split_axis=0, concat_axis=1, tiled=True)
    split_rows = home_rows.astype(jnp.float32).reshape(req_rows, 3, head_count, head_size)
    query_home = unit_rows(split_rows[:, 0])
    key_home = unit_rows(split_rows[:, 1])
    value_home = split_rows[:, 2]
    gate_vals = jax.nn.sigmoid(
        jnp.dot(normed, mesa_gates, preferred_element_type=jnp.float32) + mesa_bias
    )
    decay_home = gate_vals[:, :head_count]
    strength_home = gate_vals[:, head_count:]
    owner_hot = (page_owner[:, None] == jnp.arange(2 * group_rows)[None, :]).astype(jnp.float32)
    stored = {}

    def cache_pass(directions, decay_grp, with_values):
        far_dirs, far_decay = partner((directions, decay_grp), "group", 0)
        pair_dirs = pair_order(directions, far_dirs, parity)
        pair_decay = pair_order(decay_grp, far_decay, parity)
        if "weight" not in stored:
            stored["weight"] = slot_weights(owner_hot, pair_decay, log_weight, page_fill)
        source_rows = value_cache if with_values else key_cache
        summed = slot_terms(key_cache, source_rows, owner_hot, stored["weight"], pair_dirs)
        mine = jnp.where(parity == 0, summed[:group_rows], summed[group_rows:])
        theirs = jnp.where(parity == 0, summed[group_rows:], summed[:group_rows])
        returned = partner(theirs, "group", 0)
        return mine + returned

    def reduce_home(vectors, with_values):
        directions, decay_grp = (
            lax.all_gather(vectors, "shard", axis=0, tiled=True),
            lax.all_gather(decay_home, "shard", axis=0, tiled=True),
        )
        return lax.psum_scatter(
            cache_pass(directions, decay_grp, with_values), "shard", scatter_dimension=0, tiled=True
        )

    found = conjugate(query_home, key_home, value_home, strength_home, ridge_term, reduce_home)
    retrieved = found.reshape(req_rows, width_all).astype(jnp.bfloat16)
    columns = lax.all_to_all(retrieved, "shard", split_axis=1, concat_axis=0, tiled=True)
    attended = lax.psum_scatter(
        jnp.dot(columns, out_weight, preferred_element_type=jnp.float32),
        "shard",
        scatter_dimension=0,
        tiled=True,
    )
    mid_rows = (tokens.astype(jnp.float32) + attended).astype(jnp.bfloat16)
    mlp_in = scaled_norm(mid_rows, mlp_gain)
    piece_rows = lax.all_gather(mlp_in, "shard", axis=0, tiled=True)
    gate_part = jnp.dot(piece_rows, gate_weight, preferred_element_type=jnp.float32)
    up_part = jnp.dot(piece_rows, up_weight, preferred_element_type=jnp.float32)
    hidden_rows = (jax.nn.silu(gate_part) * up_part).astype(jnp.bfloat16)
    down_part = lax.psum_scatter(
        jnp.dot(hidden_rows, down_weight, preferred_element_type=jnp.float32),
        "shard",
        scatter_dimension=0,
        tiled=True,
    )
    layer_out = (mid_rows.astype(jnp.float32) + down_part).astype(jnp.bfloat16)
    return (retrieved, layer_out)


TILE = 8
MASKED = -1e38
PAIR = ("shard", "member")
PARAMS = pltpu.CompilerParams(vmem_limit_bytes=16 * 1024 * 1024)
PAST, TAP, GAIN, BIAS, RIDGE = slice(0, 8), slice(8, 9), slice(9, 10), slice(10, 11), slice(11, 12)
GATES = slice(16, 32)

SEND = ((0, 0), (1, 4), (4, 1), (3, 6), (6, 3), (5, 5), (7, 7), (2, 2))
FROM = tuple((b, a) if a & 2 else (a, b) for a, b in SEND)
EARLY = 4


def split_pair(value):
    high = value.astype(jnp.bfloat16)
    low = (value - high.astype(jnp.float32)).astype(jnp.bfloat16)
    return high, low


def hot(rows, columns, target_fn):
    row = lax.broadcasted_iota(jnp.int32, (rows, columns), 0)
    column = lax.broadcasted_iota(jnp.int32, (rows, columns), 1)
    return jnp.where(column == target_fn(row), 1.0, 0.0).astype(jnp.bfloat16)


def here():
    return lax.axis_index("shard") * 2 + lax.axis_index("member")


def at_step(table, step, me):
    return me ^ jnp.where((me & 2) == 0, table[step][0], table[step][1])


def silu(value):
    return value / (1.0 + jnp.exp(-value))


def cut_kernel(key_hbm, value_hbm, *refs):
    *piece_refs, stage_ref, sems = refs
    slots = key_hbm.shape[0]
    head_size = piece_refs[0].shape[2]
    me = here()
    loads = [
        pltpu.make_async_copy(source.at[slot], stage_ref.at[part, slot], sems.at[part * slots + slot])
        for part, source in enumerate((key_hbm, value_hbm))
        for slot in range(slots)
    ]
    for load in loads:
        load.start()
    starts = [
        pl.multiple_of(at_step(SEND, step, me) * head_size, head_size)
        for step in range(len(piece_refs))
    ]
    for part in range(2):
        for slot in range(slots):
            place = part * slots + slot
            loads[place].wait()
            for start, piece_ref in zip(starts, piece_refs):
                piece_ref[place] = stage_ref[part, slot, :, pl.ds(start, head_size)]


def pack_kernel(
    tokens_hbm,
    logs_hbm,
    owner_hbm,
    fill_hbm,
    past_hbm,
    tap_hbm,
    gain_hbm,
    gates_hbm,
    bias_hbm,
    ridge_hbm,
    send_ref,
    misc_ref,
    tokens_ref,
    logs_ref,
    owner_ref,
    fill_ref,
    state_ref,
    gates_ref,
    tap_ref,
    gain_ref,
    bias_ref,
    ridge_ref,
    sems,
):
    req_rows, width = tokens_ref.shape
    slots, head_count, page = logs_ref.shape
    copies = [
        pltpu.make_async_copy(source, target, sems.at[place])
        for place, (source, target) in enumerate(
            [
                (owner_hbm, owner_ref),
                (fill_hbm, fill_ref),
                (tokens_hbm, tokens_ref),
                (logs_hbm, logs_ref),
                (past_hbm, state_ref),
                (tap_hbm, tap_ref),
                (gain_hbm, gain_ref),
                (gates_hbm, gates_ref),
                (bias_hbm, bias_ref),
                (ridge_hbm, ridge_ref),
            ]
        )
    ]
    for copy in copies:
        copy.start()
    for copy in copies:
        copy.wait()

    tokens = tokens_ref[...].astype(jnp.float32)
    rows = [
        tokens[row : row + 1, first : first + page]
        for row in range(req_rows)
        for first in range(0, width, page)
    ]
    tile = jnp.concatenate(rows, axis=0).astype(jnp.bfloat16)
    packed = tile.shape[0] + TILE
    spot = lax.broadcasted_iota(jnp.int32, (head_count, page), 1)
    logs = []
    lane = lax.broadcasted_iota(jnp.int32, (1, page), 1)
    owners = jnp.zeros((1, page), jnp.float32)
    for slot in range(slots):
        rows = logs_ref[slot].astype(jnp.float32)
        logs.append(jnp.where(spot < fill_ref[slot], rows, MASKED))
        owners = jnp.where(lane == slot, owner_ref[slot].astype(jnp.float32), owners)
    rest = jnp.zeros((TILE - slots - 1, page), jnp.float32)
    for head in range(head_count):
        rows = [log[head : head + 1, :] for log in logs]
        side = jnp.concatenate([*rows, owners, rest], axis=0).astype(jnp.bfloat16)
        send_ref[head * packed : head * packed + tile.shape[0], :] = tile
        send_ref[head * packed + tile.shape[0] : (head + 1) * packed, :] = side

    past = tap_ref[0:1, :] * state_ref[0].astype(jnp.float32)
    past = past + tap_ref[1:2, :] * state_ref[1].astype(jnp.float32)
    past = past + tap_ref[2:3, :] * state_ref[2].astype(jnp.float32)
    columns = past.shape[1]
    misc_ref[PAST, :columns] = past
    misc_ref[TAP, :columns] = tap_ref[3:4, :]
    misc_ref[GAIN, :] = gain_ref[...]
    misc_ref[BIAS, : 2 * head_count] = bias_ref[...]
    ridges = jnp.zeros((1, page), jnp.float32)
    for head in range(head_count):
        ridges = jnp.where(lane == head, ridge_ref[head], ridges)
    misc_ref[RIDGE, :page] = ridges
    misc_ref[GATES, :] = gates_ref[...].astype(jnp.float32)


def project_kernel(
    shards,
    req_rows,
    slots,
    head_count,
    pack_ref,
    misc_ref,
    qkv_ref,
    send_ref,
    tokens_ref,
    weight_ref,
    owner_ref,
    strength_ref,
    mixed_ref,
):
    shard = lax.axis_index("shard")
    member = lax.axis_index("member")
    head = here()
    group_rows = shards * req_rows
    pair_rows = 2 * group_rows
    width = misc_ref.shape[1]
    columns = qkv_ref.shape[1]
    page = weight_ref.shape[1]
    head_size = send_ref.shape[1]
    blocks = columns // head_size
    parts = width // page
    packed = pack_ref.shape[0]
    tall = packed // (2 * shards)

    def rows_of(first, count):
        def home_of(row):
            request = row % count + first
            x = request // group_rows
            s = (request % group_rows) // req_rows
            return (s * 2 + x) * tall + request % req_rows * parts + row // count

        picked = jnp.dot(
            hot(count * parts, packed, home_of), pack_ref[...], preferred_element_type=jnp.float32
        )
        return jnp.concatenate(
            [picked[part * count : (part + 1) * count] for part in range(parts)], axis=1
        )

    own_tokens = rows_of(member * group_rows, group_rows)
    tokens_ref[...] = own_tokens
    own = scaled_norm(own_tokens, misc_ref[GAIN, :])
    fresh = jnp.dot(own, qkv_ref[...], preferred_element_type=jnp.float32)
    before = misc_ref[TAP, :columns] * fresh + misc_ref[PAST, :columns]
    mixed_ref[...] = silu(before)
    for target in range(head_count):
        place = jnp.int32(0)
        for part in range(3):
            local = target + part * head_count - shard * blocks
            place = jnp.where((local >= 0) & (local < blocks), local, place)
        start = pl.multiple_of(place * head_size, head_size)
        send_ref[target * group_rows : (target + 1) * group_rows, :] = mixed_ref[
            :, pl.ds(start, head_size)
        ].astype(jnp.bfloat16)

    normed = scaled_norm(rows_of(0, pair_rows), misc_ref[GAIN, :])
    raw = lax.dot_general(
        normed,
        misc_ref[GATES, :].astype(jnp.bfloat16),
        (((1,), (1,)), ((), ())),
        preferred_element_type=jnp.float32,
    )
    gate_vals = 1.0 / (1.0 + jnp.exp(-(raw + misc_ref[BIAS, : 2 * head_count])))
    column = lax.broadcasted_iota(jnp.int32, gate_vals.shape, 1)
    decay = jnp.sum(jnp.where(column == head, gate_vals, 0.0), axis=1, keepdims=True)
    strength = jnp.sum(
        jnp.where(column == head + head_count, gate_vals, 0.0), axis=1, keepdims=True
    )
    strength_ref[:pair_rows, :] = jnp.broadcast_to(strength, (pair_rows, head_size))
    ridges = misc_ref[RIDGE, :page]
    spot = lax.broadcasted_iota(jnp.int32, ridges.shape, 1)
    ridge = jnp.sum(jnp.where(spot == head, ridges, 0.0), axis=1, keepdims=True)
    strength_ref[pair_rows:, :] = jnp.broadcast_to(ridge, (TILE, head_size))

    all_slots = 2 * shards * slots
    side = tall - TILE
    pick_slot = hot(all_slots, packed, lambda row: (row // slots) * tall + side + row % slots)
    logs = jnp.dot(pick_slot, pack_ref[...], preferred_element_type=jnp.float32)
    pick_owner = hot(all_slots, packed, lambda row: (row // slots) * tall + side + slots)
    owners = jnp.dot(pick_owner, pack_ref[...], preferred_element_type=jnp.float32)
    at_slot = hot(all_slots, page, lambda row: row % slots).astype(jnp.float32)
    owner = jnp.sum(at_slot * owners, axis=1, keepdims=True).astype(jnp.int32)
    owner_ref[...] = jnp.broadcast_to(owner, owner_ref.shape)
    request = lax.broadcasted_iota(jnp.int32, (all_slots, pair_rows), 1)
    owner_hot = jnp.where(request == owner, 1.0, 0.0)
    wide_decay = jnp.broadcast_to(decay, (pair_rows, page))
    slot_decay = jnp.dot(
        owner_hot, wide_decay, precision=precise, preferred_element_type=jnp.float32
    )
    weight_ref[...] = slot_decay * jnp.exp(logs)


def gram_kernel(first, owner_ref, weight_ref, *refs):
    if first:
        *piece_refs, before_ref, gram_ref = refs
    else:
        *piece_refs, gram_ref = refs
        gram_ref[...] = jnp.zeros_like(gram_ref)
    me = here()
    slots = piece_refs[0].shape[0] // 2
    for step, piece_ref in enumerate(piece_refs, first):
        for spot in range(slots):
            slot = at_step(FROM, step, me) * slots + spot
            keys = piece_ref[spot]
            both = jnp.concatenate([keys, piece_ref[slots + spot]], axis=1)
            turned = keys.T.astype(jnp.float32) * weight_ref[pl.ds(slot, 1), :]
            high, low = split_pair(turned)
            piece = jnp.dot(high, both, preferred_element_type=jnp.float32) + jnp.dot(
                low, both, preferred_element_type=jnp.float32
            )
            owner = owner_ref[slot, 0]
            gram_ref[owner] = gram_ref[owner] + piece


def solve_kernel(
    head_count, blocks, mixed_ref, strength_ref, gram_ref, out_ref, send_ref
):
    head = here()
    member = lax.axis_index("member")
    pair_rows, head_size, _ = gram_ref.shape
    width = out_ref.shape[1]

    def columns_of(block):
        first = pl.multiple_of(block // blocks * pair_rows, pair_rows)
        return mixed_ref[pl.ds(first, pair_rows), :].astype(jnp.float32)

    query = unit_rows(columns_of(head))
    key_new = unit_rows(columns_of(head + head_count))
    value_new = columns_of(head + 2 * head_count)
    strength = strength_ref[:pair_rows, :]
    ridge = strength_ref[pair_rows : pair_rows + 1, :]

    def image_of(vectors, columns):
        turned = vectors.T
        pieces = []
        for row in range(pair_rows):
            spread = jnp.broadcast_to(turned[:, row : row + 1], (head_size, head_size))
            pieces.append(jnp.sum(gram_ref[row, :, columns] * spread, axis=0, keepdims=True))
        return jnp.concatenate(pieces, axis=0)

    found = jnp.zeros_like(query)
    residual = query
    direction = query
    res_norm = jnp.sum(residual * residual, axis=-1, keepdims=True)
    for iteration in range(ITERS):
        along = jnp.sum(key_new * direction, axis=-1, keepdims=True)
        image = image_of(direction, slice(0, head_size))
        image = image + strength * key_new * along + ridge * direction
        step = res_norm / jnp.sum(direction * image, axis=-1, keepdims=True)
        found = found + step * direction
        residual = residual - step * image
        next_norm = jnp.sum(residual * residual, axis=-1, keepdims=True)
        direction = residual + (next_norm / res_norm) * direction
        res_norm = next_norm

    total = image_of(found, slice(head_size, 2 * head_size))
    total = total + strength * value_new * jnp.sum(key_new * found, axis=-1, keepdims=True)
    retrieved = total.astype(jnp.bfloat16)
    start = pl.multiple_of(member * head_size, head_size)
    part = jnp.dot(
        retrieved, out_ref[pl.ds(start, head_size), :], preferred_element_type=jnp.float32
    ).astype(jnp.bfloat16)
    half = pair_rows // 2
    for target in range(head_count):
        x = target % 2
        spot = slice(target * half, (target + 1) * half)
        send_ref[spot, :width] = part[x * half : (x + 1) * half]
        send_ref[spot, width:] = retrieved[x * half : (x + 1) * half]


def home_rows(value, req_rows):
    first = lax.axis_index("shard") * req_rows
    row = lax.broadcasted_iota(jnp.int32, value.shape, 0)
    picked = [
        jnp.sum(jnp.where(row == first + i, value, 0.0), axis=0, keepdims=True)
        for i in range(req_rows)
    ]
    return jnp.concatenate(picked, axis=0)


def mlp_kernel(
    shards,
    part_ref,
    tokens_ref,
    gain_ref,
    gate_ref,
    up_ref,
    down_ref,
    mid_ref,
    retrieved_ref,
    *refs,
):
    *send_refs, down_scr = refs
    shard = lax.axis_index("shard")
    group_rows, width = tokens_ref.shape
    devices = 2 * shards
    req_rows = group_rows // shards
    attended = part_ref[:group_rows, :width].astype(jnp.float32)
    for source in range(1, devices):
        spot = slice(source * group_rows, (source + 1) * group_rows)
        attended += part_ref[spot, :width].astype(jnp.float32)
    mid_rows = (tokens_ref[...] + attended).astype(jnp.bfloat16)
    mlp_in = scaled_norm(mid_rows, gain_ref[...])
    contract = (((1,), (1,)), ((), ()))
    gate_part = lax.dot_general(
        mlp_in, gate_ref[...], contract, preferred_element_type=jnp.float32
    )
    up_part = lax.dot_general(mlp_in, up_ref[...], contract, preferred_element_type=jnp.float32)
    hidden = (silu(gate_part) * up_part).astype(jnp.bfloat16)
    down = jnp.dot(hidden, down_ref[...], preferred_element_type=jnp.float32)
    down_scr[...] = down.reshape(down_scr.shape)
    rows = send_refs[0].shape[0]
    for apart, send_ref in enumerate(send_refs):
        send_ref[...] = down_scr[pl.ds(pl.multiple_of((shard ^ apart) * rows, rows), rows), :]
    mid_ref[...] = home_rows(mid_rows.astype(jnp.float32), mid_ref.shape[0])
    heads = [
        home_rows(
            part_ref[source * group_rows : (source + 1) * group_rows, width:].astype(jnp.float32),
            req_rows,
        )
        for source in range(devices)
    ]
    retrieved_ref[...] = jnp.concatenate(heads, axis=1).astype(jnp.bfloat16)


def finish_kernel(mid_ref, *refs):
    *down_refs, layer_ref = refs
    total = down_refs[0][...]
    for down_ref in down_refs[1:]:
        total = total + down_ref[...]
    layer_ref[...] = (mid_ref[...] + total.reshape(mid_ref.shape)).astype(jnp.bfloat16)


def head_body(
    tokens,
    norm_gain,
    qkv_weight,
    conv_weight,
    conv_state,
    mesa_gates,
    mesa_bias,
    ridge_term,
    key_cache,
    value_cache,
    log_weight,
    page_owner,
    page_fill,
    out_weight,
    mlp_gain,
    gate_weight,
    up_weight,
    down_weight,
):
    shards = lax.axis_size("shard")
    devices = 2 * shards
    req_rows, width = tokens.shape
    slots, page, _ = key_cache.shape
    head_count = ridge_term.shape[0]
    head_size = width // head_count
    group_rows = shards * req_rows
    pair_rows = 2 * group_rows
    all_slots = devices * slots
    columns = qkv_weight.shape[1]
    shape = jax.ShapeDtypeStruct
    bf16, f32 = jnp.bfloat16, jnp.float32

    def exchange(value, axes):
        return lax.all_to_all(value, axes, split_axis=0, concat_axis=0, tiled=True)

    def spot(number):
        return number % 2 * shards + number // 2

    hbm = pl.BlockSpec(memory_space=pltpu.HBM)
    past_rows = jnp.transpose(conv_state, (1, 0, 2))
    gates = mesa_gates.T

    def pinned(*values):
        return [pltpu.with_memory_space_constraint(value, pltpu.HBM) for value in values]

    pieces = pl.pallas_call(
        cut_kernel,
        out_shape=(shape((2 * slots, page, head_size), bf16),) * devices,
        in_specs=[hbm] * 2,
        out_specs=(VMEM,) * devices,
        scratch_shapes=[
            pltpu.VMEM((2, *key_cache.shape), bf16),
            pltpu.SemaphoreType.DMA((2 * slots,)),
        ],
        compiler_params=PARAMS,
        name="cut",
    )(*pinned(key_cache, value_cache))

    def move(step):
        pairs = [
            (spot(source), spot(source ^ SEND[step][source >> 1 & 1])) for source in range(devices)
        ]
        return lax.ppermute(pieces[step], ("member", "shard"), pairs)

    moved = [pieces[0]] + [move(step) for step in range(1, 1 + EARLY)]
    tokens, pieces = lax.optimization_barrier((tokens, pieces))
    pack, misc = pl.pallas_call(
        pack_kernel,
        out_shape=(
            shape((devices * (req_rows * width // page + TILE), page), bf16),
            shape((GATES.stop, width), f32),
        ),
        in_specs=[hbm] * 10,
        out_specs=(VMEM,) * 2,
        scratch_shapes=[
            pltpu.VMEM(tokens.shape, bf16),
            pltpu.VMEM(log_weight.shape, bf16),
            pltpu.SMEM(page_owner.shape, jnp.int32),
            pltpu.SMEM(page_fill.shape, jnp.int32),
            pltpu.VMEM(past_rows.shape, bf16),
            pltpu.VMEM(gates.shape, bf16),
            pltpu.VMEM(conv_weight.shape, f32),
            pltpu.VMEM((1, width), f32),
            pltpu.VMEM((1, 2 * head_count), f32),
            pltpu.SMEM(ridge_term.shape, f32),
            pltpu.SemaphoreType.DMA((10,)),
        ],
        compiler_params=PARAMS,
        name="pack",
    )(
        *pinned(
            tokens,
            log_weight,
            page_owner,
            page_fill,
            past_rows,
            conv_weight,
            norm_gain[None, :],
            gates,
            mesa_bias[None, :],
            ridge_term,
        )
    )
    packs = exchange(pack, PAIR)

    pieces, packs = lax.optimization_barrier((pieces, packs))
    moved += [move(step) for step in range(1 + EARLY, devices)]

    mixed, own_tokens, weight, owner, strength = pl.pallas_call(
        functools.partial(project_kernel, shards, req_rows, slots, head_count),
        out_shape=(
            shape((devices * group_rows, head_size), bf16),
            shape((group_rows, width), f32),
            shape((all_slots, page), f32),
            shape((all_slots, page), jnp.int32),
            shape((pair_rows + TILE, head_size), f32),
        ),
        in_specs=[VMEM] * 3,
        out_specs=(VMEM,) * 5,
        scratch_shapes=[pltpu.VMEM((group_rows, columns), f32)],
        compiler_params=PARAMS,
        name="project",
    )(packs, misc, qkv_weight)

    def add_up(first, last, before, owner, weight):
        known = [] if before is None else [before]
        count = last - first + len(known)
        return pl.pallas_call(
            functools.partial(gram_kernel, first),
            out_shape=shape((pair_rows, head_size, 2 * head_size), f32),
            in_specs=[SMEM] + [VMEM] * (1 + count),
            out_specs=VMEM,
            input_output_aliases={1 + count: 0} if known else {},
            compiler_params=PARAMS,
            name="gram",
        )(owner, weight, *moved[first:last], *known)

    gram = add_up(0, 1 + EARLY, None, owner, weight)
    mixed, gram = lax.optimization_barrier((mixed, gram))
    all_mixed = exchange(mixed, PAIR)
    all_mixed, owner, weight, gram = lax.optimization_barrier((all_mixed, owner, weight, gram))
    gram = add_up(1 + EARLY, devices, gram, owner, weight)

    parts = pl.pallas_call(
        functools.partial(solve_kernel, head_count, columns // head_size),
        out_shape=shape((devices * group_rows, width + head_size), bf16),
        in_specs=[VMEM] * 4,
        out_specs=VMEM,
        compiler_params=PARAMS,
        name="solve",
    )(all_mixed, strength, gram, out_weight)
    all_parts = exchange(parts, PAIR)

    mid_home, retrieved, *down = pl.pallas_call(
        functools.partial(mlp_kernel, shards),
        out_shape=(
            shape((req_rows, width), f32),
            shape((req_rows, width), bf16),
        )
        + (shape((req_rows * head_count, head_size), f32),) * shards,
        in_specs=[VMEM] * 6,
        out_specs=(VMEM,) * (2 + shards),
        scratch_shapes=[pltpu.VMEM((group_rows * head_count, head_size), f32)],
        compiler_params=PARAMS,
        name="mlp",
    )(
        all_parts,
        own_tokens,
        mlp_gain[None, :],
        gate_weight.T,
        up_weight.T,
        down_weight,
    )
    arrived = [down[0]]
    for apart in range(1, shards):
        pairs = [(source, source ^ apart) for source in range(shards)]
        arrived.append(lax.ppermute(down[apart], "shard", pairs))
    layer_out = pl.pallas_call(
        finish_kernel,
        out_shape=shape((req_rows, width), bf16),
        in_specs=[VMEM] * (1 + shards),
        out_specs=VMEM,
        compiler_params=PARAMS,
        name="finish",
    )(mid_home, *arrived)
    return (retrieved, layer_out)


def specs(group):
    rows = P((*group, "shard"))
    return (
        (
            rows,
            P(),
            P(None, "shard"),
            P(None, "shard"),
            P(group, None, "shard"),
            P(),
            P(),
            P(),
            rows,
            rows,
            rows,
            rows,
            rows,
            P("shard", None),
            P(),
            P(None, "shard"),
            P(None, "shard"),
            P("shard", None),
        ),
        (rows, rows),
    )


def solution(mesh):
    groups, shards = mesh.devices.shape

    def run(*args):
        head_count = args[7].shape[0]
        if 2 * shards == head_count == len(SEND):
            axes = ("pair", "member", "shard")
            used = Mesh(mesh.devices.reshape(groups // 2, 2, shards), axes)
            body, group = head_body, ("pair", "member")
        else:
            used, body, group = mesh, spread_body, ("group",)
        in_specs, out_specs = specs(group)
        return jax.shard_map(
            body, mesh=used, in_specs=in_specs, out_specs=out_specs, check_vma=False
        )(*args)

    return run
```

```python
import functools

import jax
import jax.numpy as jnp
from jax import lax
from jax.experimental import pallas as pl
from jax.experimental.pallas import tpu as pltpu
from jax.sharding import Mesh
from jax.sharding import PartitionSpec as P

ITERS = 4


precise = lax.Precision.HIGHEST

VMEM = pl.BlockSpec(memory_space=pltpu.VMEM)
SMEM = pl.BlockSpec(memory_space=pltpu.SMEM)


def partner(value, axis, apart):
    mask = 2**apart
    pairs = [(source, source ^ mask) for source in range(lax.axis_size(axis))]
    return lax.ppermute(value, axis, pairs)


def scaled_norm(row_vals, gain_vec):
    wide_rows = row_vals.astype(jnp.float32)
    factor = lax.rsqrt(jnp.mean(wide_rows * wide_rows, axis=-1, keepdims=True) + 1e-05)
    return (wide_rows * factor * gain_vec).astype(jnp.bfloat16)


def unit_rows(vectors):
    return vectors * lax.rsqrt(jnp.sum(vectors * vectors, axis=-1, keepdims=True) + 1e-06)


def slot_weights(owner_hot, decay_rows, log_weight, page_fill):
    page_len = log_weight.shape[2]
    slot_decay = jnp.dot(owner_hot, decay_rows, precision=precise)
    live_mask = (jnp.arange(page_len)[None, :] < page_fill[:, None]).astype(jnp.float32)
    return slot_decay[:, :, None] * jnp.exp(log_weight.astype(jnp.float32)) * live_mask[:, None, :]


def slot_terms(key_rows, source_rows, owner_hot, slot_weight, directions):
    slot_count, page_len, width_all = key_rows.shape
    head_count = slot_weight.shape[1]
    head_size = width_all // head_count
    member_count = owner_hot.shape[1]
    slot_dir = jnp.dot(owner_hot, directions.reshape(member_count, width_all), precision=precise)
    slot_dir = slot_dir.reshape(slot_count, head_count, head_size)
    key_wide = key_rows.astype(jnp.float32).reshape(slot_count, page_len, head_count, head_size)
    scores = jnp.einsum("sthd,shd->sht", key_wide, slot_dir, precision=precise)
    source_wide = source_rows.astype(jnp.float32).reshape(
        slot_count, page_len, head_count, head_size
    )
    contribution = jnp.einsum("sht,sthd->shd", slot_weight * scores, source_wide, precision=precise)
    summed = jnp.dot(owner_hot.T, contribution.reshape(slot_count, width_all), precision=precise)
    return summed.reshape(member_count, head_count, head_size)


def new_term(vectors, source_rows, strength_rows, key_new):
    return (
        strength_rows[:, :, None] * source_rows * jnp.sum(key_new * vectors, axis=-1, keepdims=True)
    )


def conjugate(query_rows, key_new, value_new, strength_rows, ridge_term, reduce_fn):
    solution = jnp.zeros_like(query_rows)
    residual = query_rows
    direction = query_rows
    res_norm = jnp.sum(residual * residual, axis=-1)
    for iteration in range(ITERS):
        image_vec = (
            reduce_fn(direction, False)
            + new_term(direction, key_new, strength_rows, key_new)
            + ridge_term[None, :, None] * direction
        )
        step_size = res_norm / jnp.sum(direction * image_vec, axis=-1)
        solution = solution + step_size[:, :, None] * direction
        residual = residual - step_size[:, :, None] * image_vec
        next_norm = jnp.sum(residual * residual, axis=-1)
        direction = residual + (next_norm / res_norm)[:, :, None] * direction
        res_norm = next_norm
    return reduce_fn(solution, True) + new_term(solution, value_new, strength_rows, key_new)


def pair_order(mine, theirs, parity):
    first = jnp.where(parity == 0, mine, theirs)
    second = jnp.where(parity == 0, theirs, mine)
    return jnp.concatenate([first, second], axis=0)


def spread_body(
    tokens,
    norm_gain,
    qkv_weight,
    conv_weight,
    conv_state,
    mesa_gates,
    mesa_bias,
    ridge_term,
    key_cache,
    value_cache,
    log_weight,
    page_owner,
    page_fill,
    out_weight,
    mlp_gain,
    gate_weight,
    up_weight,
    down_weight,
):
    req_rows = tokens.shape[0]
    group_rows = req_rows * lax.axis_size("shard")
    head_count = ridge_term.shape[0]
    width_all = key_cache.shape[2]
    head_size = width_all // head_count
    parity = lax.axis_index("group") % 2
    normed = scaled_norm(tokens, norm_gain)
    fresh_proj = jnp.dot(
        lax.all_gather(normed, "shard", axis=0, tiled=True),
        qkv_weight,
        preferred_element_type=jnp.float32,
    )
    past_rows = conv_state.astype(jnp.float32)
    pre_conv = (
        conv_weight[3] * fresh_proj
        + conv_weight[0] * past_rows[:, 0]
        + conv_weight[1] * past_rows[:, 1]
        + conv_weight[2] * past_rows[:, 2]
    )
    mixed_cols = jax.nn.silu(pre_conv).astype(jnp.bfloat16)
    home_rows = lax.all_to_all(mixed_cols, "shard", split_axis=0, concat_axis=1, tiled=True)
    split_rows = home_rows.astype(jnp.float32).reshape(req_rows, 3, head_count, head_size)
    query_home = unit_rows(split_rows[:, 0])
    key_home = unit_rows(split_rows[:, 1])
    value_home = split_rows[:, 2]
    gate_vals = jax.nn.sigmoid(
        jnp.dot(normed, mesa_gates, preferred_element_type=jnp.float32) + mesa_bias
    )
    decay_home = gate_vals[:, :head_count]
    strength_home = gate_vals[:, head_count:]
    owner_hot = (page_owner[:, None] == jnp.arange(2 * group_rows)[None, :]).astype(jnp.float32)
    stored = {}

    def cache_pass(directions, decay_grp, with_values):
        far_dirs, far_decay = partner((directions, decay_grp), "group", 0)
        pair_dirs = pair_order(directions, far_dirs, parity)
        pair_decay = pair_order(decay_grp, far_decay, parity)
        if "weight" not in stored:
            stored["weight"] = slot_weights(owner_hot, pair_decay, log_weight, page_fill)
        source_rows = value_cache if with_values else key_cache
        summed = slot_terms(key_cache, source_rows, owner_hot, stored["weight"], pair_dirs)
        mine = jnp.where(parity == 0, summed[:group_rows], summed[group_rows:])
        theirs = jnp.where(parity == 0, summed[group_rows:], summed[:group_rows])
        returned = partner(theirs, "group", 0)
        return mine + returned

    def reduce_home(vectors, with_values):
        directions, decay_grp = (
            lax.all_gather(vectors, "shard", axis=0, tiled=True),
            lax.all_gather(decay_home, "shard", axis=0, tiled=True),
        )
        return lax.psum_scatter(
            cache_pass(directions, decay_grp, with_values), "shard", scatter_dimension=0, tiled=True
        )

    found = conjugate(query_home, key_home, value_home, strength_home, ridge_term, reduce_home)
    retrieved = found.reshape(req_rows, width_all).astype(jnp.bfloat16)
    columns = lax.all_to_all(retrieved, "shard", split_axis=1, concat_axis=0, tiled=True)
    attended = lax.psum_scatter(
        jnp.dot(columns, out_weight, preferred_element_type=jnp.float32),
        "shard",
        scatter_dimension=0,
        tiled=True,
    )
    mid_rows = (tokens.astype(jnp.float32) + attended).astype(jnp.bfloat16)
    mlp_in = scaled_norm(mid_rows, mlp_gain)
    piece_rows = lax.all_gather(mlp_in, "shard", axis=0, tiled=True)
    gate_part = jnp.dot(piece_rows, gate_weight, preferred_element_type=jnp.float32)
    up_part = jnp.dot(piece_rows, up_weight, preferred_element_type=jnp.float32)
    hidden_rows = (jax.nn.silu(gate_part) * up_part).astype(jnp.bfloat16)
    down_part = lax.psum_scatter(
        jnp.dot(hidden_rows, down_weight, preferred_element_type=jnp.float32),
        "shard",
        scatter_dimension=0,
        tiled=True,
    )
    layer_out = (mid_rows.astype(jnp.float32) + down_part).astype(jnp.bfloat16)
    return (retrieved, layer_out)


TILE = 8
MASKED = -1e38
PAIR = ("shard", "member")
PARAMS = pltpu.CompilerParams(vmem_limit_bytes=16 * 1024 * 1024)
PAST, TAP, GAIN, BIAS, RIDGE = slice(0, 8), slice(8, 9), slice(9, 10), slice(10, 11), slice(11, 12)
GATES = slice(16, 32)

SEND = ((0, 0), (1, 4), (4, 1), (3, 6), (6, 3), (5, 5), (7, 7), (2, 2))
FROM = tuple((b, a) if a & 2 else (a, b) for a, b in SEND)
EARLY = 4
NEAR = 3


def split_pair(value):
    high = value.astype(jnp.bfloat16)
    low = (value - high.astype(jnp.float32)).astype(jnp.bfloat16)
    return high, low


def hot(rows, columns, target_fn):
    row = lax.broadcasted_iota(jnp.int32, (rows, columns), 0)
    column = lax.broadcasted_iota(jnp.int32, (rows, columns), 1)
    return jnp.where(column == target_fn(row), 1.0, 0.0).astype(jnp.bfloat16)


def here():
    return lax.axis_index("shard") * 2 + lax.axis_index("member")


def at_step(table, step, me):
    return me ^ jnp.where((me & 2) == 0, table[step][0], table[step][1])


def silu(value):
    return value / (1.0 + jnp.exp(-value))


def cut_kernel(key_hbm, value_hbm, *refs):
    *piece_refs, stage_ref, load_sems, cut_sems = refs
    slots = key_hbm.shape[0]
    head_size = piece_refs[0].shape[2]
    me = here()
    loads = [
        pltpu.make_async_copy(
            source.at[slot], stage_ref.at[part, slot], load_sems.at[part * slots + slot]
        )
        for part, source in enumerate((key_hbm, value_hbm))
        for slot in range(slots)
    ]
    for load in loads:
        load.start()
    starts = [
        pl.multiple_of(at_step(SEND, step, me) * head_size, head_size)
        for step in range(len(piece_refs))
    ]
    cuts = []
    for part in range(2):
        for slot in range(slots):
            loads[part * slots + slot].wait()
        for step in range(NEAR, len(piece_refs)):
            cut = pltpu.make_async_copy(
                stage_ref.at[part, :, :, pl.ds(starts[step], head_size)],
                piece_refs[step].at[pl.ds(part * slots, slots)],
                cut_sems.at[2 * step + part],
            )
            cut.start()
            cuts.append(cut)
        for slot in range(slots):
            for start, piece_ref in zip(starts[:NEAR], piece_refs):
                piece_ref[part * slots + slot] = stage_ref[part, slot, :, pl.ds(start, head_size)]
    for cut in cuts:
        cut.wait()


def pack_kernel(
    tokens_hbm,
    logs_hbm,
    owner_hbm,
    fill_hbm,
    past_hbm,
    tap_hbm,
    gain_hbm,
    gates_hbm,
    bias_hbm,
    ridge_hbm,
    send_ref,
    misc_ref,
    tokens_ref,
    logs_ref,
    owner_ref,
    fill_ref,
    state_ref,
    gates_ref,
    tap_ref,
    gain_ref,
    bias_ref,
    ridge_ref,
    sems,
):
    req_rows, width = tokens_ref.shape
    slots, head_count, page = logs_ref.shape
    copies = [
        pltpu.make_async_copy(source, target, sems.at[place])
        for place, (source, target) in enumerate(
            [
                (owner_hbm, owner_ref),
                (fill_hbm, fill_ref),
                (tokens_hbm, tokens_ref),
                (logs_hbm, logs_ref),
                (past_hbm, state_ref),
                (tap_hbm, tap_ref),
                (gain_hbm, gain_ref),
                (gates_hbm, gates_ref),
                (bias_hbm, bias_ref),
                (ridge_hbm, ridge_ref),
            ]
        )
    ]
    for copy in copies:
        copy.start()
    for copy in copies:
        copy.wait()

    tokens = tokens_ref[...].astype(jnp.float32)
    rows = [
        tokens[row : row + 1, first : first + page]
        for row in range(req_rows)
        for first in range(0, width, page)
    ]
    tile = jnp.concatenate(rows, axis=0).astype(jnp.bfloat16)
    packed = tile.shape[0] + TILE
    spot = lax.broadcasted_iota(jnp.int32, (head_count, page), 1)
    logs = []
    lane = lax.broadcasted_iota(jnp.int32, (1, page), 1)
    owners = jnp.zeros((1, page), jnp.float32)
    for slot in range(slots):
        rows = logs_ref[slot].astype(jnp.float32)
        logs.append(jnp.where(spot < fill_ref[slot], rows, MASKED))
        owners = jnp.where(lane == slot, owner_ref[slot].astype(jnp.float32), owners)
    rest = jnp.zeros((TILE - slots - 1, page), jnp.float32)
    for head in range(head_count):
        rows = [log[head : head + 1, :] for log in logs]
        side = jnp.concatenate([*rows, owners, rest], axis=0).astype(jnp.bfloat16)
        send_ref[head * packed : head * packed + tile.shape[0], :] = tile
        send_ref[head * packed + tile.shape[0] : (head + 1) * packed, :] = side

    past = tap_ref[0:1, :] * state_ref[0].astype(jnp.float32)
    past = past + tap_ref[1:2, :] * state_ref[1].astype(jnp.float32)
    past = past + tap_ref[2:3, :] * state_ref[2].astype(jnp.float32)
    columns = past.shape[1]
    misc_ref[PAST, :columns] = past
    misc_ref[TAP, :columns] = tap_ref[3:4, :]
    misc_ref[GAIN, :] = gain_ref[...]
    misc_ref[BIAS, : 2 * head_count] = bias_ref[...]
    ridges = jnp.zeros((1, page), jnp.float32)
    for head in range(head_count):
        ridges = jnp.where(lane == head, ridge_ref[head], ridges)
    misc_ref[RIDGE, :page] = ridges
    misc_ref[GATES, :] = gates_ref[...].astype(jnp.float32)


def project_kernel(
    shards,
    req_rows,
    slots,
    head_count,
    pack_ref,
    misc_ref,
    qkv_ref,
    send_ref,
    tokens_ref,
    weight_ref,
    owner_ref,
    strength_ref,
    mixed_ref,
):
    shard = lax.axis_index("shard")
    member = lax.axis_index("member")
    head = here()
    group_rows = shards * req_rows
    pair_rows = 2 * group_rows
    width = misc_ref.shape[1]
    columns = qkv_ref.shape[1]
    page = weight_ref.shape[1]
    head_size = send_ref.shape[1]
    blocks = columns // head_size
    parts = width // page
    packed = pack_ref.shape[0]
    tall = packed // (2 * shards)

    def rows_of(first, count):
        def home_of(row):
            request = row % count + first
            x = request // group_rows
            s = (request % group_rows) // req_rows
            return (s * 2 + x) * tall + request % req_rows * parts + row // count

        picked = jnp.dot(
            hot(count * parts, packed, home_of), pack_ref[...], preferred_element_type=jnp.float32
        )
        return jnp.concatenate(
            [picked[part * count : (part + 1) * count] for part in range(parts)], axis=1
        )

    own_tokens = rows_of(member * group_rows, group_rows)
    tokens_ref[...] = own_tokens
    own = scaled_norm(own_tokens, misc_ref[GAIN, :])
    fresh = jnp.dot(own, qkv_ref[...], preferred_element_type=jnp.float32)
    before = misc_ref[TAP, :columns] * fresh + misc_ref[PAST, :columns]
    mixed_ref[...] = silu(before)
    for target in range(head_count):
        place = jnp.int32(0)
        for part in range(3):
            local = target + part * head_count - shard * blocks
            place = jnp.where((local >= 0) & (local < blocks), local, place)
        start = pl.multiple_of(place * head_size, head_size)
        send_ref[target * group_rows : (target + 1) * group_rows, :] = mixed_ref[
            :, pl.ds(start, head_size)
        ].astype(jnp.bfloat16)

    normed = scaled_norm(rows_of(0, pair_rows), misc_ref[GAIN, :])
    raw = lax.dot_general(
        normed,
        misc_ref[GATES, :].astype(jnp.bfloat16),
        (((1,), (1,)), ((), ())),
        preferred_element_type=jnp.float32,
    )
    gate_vals = 1.0 / (1.0 + jnp.exp(-(raw + misc_ref[BIAS, : 2 * head_count])))
    column = lax.broadcasted_iota(jnp.int32, gate_vals.shape, 1)
    decay = jnp.sum(jnp.where(column == head, gate_vals, 0.0), axis=1, keepdims=True)
    strength = jnp.sum(
        jnp.where(column == head + head_count, gate_vals, 0.0), axis=1, keepdims=True
    )
    strength_ref[:pair_rows, :] = jnp.broadcast_to(strength, (pair_rows, head_size))
    ridges = misc_ref[RIDGE, :page]
    spot = lax.broadcasted_iota(jnp.int32, ridges.shape, 1)
    ridge = jnp.sum(jnp.where(spot == head, ridges, 0.0), axis=1, keepdims=True)
    strength_ref[pair_rows:, :] = jnp.broadcast_to(ridge, (TILE, head_size))

    all_slots = 2 * shards * slots
    side = tall - TILE
    pick_slot = hot(all_slots, packed, lambda row: (row // slots) * tall + side + row % slots)
    logs = jnp.dot(pick_slot, pack_ref[...], preferred_element_type=jnp.float32)
    pick_owner = hot(all_slots, packed, lambda row: (row // slots) * tall + side + slots)
    owners = jnp.dot(pick_owner, pack_ref[...], preferred_element_type=jnp.float32)
    at_slot = hot(all_slots, page, lambda row: row % slots).astype(jnp.float32)
    owner = jnp.sum(at_slot * owners, axis=1, keepdims=True).astype(jnp.int32)
    owner_ref[...] = jnp.broadcast_to(owner, owner_ref.shape)
    request = lax.broadcasted_iota(jnp.int32, (all_slots, pair_rows), 1)
    owner_hot = jnp.where(request == owner, 1.0, 0.0)
    wide_decay = jnp.broadcast_to(decay, (pair_rows, page))
    slot_decay = jnp.dot(
        owner_hot, wide_decay, precision=precise, preferred_element_type=jnp.float32
    )
    weight_ref[...] = slot_decay * jnp.exp(logs)


def gram_kernel(first, owner_ref, weight_ref, *refs):
    if first:
        *piece_refs, before_ref, gram_ref = refs
    else:
        *piece_refs, gram_ref = refs
        gram_ref[...] = jnp.zeros_like(gram_ref)
    me = here()
    slots = piece_refs[0].shape[0] // 2
    for step, piece_ref in enumerate(piece_refs, first):
        for spot in range(slots):
            slot = at_step(FROM, step, me) * slots + spot
            keys = piece_ref[spot]
            both = jnp.concatenate([keys, piece_ref[slots + spot]], axis=1)
            turned = keys.T.astype(jnp.float32) * weight_ref[pl.ds(slot, 1), :]
            high, low = split_pair(turned)
            piece = jnp.dot(high, both, preferred_element_type=jnp.float32) + jnp.dot(
                low, both, preferred_element_type=jnp.float32
            )
            owner = owner_ref[slot, 0]
            gram_ref[owner] = gram_ref[owner] + piece


def solve_kernel(
    head_count,
    blocks,
    mixed_ref,
    strength_ref,
    gram_ref,
    out_ref,
    own_ref,
    other_ref,
    part_ref,
):
    head = here()
    member = lax.axis_index("member")
    pair_rows, head_size, _ = gram_ref.shape
    width = out_ref.shape[1]

    def columns_of(block):
        first = pl.multiple_of(block // blocks * pair_rows, pair_rows)
        return mixed_ref[pl.ds(first, pair_rows), :].astype(jnp.float32)

    query = unit_rows(columns_of(head))
    key_new = unit_rows(columns_of(head + head_count))
    value_new = columns_of(head + 2 * head_count)
    strength = strength_ref[:pair_rows, :]
    ridge = strength_ref[pair_rows : pair_rows + 1, :]

    def image_of(vectors, columns):
        turned = vectors.T
        pieces = []
        for row in range(pair_rows):
            spread = jnp.broadcast_to(turned[:, row : row + 1], (head_size, head_size))
            pieces.append(jnp.sum(gram_ref[row, :, columns] * spread, axis=0, keepdims=True))
        return jnp.concatenate(pieces, axis=0)

    found = jnp.zeros_like(query)
    residual = query
    direction = query
    res_norm = jnp.sum(residual * residual, axis=-1, keepdims=True)
    for iteration in range(ITERS):
        along = jnp.sum(key_new * direction, axis=-1, keepdims=True)
        image = image_of(direction, slice(0, head_size))
        image = image + strength * key_new * along + ridge * direction
        step = res_norm / jnp.sum(direction * image, axis=-1, keepdims=True)
        found = found + step * direction
        residual = residual - step * image
        next_norm = jnp.sum(residual * residual, axis=-1, keepdims=True)
        direction = residual + (next_norm / res_norm) * direction
        res_norm = next_norm

    total = image_of(found, slice(head_size, 2 * head_size))
    total = total + strength * value_new * jnp.sum(key_new * found, axis=-1, keepdims=True)
    retrieved = total.astype(jnp.bfloat16)
    start = pl.multiple_of(member * head_size, head_size)
    part_ref[:, :width] = jnp.dot(
        retrieved, out_ref[pl.ds(start, head_size), :], preferred_element_type=jnp.float32
    )
    part_ref[:, width:] = retrieved.astype(jnp.float32)
    half = pair_rows // 2
    mine = pl.multiple_of(member * half, half)
    theirs = pl.multiple_of((1 - member) * half, half)
    own_ref[...] = part_ref[pl.ds(mine, half), :].astype(jnp.bfloat16)
    other_ref[...] = part_ref[pl.ds(theirs, half), :].astype(jnp.bfloat16)


def home_rows(value, req_rows):
    first = lax.axis_index("shard") * req_rows
    row = lax.broadcasted_iota(jnp.int32, value.shape, 0)
    picked = [
        jnp.sum(jnp.where(row == first + i, value, 0.0), axis=0, keepdims=True)
        for i in range(req_rows)
    ]
    return jnp.concatenate(picked, axis=0)


def mlp_kernel(
    devices,
    tokens_ref,
    gain_ref,
    gate_ref,
    up_ref,
    down_ref,
    *refs,
):
    part_refs, refs = refs[:devices], refs[devices:]
    mid_ref, retrieved_ref, *send_refs, down_scr, heads_ref = refs
    shard = lax.axis_index("shard")
    me = here()
    group_rows, width = tokens_ref.shape
    req_rows = mid_ref.shape[0]
    head_size = part_refs[0].shape[1] - width
    attended = part_refs[0][:, :width].astype(jnp.float32)
    for part_ref in part_refs[1:]:
        attended += part_ref[:, :width].astype(jnp.float32)
    mid_rows = (tokens_ref[...] + attended).astype(jnp.bfloat16)
    mlp_in = scaled_norm(mid_rows, gain_ref[...])
    contract = (((1,), (1,)), ((), ()))
    gate_part = lax.dot_general(
        mlp_in, gate_ref[...], contract, preferred_element_type=jnp.float32
    )
    up_part = lax.dot_general(mlp_in, up_ref[...], contract, preferred_element_type=jnp.float32)
    hidden = (silu(gate_part) * up_part).astype(jnp.bfloat16)
    down = jnp.dot(hidden, down_ref[...], preferred_element_type=jnp.float32)
    down_scr[...] = down.reshape(down_scr.shape)
    rows = send_refs[0].shape[0]
    for apart, send_ref in enumerate(send_refs):
        send_ref[...] = down_scr[pl.ds(pl.multiple_of((shard ^ apart) * rows, rows), rows), :]
    mid_ref[...] = home_rows(mid_rows.astype(jnp.float32), mid_ref.shape[0])
    for apart, part_ref in enumerate(part_refs):
        first = pl.multiple_of((me ^ apart) * head_size, head_size)
        heads_ref[:, pl.ds(first, head_size)] = home_rows(
            part_ref[:, width:].astype(jnp.float32), req_rows
        )
    retrieved_ref[...] = heads_ref[...].astype(jnp.bfloat16)


def finish_kernel(mid_ref, *refs):
    *down_refs, layer_ref = refs
    total = down_refs[0][...]
    for down_ref in down_refs[1:]:
        total = total + down_ref[...]
    layer_ref[...] = (mid_ref[...] + total.reshape(mid_ref.shape)).astype(jnp.bfloat16)


def head_body(
    tokens,
    norm_gain,
    qkv_weight,
    conv_weight,
    conv_state,
    mesa_gates,
    mesa_bias,
    ridge_term,
    key_cache,
    value_cache,
    log_weight,
    page_owner,
    page_fill,
    out_weight,
    mlp_gain,
    gate_weight,
    up_weight,
    down_weight,
):
    shards = lax.axis_size("shard")
    devices = 2 * shards
    req_rows, width = tokens.shape
    slots, page, _ = key_cache.shape
    head_count = ridge_term.shape[0]
    head_size = width // head_count
    group_rows = shards * req_rows
    pair_rows = 2 * group_rows
    all_slots = devices * slots
    columns = qkv_weight.shape[1]
    shape = jax.ShapeDtypeStruct
    bf16, f32 = jnp.bfloat16, jnp.float32

    def exchange(value, axes):
        return lax.all_to_all(value, axes, split_axis=0, concat_axis=0, tiled=True)

    def spot(number):
        return number % 2 * shards + number // 2

    hbm = pl.BlockSpec(memory_space=pltpu.HBM)
    past_rows = jnp.transpose(conv_state, (1, 0, 2))
    gates = mesa_gates.T

    def pinned(*values):
        return [pltpu.with_memory_space_constraint(value, pltpu.HBM) for value in values]

    pieces = pl.pallas_call(
        cut_kernel,
        out_shape=(pltpu.VMEM((2 * slots, page, head_size), bf16),) * NEAR
        + (pltpu.HBM((2 * slots, page, head_size), bf16),) * (devices - NEAR),
        in_specs=[hbm] * 2,
        out_specs=(VMEM,) * NEAR + (hbm,) * (devices - NEAR),
        scratch_shapes=[
            pltpu.VMEM((2, *key_cache.shape), bf16),
            pltpu.SemaphoreType.DMA((2 * slots,)),
            pltpu.SemaphoreType.DMA((2 * devices,)),
        ],
        compiler_params=PARAMS,
        name="cut",
    )(*pinned(key_cache, value_cache))

    def move(step):
        pairs = [
            (spot(source), spot(source ^ SEND[step][source >> 1 & 1])) for source in range(devices)
        ]
        return lax.ppermute(pieces[step], ("member", "shard"), pairs)

    moved = [pieces[0]] + [move(step) for step in range(1, 1 + EARLY)]
    tokens, pieces = lax.optimization_barrier((tokens, pieces))
    pack, misc = pl.pallas_call(
        pack_kernel,
        out_shape=(
            shape((devices * (req_rows * width // page + TILE), page), bf16),
            shape((GATES.stop, width), f32),
        ),
        in_specs=[hbm] * 10,
        out_specs=(VMEM,) * 2,
        scratch_shapes=[
            pltpu.VMEM(tokens.shape, bf16),
            pltpu.VMEM(log_weight.shape, bf16),
            pltpu.SMEM(page_owner.shape, jnp.int32),
            pltpu.SMEM(page_fill.shape, jnp.int32),
            pltpu.VMEM(past_rows.shape, bf16),
            pltpu.VMEM(gates.shape, bf16),
            pltpu.VMEM(conv_weight.shape, f32),
            pltpu.VMEM((1, width), f32),
            pltpu.VMEM((1, 2 * head_count), f32),
            pltpu.SMEM(ridge_term.shape, f32),
            pltpu.SemaphoreType.DMA((10,)),
        ],
        compiler_params=PARAMS,
        name="pack",
    )(
        *pinned(
            tokens,
            log_weight,
            page_owner,
            page_fill,
            past_rows,
            conv_weight,
            norm_gain[None, :],
            gates,
            mesa_bias[None, :],
            ridge_term,
        )
    )
    packs = exchange(pack, PAIR)

    pieces, packs = lax.optimization_barrier((pieces, packs))
    moved += [move(step) for step in range(1 + EARLY, devices)]

    mixed, own_tokens, weight, owner, strength = pl.pallas_call(
        functools.partial(project_kernel, shards, req_rows, slots, head_count),
        out_shape=(
            shape((devices * group_rows, head_size), bf16),
            shape((group_rows, width), f32),
            shape((all_slots, page), f32),
            shape((all_slots, page), jnp.int32),
            shape((pair_rows + TILE, head_size), f32),
        ),
        in_specs=[VMEM] * 3,
        out_specs=(VMEM,) * 5,
        scratch_shapes=[pltpu.VMEM((group_rows, columns), f32)],
        compiler_params=PARAMS,
        name="project",
    )(packs, misc, qkv_weight)

    def add_up(first, last, before, owner, weight):
        known = [] if before is None else [before]
        count = last - first + len(known)
        return pl.pallas_call(
            functools.partial(gram_kernel, first),
            out_shape=shape((pair_rows, head_size, 2 * head_size), f32),
            in_specs=[SMEM] + [VMEM] * (1 + count),
            out_specs=VMEM,
            input_output_aliases={1 + count: 0} if known else {},
            compiler_params=PARAMS,
            name="gram",
        )(owner, weight, *moved[first:last], *known)

    gram = add_up(0, 1 + EARLY, None, owner, weight)
    mixed, gram = lax.optimization_barrier((mixed, gram))
    all_mixed = exchange(mixed, PAIR)
    all_mixed, owner, weight, gram = lax.optimization_barrier((all_mixed, owner, weight, gram))
    gram = add_up(1 + EARLY, devices, gram, owner, weight)

    own_part, other_part = pl.pallas_call(
        functools.partial(solve_kernel, head_count, columns // head_size),
        out_shape=(shape((group_rows, width + head_size), bf16),) * 2,
        in_specs=[VMEM] * 4,
        out_specs=(VMEM,) * 2,
        scratch_shapes=[pltpu.VMEM((pair_rows, width + head_size), f32)],
        compiler_params=PARAMS,
        name="solve",
    )(all_mixed, strength, gram, out_weight)
    parts = [own_part]
    for apart in range(1, devices):
        pairs = [(spot(source), spot(source ^ apart)) for source in range(devices)]
        sent = other_part if apart % 2 else own_part
        parts.append(lax.ppermute(sent, ("member", "shard"), pairs))

    mid_home, retrieved, *down = pl.pallas_call(
        functools.partial(mlp_kernel, devices),
        out_shape=(
            shape((req_rows, width), f32),
            shape((req_rows, width), bf16),
        )
        + (shape((req_rows * head_count, head_size), f32),) * shards,
        in_specs=[VMEM] * (5 + devices),
        out_specs=(VMEM,) * (2 + shards),
        scratch_shapes=[
            pltpu.VMEM((group_rows * head_count, head_size), f32),
            pltpu.VMEM((req_rows, width), f32),
        ],
        compiler_params=PARAMS,
        name="mlp",
    )(
        own_tokens,
        mlp_gain[None, :],
        gate_weight.T,
        up_weight.T,
        down_weight,
        *parts,
    )
    arrived = [down[0]]
    for apart in range(1, shards):
        pairs = [(source, source ^ apart) for source in range(shards)]
        arrived.append(lax.ppermute(down[apart], "shard", pairs))
    layer_out = pl.pallas_call(
        finish_kernel,
        out_shape=shape((req_rows, width), bf16),
        in_specs=[VMEM] * (1 + shards),
        out_specs=VMEM,
        compiler_params=PARAMS,
        name="finish",
    )(mid_home, *arrived)
    return (retrieved, layer_out)


def specs(group):
    rows = P((*group, "shard"))
    return (
        (
            rows,
            P(),
            P(None, "shard"),
            P(None, "shard"),
            P(group, None, "shard"),
            P(),
            P(),
            P(),
            rows,
            rows,
            rows,
            rows,
            rows,
            P("shard", None),
            P(),
            P(None, "shard"),
            P(None, "shard"),
            P("shard", None),
        ),
        (rows, rows),
    )


def solution(mesh):
    groups, shards = mesh.devices.shape

    def run(*args):
        head_count = args[7].shape[0]
        if 2 * shards == head_count == len(SEND):
            axes = ("pair", "member", "shard")
            used = Mesh(mesh.devices.reshape(groups // 2, 2, shards), axes)
            body, group = head_body, ("pair", "member")
        else:
            used, body, group = mesh, spread_body, ("group",)
        in_specs, out_specs = specs(group)
        return jax.shard_map(
            body, mesh=used, in_specs=in_specs, out_specs=out_specs, check_vma=False
        )(*args)

    return run
```

```python
import functools

import jax
import jax.numpy as jnp
from jax import lax
from jax.experimental import pallas as pl
from jax.experimental.pallas import tpu as pltpu
from jax.sharding import Mesh
from jax.sharding import PartitionSpec as P

ITERS = 4


precise = lax.Precision.HIGHEST

VMEM = pl.BlockSpec(memory_space=pltpu.VMEM)
SMEM = pl.BlockSpec(memory_space=pltpu.SMEM)


def partner(value, axis, apart):
    mask = 2**apart
    pairs = [(source, source ^ mask) for source in range(lax.axis_size(axis))]
    return lax.ppermute(value, axis, pairs)


def scaled_norm(row_vals, gain_vec):
    wide_rows = row_vals.astype(jnp.float32)
    factor = lax.rsqrt(jnp.mean(wide_rows * wide_rows, axis=-1, keepdims=True) + 1e-05)
    return (wide_rows * factor * gain_vec).astype(jnp.bfloat16)


def unit_rows(vectors):
    return vectors * lax.rsqrt(jnp.sum(vectors * vectors, axis=-1, keepdims=True) + 1e-06)


def slot_weights(owner_hot, decay_rows, log_weight, page_fill):
    page_len = log_weight.shape[2]
    slot_decay = jnp.dot(owner_hot, decay_rows, precision=precise)
    live_mask = (jnp.arange(page_len)[None, :] < page_fill[:, None]).astype(jnp.float32)
    return slot_decay[:, :, None] * jnp.exp(log_weight.astype(jnp.float32)) * live_mask[:, None, :]


def slot_terms(key_rows, source_rows, owner_hot, slot_weight, directions):
    slot_count, page_len, width_all = key_rows.shape
    head_count = slot_weight.shape[1]
    head_size = width_all // head_count
    member_count = owner_hot.shape[1]
    slot_dir = jnp.dot(owner_hot, directions.reshape(member_count, width_all), precision=precise)
    slot_dir = slot_dir.reshape(slot_count, head_count, head_size)
    key_wide = key_rows.astype(jnp.float32).reshape(slot_count, page_len, head_count, head_size)
    scores = jnp.einsum("sthd,shd->sht", key_wide, slot_dir, precision=precise)
    source_wide = source_rows.astype(jnp.float32).reshape(
        slot_count, page_len, head_count, head_size
    )
    contribution = jnp.einsum("sht,sthd->shd", slot_weight * scores, source_wide, precision=precise)
    summed = jnp.dot(owner_hot.T, contribution.reshape(slot_count, width_all), precision=precise)
    return summed.reshape(member_count, head_count, head_size)


def new_term(vectors, source_rows, strength_rows, key_new):
    return (
        strength_rows[:, :, None] * source_rows * jnp.sum(key_new * vectors, axis=-1, keepdims=True)
    )


def conjugate(query_rows, key_new, value_new, strength_rows, ridge_term, reduce_fn):
    solution = jnp.zeros_like(query_rows)
    residual = query_rows
    direction = query_rows
    res_norm = jnp.sum(residual * residual, axis=-1)
    for iteration in range(ITERS):
        image_vec = (
            reduce_fn(direction, False)
            + new_term(direction, key_new, strength_rows, key_new)
            + ridge_term[None, :, None] * direction
        )
        step_size = res_norm / jnp.sum(direction * image_vec, axis=-1)
        solution = solution + step_size[:, :, None] * direction
        residual = residual - step_size[:, :, None] * image_vec
        next_norm = jnp.sum(residual * residual, axis=-1)
        direction = residual + (next_norm / res_norm)[:, :, None] * direction
        res_norm = next_norm
    return reduce_fn(solution, True) + new_term(solution, value_new, strength_rows, key_new)


def pair_order(mine, theirs, parity):
    first = jnp.where(parity == 0, mine, theirs)
    second = jnp.where(parity == 0, theirs, mine)
    return jnp.concatenate([first, second], axis=0)


def spread_body(
    tokens,
    norm_gain,
    qkv_weight,
    conv_weight,
    conv_state,
    mesa_gates,
    mesa_bias,
    ridge_term,
    key_cache,
    value_cache,
    log_weight,
    page_owner,
    page_fill,
    out_weight,
    mlp_gain,
    gate_weight,
    up_weight,
    down_weight,
):
    req_rows = tokens.shape[0]
    group_rows = req_rows * lax.axis_size("shard")
    head_count = ridge_term.shape[0]
    width_all = key_cache.shape[2]
    head_size = width_all // head_count
    parity = lax.axis_index("group") % 2
    normed = scaled_norm(tokens, norm_gain)
    fresh_proj = jnp.dot(
        lax.all_gather(normed, "shard", axis=0, tiled=True),
        qkv_weight,
        preferred_element_type=jnp.float32,
    )
    past_rows = conv_state.astype(jnp.float32)
    pre_conv = (
        conv_weight[3] * fresh_proj
        + conv_weight[0] * past_rows[:, 0]
        + conv_weight[1] * past_rows[:, 1]
        + conv_weight[2] * past_rows[:, 2]
    )
    mixed_cols = jax.nn.silu(pre_conv).astype(jnp.bfloat16)
    home_rows = lax.all_to_all(mixed_cols, "shard", split_axis=0, concat_axis=1, tiled=True)
    split_rows = home_rows.astype(jnp.float32).reshape(req_rows, 3, head_count, head_size)
    query_home = unit_rows(split_rows[:, 0])
    key_home = unit_rows(split_rows[:, 1])
    value_home = split_rows[:, 2]
    gate_vals = jax.nn.sigmoid(
        jnp.dot(normed, mesa_gates, preferred_element_type=jnp.float32) + mesa_bias
    )
    decay_home = gate_vals[:, :head_count]
    strength_home = gate_vals[:, head_count:]
    owner_hot = (page_owner[:, None] == jnp.arange(2 * group_rows)[None, :]).astype(jnp.float32)
    stored = {}

    def cache_pass(directions, decay_grp, with_values):
        far_dirs, far_decay = partner((directions, decay_grp), "group", 0)
        pair_dirs = pair_order(directions, far_dirs, parity)
        pair_decay = pair_order(decay_grp, far_decay, parity)
        if "weight" not in stored:
            stored["weight"] = slot_weights(owner_hot, pair_decay, log_weight, page_fill)
        source_rows = value_cache if with_values else key_cache
        summed = slot_terms(key_cache, source_rows, owner_hot, stored["weight"], pair_dirs)
        mine = jnp.where(parity == 0, summed[:group_rows], summed[group_rows:])
        theirs = jnp.where(parity == 0, summed[group_rows:], summed[:group_rows])
        returned = partner(theirs, "group", 0)
        return mine + returned

    def reduce_home(vectors, with_values):
        directions, decay_grp = (
            lax.all_gather(vectors, "shard", axis=0, tiled=True),
            lax.all_gather(decay_home, "shard", axis=0, tiled=True),
        )
        return lax.psum_scatter(
            cache_pass(directions, decay_grp, with_values), "shard", scatter_dimension=0, tiled=True
        )

    found = conjugate(query_home, key_home, value_home, strength_home, ridge_term, reduce_home)
    retrieved = found.reshape(req_rows, width_all).astype(jnp.bfloat16)
    columns = lax.all_to_all(retrieved, "shard", split_axis=1, concat_axis=0, tiled=True)
    attended = lax.psum_scatter(
        jnp.dot(columns, out_weight, preferred_element_type=jnp.float32),
        "shard",
        scatter_dimension=0,
        tiled=True,
    )
    mid_rows = (tokens.astype(jnp.float32) + attended).astype(jnp.bfloat16)
    mlp_in = scaled_norm(mid_rows, mlp_gain)
    piece_rows = lax.all_gather(mlp_in, "shard", axis=0, tiled=True)
    gate_part = jnp.dot(piece_rows, gate_weight, preferred_element_type=jnp.float32)
    up_part = jnp.dot(piece_rows, up_weight, preferred_element_type=jnp.float32)
    hidden_rows = (jax.nn.silu(gate_part) * up_part).astype(jnp.bfloat16)
    down_part = lax.psum_scatter(
        jnp.dot(hidden_rows, down_weight, preferred_element_type=jnp.float32),
        "shard",
        scatter_dimension=0,
        tiled=True,
    )
    layer_out = (mid_rows.astype(jnp.float32) + down_part).astype(jnp.bfloat16)
    return (retrieved, layer_out)


TILE = 8
MASKED = -1e38
PAIR = ("shard", "member")
PARAMS = pltpu.CompilerParams(vmem_limit_bytes=16 * 1024 * 1024)
PAST, TAP, GAIN, BIAS, RIDGE = slice(0, 8), slice(8, 9), slice(9, 10), slice(10, 11), slice(11, 12)
GATES = slice(16, 32)

SEND = ((0, 0), (1, 4), (4, 1), (3, 6), (6, 3), (5, 5), (7, 7), (2, 2))
FROM = tuple((b, a) if a & 2 else (a, b) for a, b in SEND)
EARLY = 4


def split_pair(value):
    high = value.astype(jnp.bfloat16)
    low = (value - high.astype(jnp.float32)).astype(jnp.bfloat16)
    return high, low


def hot(rows, columns, target_fn):
    row = lax.broadcasted_iota(jnp.int32, (rows, columns), 0)
    column = lax.broadcasted_iota(jnp.int32, (rows, columns), 1)
    return jnp.where(column == target_fn(row), 1.0, 0.0).astype(jnp.bfloat16)


def here():
    return lax.axis_index("shard") * 2 + lax.axis_index("member")


def at_step(table, step, me):
    return me ^ jnp.where((me & 2) == 0, table[step][0], table[step][1])


def silu(value):
    return value / (1.0 + jnp.exp(-value))


def cut_kernel(key_hbm, value_hbm, *refs):
    *piece_refs, stage_ref, sems = refs
    slots = key_hbm.shape[0]
    head_size = piece_refs[0].shape[2]
    me = here()
    loads = [
        pltpu.make_async_copy(source.at[slot], stage_ref.at[part, slot], sems.at[part * slots + slot])
        for part, source in enumerate((key_hbm, value_hbm))
        for slot in range(slots)
    ]
    for load in loads:
        load.start()
    starts = [
        pl.multiple_of(at_step(SEND, step, me) * head_size, head_size)
        for step in range(len(piece_refs))
    ]
    for part in range(2):
        for slot in range(slots):
            place = part * slots + slot
            loads[place].wait()
            for start, piece_ref in zip(starts, piece_refs):
                piece_ref[place] = stage_ref[part, slot, :, pl.ds(start, head_size)]


def pack_kernel(
    tokens_hbm,
    logs_hbm,
    owner_hbm,
    fill_hbm,
    past_hbm,
    tap_hbm,
    gain_hbm,
    gates_hbm,
    bias_hbm,
    ridge_hbm,
    send_ref,
    misc_ref,
    tokens_ref,
    logs_ref,
    owner_ref,
    fill_ref,
    state_ref,
    gates_ref,
    tap_ref,
    gain_ref,
    bias_ref,
    ridge_ref,
    sems,
):
    req_rows, width = tokens_ref.shape
    slots, head_count, page = logs_ref.shape
    copies = [
        pltpu.make_async_copy(source, target, sems.at[place])
        for place, (source, target) in enumerate(
            [
                (owner_hbm, owner_ref),
                (fill_hbm, fill_ref),
                (tokens_hbm, tokens_ref),
                (logs_hbm, logs_ref),
                (past_hbm, state_ref),
                (tap_hbm, tap_ref),
                (gain_hbm, gain_ref),
                (gates_hbm, gates_ref),
                (bias_hbm, bias_ref),
                (ridge_hbm, ridge_ref),
            ]
        )
    ]
    for copy in copies:
        copy.start()
    for copy in copies:
        copy.wait()

    tokens = tokens_ref[...].astype(jnp.float32)
    rows = [
        tokens[row : row + 1, first : first + page]
        for row in range(req_rows)
        for first in range(0, width, page)
    ]
    tile = jnp.concatenate(rows, axis=0).astype(jnp.bfloat16)
    packed = tile.shape[0] + TILE
    spot = lax.broadcasted_iota(jnp.int32, (head_count, page), 1)
    logs = []
    lane = lax.broadcasted_iota(jnp.int32, (1, page), 1)
    owners = jnp.zeros((1, page), jnp.float32)
    for slot in range(slots):
        rows = logs_ref[slot].astype(jnp.float32)
        logs.append(jnp.where(spot < fill_ref[slot], rows, MASKED))
        owners = jnp.where(lane == slot, owner_ref[slot].astype(jnp.float32), owners)
    rest = jnp.zeros((TILE - slots - 1, page), jnp.float32)
    for head in range(head_count):
        rows = [log[head : head + 1, :] for log in logs]
        side = jnp.concatenate([*rows, owners, rest], axis=0).astype(jnp.bfloat16)
        send_ref[head * packed : head * packed + tile.shape[0], :] = tile
        send_ref[head * packed + tile.shape[0] : (head + 1) * packed, :] = side

    past = tap_ref[0:1, :] * state_ref[0].astype(jnp.float32)
    past = past + tap_ref[1:2, :] * state_ref[1].astype(jnp.float32)
    past = past + tap_ref[2:3, :] * state_ref[2].astype(jnp.float32)
    columns = past.shape[1]
    misc_ref[PAST, :columns] = past
    misc_ref[TAP, :columns] = tap_ref[3:4, :]
    misc_ref[GAIN, :] = gain_ref[...]
    misc_ref[BIAS, : 2 * head_count] = bias_ref[...]
    ridges = jnp.zeros((1, page), jnp.float32)
    for head in range(head_count):
        ridges = jnp.where(lane == head, ridge_ref[head], ridges)
    misc_ref[RIDGE, :page] = ridges
    misc_ref[GATES, :] = gates_ref[...].astype(jnp.float32)


def project_kernel(
    shards,
    req_rows,
    slots,
    head_count,
    pack_ref,
    misc_ref,
    qkv_hbm,
    send_ref,
    tokens_ref,
    weight_ref,
    owner_ref,
    strength_ref,
    mixed_ref,
    qkv_ref,
    sems,
):
    chunk = qkv_ref.shape[0] // sems.shape[0]
    loads = [
        pltpu.make_async_copy(
            qkv_hbm.at[pl.ds(part * chunk, chunk)],
            qkv_ref.at[pl.ds(part * chunk, chunk)],
            sems.at[part],
        )
        for part in range(sems.shape[0])
    ]
    for load in loads:
        load.start()
    shard = lax.axis_index("shard")
    member = lax.axis_index("member")
    head = here()
    group_rows = shards * req_rows
    pair_rows = 2 * group_rows
    width = misc_ref.shape[1]
    columns = qkv_ref.shape[1]
    page = weight_ref.shape[1]
    head_size = send_ref.shape[1]
    blocks = columns // head_size
    parts = width // page
    packed = pack_ref.shape[0]
    tall = packed // (2 * shards)

    def rows_of(first, count):
        def home_of(row):
            request = row % count + first
            x = request // group_rows
            s = (request % group_rows) // req_rows
            return (s * 2 + x) * tall + request % req_rows * parts + row // count

        picked = jnp.dot(
            hot(count * parts, packed, home_of), pack_ref[...], preferred_element_type=jnp.float32
        )
        return jnp.concatenate(
            [picked[part * count : (part + 1) * count] for part in range(parts)], axis=1
        )

    own_tokens = rows_of(member * group_rows, group_rows)
    tokens_ref[...] = own_tokens
    own = scaled_norm(own_tokens, misc_ref[GAIN, :])
    normed = scaled_norm(rows_of(0, pair_rows), misc_ref[GAIN, :])
    raw = lax.dot_general(
        normed,
        misc_ref[GATES, :].astype(jnp.bfloat16),
        (((1,), (1,)), ((), ())),
        preferred_element_type=jnp.float32,
    )
    gate_vals = 1.0 / (1.0 + jnp.exp(-(raw + misc_ref[BIAS, : 2 * head_count])))
    column = lax.broadcasted_iota(jnp.int32, gate_vals.shape, 1)
    decay = jnp.sum(jnp.where(column == head, gate_vals, 0.0), axis=1, keepdims=True)
    strength = jnp.sum(
        jnp.where(column == head + head_count, gate_vals, 0.0), axis=1, keepdims=True
    )
    strength_ref[:pair_rows, :] = jnp.broadcast_to(strength, (pair_rows, head_size))
    ridges = misc_ref[RIDGE, :page]
    spot = lax.broadcasted_iota(jnp.int32, ridges.shape, 1)
    ridge = jnp.sum(jnp.where(spot == head, ridges, 0.0), axis=1, keepdims=True)
    strength_ref[pair_rows:, :] = jnp.broadcast_to(ridge, (TILE, head_size))

    all_slots = 2 * shards * slots
    side = tall - TILE
    pick_slot = hot(all_slots, packed, lambda row: (row // slots) * tall + side + row % slots)
    logs = jnp.dot(pick_slot, pack_ref[...], preferred_element_type=jnp.float32)
    pick_owner = hot(all_slots, packed, lambda row: (row // slots) * tall + side + slots)
    owners = jnp.dot(pick_owner, pack_ref[...], preferred_element_type=jnp.float32)
    at_slot = hot(all_slots, page, lambda row: row % slots).astype(jnp.float32)
    owner = jnp.sum(at_slot * owners, axis=1, keepdims=True).astype(jnp.int32)
    owner_ref[...] = jnp.broadcast_to(owner, owner_ref.shape)
    request = lax.broadcasted_iota(jnp.int32, (all_slots, pair_rows), 1)
    owner_hot = jnp.where(request == owner, 1.0, 0.0)
    wide_decay = jnp.broadcast_to(decay, (pair_rows, page))
    slot_decay = jnp.dot(
        owner_hot, wide_decay, precision=precise, preferred_element_type=jnp.float32
    )
    weight_ref[...] = slot_decay * jnp.exp(logs)

    for load in loads:
        load.wait()
    fresh = jnp.dot(own, qkv_ref[...], preferred_element_type=jnp.float32)
    before = misc_ref[TAP, :columns] * fresh + misc_ref[PAST, :columns]
    mixed_ref[...] = silu(before)
    for target in range(head_count):
        place = jnp.int32(0)
        for part in range(3):
            local = target + part * head_count - shard * blocks
            place = jnp.where((local >= 0) & (local < blocks), local, place)
        start = pl.multiple_of(place * head_size, head_size)
        send_ref[target * group_rows : (target + 1) * group_rows, :] = mixed_ref[
            :, pl.ds(start, head_size)
        ].astype(jnp.bfloat16)


def gram_kernel(first, owner_ref, weight_ref, *refs):
    if first:
        *piece_refs, before_ref, gram_ref = refs
    else:
        *piece_refs, gram_ref = refs
        gram_ref[...] = jnp.zeros_like(gram_ref)
    me = here()
    slots = piece_refs[0].shape[0] // 2
    for step, piece_ref in enumerate(piece_refs, first):
        for spot in range(slots):
            slot = at_step(FROM, step, me) * slots + spot
            keys = piece_ref[spot]
            both = jnp.concatenate([keys, piece_ref[slots + spot]], axis=1)
            turned = keys.T.astype(jnp.float32) * weight_ref[pl.ds(slot, 1), :]
            high, low = split_pair(turned)
            piece = jnp.dot(high, both, preferred_element_type=jnp.float32) + jnp.dot(
                low, both, preferred_element_type=jnp.float32
            )
            owner = owner_ref[slot, 0]
            gram_ref[owner] = gram_ref[owner] + piece


def solve_kernel(
    head_count, blocks, mixed_ref, strength_ref, gram_ref, out_ref, send_ref
):
    head = here()
    member = lax.axis_index("member")
    pair_rows, head_size, _ = gram_ref.shape
    width = out_ref.shape[1]

    def columns_of(block):
        first = pl.multiple_of(block // blocks * pair_rows, pair_rows)
        return mixed_ref[pl.ds(first, pair_rows), :].astype(jnp.float32)

    query = unit_rows(columns_of(head))
    key_new = unit_rows(columns_of(head + head_count))
    value_new = columns_of(head + 2 * head_count)
    strength = strength_ref[:pair_rows, :]
    ridge = strength_ref[pair_rows : pair_rows + 1, :]

    def image_of(vectors, columns):
        turned = vectors.T
        pieces = []
        for row in range(pair_rows):
            spread = jnp.broadcast_to(turned[:, row : row + 1], (head_size, head_size))
            pieces.append(jnp.sum(gram_ref[row, :, columns] * spread, axis=0, keepdims=True))
        return jnp.concatenate(pieces, axis=0)

    found = jnp.zeros_like(query)
    residual = query
    direction = query
    res_norm = jnp.sum(residual * residual, axis=-1, keepdims=True)
    for iteration in range(ITERS):
        along = jnp.sum(key_new * direction, axis=-1, keepdims=True)
        image = image_of(direction, slice(0, head_size))
        image = image + strength * key_new * along + ridge * direction
        step = res_norm / jnp.sum(direction * image, axis=-1, keepdims=True)
        found = found + step * direction
        residual = residual - step * image
        next_norm = jnp.sum(residual * residual, axis=-1, keepdims=True)
        direction = residual + (next_norm / res_norm) * direction
        res_norm = next_norm

    total = image_of(found, slice(head_size, 2 * head_size))
    total = total + strength * value_new * jnp.sum(key_new * found, axis=-1, keepdims=True)
    retrieved = total.astype(jnp.bfloat16)
    start = pl.multiple_of(member * head_size, head_size)
    part = jnp.dot(
        retrieved, out_ref[pl.ds(start, head_size), :], preferred_element_type=jnp.float32
    ).astype(jnp.bfloat16)
    half = pair_rows // 2
    for target in range(head_count):
        x = target % 2
        spot = slice(target * half, (target + 1) * half)
        send_ref[spot, :width] = part[x * half : (x + 1) * half]
        send_ref[spot, width:] = retrieved[x * half : (x + 1) * half]


def home_rows(value, req_rows):
    first = lax.axis_index("shard") * req_rows
    row = lax.broadcasted_iota(jnp.int32, value.shape, 0)
    picked = [
        jnp.sum(jnp.where(row == first + i, value, 0.0), axis=0, keepdims=True)
        for i in range(req_rows)
    ]
    return jnp.concatenate(picked, axis=0)


def mlp_kernel(
    shards,
    part_ref,
    tokens_ref,
    gain_ref,
    gate_ref,
    up_ref,
    down_ref,
    mid_ref,
    retrieved_ref,
    *refs,
):
    *send_refs, down_scr = refs
    shard = lax.axis_index("shard")
    group_rows, width = tokens_ref.shape
    devices = 2 * shards
    req_rows = group_rows // shards
    attended = part_ref[:group_rows, :width].astype(jnp.float32)
    for source in range(1, devices):
        spot = slice(source * group_rows, (source + 1) * group_rows)
        attended += part_ref[spot, :width].astype(jnp.float32)
    mid_rows = (tokens_ref[...] + attended).astype(jnp.bfloat16)
    mlp_in = scaled_norm(mid_rows, gain_ref[...])
    contract = (((1,), (1,)), ((), ()))
    gate_part = lax.dot_general(
        mlp_in, gate_ref[...], contract, preferred_element_type=jnp.float32
    )
    up_part = lax.dot_general(mlp_in, up_ref[...], contract, preferred_element_type=jnp.float32)
    hidden = (silu(gate_part) * up_part).astype(jnp.bfloat16)
    down = jnp.dot(hidden, down_ref[...], preferred_element_type=jnp.float32)
    down_scr[...] = down.reshape(down_scr.shape)
    rows = send_refs[0].shape[0]
    for apart, send_ref in enumerate(send_refs):
        send_ref[...] = down_scr[pl.ds(pl.multiple_of((shard ^ apart) * rows, rows), rows), :]
    mid_ref[...] = home_rows(mid_rows.astype(jnp.float32), mid_ref.shape[0])
    heads = [
        home_rows(
            part_ref[source * group_rows : (source + 1) * group_rows, width:].astype(jnp.float32),
            req_rows,
        )
        for source in range(devices)
    ]
    retrieved_ref[...] = jnp.concatenate(heads, axis=1).astype(jnp.bfloat16)


def finish_kernel(mid_ref, *refs):
    *down_refs, layer_ref = refs
    total = down_refs[0][...]
    for down_ref in down_refs[1:]:
        total = total + down_ref[...]
    layer_ref[...] = (mid_ref[...] + total.reshape(mid_ref.shape)).astype(jnp.bfloat16)


def head_body(
    tokens,
    norm_gain,
    qkv_weight,
    conv_weight,
    conv_state,
    mesa_gates,
    mesa_bias,
    ridge_term,
    key_cache,
    value_cache,
    log_weight,
    page_owner,
    page_fill,
    out_weight,
    mlp_gain,
    gate_weight,
    up_weight,
    down_weight,
):
    shards = lax.axis_size("shard")
    devices = 2 * shards
    req_rows, width = tokens.shape
    slots, page, _ = key_cache.shape
    head_count = ridge_term.shape[0]
    head_size = width // head_count
    group_rows = shards * req_rows
    pair_rows = 2 * group_rows
    all_slots = devices * slots
    columns = qkv_weight.shape[1]
    shape = jax.ShapeDtypeStruct
    bf16, f32 = jnp.bfloat16, jnp.float32

    def exchange(value, axes):
        return lax.all_to_all(value, axes, split_axis=0, concat_axis=0, tiled=True)

    def spot(number):
        return number % 2 * shards + number // 2

    hbm = pl.BlockSpec(memory_space=pltpu.HBM)
    past_rows = jnp.transpose(conv_state, (1, 0, 2))
    gates = mesa_gates.T

    def pinned(*values):
        return [pltpu.with_memory_space_constraint(value, pltpu.HBM) for value in values]

    pieces = pl.pallas_call(
        cut_kernel,
        out_shape=(shape((2 * slots, page, head_size), bf16),) * devices,
        in_specs=[hbm] * 2,
        out_specs=(VMEM,) * devices,
        scratch_shapes=[
            pltpu.VMEM((2, *key_cache.shape), bf16),
            pltpu.SemaphoreType.DMA((2 * slots,)),
        ],
        compiler_params=PARAMS,
        name="cut",
    )(*pinned(key_cache, value_cache))

    def move(step):
        pairs = [
            (spot(source), spot(source ^ SEND[step][source >> 1 & 1])) for source in range(devices)
        ]
        return lax.ppermute(pieces[step], ("member", "shard"), pairs)

    moved = [pieces[0]] + [move(step) for step in range(1, 1 + EARLY)]
    tokens, pieces = lax.optimization_barrier((tokens, pieces))
    pack, misc = pl.pallas_call(
        pack_kernel,
        out_shape=(
            shape((devices * (req_rows * width // page + TILE), page), bf16),
            shape((GATES.stop, width), f32),
        ),
        in_specs=[hbm] * 10,
        out_specs=(VMEM,) * 2,
        scratch_shapes=[
            pltpu.VMEM(tokens.shape, bf16),
            pltpu.VMEM(log_weight.shape, bf16),
            pltpu.SMEM(page_owner.shape, jnp.int32),
            pltpu.SMEM(page_fill.shape, jnp.int32),
            pltpu.VMEM(past_rows.shape, bf16),
            pltpu.VMEM(gates.shape, bf16),
            pltpu.VMEM(conv_weight.shape, f32),
            pltpu.VMEM((1, width), f32),
            pltpu.VMEM((1, 2 * head_count), f32),
            pltpu.SMEM(ridge_term.shape, f32),
            pltpu.SemaphoreType.DMA((10,)),
        ],
        compiler_params=PARAMS,
        name="pack",
    )(
        *pinned(
            tokens,
            log_weight,
            page_owner,
            page_fill,
            past_rows,
            conv_weight,
            norm_gain[None, :],
            gates,
            mesa_bias[None, :],
            ridge_term,
        )
    )
    packs = exchange(pack, PAIR)

    pieces, packs = lax.optimization_barrier((pieces, packs))
    moved += [move(step) for step in range(1 + EARLY, devices)]

    mixed, own_tokens, weight, owner, strength = pl.pallas_call(
        functools.partial(project_kernel, shards, req_rows, slots, head_count),
        out_shape=(
            shape((devices * group_rows, head_size), bf16),
            shape((group_rows, width), f32),
            shape((all_slots, page), f32),
            shape((all_slots, page), jnp.int32),
            shape((pair_rows + TILE, head_size), f32),
        ),
        in_specs=[VMEM] * 2 + [hbm],
        out_specs=(VMEM,) * 5,
        scratch_shapes=[
            pltpu.VMEM((group_rows, columns), f32),
            pltpu.VMEM(qkv_weight.shape, bf16),
            pltpu.SemaphoreType.DMA((4,)),
        ],
        compiler_params=PARAMS,
        name="project",
    )(packs, misc, *pinned(qkv_weight))

    def add_up(first, last, before, owner, weight):
        known = [] if before is None else [before]
        count = last - first + len(known)
        return pl.pallas_call(
            functools.partial(gram_kernel, first),
            out_shape=shape((pair_rows, head_size, 2 * head_size), f32),
            in_specs=[SMEM] + [VMEM] * (1 + count),
            out_specs=VMEM,
            input_output_aliases={1 + count: 0} if known else {},
            compiler_params=PARAMS,
            name="gram",
        )(owner, weight, *moved[first:last], *known)

    gram = add_up(0, 1 + EARLY, None, owner, weight)
    mixed, gram = lax.optimization_barrier((mixed, gram))
    all_mixed = exchange(mixed, PAIR)
    all_mixed, owner, weight, gram = lax.optimization_barrier((all_mixed, owner, weight, gram))
    gram = add_up(1 + EARLY, devices, gram, owner, weight)

    parts = pl.pallas_call(
        functools.partial(solve_kernel, head_count, columns // head_size),
        out_shape=shape((devices * group_rows, width + head_size), bf16),
        in_specs=[VMEM] * 4,
        out_specs=VMEM,
        compiler_params=PARAMS,
        name="solve",
    )(all_mixed, strength, gram, out_weight)
    all_parts = exchange(parts, PAIR)

    mid_home, retrieved, *down = pl.pallas_call(
        functools.partial(mlp_kernel, shards),
        out_shape=(
            shape((req_rows, width), f32),
            shape((req_rows, width), bf16),
        )
        + (shape((req_rows * head_count, head_size), f32),) * shards,
        in_specs=[VMEM] * 6,
        out_specs=(VMEM,) * (2 + shards),
        scratch_shapes=[pltpu.VMEM((group_rows * head_count, head_size), f32)],
        compiler_params=PARAMS,
        name="mlp",
    )(
        all_parts,
        own_tokens,
        mlp_gain[None, :],
        gate_weight.T,
        up_weight.T,
        down_weight,
    )
    arrived = [down[0]]
    for apart in range(1, shards):
        pairs = [(source, source ^ apart) for source in range(shards)]
        arrived.append(lax.ppermute(down[apart], "shard", pairs))
    layer_out = pl.pallas_call(
        finish_kernel,
        out_shape=shape((req_rows, width), bf16),
        in_specs=[VMEM] * (1 + shards),
        out_specs=VMEM,
        compiler_params=PARAMS,
        name="finish",
    )(mid_home, *arrived)
    return (retrieved, layer_out)


def specs(group):
    rows = P((*group, "shard"))
    return (
        (
            rows,
            P(),
            P(None, "shard"),
            P(None, "shard"),
            P(group, None, "shard"),
            P(),
            P(),
            P(),
            rows,
            rows,
            rows,
            rows,
            rows,
            P("shard", None),
            P(),
            P(None, "shard"),
            P(None, "shard"),
            P("shard", None),
        ),
        (rows, rows),
    )


def solution(mesh):
    groups, shards = mesh.devices.shape

    def run(*args):
        head_count = args[7].shape[0]
        if 2 * shards == head_count == len(SEND):
            axes = ("pair", "member", "shard")
            used = Mesh(mesh.devices.reshape(groups // 2, 2, shards), axes)
            body, group = head_body, ("pair", "member")
        else:
            used, body, group = mesh, spread_body, ("group",)
        in_specs, out_specs = specs(group)
        return jax.shard_map(
            body, mesh=used, in_specs=in_specs, out_specs=out_specs, check_vma=False
        )(*args)

    return run
```

```python
import functools

import jax
import jax.numpy as jnp
from jax import lax
from jax.experimental import pallas as pl
from jax.experimental.pallas import tpu as pltpu
from jax.sharding import Mesh
from jax.sharding import PartitionSpec as P

ITERS = 4


precise = lax.Precision.HIGHEST

VMEM = pl.BlockSpec(memory_space=pltpu.VMEM)
SMEM = pl.BlockSpec(memory_space=pltpu.SMEM)


def partner(value, axis, apart):
    mask = 2**apart
    pairs = [(source, source ^ mask) for source in range(lax.axis_size(axis))]
    return lax.ppermute(value, axis, pairs)


def scaled_norm(row_vals, gain_vec):
    wide_rows = row_vals.astype(jnp.float32)
    factor = lax.rsqrt(jnp.mean(wide_rows * wide_rows, axis=-1, keepdims=True) + 1e-05)
    return (wide_rows * factor * gain_vec).astype(jnp.bfloat16)


def unit_rows(vectors):
    return vectors * lax.rsqrt(jnp.sum(vectors * vectors, axis=-1, keepdims=True) + 1e-06)


def slot_weights(owner_hot, decay_rows, log_weight, page_fill):
    page_len = log_weight.shape[2]
    slot_decay = jnp.dot(owner_hot, decay_rows, precision=precise)
    live_mask = (jnp.arange(page_len)[None, :] < page_fill[:, None]).astype(jnp.float32)
    return slot_decay[:, :, None] * jnp.exp(log_weight.astype(jnp.float32)) * live_mask[:, None, :]


def slot_terms(key_rows, source_rows, owner_hot, slot_weight, directions):
    slot_count, page_len, width_all = key_rows.shape
    head_count = slot_weight.shape[1]
    head_size = width_all // head_count
    member_count = owner_hot.shape[1]
    slot_dir = jnp.dot(owner_hot, directions.reshape(member_count, width_all), precision=precise)
    slot_dir = slot_dir.reshape(slot_count, head_count, head_size)
    key_wide = key_rows.astype(jnp.float32).reshape(slot_count, page_len, head_count, head_size)
    scores = jnp.einsum("sthd,shd->sht", key_wide, slot_dir, precision=precise)
    source_wide = source_rows.astype(jnp.float32).reshape(
        slot_count, page_len, head_count, head_size
    )
    contribution = jnp.einsum("sht,sthd->shd", slot_weight * scores, source_wide, precision=precise)
    summed = jnp.dot(owner_hot.T, contribution.reshape(slot_count, width_all), precision=precise)
    return summed.reshape(member_count, head_count, head_size)


def new_term(vectors, source_rows, strength_rows, key_new):
    return (
        strength_rows[:, :, None] * source_rows * jnp.sum(key_new * vectors, axis=-1, keepdims=True)
    )


def conjugate(query_rows, key_new, value_new, strength_rows, ridge_term, reduce_fn):
    solution = jnp.zeros_like(query_rows)
    residual = query_rows
    direction = query_rows
    res_norm = jnp.sum(residual * residual, axis=-1)
    for iteration in range(ITERS):
        image_vec = (
            reduce_fn(direction, False)
            + new_term(direction, key_new, strength_rows, key_new)
            + ridge_term[None, :, None] * direction
        )
        step_size = res_norm / jnp.sum(direction * image_vec, axis=-1)
        solution = solution + step_size[:, :, None] * direction
        residual = residual - step_size[:, :, None] * image_vec
        next_norm = jnp.sum(residual * residual, axis=-1)
        direction = residual + (next_norm / res_norm)[:, :, None] * direction
        res_norm = next_norm
    return reduce_fn(solution, True) + new_term(solution, value_new, strength_rows, key_new)


def pair_order(mine, theirs, parity):
    first = jnp.where(parity == 0, mine, theirs)
    second = jnp.where(parity == 0, theirs, mine)
    return jnp.concatenate([first, second], axis=0)


def spread_body(
    tokens,
    norm_gain,
    qkv_weight,
    conv_weight,
    conv_state,
    mesa_gates,
    mesa_bias,
    ridge_term,
    key_cache,
    value_cache,
    log_weight,
    page_owner,
    page_fill,
    out_weight,
    mlp_gain,
    gate_weight,
    up_weight,
    down_weight,
):
    req_rows = tokens.shape[0]
    group_rows = req_rows * lax.axis_size("shard")
    head_count = ridge_term.shape[0]
    width_all = key_cache.shape[2]
    head_size = width_all // head_count
    parity = lax.axis_index("group") % 2
    normed = scaled_norm(tokens, norm_gain)
    fresh_proj = jnp.dot(
        lax.all_gather(normed, "shard", axis=0, tiled=True),
        qkv_weight,
        preferred_element_type=jnp.float32,
    )
    past_rows = conv_state.astype(jnp.float32)
    pre_conv = (
        conv_weight[3] * fresh_proj
        + conv_weight[0] * past_rows[:, 0]
        + conv_weight[1] * past_rows[:, 1]
        + conv_weight[2] * past_rows[:, 2]
    )
    mixed_cols = jax.nn.silu(pre_conv).astype(jnp.bfloat16)
    home_rows = lax.all_to_all(mixed_cols, "shard", split_axis=0, concat_axis=1, tiled=True)
    split_rows = home_rows.astype(jnp.float32).reshape(req_rows, 3, head_count, head_size)
    query_home = unit_rows(split_rows[:, 0])
    key_home = unit_rows(split_rows[:, 1])
    value_home = split_rows[:, 2]
    gate_vals = jax.nn.sigmoid(
        jnp.dot(normed, mesa_gates, preferred_element_type=jnp.float32) + mesa_bias
    )
    decay_home = gate_vals[:, :head_count]
    strength_home = gate_vals[:, head_count:]
    owner_hot = (page_owner[:, None] == jnp.arange(2 * group_rows)[None, :]).astype(jnp.float32)
    stored = {}

    def cache_pass(directions, decay_grp, with_values):
        far_dirs, far_decay = partner((directions, decay_grp), "group", 0)
        pair_dirs = pair_order(directions, far_dirs, parity)
        pair_decay = pair_order(decay_grp, far_decay, parity)
        if "weight" not in stored:
            stored["weight"] = slot_weights(owner_hot, pair_decay, log_weight, page_fill)
        source_rows = value_cache if with_values else key_cache
        summed = slot_terms(key_cache, source_rows, owner_hot, stored["weight"], pair_dirs)
        mine = jnp.where(parity == 0, summed[:group_rows], summed[group_rows:])
        theirs = jnp.where(parity == 0, summed[group_rows:], summed[:group_rows])
        returned = partner(theirs, "group", 0)
        return mine + returned

    def reduce_home(vectors, with_values):
        directions, decay_grp = (
            lax.all_gather(vectors, "shard", axis=0, tiled=True),
            lax.all_gather(decay_home, "shard", axis=0, tiled=True),
        )
        return lax.psum_scatter(
            cache_pass(directions, decay_grp, with_values), "shard", scatter_dimension=0, tiled=True
        )

    found = conjugate(query_home, key_home, value_home, strength_home, ridge_term, reduce_home)
    retrieved = found.reshape(req_rows, width_all).astype(jnp.bfloat16)
    columns = lax.all_to_all(retrieved, "shard", split_axis=1, concat_axis=0, tiled=True)
    attended = lax.psum_scatter(
        jnp.dot(columns, out_weight, preferred_element_type=jnp.float32),
        "shard",
        scatter_dimension=0,
        tiled=True,
    )
    mid_rows = (tokens.astype(jnp.float32) + attended).astype(jnp.bfloat16)
    mlp_in = scaled_norm(mid_rows, mlp_gain)
    piece_rows = lax.all_gather(mlp_in, "shard", axis=0, tiled=True)
    gate_part = jnp.dot(piece_rows, gate_weight, preferred_element_type=jnp.float32)
    up_part = jnp.dot(piece_rows, up_weight, preferred_element_type=jnp.float32)
    hidden_rows = (jax.nn.silu(gate_part) * up_part).astype(jnp.bfloat16)
    down_part = lax.psum_scatter(
        jnp.dot(hidden_rows, down_weight, preferred_element_type=jnp.float32),
        "shard",
        scatter_dimension=0,
        tiled=True,
    )
    layer_out = (mid_rows.astype(jnp.float32) + down_part).astype(jnp.bfloat16)
    return (retrieved, layer_out)


TILE = 8
MASKED = -1e38
PAIR = ("shard", "member")
PARAMS = pltpu.CompilerParams(vmem_limit_bytes=16 * 1024 * 1024)
PAST, TAP, GAIN, BIAS, RIDGE = slice(0, 8), slice(8, 9), slice(9, 10), slice(10, 11), slice(11, 12)
GATES = slice(16, 32)

SEND = ((0, 0), (2, 2), (1, 4), (4, 1), (3, 6), (6, 3), (5, 5), (7, 7))
FROM = tuple((b, a) if a & 2 else (a, b) for a, b in SEND)
EARLY = 5


def split_pair(value):
    high = value.astype(jnp.bfloat16)
    low = (value - high.astype(jnp.float32)).astype(jnp.bfloat16)
    return high, low


def hot(rows, columns, target_fn):
    row = lax.broadcasted_iota(jnp.int32, (rows, columns), 0)
    column = lax.broadcasted_iota(jnp.int32, (rows, columns), 1)
    return jnp.where(column == target_fn(row), 1.0, 0.0).astype(jnp.bfloat16)


def here():
    return lax.axis_index("shard") * 2 + lax.axis_index("member")


def at_step(table, step, me):
    return me ^ jnp.where((me & 2) == 0, table[step][0], table[step][1])


def silu(value):
    return value / (1.0 + jnp.exp(-value))


def cut_kernel(key_hbm, value_hbm, *refs):
    *piece_refs, stage_ref, sems = refs
    slots = key_hbm.shape[0]
    head_size = piece_refs[0].shape[2]
    me = here()
    loads = [
        pltpu.make_async_copy(source.at[slot], stage_ref.at[part, slot], sems.at[part * slots + slot])
        for part, source in enumerate((key_hbm, value_hbm))
        for slot in range(slots)
    ]
    for load in loads:
        load.start()
    starts = [
        pl.multiple_of(at_step(SEND, step, me) * head_size, head_size)
        for step in range(len(piece_refs))
    ]
    for part in range(2):
        for slot in range(slots):
            place = part * slots + slot
            loads[place].wait()
            for start, piece_ref in zip(starts, piece_refs):
                piece_ref[place] = stage_ref[part, slot, :, pl.ds(start, head_size)]


def pack_kernel(
    tokens_hbm,
    logs_hbm,
    owner_hbm,
    fill_hbm,
    past_hbm,
    tap_hbm,
    gain_hbm,
    gates_hbm,
    bias_hbm,
    ridge_hbm,
    send_ref,
    misc_ref,
    tokens_ref,
    logs_ref,
    owner_ref,
    fill_ref,
    state_ref,
    gates_ref,
    tap_ref,
    gain_ref,
    bias_ref,
    ridge_ref,
    sems,
):
    req_rows, width = tokens_ref.shape
    slots, head_count, page = logs_ref.shape
    copies = [
        pltpu.make_async_copy(source, target, sems.at[place])
        for place, (source, target) in enumerate(
            [
                (owner_hbm, owner_ref),
                (fill_hbm, fill_ref),
                (tokens_hbm, tokens_ref),
                (logs_hbm, logs_ref),
                (past_hbm, state_ref),
                (tap_hbm, tap_ref),
                (gain_hbm, gain_ref),
                (gates_hbm, gates_ref),
                (bias_hbm, bias_ref),
                (ridge_hbm, ridge_ref),
            ]
        )
    ]
    for copy in copies:
        copy.start()
    for copy in copies:
        copy.wait()

    tokens = tokens_ref[...].astype(jnp.float32)
    rows = [
        tokens[row : row + 1, first : first + page]
        for row in range(req_rows)
        for first in range(0, width, page)
    ]
    tile = jnp.concatenate(rows, axis=0).astype(jnp.bfloat16)
    packed = tile.shape[0] + TILE
    spot = lax.broadcasted_iota(jnp.int32, (head_count, page), 1)
    logs = []
    lane = lax.broadcasted_iota(jnp.int32, (1, page), 1)
    owners = jnp.zeros((1, page), jnp.float32)
    for slot in range(slots):
        rows = logs_ref[slot].astype(jnp.float32)
        logs.append(jnp.where(spot < fill_ref[slot], rows, MASKED))
        owners = jnp.where(lane == slot, owner_ref[slot].astype(jnp.float32), owners)
    rest = jnp.zeros((TILE - slots - 1, page), jnp.float32)
    for head in range(head_count):
        rows = [log[head : head + 1, :] for log in logs]
        side = jnp.concatenate([*rows, owners, rest], axis=0).astype(jnp.bfloat16)
        send_ref[head * packed : head * packed + tile.shape[0], :] = tile
        send_ref[head * packed + tile.shape[0] : (head + 1) * packed, :] = side

    past = tap_ref[0:1, :] * state_ref[0].astype(jnp.float32)
    past = past + tap_ref[1:2, :] * state_ref[1].astype(jnp.float32)
    past = past + tap_ref[2:3, :] * state_ref[2].astype(jnp.float32)
    columns = past.shape[1]
    misc_ref[PAST, :columns] = past
    misc_ref[TAP, :columns] = tap_ref[3:4, :]
    misc_ref[GAIN, :] = gain_ref[...]
    misc_ref[BIAS, : 2 * head_count] = bias_ref[...]
    ridges = jnp.zeros((1, page), jnp.float32)
    for head in range(head_count):
        ridges = jnp.where(lane == head, ridge_ref[head], ridges)
    misc_ref[RIDGE, :page] = ridges
    misc_ref[GATES, :] = gates_ref[...].astype(jnp.float32)


def project_kernel(
    shards,
    req_rows,
    slots,
    head_count,
    pack_ref,
    misc_ref,
    qkv_hbm,
    send_ref,
    tokens_ref,
    weight_ref,
    owner_ref,
    strength_ref,
    mixed_ref,
    qkv_ref,
    sems,
):
    chunk = qkv_ref.shape[0] // sems.shape[0]
    loads = [
        pltpu.make_async_copy(
            qkv_hbm.at[pl.ds(part * chunk, chunk)],
            qkv_ref.at[pl.ds(part * chunk, chunk)],
            sems.at[part],
        )
        for part in range(sems.shape[0])
    ]
    for load in loads:
        load.start()
    shard = lax.axis_index("shard")
    member = lax.axis_index("member")
    head = here()
    group_rows = shards * req_rows
    pair_rows = 2 * group_rows
    width = misc_ref.shape[1]
    columns = qkv_ref.shape[1]
    page = weight_ref.shape[1]
    head_size = send_ref.shape[1]
    blocks = columns // head_size
    parts = width // page
    packed = pack_ref.shape[0]
    tall = packed // (2 * shards)

    def rows_of(first, count):
        def home_of(row):
            request = row % count + first
            x = request // group_rows
            s = (request % group_rows) // req_rows
            return (s * 2 + x) * tall + request % req_rows * parts + row // count

        picked = jnp.dot(
            hot(count * parts, packed, home_of), pack_ref[...], preferred_element_type=jnp.float32
        )
        return jnp.concatenate(
            [picked[part * count : (part + 1) * count] for part in range(parts)], axis=1
        )

    own_tokens = rows_of(member * group_rows, group_rows)
    tokens_ref[...] = own_tokens
    own = scaled_norm(own_tokens, misc_ref[GAIN, :])
    normed = scaled_norm(rows_of(0, pair_rows), misc_ref[GAIN, :])
    raw = lax.dot_general(
        normed,
        misc_ref[GATES, :].astype(jnp.bfloat16),
        (((1,), (1,)), ((), ())),
        preferred_element_type=jnp.float32,
    )
    gate_vals = 1.0 / (1.0 + jnp.exp(-(raw + misc_ref[BIAS, : 2 * head_count])))
    column = lax.broadcasted_iota(jnp.int32, gate_vals.shape, 1)
    decay = jnp.sum(jnp.where(column == head, gate_vals, 0.0), axis=1, keepdims=True)
    strength = jnp.sum(
        jnp.where(column == head + head_count, gate_vals, 0.0), axis=1, keepdims=True
    )
    strength_ref[:pair_rows, :] = jnp.broadcast_to(strength, (pair_rows, head_size))
    ridges = misc_ref[RIDGE, :page]
    spot = lax.broadcasted_iota(jnp.int32, ridges.shape, 1)
    ridge = jnp.sum(jnp.where(spot == head, ridges, 0.0), axis=1, keepdims=True)
    strength_ref[pair_rows:, :] = jnp.broadcast_to(ridge, (TILE, head_size))

    all_slots = 2 * shards * slots
    side = tall - TILE
    pick_slot = hot(all_slots, packed, lambda row: (row // slots) * tall + side + row % slots)
    logs = jnp.dot(pick_slot, pack_ref[...], preferred_element_type=jnp.float32)
    pick_owner = hot(all_slots, packed, lambda row: (row // slots) * tall + side + slots)
    owners = jnp.dot(pick_owner, pack_ref[...], preferred_element_type=jnp.float32)
    at_slot = hot(all_slots, page, lambda row: row % slots).astype(jnp.float32)
    owner = jnp.sum(at_slot * owners, axis=1, keepdims=True).astype(jnp.int32)
    owner_ref[...] = jnp.broadcast_to(owner, owner_ref.shape)
    request = lax.broadcasted_iota(jnp.int32, (all_slots, pair_rows), 1)
    owner_hot = jnp.where(request == owner, 1.0, 0.0)
    wide_decay = jnp.broadcast_to(decay, (pair_rows, page))
    slot_decay = jnp.dot(
        owner_hot, wide_decay, precision=precise, preferred_element_type=jnp.float32
    )
    weight_ref[...] = slot_decay * jnp.exp(logs)

    for load in loads:
        load.wait()
    fresh = jnp.dot(own, qkv_ref[...], preferred_element_type=jnp.float32)
    before = misc_ref[TAP, :columns] * fresh + misc_ref[PAST, :columns]
    mixed_ref[...] = silu(before)
    for target in range(head_count):
        place = jnp.int32(0)
        for part in range(3):
            local = target + part * head_count - shard * blocks
            place = jnp.where((local >= 0) & (local < blocks), local, place)
        start = pl.multiple_of(place * head_size, head_size)
        send_ref[target * group_rows : (target + 1) * group_rows, :] = mixed_ref[
            :, pl.ds(start, head_size)
        ].astype(jnp.bfloat16)


def gram_kernel(first, owner_ref, weight_ref, *refs):
    if first:
        *piece_refs, before_ref, gram_ref = refs
    else:
        *piece_refs, gram_ref = refs
        gram_ref[...] = jnp.zeros_like(gram_ref)
    me = here()
    slots = piece_refs[0].shape[0] // 2
    for step, piece_ref in enumerate(piece_refs, first):
        for spot in range(slots):
            slot = at_step(FROM, step, me) * slots + spot
            keys = piece_ref[spot]
            both = jnp.concatenate([keys, piece_ref[slots + spot]], axis=1)
            turned = keys.T.astype(jnp.float32) * weight_ref[pl.ds(slot, 1), :]
            high, low = split_pair(turned)
            piece = jnp.dot(high, both, preferred_element_type=jnp.float32) + jnp.dot(
                low, both, preferred_element_type=jnp.float32
            )
            owner = owner_ref[slot, 0]
            gram_ref[owner] = gram_ref[owner] + piece


def solve_kernel(
    head_count, blocks, mixed_ref, strength_ref, gram_ref, out_ref, send_ref
):
    head = here()
    member = lax.axis_index("member")
    pair_rows, head_size, _ = gram_ref.shape
    width = out_ref.shape[1]

    def columns_of(block):
        first = pl.multiple_of(block // blocks * pair_rows, pair_rows)
        return mixed_ref[pl.ds(first, pair_rows), :].astype(jnp.float32)

    query = unit_rows(columns_of(head))
    key_new = unit_rows(columns_of(head + head_count))
    value_new = columns_of(head + 2 * head_count)
    strength = strength_ref[:pair_rows, :]
    ridge = strength_ref[pair_rows : pair_rows + 1, :]

    def image_of(vectors, columns):
        turned = vectors.T
        pieces = []
        for row in range(pair_rows):
            spread = jnp.broadcast_to(turned[:, row : row + 1], (head_size, head_size))
            pieces.append(jnp.sum(gram_ref[row, :, columns] * spread, axis=0, keepdims=True))
        return jnp.concatenate(pieces, axis=0)

    found = jnp.zeros_like(query)
    residual = query
    direction = query
    res_norm = jnp.sum(residual * residual, axis=-1, keepdims=True)
    for iteration in range(ITERS):
        along = jnp.sum(key_new * direction, axis=-1, keepdims=True)
        image = image_of(direction, slice(0, head_size))
        image = image + strength * key_new * along + ridge * direction
        step = res_norm / jnp.sum(direction * image, axis=-1, keepdims=True)
        found = found + step * direction
        residual = residual - step * image
        next_norm = jnp.sum(residual * residual, axis=-1, keepdims=True)
        direction = residual + (next_norm / res_norm) * direction
        res_norm = next_norm

    total = image_of(found, slice(head_size, 2 * head_size))
    total = total + strength * value_new * jnp.sum(key_new * found, axis=-1, keepdims=True)
    retrieved = total.astype(jnp.bfloat16)
    start = pl.multiple_of(member * head_size, head_size)
    part = jnp.dot(
        retrieved, out_ref[pl.ds(start, head_size), :], preferred_element_type=jnp.float32
    ).astype(jnp.bfloat16)
    half = pair_rows // 2
    for target in range(head_count):
        x = target % 2
        spot = slice(target * half, (target + 1) * half)
        send_ref[spot, :width] = part[x * half : (x + 1) * half]
        send_ref[spot, width:] = retrieved[x * half : (x + 1) * half]


def home_rows(value, req_rows):
    first = lax.axis_index("shard") * req_rows
    row = lax.broadcasted_iota(jnp.int32, value.shape, 0)
    picked = [
        jnp.sum(jnp.where(row == first + i, value, 0.0), axis=0, keepdims=True)
        for i in range(req_rows)
    ]
    return jnp.concatenate(picked, axis=0)


def mlp_kernel(
    shards,
    part_ref,
    tokens_ref,
    gain_ref,
    gate_ref,
    up_ref,
    down_ref,
    mid_ref,
    retrieved_ref,
    *refs,
):
    *send_refs, down_scr = refs
    shard = lax.axis_index("shard")
    group_rows, width = tokens_ref.shape
    devices = 2 * shards
    req_rows = group_rows // shards
    attended = part_ref[:group_rows, :width].astype(jnp.float32)
    for source in range(1, devices):
        spot = slice(source * group_rows, (source + 1) * group_rows)
        attended += part_ref[spot, :width].astype(jnp.float32)
    mid_rows = (tokens_ref[...] + attended).astype(jnp.bfloat16)
    mlp_in = scaled_norm(mid_rows, gain_ref[...])
    contract = (((1,), (1,)), ((), ()))
    gate_part = lax.dot_general(
        mlp_in, gate_ref[...], contract, preferred_element_type=jnp.float32
    )
    up_part = lax.dot_general(mlp_in, up_ref[...], contract, preferred_element_type=jnp.float32)
    hidden = (silu(gate_part) * up_part).astype(jnp.bfloat16)
    down = jnp.dot(hidden, down_ref[...], preferred_element_type=jnp.float32)
    down_scr[...] = down.reshape(down_scr.shape)
    rows = send_refs[0].shape[0]
    for apart, send_ref in enumerate(send_refs):
        send_ref[...] = down_scr[pl.ds(pl.multiple_of((shard ^ apart) * rows, rows), rows), :]
    mid_ref[...] = home_rows(mid_rows.astype(jnp.float32), mid_ref.shape[0])
    heads = [
        home_rows(
            part_ref[source * group_rows : (source + 1) * group_rows, width:].astype(jnp.float32),
            req_rows,
        )
        for source in range(devices)
    ]
    retrieved_ref[...] = jnp.concatenate(heads, axis=1).astype(jnp.bfloat16)


def finish_kernel(mid_ref, *refs):
    *down_refs, layer_ref = refs
    total = down_refs[0][...]
    for down_ref in down_refs[1:]:
        total = total + down_ref[...]
    layer_ref[...] = (mid_ref[...] + total.reshape(mid_ref.shape)).astype(jnp.bfloat16)


def head_body(
    tokens,
    norm_gain,
    qkv_weight,
    conv_weight,
    conv_state,
    mesa_gates,
    mesa_bias,
    ridge_term,
    key_cache,
    value_cache,
    log_weight,
    page_owner,
    page_fill,
    out_weight,
    mlp_gain,
    gate_weight,
    up_weight,
    down_weight,
):
    shards = lax.axis_size("shard")
    devices = 2 * shards
    req_rows, width = tokens.shape
    slots, page, _ = key_cache.shape
    head_count = ridge_term.shape[0]
    head_size = width // head_count
    group_rows = shards * req_rows
    pair_rows = 2 * group_rows
    all_slots = devices * slots
    columns = qkv_weight.shape[1]
    shape = jax.ShapeDtypeStruct
    bf16, f32 = jnp.bfloat16, jnp.float32

    def exchange(value, axes):
        return lax.all_to_all(value, axes, split_axis=0, concat_axis=0, tiled=True)

    def spot(number):
        return number % 2 * shards + number // 2

    hbm = pl.BlockSpec(memory_space=pltpu.HBM)
    past_rows = jnp.transpose(conv_state, (1, 0, 2))
    gates = mesa_gates.T

    def pinned(*values):
        return [pltpu.with_memory_space_constraint(value, pltpu.HBM) for value in values]

    pieces = pl.pallas_call(
        cut_kernel,
        out_shape=(shape((2 * slots, page, head_size), bf16),) * devices,
        in_specs=[hbm] * 2,
        out_specs=(VMEM,) * devices,
        scratch_shapes=[
            pltpu.VMEM((2, *key_cache.shape), bf16),
            pltpu.SemaphoreType.DMA((2 * slots,)),
        ],
        compiler_params=PARAMS,
        name="cut",
    )(*pinned(key_cache, value_cache))

    def move(step):
        pairs = [
            (spot(source), spot(source ^ SEND[step][source >> 1 & 1])) for source in range(devices)
        ]
        return lax.ppermute(pieces[step], ("member", "shard"), pairs)

    moved = [pieces[0]] + [move(step) for step in range(1, 1 + EARLY)]
    tokens, pieces = lax.optimization_barrier((tokens, pieces))
    pack, misc = pl.pallas_call(
        pack_kernel,
        out_shape=(
            shape((devices * (req_rows * width // page + TILE), page), bf16),
            shape((GATES.stop, width), f32),
        ),
        in_specs=[hbm] * 10,
        out_specs=(VMEM,) * 2,
        scratch_shapes=[
            pltpu.VMEM(tokens.shape, bf16),
            pltpu.VMEM(log_weight.shape, bf16),
            pltpu.SMEM(page_owner.shape, jnp.int32),
            pltpu.SMEM(page_fill.shape, jnp.int32),
            pltpu.VMEM(past_rows.shape, bf16),
            pltpu.VMEM(gates.shape, bf16),
            pltpu.VMEM(conv_weight.shape, f32),
            pltpu.VMEM((1, width), f32),
            pltpu.VMEM((1, 2 * head_count), f32),
            pltpu.SMEM(ridge_term.shape, f32),
            pltpu.SemaphoreType.DMA((10,)),
        ],
        compiler_params=PARAMS,
        name="pack",
    )(
        *pinned(
            tokens,
            log_weight,
            page_owner,
            page_fill,
            past_rows,
            conv_weight,
            norm_gain[None, :],
            gates,
            mesa_bias[None, :],
            ridge_term,
        )
    )
    packs = exchange(pack, PAIR)

    pieces, packs = lax.optimization_barrier((pieces, packs))
    moved += [move(step) for step in range(1 + EARLY, devices)]

    mixed, own_tokens, weight, owner, strength = pl.pallas_call(
        functools.partial(project_kernel, shards, req_rows, slots, head_count),
        out_shape=(
            shape((devices * group_rows, head_size), bf16),
            shape((group_rows, width), f32),
            shape((all_slots, page), f32),
            shape((all_slots, page), jnp.int32),
            shape((pair_rows + TILE, head_size), f32),
        ),
        in_specs=[VMEM] * 2 + [hbm],
        out_specs=(VMEM,) * 5,
        scratch_shapes=[
            pltpu.VMEM((group_rows, columns), f32),
            pltpu.VMEM(qkv_weight.shape, bf16),
            pltpu.SemaphoreType.DMA((4,)),
        ],
        compiler_params=PARAMS,
        name="project",
    )(packs, misc, *pinned(qkv_weight))

    def add_up(first, last, before, owner, weight):
        known = [] if before is None else [before]
        count = last - first + len(known)
        return pl.pallas_call(
            functools.partial(gram_kernel, first),
            out_shape=shape((pair_rows, head_size, 2 * head_size), f32),
            in_specs=[SMEM] + [VMEM] * (1 + count),
            out_specs=VMEM,
            input_output_aliases={1 + count: 0} if known else {},
            compiler_params=PARAMS,
            name="gram",
        )(owner, weight, *moved[first:last], *known)

    gram = add_up(0, 1 + EARLY, None, owner, weight)
    mixed, gram = lax.optimization_barrier((mixed, gram))
    all_mixed = exchange(mixed, PAIR)
    all_mixed, owner, weight, gram = lax.optimization_barrier((all_mixed, owner, weight, gram))
    gram = add_up(1 + EARLY, devices, gram, owner, weight)

    parts = pl.pallas_call(
        functools.partial(solve_kernel, head_count, columns // head_size),
        out_shape=shape((devices * group_rows, width + head_size), bf16),
        in_specs=[VMEM] * 4,
        out_specs=VMEM,
        compiler_params=PARAMS,
        name="solve",
    )(all_mixed, strength, gram, out_weight)
    all_parts = exchange(parts, PAIR)

    mid_home, retrieved, *down = pl.pallas_call(
        functools.partial(mlp_kernel, shards),
        out_shape=(
            shape((req_rows, width), f32),
            shape((req_rows, width), bf16),
        )
        + (shape((req_rows * head_count, head_size), f32),) * shards,
        in_specs=[VMEM] * 6,
        out_specs=(VMEM,) * (2 + shards),
        scratch_shapes=[pltpu.VMEM((group_rows * head_count, head_size), f32)],
        compiler_params=PARAMS,
        name="mlp",
    )(
        all_parts,
        own_tokens,
        mlp_gain[None, :],
        gate_weight.T,
        up_weight.T,
        down_weight,
    )
    arrived = [down[0]]
    for apart in range(1, shards):
        pairs = [(source, source ^ apart) for source in range(shards)]
        arrived.append(lax.ppermute(down[apart], "shard", pairs))
    layer_out = pl.pallas_call(
        finish_kernel,
        out_shape=shape((req_rows, width), bf16),
        in_specs=[VMEM] * (1 + shards),
        out_specs=VMEM,
        compiler_params=PARAMS,
        name="finish",
    )(mid_home, *arrived)
    return (retrieved, layer_out)


def specs(group):
    rows = P((*group, "shard"))
    return (
        (
            rows,
            P(),
            P(None, "shard"),
            P(None, "shard"),
            P(group, None, "shard"),
            P(),
            P(),
            P(),
            rows,
            rows,
            rows,
            rows,
            rows,
            P("shard", None),
            P(),
            P(None, "shard"),
            P(None, "shard"),
            P("shard", None),
        ),
        (rows, rows),
    )


def solution(mesh):
    groups, shards = mesh.devices.shape

    def run(*args):
        head_count = args[7].shape[0]
        if 2 * shards == head_count == len(SEND):
            axes = ("pair", "member", "shard")
            used = Mesh(mesh.devices.reshape(groups // 2, 2, shards), axes)
            body, group = head_body, ("pair", "member")
        else:
            used, body, group = mesh, spread_body, ("group",)
        in_specs, out_specs = specs(group)
        return jax.shard_map(
            body, mesh=used, in_specs=in_specs, out_specs=out_specs, check_vma=False
        )(*args)

    return run
```

```python
import functools

import jax
import jax.numpy as jnp
from jax import lax
from jax.experimental import pallas as pl
from jax.experimental.pallas import tpu as pltpu
from jax.sharding import Mesh
from jax.sharding import PartitionSpec as P

ITERS = 4


precise = lax.Precision.HIGHEST

VMEM = pl.BlockSpec(memory_space=pltpu.VMEM)
SMEM = pl.BlockSpec(memory_space=pltpu.SMEM)


def partner(value, axis, apart):
    mask = 2**apart
    pairs = [(source, source ^ mask) for source in range(lax.axis_size(axis))]
    return lax.ppermute(value, axis, pairs)


def scaled_norm(row_vals, gain_vec):
    wide_rows = row_vals.astype(jnp.float32)
    factor = lax.rsqrt(jnp.mean(wide_rows * wide_rows, axis=-1, keepdims=True) + 1e-05)
    return (wide_rows * factor * gain_vec).astype(jnp.bfloat16)


def unit_rows(vectors):
    return vectors * lax.rsqrt(jnp.sum(vectors * vectors, axis=-1, keepdims=True) + 1e-06)


def slot_weights(owner_hot, decay_rows, log_weight, page_fill):
    page_len = log_weight.shape[2]
    slot_decay = jnp.dot(owner_hot, decay_rows, precision=precise)
    live_mask = (jnp.arange(page_len)[None, :] < page_fill[:, None]).astype(jnp.float32)
    return slot_decay[:, :, None] * jnp.exp(log_weight.astype(jnp.float32)) * live_mask[:, None, :]


def slot_terms(key_rows, source_rows, owner_hot, slot_weight, directions):
    slot_count, page_len, width_all = key_rows.shape
    head_count = slot_weight.shape[1]
    head_size = width_all // head_count
    member_count = owner_hot.shape[1]
    slot_dir = jnp.dot(owner_hot, directions.reshape(member_count, width_all), precision=precise)
    slot_dir = slot_dir.reshape(slot_count, head_count, head_size)
    key_wide = key_rows.astype(jnp.float32).reshape(slot_count, page_len, head_count, head_size)
    scores = jnp.einsum("sthd,shd->sht", key_wide, slot_dir, precision=precise)
    source_wide = source_rows.astype(jnp.float32).reshape(
        slot_count, page_len, head_count, head_size
    )
    contribution = jnp.einsum("sht,sthd->shd", slot_weight * scores, source_wide, precision=precise)
    summed = jnp.dot(owner_hot.T, contribution.reshape(slot_count, width_all), precision=precise)
    return summed.reshape(member_count, head_count, head_size)


def new_term(vectors, source_rows, strength_rows, key_new):
    return (
        strength_rows[:, :, None] * source_rows * jnp.sum(key_new * vectors, axis=-1, keepdims=True)
    )


def conjugate(query_rows, key_new, value_new, strength_rows, ridge_term, reduce_fn):
    solution = jnp.zeros_like(query_rows)
    residual = query_rows
    direction = query_rows
    res_norm = jnp.sum(residual * residual, axis=-1)
    for iteration in range(ITERS):
        image_vec = (
            reduce_fn(direction, False)
            + new_term(direction, key_new, strength_rows, key_new)
            + ridge_term[None, :, None] * direction
        )
        step_size = res_norm / jnp.sum(direction * image_vec, axis=-1)
        solution = solution + step_size[:, :, None] * direction
        residual = residual - step_size[:, :, None] * image_vec
        next_norm = jnp.sum(residual * residual, axis=-1)
        direction = residual + (next_norm / res_norm)[:, :, None] * direction
        res_norm = next_norm
    return reduce_fn(solution, True) + new_term(solution, value_new, strength_rows, key_new)


def pair_order(mine, theirs, parity):
    first = jnp.where(parity == 0, mine, theirs)
    second = jnp.where(parity == 0, theirs, mine)
    return jnp.concatenate([first, second], axis=0)


def spread_body(
    tokens,
    norm_gain,
    qkv_weight,
    conv_weight,
    conv_state,
    mesa_gates,
    mesa_bias,
    ridge_term,
    key_cache,
    value_cache,
    log_weight,
    page_owner,
    page_fill,
    out_weight,
    mlp_gain,
    gate_weight,
    up_weight,
    down_weight,
):
    req_rows = tokens.shape[0]
    group_rows = req_rows * lax.axis_size("shard")
    head_count = ridge_term.shape[0]
    width_all = key_cache.shape[2]
    head_size = width_all // head_count
    parity = lax.axis_index("group") % 2
    normed = scaled_norm(tokens, norm_gain)
    fresh_proj = jnp.dot(
        lax.all_gather(normed, "shard", axis=0, tiled=True),
        qkv_weight,
        preferred_element_type=jnp.float32,
    )
    past_rows = conv_state.astype(jnp.float32)
    pre_conv = (
        conv_weight[3] * fresh_proj
        + conv_weight[0] * past_rows[:, 0]
        + conv_weight[1] * past_rows[:, 1]
        + conv_weight[2] * past_rows[:, 2]
    )
    mixed_cols = jax.nn.silu(pre_conv).astype(jnp.bfloat16)
    home_rows = lax.all_to_all(mixed_cols, "shard", split_axis=0, concat_axis=1, tiled=True)
    split_rows = home_rows.astype(jnp.float32).reshape(req_rows, 3, head_count, head_size)
    query_home = unit_rows(split_rows[:, 0])
    key_home = unit_rows(split_rows[:, 1])
    value_home = split_rows[:, 2]
    gate_vals = jax.nn.sigmoid(
        jnp.dot(normed, mesa_gates, preferred_element_type=jnp.float32) + mesa_bias
    )
    decay_home = gate_vals[:, :head_count]
    strength_home = gate_vals[:, head_count:]
    owner_hot = (page_owner[:, None] == jnp.arange(2 * group_rows)[None, :]).astype(jnp.float32)
    stored = {}

    def cache_pass(directions, decay_grp, with_values):
        far_dirs, far_decay = partner((directions, decay_grp), "group", 0)
        pair_dirs = pair_order(directions, far_dirs, parity)
        pair_decay = pair_order(decay_grp, far_decay, parity)
        if "weight" not in stored:
            stored["weight"] = slot_weights(owner_hot, pair_decay, log_weight, page_fill)
        source_rows = value_cache if with_values else key_cache
        summed = slot_terms(key_cache, source_rows, owner_hot, stored["weight"], pair_dirs)
        mine = jnp.where(parity == 0, summed[:group_rows], summed[group_rows:])
        theirs = jnp.where(parity == 0, summed[group_rows:], summed[:group_rows])
        returned = partner(theirs, "group", 0)
        return mine + returned

    def reduce_home(vectors, with_values):
        directions, decay_grp = (
            lax.all_gather(vectors, "shard", axis=0, tiled=True),
            lax.all_gather(decay_home, "shard", axis=0, tiled=True),
        )
        return lax.psum_scatter(
            cache_pass(directions, decay_grp, with_values), "shard", scatter_dimension=0, tiled=True
        )

    found = conjugate(query_home, key_home, value_home, strength_home, ridge_term, reduce_home)
    retrieved = found.reshape(req_rows, width_all).astype(jnp.bfloat16)
    columns = lax.all_to_all(retrieved, "shard", split_axis=1, concat_axis=0, tiled=True)
    attended = lax.psum_scatter(
        jnp.dot(columns, out_weight, preferred_element_type=jnp.float32),
        "shard",
        scatter_dimension=0,
        tiled=True,
    )
    mid_rows = (tokens.astype(jnp.float32) + attended).astype(jnp.bfloat16)
    mlp_in = scaled_norm(mid_rows, mlp_gain)
    piece_rows = lax.all_gather(mlp_in, "shard", axis=0, tiled=True)
    gate_part = jnp.dot(piece_rows, gate_weight, preferred_element_type=jnp.float32)
    up_part = jnp.dot(piece_rows, up_weight, preferred_element_type=jnp.float32)
    hidden_rows = (jax.nn.silu(gate_part) * up_part).astype(jnp.bfloat16)
    down_part = lax.psum_scatter(
        jnp.dot(hidden_rows, down_weight, preferred_element_type=jnp.float32),
        "shard",
        scatter_dimension=0,
        tiled=True,
    )
    layer_out = (mid_rows.astype(jnp.float32) + down_part).astype(jnp.bfloat16)
    return (retrieved, layer_out)


TILE = 8
MASKED = -1e38
PAIR = ("shard", "member")
PARAMS = pltpu.CompilerParams(vmem_limit_bytes=16 * 1024 * 1024)
PAST, TAP, GAIN, BIAS, RIDGE = slice(0, 8), slice(8, 9), slice(9, 10), slice(10, 11), slice(11, 12)
GATES = slice(16, 32)

SEND = ((0, 0), (1, 4), (4, 1), (3, 6), (6, 3), (5, 5), (7, 7), (2, 2))
FROM = tuple((b, a) if a & 2 else (a, b) for a, b in SEND)
EARLY = 4


def split_pair(value):
    high = value.astype(jnp.bfloat16)
    low = (value - high.astype(jnp.float32)).astype(jnp.bfloat16)
    return high, low


def hot(rows, columns, target_fn):
    row = lax.broadcasted_iota(jnp.int32, (rows, columns), 0)
    column = lax.broadcasted_iota(jnp.int32, (rows, columns), 1)
    return jnp.where(column == target_fn(row), 1.0, 0.0).astype(jnp.bfloat16)


def here():
    return lax.axis_index("shard") * 2 + lax.axis_index("member")


def at_step(table, step, me):
    return me ^ jnp.where((me & 2) == 0, table[step][0], table[step][1])


def silu(value):
    return value / (1.0 + jnp.exp(-value))


def cut_kernel(key_hbm, value_hbm, *refs):
    *piece_refs, stage_ref, sems = refs
    slots = key_hbm.shape[0]
    head_size = piece_refs[0].shape[2]
    me = here()
    loads = [
        pltpu.make_async_copy(source.at[slot], stage_ref.at[part, slot], sems.at[part * slots + slot])
        for part, source in enumerate((key_hbm, value_hbm))
        for slot in range(slots)
    ]
    for load in loads:
        load.start()
    starts = [
        pl.multiple_of(at_step(SEND, step, me) * head_size, head_size)
        for step in range(len(piece_refs))
    ]
    for part in range(2):
        for slot in range(slots):
            place = part * slots + slot
            loads[place].wait()
            for start, piece_ref in zip(starts, piece_refs):
                piece_ref[place] = stage_ref[part, slot, :, pl.ds(start, head_size)]


def pack_kernel(
    tokens_hbm,
    logs_hbm,
    owner_hbm,
    fill_hbm,
    past_hbm,
    tap_hbm,
    gain_hbm,
    gates_hbm,
    bias_hbm,
    ridge_hbm,
    send_ref,
    misc_ref,
    tokens_ref,
    logs_ref,
    owner_ref,
    fill_ref,
    state_ref,
    gates_ref,
    tap_ref,
    gain_ref,
    bias_ref,
    ridge_ref,
    sems,
):
    req_rows, width = tokens_ref.shape
    slots, head_count, page = logs_ref.shape
    copies = [
        pltpu.make_async_copy(source, target, sems.at[place])
        for place, (source, target) in enumerate(
            [
                (owner_hbm, owner_ref),
                (fill_hbm, fill_ref),
                (tokens_hbm, tokens_ref),
                (logs_hbm, logs_ref),
                (past_hbm, state_ref),
                (tap_hbm, tap_ref),
                (gain_hbm, gain_ref),
                (gates_hbm, gates_ref),
                (bias_hbm, bias_ref),
                (ridge_hbm, ridge_ref),
            ]
        )
    ]
    for copy in copies:
        copy.start()
    for copy in copies:
        copy.wait()

    tokens = tokens_ref[...].astype(jnp.float32)
    rows = [
        tokens[row : row + 1, first : first + page]
        for row in range(req_rows)
        for first in range(0, width, page)
    ]
    tile = jnp.concatenate(rows, axis=0).astype(jnp.bfloat16)
    packed = tile.shape[0] + TILE
    spot = lax.broadcasted_iota(jnp.int32, (head_count, page), 1)
    logs = []
    lane = lax.broadcasted_iota(jnp.int32, (1, page), 1)
    owners = jnp.zeros((1, page), jnp.float32)
    for slot in range(slots):
        rows = logs_ref[slot].astype(jnp.float32)
        logs.append(jnp.where(spot < fill_ref[slot], rows, MASKED))
        owners = jnp.where(lane == slot, owner_ref[slot].astype(jnp.float32), owners)
    rest = jnp.zeros((TILE - slots - 1, page), jnp.float32)
    for head in range(head_count):
        rows = [log[head : head + 1, :] for log in logs]
        side = jnp.concatenate([*rows, owners, rest], axis=0).astype(jnp.bfloat16)
        send_ref[head * packed : head * packed + tile.shape[0], :] = tile
        send_ref[head * packed + tile.shape[0] : (head + 1) * packed, :] = side

    past = tap_ref[0:1, :] * state_ref[0].astype(jnp.float32)
    past = past + tap_ref[1:2, :] * state_ref[1].astype(jnp.float32)
    past = past + tap_ref[2:3, :] * state_ref[2].astype(jnp.float32)
    columns = past.shape[1]
    misc_ref[PAST, :columns] = past
    misc_ref[TAP, :columns] = tap_ref[3:4, :]
    misc_ref[GAIN, :] = gain_ref[...]
    misc_ref[BIAS, : 2 * head_count] = bias_ref[...]
    ridges = jnp.zeros((1, page), jnp.float32)
    for head in range(head_count):
        ridges = jnp.where(lane == head, ridge_ref[head], ridges)
    misc_ref[RIDGE, :page] = ridges
    misc_ref[GATES, :] = gates_ref[...].astype(jnp.float32)


def project_kernel(
    shards,
    req_rows,
    slots,
    head_count,
    pack_ref,
    misc_ref,
    qkv_hbm,
    send_ref,
    tokens_ref,
    weight_ref,
    owner_ref,
    strength_ref,
    mixed_ref,
    qkv_ref,
    sems,
):
    chunk = qkv_ref.shape[0] // sems.shape[0]
    loads = [
        pltpu.make_async_copy(
            qkv_hbm.at[pl.ds(part * chunk, chunk)],
            qkv_ref.at[pl.ds(part * chunk, chunk)],
            sems.at[part],
        )
        for part in range(sems.shape[0])
    ]
    for load in loads:
        load.start()
    shard = lax.axis_index("shard")
    member = lax.axis_index("member")
    head = here()
    group_rows = shards * req_rows
    pair_rows = 2 * group_rows
    width = misc_ref.shape[1]
    columns = qkv_ref.shape[1]
    page = weight_ref.shape[1]
    head_size = send_ref.shape[1]
    blocks = columns // head_size
    parts = width // page
    packed = pack_ref.shape[0]
    tall = packed // (2 * shards)

    def rows_of(first, count):
        def home_of(row):
            request = row % count + first
            x = request // group_rows
            s = (request % group_rows) // req_rows
            return (s * 2 + x) * tall + request % req_rows * parts + row // count

        picked = jnp.dot(
            hot(count * parts, packed, home_of), pack_ref[...], preferred_element_type=jnp.float32
        )
        return jnp.concatenate(
            [picked[part * count : (part + 1) * count] for part in range(parts)], axis=1
        )

    own_tokens = rows_of(member * group_rows, group_rows)
    tokens_ref[...] = own_tokens
    own = scaled_norm(own_tokens, misc_ref[GAIN, :])
    normed = scaled_norm(rows_of(0, pair_rows), misc_ref[GAIN, :])
    raw = lax.dot_general(
        normed,
        misc_ref[GATES, :].astype(jnp.bfloat16),
        (((1,), (1,)), ((), ())),
        preferred_element_type=jnp.float32,
    )
    gate_vals = 1.0 / (1.0 + jnp.exp(-(raw + misc_ref[BIAS, : 2 * head_count])))
    column = lax.broadcasted_iota(jnp.int32, gate_vals.shape, 1)
    decay = jnp.sum(jnp.where(column == head, gate_vals, 0.0), axis=1, keepdims=True)
    strength = jnp.sum(
        jnp.where(column == head + head_count, gate_vals, 0.0), axis=1, keepdims=True
    )
    strength_ref[:pair_rows, :] = jnp.broadcast_to(strength, (pair_rows, head_size))
    ridges = misc_ref[RIDGE, :page]
    spot = lax.broadcasted_iota(jnp.int32, ridges.shape, 1)
    ridge = jnp.sum(jnp.where(spot == head, ridges, 0.0), axis=1, keepdims=True)
    strength_ref[pair_rows:, :] = jnp.broadcast_to(ridge, (TILE, head_size))

    all_slots = 2 * shards * slots
    side = tall - TILE
    pick_slot = hot(all_slots, packed, lambda row: (row // slots) * tall + side + row % slots)
    logs = jnp.dot(pick_slot, pack_ref[...], preferred_element_type=jnp.float32)
    pick_owner = hot(all_slots, packed, lambda row: (row // slots) * tall + side + slots)
    owners = jnp.dot(pick_owner, pack_ref[...], preferred_element_type=jnp.float32)
    at_slot = hot(all_slots, page, lambda row: row % slots).astype(jnp.float32)
    owner = jnp.sum(at_slot * owners, axis=1, keepdims=True).astype(jnp.int32)
    owner_ref[...] = jnp.broadcast_to(owner, owner_ref.shape)
    request = lax.broadcasted_iota(jnp.int32, (all_slots, pair_rows), 1)
    owner_hot = jnp.where(request == owner, 1.0, 0.0)
    wide_decay = jnp.broadcast_to(decay, (pair_rows, page))
    slot_decay = jnp.dot(
        owner_hot, wide_decay, precision=precise, preferred_element_type=jnp.float32
    )
    weight_ref[...] = slot_decay * jnp.exp(logs)

    for load in loads:
        load.wait()
    fresh = jnp.dot(own, qkv_ref[...], preferred_element_type=jnp.float32)
    before = misc_ref[TAP, :columns] * fresh + misc_ref[PAST, :columns]
    mixed_ref[...] = silu(before)
    for target in range(head_count):
        place = jnp.int32(0)
        for part in range(3):
            local = target + part * head_count - shard * blocks
            place = jnp.where((local >= 0) & (local < blocks), local, place)
        start = pl.multiple_of(place * head_size, head_size)
        send_ref[target * group_rows : (target + 1) * group_rows, :] = mixed_ref[
            :, pl.ds(start, head_size)
        ].astype(jnp.bfloat16)


def add_pieces(first, owner_ref, weight_ref, piece_refs, gram_ref):
    me = here()
    slots = piece_refs[0].shape[0] // 2
    for step, piece_ref in enumerate(piece_refs, first):
        for spot in range(slots):
            slot = at_step(FROM, step, me) * slots + spot
            keys = piece_ref[spot]
            both = jnp.concatenate([keys, piece_ref[slots + spot]], axis=1)
            turned = keys.T.astype(jnp.float32) * weight_ref[pl.ds(slot, 1), :]
            piece = jnp.dot(
                jnp.concatenate(split_pair(turned), axis=1),
                jnp.concatenate([both, both], axis=0),
                preferred_element_type=jnp.float32,
            )
            owner = owner_ref[slot, 0]
            gram_ref[owner] = gram_ref[owner] + piece


def gram_kernel(owner_ref, weight_ref, *refs):
    *piece_refs, gram_ref = refs
    gram_ref[...] = jnp.zeros_like(gram_ref)
    add_pieces(0, owner_ref, weight_ref, piece_refs, gram_ref)


def solve_kernel(
    first, head_count, blocks, owner_ref, weight_ref, mixed_ref, strength_ref, before_ref, *refs
):
    *piece_refs, own_ref, other_ref, gram_ref, rows_ref = refs
    head = here()
    member = lax.axis_index("member")
    pair_rows, head_size, _ = gram_ref.shape
    gram_ref[...] = before_ref[...]
    add_pieces(first, owner_ref, weight_ref, piece_refs, gram_ref)

    def columns_of(block):
        first = pl.multiple_of(block // blocks * pair_rows, pair_rows)
        return mixed_ref[pl.ds(first, pair_rows), :].astype(jnp.float32)

    query = unit_rows(columns_of(head))
    key_new = unit_rows(columns_of(head + head_count))
    value_new = columns_of(head + 2 * head_count)
    strength = strength_ref[:pair_rows, :]
    ridge = strength_ref[pair_rows : pair_rows + 1, :]

    def image_of(vectors, columns):
        turned = vectors.T
        pieces = []
        for row in range(pair_rows):
            spread = jnp.broadcast_to(turned[:, row : row + 1], (head_size, head_size))
            pieces.append(jnp.sum(gram_ref[row, :, columns] * spread, axis=0, keepdims=True))
        return jnp.concatenate(pieces, axis=0)

    found = jnp.zeros_like(query)
    residual = query
    direction = query
    res_norm = jnp.sum(residual * residual, axis=-1, keepdims=True)
    for iteration in range(ITERS):
        along = jnp.sum(key_new * direction, axis=-1, keepdims=True)
        image = image_of(direction, slice(0, head_size))
        image = image + strength * key_new * along + ridge * direction
        step = res_norm / jnp.sum(direction * image, axis=-1, keepdims=True)
        found = found + step * direction
        residual = residual - step * image
        next_norm = jnp.sum(residual * residual, axis=-1, keepdims=True)
        direction = residual + (next_norm / res_norm) * direction
        res_norm = next_norm

    total = image_of(found, slice(head_size, 2 * head_size))
    total = total + strength * value_new * jnp.sum(key_new * found, axis=-1, keepdims=True)
    rows_ref[...] = total
    half = pair_rows // 2
    mine = pl.multiple_of(member * half, half)
    theirs = pl.multiple_of((1 - member) * half, half)
    own_ref[...] = rows_ref[pl.ds(mine, half), :].astype(jnp.bfloat16)
    other_ref[...] = rows_ref[pl.ds(theirs, half), :].astype(jnp.bfloat16)


def out_kernel(own_ref, come_ref, out_ref, send_ref):
    first = lax.axis_index("member") == 0
    width = out_ref.shape[1]
    own = own_ref[...].astype(jnp.float32)
    come = come_ref[...].astype(jnp.float32)
    heads = jnp.concatenate([jnp.where(first, own, come), jnp.where(first, come, own)], axis=1)
    heads = heads.astype(jnp.bfloat16)
    part = jnp.dot(heads, out_ref[...], preferred_element_type=jnp.float32)
    send_ref[:, :width] = part.astype(jnp.bfloat16)
    send_ref[:, width:] = heads


def home_rows(value, req_rows):
    first = lax.axis_index("shard") * req_rows
    row = lax.broadcasted_iota(jnp.int32, value.shape, 0)
    picked = [
        jnp.sum(jnp.where(row == first + i, value, 0.0), axis=0, keepdims=True)
        for i in range(req_rows)
    ]
    return jnp.concatenate(picked, axis=0)


def mlp_kernel(
    shards,
    tokens_ref,
    gain_ref,
    gate_ref,
    up_ref,
    down_ref,
    *refs,
):
    part_refs, refs = refs[:shards], refs[shards:]
    mid_ref, retrieved_ref, *send_refs, down_scr, heads_ref = refs
    shard = lax.axis_index("shard")
    group_rows, width = tokens_ref.shape
    req_rows = mid_ref.shape[0]
    span = part_refs[0].shape[1] - width
    attended = part_refs[0][:, :width].astype(jnp.float32)
    for part_ref in part_refs[1:]:
        attended += part_ref[:, :width].astype(jnp.float32)
    mid_rows = (tokens_ref[...] + attended).astype(jnp.bfloat16)
    mlp_in = scaled_norm(mid_rows, gain_ref[...])
    contract = (((1,), (1,)), ((), ()))
    gate_part = lax.dot_general(
        mlp_in, gate_ref[...], contract, preferred_element_type=jnp.float32
    )
    up_part = lax.dot_general(mlp_in, up_ref[...], contract, preferred_element_type=jnp.float32)
    hidden = (silu(gate_part) * up_part).astype(jnp.bfloat16)
    down = jnp.dot(hidden, down_ref[...], preferred_element_type=jnp.float32)
    down_scr[...] = down.reshape(down_scr.shape)
    rows = send_refs[0].shape[0]
    for apart, send_ref in enumerate(send_refs):
        send_ref[...] = down_scr[pl.ds(pl.multiple_of((shard ^ apart) * rows, rows), rows), :]
    mid_ref[...] = home_rows(mid_rows.astype(jnp.float32), mid_ref.shape[0])
    for apart, part_ref in enumerate(part_refs):
        first = pl.multiple_of((shard ^ apart) * span, span)
        heads_ref[:, pl.ds(first, span)] = home_rows(
            part_ref[:, width:].astype(jnp.float32), req_rows
        )
    retrieved_ref[...] = heads_ref[...].astype(jnp.bfloat16)


def finish_kernel(mid_ref, *refs):
    *down_refs, layer_ref = refs
    total = down_refs[0][...]
    for down_ref in down_refs[1:]:
        total = total + down_ref[...]
    layer_ref[...] = (mid_ref[...] + total.reshape(mid_ref.shape)).astype(jnp.bfloat16)


def head_body(
    tokens,
    norm_gain,
    qkv_weight,
    conv_weight,
    conv_state,
    mesa_gates,
    mesa_bias,
    ridge_term,
    key_cache,
    value_cache,
    log_weight,
    page_owner,
    page_fill,
    out_weight,
    mlp_gain,
    gate_weight,
    up_weight,
    down_weight,
):
    shards = lax.axis_size("shard")
    devices = 2 * shards
    req_rows, width = tokens.shape
    slots, page, _ = key_cache.shape
    head_count = ridge_term.shape[0]
    head_size = width // head_count
    group_rows = shards * req_rows
    pair_rows = 2 * group_rows
    all_slots = devices * slots
    columns = qkv_weight.shape[1]
    shape = jax.ShapeDtypeStruct
    bf16, f32 = jnp.bfloat16, jnp.float32

    def exchange(value, axes):
        return lax.all_to_all(value, axes, split_axis=0, concat_axis=0, tiled=True)

    def spot(number):
        return number % 2 * shards + number // 2

    hbm = pl.BlockSpec(memory_space=pltpu.HBM)
    past_rows = jnp.transpose(conv_state, (1, 0, 2))
    gates = mesa_gates.T

    def pinned(*values):
        return [pltpu.with_memory_space_constraint(value, pltpu.HBM) for value in values]

    pieces = pl.pallas_call(
        cut_kernel,
        out_shape=(shape((2 * slots, page, head_size), bf16),) * devices,
        in_specs=[hbm] * 2,
        out_specs=(VMEM,) * devices,
        scratch_shapes=[
            pltpu.VMEM((2, *key_cache.shape), bf16),
            pltpu.SemaphoreType.DMA((2 * slots,)),
        ],
        compiler_params=PARAMS,
        name="cut",
    )(*pinned(key_cache, value_cache))

    def move(step):
        pairs = [
            (spot(source), spot(source ^ SEND[step][source >> 1 & 1])) for source in range(devices)
        ]
        return lax.ppermute(pieces[step], ("member", "shard"), pairs)

    moved = [pieces[0]] + [move(step) for step in range(1, 1 + EARLY)]
    tokens, pieces = lax.optimization_barrier((tokens, pieces))
    pack, misc = pl.pallas_call(
        pack_kernel,
        out_shape=(
            shape((devices * (req_rows * width // page + TILE), page), bf16),
            shape((GATES.stop, width), f32),
        ),
        in_specs=[hbm] * 10,
        out_specs=(VMEM,) * 2,
        scratch_shapes=[
            pltpu.VMEM(tokens.shape, bf16),
            pltpu.VMEM(log_weight.shape, bf16),
            pltpu.SMEM(page_owner.shape, jnp.int32),
            pltpu.SMEM(page_fill.shape, jnp.int32),
            pltpu.VMEM(past_rows.shape, bf16),
            pltpu.VMEM(gates.shape, bf16),
            pltpu.VMEM(conv_weight.shape, f32),
            pltpu.VMEM((1, width), f32),
            pltpu.VMEM((1, 2 * head_count), f32),
            pltpu.SMEM(ridge_term.shape, f32),
            pltpu.SemaphoreType.DMA((10,)),
        ],
        compiler_params=PARAMS,
        name="pack",
    )(
        *pinned(
            tokens,
            log_weight,
            page_owner,
            page_fill,
            past_rows,
            conv_weight,
            norm_gain[None, :],
            gates,
            mesa_bias[None, :],
            ridge_term,
        )
    )
    packs = exchange(pack, PAIR)

    pieces, packs = lax.optimization_barrier((pieces, packs))
    moved += [move(step) for step in range(1 + EARLY, devices)]

    mixed, own_tokens, weight, owner, strength = pl.pallas_call(
        functools.partial(project_kernel, shards, req_rows, slots, head_count),
        out_shape=(
            shape((devices * group_rows, head_size), bf16),
            shape((group_rows, width), f32),
            shape((all_slots, page), f32),
            shape((all_slots, page), jnp.int32),
            shape((pair_rows + TILE, head_size), f32),
        ),
        in_specs=[VMEM] * 2 + [hbm],
        out_specs=(VMEM,) * 5,
        scratch_shapes=[
            pltpu.VMEM((group_rows, columns), f32),
            pltpu.VMEM(qkv_weight.shape, bf16),
            pltpu.SemaphoreType.DMA((4,)),
        ],
        compiler_params=PARAMS,
        name="project",
    )(packs, misc, *pinned(qkv_weight))

    held = 1 + EARLY
    gram = pl.pallas_call(
        gram_kernel,
        out_shape=shape((pair_rows, head_size, 2 * head_size), f32),
        in_specs=[SMEM] + [VMEM] * (1 + held),
        out_specs=VMEM,
        compiler_params=PARAMS,
        name="gram",
    )(owner, weight, *moved[:held])
    mixed, gram = lax.optimization_barrier((mixed, gram))
    all_mixed = exchange(mixed, PAIR)
    all_mixed, owner, weight, gram = lax.optimization_barrier((all_mixed, owner, weight, gram))

    own_head, other_head = pl.pallas_call(
        functools.partial(solve_kernel, held, head_count, columns // head_size),
        out_shape=(shape((group_rows, head_size), bf16),) * 2,
        in_specs=[SMEM] + [VMEM] * (4 + devices - held),
        out_specs=(VMEM,) * 2,
        scratch_shapes=[
            pltpu.VMEM((pair_rows, head_size, 2 * head_size), f32),
            pltpu.VMEM((pair_rows, head_size), f32),
        ],
        compiler_params=PARAMS,
        name="solve",
    )(owner, weight, all_mixed, strength, gram, *moved[held:])
    part = pl.pallas_call(
        out_kernel,
        out_shape=shape((group_rows, width + 2 * head_size), bf16),
        in_specs=[VMEM] * 3,
        out_specs=VMEM,
        compiler_params=PARAMS,
        name="out",
    )(own_head, lax.ppermute(other_head, "member", [(0, 1), (1, 0)]), out_weight)

    def over_shards(sent):
        arrived = [sent[0]]
        for apart in range(1, shards):
            pairs = [(source, source ^ apart) for source in range(shards)]
            arrived.append(lax.ppermute(sent[apart], "shard", pairs))
        return arrived

    parts = over_shards([part] * shards)

    mid_home, retrieved, *down = pl.pallas_call(
        functools.partial(mlp_kernel, shards),
        out_shape=(
            shape((req_rows, width), f32),
            shape((req_rows, width), bf16),
        )
        + (shape((req_rows * head_count, head_size), f32),) * shards,
        in_specs=[VMEM] * (5 + shards),
        out_specs=(VMEM,) * (2 + shards),
        scratch_shapes=[
            pltpu.VMEM((group_rows * head_count, head_size), f32),
            pltpu.VMEM((req_rows, width), f32),
        ],
        compiler_params=PARAMS,
        name="mlp",
    )(
        own_tokens,
        mlp_gain[None, :],
        gate_weight.T,
        up_weight.T,
        down_weight,
        *parts,
    )
    layer_out = pl.pallas_call(
        finish_kernel,
        out_shape=shape((req_rows, width), bf16),
        in_specs=[VMEM] * (1 + shards),
        out_specs=VMEM,
        compiler_params=PARAMS,
        name="finish",
    )(mid_home, *over_shards(down))
    return (retrieved, layer_out)


def specs(group):
    rows = P((*group, "shard"))
    return (
        (
            rows,
            P(),
            P(None, "shard"),
            P(None, "shard"),
            P(group, None, "shard"),
            P(),
            P(),
            P(),
            rows,
            rows,
            rows,
            rows,
            rows,
            P("shard", None),
            P(),
            P(None, "shard"),
            P(None, "shard"),
            P("shard", None),
        ),
        (rows, rows),
    )


def solution(mesh):
    groups, shards = mesh.devices.shape

    def run(*args):
        head_count = args[7].shape[0]
        if 2 * shards == head_count == len(SEND):
            axes = ("pair", "member", "shard")
            used = Mesh(mesh.devices.reshape(groups // 2, 2, shards), axes)
            body, group = head_body, ("pair", "member")
        else:
            used, body, group = mesh, spread_body, ("group",)
        in_specs, out_specs = specs(group)
        return jax.shard_map(
            body, mesh=used, in_specs=in_specs, out_specs=out_specs, check_vma=False
        )(*args)

    return run
```

```python
import functools

import jax
import jax.numpy as jnp
from jax import lax
from jax.experimental import pallas as pl
from jax.experimental.pallas import tpu as pltpu
from jax.sharding import Mesh
from jax.sharding import PartitionSpec as P

ITERS = 4


precise = lax.Precision.HIGHEST

VMEM = pl.BlockSpec(memory_space=pltpu.VMEM)
SMEM = pl.BlockSpec(memory_space=pltpu.SMEM)


def partner(value, axis, apart):
    mask = 2**apart
    pairs = [(source, source ^ mask) for source in range(lax.axis_size(axis))]
    return lax.ppermute(value, axis, pairs)


def scaled_norm(row_vals, gain_vec):
    wide_rows = row_vals.astype(jnp.float32)
    factor = lax.rsqrt(jnp.mean(wide_rows * wide_rows, axis=-1, keepdims=True) + 1e-05)
    return (wide_rows * factor * gain_vec).astype(jnp.bfloat16)


def unit_rows(vectors):
    return vectors * lax.rsqrt(jnp.sum(vectors * vectors, axis=-1, keepdims=True) + 1e-06)


def slot_weights(owner_hot, decay_rows, log_weight, page_fill):
    page_len = log_weight.shape[2]
    slot_decay = jnp.dot(owner_hot, decay_rows, precision=precise)
    live_mask = (jnp.arange(page_len)[None, :] < page_fill[:, None]).astype(jnp.float32)
    return slot_decay[:, :, None] * jnp.exp(log_weight.astype(jnp.float32)) * live_mask[:, None, :]


def slot_terms(key_rows, source_rows, owner_hot, slot_weight, directions):
    slot_count, page_len, width_all = key_rows.shape
    head_count = slot_weight.shape[1]
    head_size = width_all // head_count
    member_count = owner_hot.shape[1]
    slot_dir = jnp.dot(owner_hot, directions.reshape(member_count, width_all), precision=precise)
    slot_dir = slot_dir.reshape(slot_count, head_count, head_size)
    key_wide = key_rows.astype(jnp.float32).reshape(slot_count, page_len, head_count, head_size)
    scores = jnp.einsum("sthd,shd->sht", key_wide, slot_dir, precision=precise)
    source_wide = source_rows.astype(jnp.float32).reshape(
        slot_count, page_len, head_count, head_size
    )
    contribution = jnp.einsum("sht,sthd->shd", slot_weight * scores, source_wide, precision=precise)
    summed = jnp.dot(owner_hot.T, contribution.reshape(slot_count, width_all), precision=precise)
    return summed.reshape(member_count, head_count, head_size)


def new_term(vectors, source_rows, strength_rows, key_new):
    return (
        strength_rows[:, :, None] * source_rows * jnp.sum(key_new * vectors, axis=-1, keepdims=True)
    )


def conjugate(query_rows, key_new, value_new, strength_rows, ridge_term, reduce_fn):
    solution = jnp.zeros_like(query_rows)
    residual = query_rows
    direction = query_rows
    res_norm = jnp.sum(residual * residual, axis=-1)
    for iteration in range(ITERS):
        image_vec = (
            reduce_fn(direction, False)
            + new_term(direction, key_new, strength_rows, key_new)
            + ridge_term[None, :, None] * direction
        )
        step_size = res_norm / jnp.sum(direction * image_vec, axis=-1)
        solution = solution + step_size[:, :, None] * direction
        residual = residual - step_size[:, :, None] * image_vec
        next_norm = jnp.sum(residual * residual, axis=-1)
        direction = residual + (next_norm / res_norm)[:, :, None] * direction
        res_norm = next_norm
    return reduce_fn(solution, True) + new_term(solution, value_new, strength_rows, key_new)


def pair_order(mine, theirs, parity):
    first = jnp.where(parity == 0, mine, theirs)
    second = jnp.where(parity == 0, theirs, mine)
    return jnp.concatenate([first, second], axis=0)


def spread_body(
    tokens,
    norm_gain,
    qkv_weight,
    conv_weight,
    conv_state,
    mesa_gates,
    mesa_bias,
    ridge_term,
    key_cache,
    value_cache,
    log_weight,
    page_owner,
    page_fill,
    out_weight,
    mlp_gain,
    gate_weight,
    up_weight,
    down_weight,
):
    req_rows = tokens.shape[0]
    group_rows = req_rows * lax.axis_size("shard")
    head_count = ridge_term.shape[0]
    width_all = key_cache.shape[2]
    head_size = width_all // head_count
    parity = lax.axis_index("group") % 2
    normed = scaled_norm(tokens, norm_gain)
    fresh_proj = jnp.dot(
        lax.all_gather(normed, "shard", axis=0, tiled=True),
        qkv_weight,
        preferred_element_type=jnp.float32,
    )
    past_rows = conv_state.astype(jnp.float32)
    pre_conv = (
        conv_weight[3] * fresh_proj
        + conv_weight[0] * past_rows[:, 0]
        + conv_weight[1] * past_rows[:, 1]
        + conv_weight[2] * past_rows[:, 2]
    )
    mixed_cols = jax.nn.silu(pre_conv).astype(jnp.bfloat16)
    home_rows = lax.all_to_all(mixed_cols, "shard", split_axis=0, concat_axis=1, tiled=True)
    split_rows = home_rows.astype(jnp.float32).reshape(req_rows, 3, head_count, head_size)
    query_home = unit_rows(split_rows[:, 0])
    key_home = unit_rows(split_rows[:, 1])
    value_home = split_rows[:, 2]
    gate_vals = jax.nn.sigmoid(
        jnp.dot(normed, mesa_gates, preferred_element_type=jnp.float32) + mesa_bias
    )
    decay_home = gate_vals[:, :head_count]
    strength_home = gate_vals[:, head_count:]
    owner_hot = (page_owner[:, None] == jnp.arange(2 * group_rows)[None, :]).astype(jnp.float32)
    stored = {}

    def cache_pass(directions, decay_grp, with_values):
        far_dirs, far_decay = partner((directions, decay_grp), "group", 0)
        pair_dirs = pair_order(directions, far_dirs, parity)
        pair_decay = pair_order(decay_grp, far_decay, parity)
        if "weight" not in stored:
            stored["weight"] = slot_weights(owner_hot, pair_decay, log_weight, page_fill)
        source_rows = value_cache if with_values else key_cache
        summed = slot_terms(key_cache, source_rows, owner_hot, stored["weight"], pair_dirs)
        mine = jnp.where(parity == 0, summed[:group_rows], summed[group_rows:])
        theirs = jnp.where(parity == 0, summed[group_rows:], summed[:group_rows])
        returned = partner(theirs, "group", 0)
        return mine + returned

    def reduce_home(vectors, with_values):
        directions, decay_grp = (
            lax.all_gather(vectors, "shard", axis=0, tiled=True),
            lax.all_gather(decay_home, "shard", axis=0, tiled=True),
        )
        return lax.psum_scatter(
            cache_pass(directions, decay_grp, with_values), "shard", scatter_dimension=0, tiled=True
        )

    found = conjugate(query_home, key_home, value_home, strength_home, ridge_term, reduce_home)
    retrieved = found.reshape(req_rows, width_all).astype(jnp.bfloat16)
    columns = lax.all_to_all(retrieved, "shard", split_axis=1, concat_axis=0, tiled=True)
    attended = lax.psum_scatter(
        jnp.dot(columns, out_weight, preferred_element_type=jnp.float32),
        "shard",
        scatter_dimension=0,
        tiled=True,
    )
    mid_rows = (tokens.astype(jnp.float32) + attended).astype(jnp.bfloat16)
    mlp_in = scaled_norm(mid_rows, mlp_gain)
    piece_rows = lax.all_gather(mlp_in, "shard", axis=0, tiled=True)
    gate_part = jnp.dot(piece_rows, gate_weight, preferred_element_type=jnp.float32)
    up_part = jnp.dot(piece_rows, up_weight, preferred_element_type=jnp.float32)
    hidden_rows = (jax.nn.silu(gate_part) * up_part).astype(jnp.bfloat16)
    down_part = lax.psum_scatter(
        jnp.dot(hidden_rows, down_weight, preferred_element_type=jnp.float32),
        "shard",
        scatter_dimension=0,
        tiled=True,
    )
    layer_out = (mid_rows.astype(jnp.float32) + down_part).astype(jnp.bfloat16)
    return (retrieved, layer_out)


TILE = 8
MASKED = -1e38
PAIR = ("shard", "member")
PARAMS = pltpu.CompilerParams(vmem_limit_bytes=16 * 1024 * 1024)
PAST, TAP, GAIN, BIAS, RIDGE = slice(0, 8), slice(8, 9), slice(9, 10), slice(10, 11), slice(11, 12)
GATES = slice(16, 32)

SEND = ((0, 0), (2, 2), (5, 5), (7, 7), (1, 4), (4, 1), (3, 6), (6, 3))
FROM = tuple((b, a) if a & 2 else (a, b) for a, b in SEND)
EARLY = 4


def split_pair(value):
    high = value.astype(jnp.bfloat16)
    low = (value - high.astype(jnp.float32)).astype(jnp.bfloat16)
    return high, low


def hot(rows, columns, target_fn):
    row = lax.broadcasted_iota(jnp.int32, (rows, columns), 0)
    column = lax.broadcasted_iota(jnp.int32, (rows, columns), 1)
    return jnp.where(column == target_fn(row), 1.0, 0.0).astype(jnp.bfloat16)


def here():
    return lax.axis_index("shard") * 2 + lax.axis_index("member")


def at_step(table, step, me):
    return me ^ jnp.where((me & 2) == 0, table[step][0], table[step][1])


def silu(value):
    return value / (1.0 + jnp.exp(-value))


def cut_kernel(key_hbm, value_hbm, *refs):
    *piece_refs, stage_ref, sems = refs
    slots = key_hbm.shape[0]
    head_size = piece_refs[0].shape[2]
    me = here()
    loads = [
        pltpu.make_async_copy(source.at[slot], stage_ref.at[part, slot], sems.at[part * slots + slot])
        for part, source in enumerate((key_hbm, value_hbm))
        for slot in range(slots)
    ]
    for load in loads:
        load.start()
    starts = [
        pl.multiple_of(at_step(SEND, step, me) * head_size, head_size)
        for step in range(len(piece_refs))
    ]
    for part in range(2):
        for slot in range(slots):
            place = part * slots + slot
            loads[place].wait()
            for start, piece_ref in zip(starts, piece_refs):
                piece_ref[place] = stage_ref[part, slot, :, pl.ds(start, head_size)]


def pack_kernel(
    tokens_hbm,
    logs_hbm,
    owner_hbm,
    fill_hbm,
    past_hbm,
    tap_hbm,
    gain_hbm,
    gates_hbm,
    bias_hbm,
    ridge_hbm,
    send_ref,
    misc_ref,
    tokens_ref,
    logs_ref,
    owner_ref,
    fill_ref,
    state_ref,
    gates_ref,
    tap_ref,
    gain_ref,
    bias_ref,
    ridge_ref,
    sems,
):
    req_rows, width = tokens_ref.shape
    slots, head_count, page = logs_ref.shape
    copies = [
        pltpu.make_async_copy(source, target, sems.at[place])
        for place, (source, target) in enumerate(
            [
                (owner_hbm, owner_ref),
                (fill_hbm, fill_ref),
                (tokens_hbm, tokens_ref),
                (logs_hbm, logs_ref),
                (past_hbm, state_ref),
                (tap_hbm, tap_ref),
                (gain_hbm, gain_ref),
                (gates_hbm, gates_ref),
                (bias_hbm, bias_ref),
                (ridge_hbm, ridge_ref),
            ]
        )
    ]
    for copy in copies:
        copy.start()
    for copy in copies:
        copy.wait()

    tokens = tokens_ref[...].astype(jnp.float32)
    rows = [
        tokens[row : row + 1, first : first + page]
        for row in range(req_rows)
        for first in range(0, width, page)
    ]
    tile = jnp.concatenate(rows, axis=0).astype(jnp.bfloat16)
    packed = tile.shape[0] + TILE
    spot = lax.broadcasted_iota(jnp.int32, (head_count, page), 1)
    logs = []
    lane = lax.broadcasted_iota(jnp.int32, (1, page), 1)
    owners = jnp.zeros((1, page), jnp.float32)
    for slot in range(slots):
        rows = logs_ref[slot].astype(jnp.float32)
        logs.append(jnp.where(spot < fill_ref[slot], rows, MASKED))
        owners = jnp.where(lane == slot, owner_ref[slot].astype(jnp.float32), owners)
    rest = jnp.zeros((TILE - slots - 1, page), jnp.float32)
    for head in range(head_count):
        rows = [log[head : head + 1, :] for log in logs]
        side = jnp.concatenate([*rows, owners, rest], axis=0).astype(jnp.bfloat16)
        send_ref[head * packed : head * packed + tile.shape[0], :] = tile
        send_ref[head * packed + tile.shape[0] : (head + 1) * packed, :] = side

    past = tap_ref[0:1, :] * state_ref[0].astype(jnp.float32)
    past = past + tap_ref[1:2, :] * state_ref[1].astype(jnp.float32)
    past = past + tap_ref[2:3, :] * state_ref[2].astype(jnp.float32)
    columns = past.shape[1]
    misc_ref[PAST, :columns] = past
    misc_ref[TAP, :columns] = tap_ref[3:4, :]
    misc_ref[GAIN, :] = gain_ref[...]
    misc_ref[BIAS, : 2 * head_count] = bias_ref[...]
    ridges = jnp.zeros((1, page), jnp.float32)
    for head in range(head_count):
        ridges = jnp.where(lane == head, ridge_ref[head], ridges)
    misc_ref[RIDGE, :page] = ridges
    misc_ref[GATES, :] = gates_ref[...].astype(jnp.float32)


def project_kernel(
    shards,
    req_rows,
    slots,
    head_count,
    pack_ref,
    misc_ref,
    qkv_hbm,
    send_ref,
    tokens_ref,
    weight_ref,
    owner_ref,
    strength_ref,
    mixed_ref,
    qkv_ref,
    sems,
):
    chunk = qkv_ref.shape[0] // sems.shape[0]
    loads = [
        pltpu.make_async_copy(
            qkv_hbm.at[pl.ds(part * chunk, chunk)],
            qkv_ref.at[pl.ds(part * chunk, chunk)],
            sems.at[part],
        )
        for part in range(sems.shape[0])
    ]
    for load in loads:
        load.start()
    shard = lax.axis_index("shard")
    member = lax.axis_index("member")
    head = here()
    group_rows = shards * req_rows
    pair_rows = 2 * group_rows
    width = misc_ref.shape[1]
    columns = qkv_ref.shape[1]
    page = weight_ref.shape[1]
    head_size = send_ref.shape[1]
    blocks = columns // head_size
    parts = width // page
    packed = pack_ref.shape[0]
    tall = packed // (2 * shards)

    def rows_of(first, count):
        def home_of(row):
            request = row % count + first
            x = request // group_rows
            s = (request % group_rows) // req_rows
            return (s * 2 + x) * tall + request % req_rows * parts + row // count

        picked = jnp.dot(
            hot(count * parts, packed, home_of), pack_ref[...], preferred_element_type=jnp.float32
        )
        return jnp.concatenate(
            [picked[part * count : (part + 1) * count] for part in range(parts)], axis=1
        )

    own_tokens = rows_of(member * group_rows, group_rows)
    tokens_ref[...] = own_tokens
    own = scaled_norm(own_tokens, misc_ref[GAIN, :])
    normed = scaled_norm(rows_of(0, pair_rows), misc_ref[GAIN, :])
    raw = lax.dot_general(
        normed,
        misc_ref[GATES, :].astype(jnp.bfloat16),
        (((1,), (1,)), ((), ())),
        preferred_element_type=jnp.float32,
    )
    gate_vals = 1.0 / (1.0 + jnp.exp(-(raw + misc_ref[BIAS, : 2 * head_count])))
    column = lax.broadcasted_iota(jnp.int32, gate_vals.shape, 1)
    decay = jnp.sum(jnp.where(column == head, gate_vals, 0.0), axis=1, keepdims=True)
    strength = jnp.sum(
        jnp.where(column == head + head_count, gate_vals, 0.0), axis=1, keepdims=True
    )
    strength_ref[:pair_rows, :] = jnp.broadcast_to(strength, (pair_rows, head_size))
    ridges = misc_ref[RIDGE, :page]
    spot = lax.broadcasted_iota(jnp.int32, ridges.shape, 1)
    ridge = jnp.sum(jnp.where(spot == head, ridges, 0.0), axis=1, keepdims=True)
    strength_ref[pair_rows:, :] = jnp.broadcast_to(ridge, (TILE, head_size))

    all_slots = 2 * shards * slots
    side = tall - TILE
    pick_slot = hot(all_slots, packed, lambda row: (row // slots) * tall + side + row % slots)
    logs = jnp.dot(pick_slot, pack_ref[...], preferred_element_type=jnp.float32)
    pick_owner = hot(all_slots, packed, lambda row: (row // slots) * tall + side + slots)
    owners = jnp.dot(pick_owner, pack_ref[...], preferred_element_type=jnp.float32)
    at_slot = hot(all_slots, page, lambda row: row % slots).astype(jnp.float32)
    owner = jnp.sum(at_slot * owners, axis=1, keepdims=True).astype(jnp.int32)
    owner_ref[...] = jnp.broadcast_to(owner, owner_ref.shape)
    request = lax.broadcasted_iota(jnp.int32, (all_slots, pair_rows), 1)
    owner_hot = jnp.where(request == owner, 1.0, 0.0)
    wide_decay = jnp.broadcast_to(decay, (pair_rows, page))
    slot_decay = jnp.dot(
        owner_hot, wide_decay, precision=precise, preferred_element_type=jnp.float32
    )
    weight_ref[...] = slot_decay * jnp.exp(logs)

    for load in loads:
        load.wait()
    fresh = jnp.dot(own, qkv_ref[...], preferred_element_type=jnp.float32)
    before = misc_ref[TAP, :columns] * fresh + misc_ref[PAST, :columns]
    mixed_ref[...] = silu(before)
    for target in range(head_count):
        place = jnp.int32(0)
        for part in range(3):
            local = target + part * head_count - shard * blocks
            place = jnp.where((local >= 0) & (local < blocks), local, place)
        start = pl.multiple_of(place * head_size, head_size)
        send_ref[target * group_rows : (target + 1) * group_rows, :] = mixed_ref[
            :, pl.ds(start, head_size)
        ].astype(jnp.bfloat16)


def add_pieces(first, owner_ref, weight_ref, piece_refs, gram_ref):
    me = here()
    slots = piece_refs[0].shape[0] // 2
    for step, piece_ref in enumerate(piece_refs, first):
        for spot in range(slots):
            slot = at_step(FROM, step, me) * slots + spot
            keys = piece_ref[spot]
            both = jnp.concatenate([keys, piece_ref[slots + spot]], axis=1)
            turned = keys.T.astype(jnp.float32) * weight_ref[pl.ds(slot, 1), :]
            piece = jnp.dot(
                jnp.concatenate(split_pair(turned), axis=1),
                jnp.concatenate([both, both], axis=0),
                preferred_element_type=jnp.float32,
            )
            owner = owner_ref[slot, 0]
            gram_ref[owner] = gram_ref[owner] + piece


def gram_kernel(owner_ref, weight_ref, *refs):
    *piece_refs, gram_ref = refs
    gram_ref[...] = jnp.zeros_like(gram_ref)
    add_pieces(0, owner_ref, weight_ref, piece_refs, gram_ref)


def solve_kernel(
    first, head_count, blocks, owner_ref, weight_ref, mixed_ref, strength_ref, before_ref, *refs
):
    *piece_refs, own_ref, other_ref, gram_ref, rows_ref = refs
    head = here()
    member = lax.axis_index("member")
    pair_rows, head_size, _ = gram_ref.shape
    gram_ref[...] = before_ref[...]
    add_pieces(first, owner_ref, weight_ref, piece_refs, gram_ref)

    def columns_of(block):
        first = pl.multiple_of(block // blocks * pair_rows, pair_rows)
        return mixed_ref[pl.ds(first, pair_rows), :].astype(jnp.float32)

    query = unit_rows(columns_of(head))
    key_new = unit_rows(columns_of(head + head_count))
    value_new = columns_of(head + 2 * head_count)
    strength = strength_ref[:pair_rows, :]
    ridge = strength_ref[pair_rows : pair_rows + 1, :]

    def image_of(vectors, columns):
        turned = vectors.T
        pieces = []
        for row in range(pair_rows):
            spread = jnp.broadcast_to(turned[:, row : row + 1], (head_size, head_size))
            pieces.append(jnp.sum(gram_ref[row, :, columns] * spread, axis=0, keepdims=True))
        return jnp.concatenate(pieces, axis=0)

    found = jnp.zeros_like(query)
    residual = query
    direction = query
    res_norm = jnp.sum(residual * residual, axis=-1, keepdims=True)
    for iteration in range(ITERS):
        along = jnp.sum(key_new * direction, axis=-1, keepdims=True)
        image = image_of(direction, slice(0, head_size))
        image = image + strength * key_new * along + ridge * direction
        step = res_norm / jnp.sum(direction * image, axis=-1, keepdims=True)
        found = found + step * direction
        residual = residual - step * image
        next_norm = jnp.sum(residual * residual, axis=-1, keepdims=True)
        direction = residual + (next_norm / res_norm) * direction
        res_norm = next_norm

    total = image_of(found, slice(head_size, 2 * head_size))
    total = total + strength * value_new * jnp.sum(key_new * found, axis=-1, keepdims=True)
    rows_ref[...] = total
    half = pair_rows // 2
    mine = pl.multiple_of(member * half, half)
    theirs = pl.multiple_of((1 - member) * half, half)
    own_ref[...] = rows_ref[pl.ds(mine, half), :].astype(jnp.bfloat16)
    other_ref[...] = rows_ref[pl.ds(theirs, half), :].astype(jnp.bfloat16)


def out_kernel(own_ref, come_ref, out_ref, send_ref):
    first = lax.axis_index("member") == 0
    width = out_ref.shape[1]
    own = own_ref[...].astype(jnp.float32)
    come = come_ref[...].astype(jnp.float32)
    heads = jnp.concatenate([jnp.where(first, own, come), jnp.where(first, come, own)], axis=1)
    heads = heads.astype(jnp.bfloat16)
    part = jnp.dot(heads, out_ref[...], preferred_element_type=jnp.float32)
    send_ref[:, :width] = part.astype(jnp.bfloat16)
    send_ref[:, width:] = heads


def home_rows(value, req_rows):
    first = lax.axis_index("shard") * req_rows
    row = lax.broadcasted_iota(jnp.int32, value.shape, 0)
    picked = [
        jnp.sum(jnp.where(row == first + i, value, 0.0), axis=0, keepdims=True)
        for i in range(req_rows)
    ]
    return jnp.concatenate(picked, axis=0)


def mlp_kernel(
    shards,
    tokens_ref,
    gain_ref,
    gate_ref,
    up_ref,
    down_ref,
    *refs,
):
    part_refs, refs = refs[:shards], refs[shards:]
    mid_ref, retrieved_ref, *send_refs, down_scr, heads_ref = refs
    shard = lax.axis_index("shard")
    group_rows, width = tokens_ref.shape
    req_rows = mid_ref.shape[0]
    span = part_refs[0].shape[1] - width
    attended = part_refs[0][:, :width].astype(jnp.float32)
    for part_ref in part_refs[1:]:
        attended += part_ref[:, :width].astype(jnp.float32)
    mid_rows = (tokens_ref[...] + attended).astype(jnp.bfloat16)
    mlp_in = scaled_norm(mid_rows, gain_ref[...])
    contract = (((1,), (1,)), ((), ()))
    gate_part = lax.dot_general(
        mlp_in, gate_ref[...], contract, preferred_element_type=jnp.float32
    )
    up_part = lax.dot_general(mlp_in, up_ref[...], contract, preferred_element_type=jnp.float32)
    hidden = (silu(gate_part) * up_part).astype(jnp.bfloat16)
    down = jnp.dot(hidden, down_ref[...], preferred_element_type=jnp.float32)
    down_scr[...] = down.reshape(down_scr.shape)
    rows = send_refs[0].shape[0]
    for apart, send_ref in enumerate(send_refs):
        send_ref[...] = down_scr[pl.ds(pl.multiple_of((shard ^ apart) * rows, rows), rows), :]
    mid_ref[...] = home_rows(mid_rows.astype(jnp.float32), mid_ref.shape[0])
    for apart, part_ref in enumerate(part_refs):
        first = pl.multiple_of((shard ^ apart) * span, span)
        heads_ref[:, pl.ds(first, span)] = home_rows(
            part_ref[:, width:].astype(jnp.float32), req_rows
        )
    retrieved_ref[...] = heads_ref[...].astype(jnp.bfloat16)


def finish_kernel(mid_ref, *refs):
    *down_refs, layer_ref = refs
    total = down_refs[0][...]
    for down_ref in down_refs[1:]:
        total = total + down_ref[...]
    layer_ref[...] = (mid_ref[...] + total.reshape(mid_ref.shape)).astype(jnp.bfloat16)


def head_body(
    tokens,
    norm_gain,
    qkv_weight,
    conv_weight,
    conv_state,
    mesa_gates,
    mesa_bias,
    ridge_term,
    key_cache,
    value_cache,
    log_weight,
    page_owner,
    page_fill,
    out_weight,
    mlp_gain,
    gate_weight,
    up_weight,
    down_weight,
):
    shards = lax.axis_size("shard")
    devices = 2 * shards
    req_rows, width = tokens.shape
    slots, page, _ = key_cache.shape
    head_count = ridge_term.shape[0]
    head_size = width // head_count
    group_rows = shards * req_rows
    pair_rows = 2 * group_rows
    all_slots = devices * slots
    columns = qkv_weight.shape[1]
    shape = jax.ShapeDtypeStruct
    bf16, f32 = jnp.bfloat16, jnp.float32

    def exchange(value, axes):
        return lax.all_to_all(value, axes, split_axis=0, concat_axis=0, tiled=True)

    def spot(number):
        return number % 2 * shards + number // 2

    hbm = pl.BlockSpec(memory_space=pltpu.HBM)
    past_rows = jnp.transpose(conv_state, (1, 0, 2))
    gates = mesa_gates.T

    def pinned(*values):
        return [pltpu.with_memory_space_constraint(value, pltpu.HBM) for value in values]

    pieces = pl.pallas_call(
        cut_kernel,
        out_shape=(shape((2 * slots, page, head_size), bf16),) * devices,
        in_specs=[hbm] * 2,
        out_specs=(VMEM,) * devices,
        scratch_shapes=[
            pltpu.VMEM((2, *key_cache.shape), bf16),
            pltpu.SemaphoreType.DMA((2 * slots,)),
        ],
        compiler_params=PARAMS,
        name="cut",
    )(*pinned(key_cache, value_cache))

    def move(step):
        pairs = [
            (spot(source), spot(source ^ SEND[step][source >> 1 & 1])) for source in range(devices)
        ]
        return lax.ppermute(pieces[step], ("member", "shard"), pairs)

    moved = [pieces[0]] + [move(step) for step in range(1, 1 + EARLY)]
    tokens, pieces = lax.optimization_barrier((tokens, pieces))
    pack, misc = pl.pallas_call(
        pack_kernel,
        out_shape=(
            shape((devices * (req_rows * width // page + TILE), page), bf16),
            shape((GATES.stop, width), f32),
        ),
        in_specs=[hbm] * 10,
        out_specs=(VMEM,) * 2,
        scratch_shapes=[
            pltpu.VMEM(tokens.shape, bf16),
            pltpu.VMEM(log_weight.shape, bf16),
            pltpu.SMEM(page_owner.shape, jnp.int32),
            pltpu.SMEM(page_fill.shape, jnp.int32),
            pltpu.VMEM(past_rows.shape, bf16),
            pltpu.VMEM(gates.shape, bf16),
            pltpu.VMEM(conv_weight.shape, f32),
            pltpu.VMEM((1, width), f32),
            pltpu.VMEM((1, 2 * head_count), f32),
            pltpu.SMEM(ridge_term.shape, f32),
            pltpu.SemaphoreType.DMA((10,)),
        ],
        compiler_params=PARAMS,
        name="pack",
    )(
        *pinned(
            tokens,
            log_weight,
            page_owner,
            page_fill,
            past_rows,
            conv_weight,
            norm_gain[None, :],
            gates,
            mesa_bias[None, :],
            ridge_term,
        )
    )
    packs = exchange(pack, PAIR)

    pieces, packs = lax.optimization_barrier((pieces, packs))
    moved += [move(step) for step in range(1 + EARLY, devices)]

    mixed, own_tokens, weight, owner, strength = pl.pallas_call(
        functools.partial(project_kernel, shards, req_rows, slots, head_count),
        out_shape=(
            shape((devices * group_rows, head_size), bf16),
            shape((group_rows, width), f32),
            shape((all_slots, page), f32),
            shape((all_slots, page), jnp.int32),
            shape((pair_rows + TILE, head_size), f32),
        ),
        in_specs=[VMEM] * 2 + [hbm],
        out_specs=(VMEM,) * 5,
        scratch_shapes=[
            pltpu.VMEM((group_rows, columns), f32),
            pltpu.VMEM(qkv_weight.shape, bf16),
            pltpu.SemaphoreType.DMA((4,)),
        ],
        compiler_params=PARAMS,
        name="project",
    )(packs, misc, *pinned(qkv_weight))

    held = 1 + EARLY
    gram = pl.pallas_call(
        gram_kernel,
        out_shape=shape((pair_rows, head_size, 2 * head_size), f32),
        in_specs=[SMEM] + [VMEM] * (1 + held),
        out_specs=VMEM,
        compiler_params=PARAMS,
        name="gram",
    )(owner, weight, *moved[:held])
    mixed, gram = lax.optimization_barrier((mixed, gram))
    all_mixed = exchange(mixed, PAIR)
    all_mixed, owner, weight, gram = lax.optimization_barrier((all_mixed, owner, weight, gram))

    own_head, other_head = pl.pallas_call(
        functools.partial(solve_kernel, held, head_count, columns // head_size),
        out_shape=(shape((group_rows, head_size), bf16),) * 2,
        in_specs=[SMEM] + [VMEM] * (4 + devices - held),
        out_specs=(VMEM,) * 2,
        scratch_shapes=[
            pltpu.VMEM((pair_rows, head_size, 2 * head_size), f32),
            pltpu.VMEM((pair_rows, head_size), f32),
        ],
        compiler_params=PARAMS,
        name="solve",
    )(owner, weight, all_mixed, strength, gram, *moved[held:])
    part = pl.pallas_call(
        out_kernel,
        out_shape=shape((group_rows, width + 2 * head_size), bf16),
        in_specs=[VMEM] * 3,
        out_specs=VMEM,
        compiler_params=PARAMS,
        name="out",
    )(own_head, lax.ppermute(other_head, "member", [(0, 1), (1, 0)]), out_weight)

    def over_shards(sent):
        arrived = [sent[0]]
        for apart in range(1, shards):
            pairs = [(source, source ^ apart) for source in range(shards)]
            arrived.append(lax.ppermute(sent[apart], "shard", pairs))
        return arrived

    parts = over_shards([part] * shards)

    mid_home, retrieved, *down = pl.pallas_call(
        functools.partial(mlp_kernel, shards),
        out_shape=(
            shape((req_rows, width), f32),
            shape((req_rows, width), bf16),
        )
        + (shape((req_rows * head_count, head_size), f32),) * shards,
        in_specs=[VMEM] * (5 + shards),
        out_specs=(VMEM,) * (2 + shards),
        scratch_shapes=[
            pltpu.VMEM((group_rows * head_count, head_size), f32),
            pltpu.VMEM((req_rows, width), f32),
        ],
        compiler_params=PARAMS,
        name="mlp",
    )(
        own_tokens,
        mlp_gain[None, :],
        gate_weight.T,
        up_weight.T,
        down_weight,
        *parts,
    )
    layer_out = pl.pallas_call(
        finish_kernel,
        out_shape=shape((req_rows, width), bf16),
        in_specs=[VMEM] * (1 + shards),
        out_specs=VMEM,
        compiler_params=PARAMS,
        name="finish",
    )(mid_home, *over_shards(down))
    return (retrieved, layer_out)


def specs(group):
    rows = P((*group, "shard"))
    return (
        (
            rows,
            P(),
            P(None, "shard"),
            P(None, "shard"),
            P(group, None, "shard"),
            P(),
            P(),
            P(),
            rows,
            rows,
            rows,
            rows,
            rows,
            P("shard", None),
            P(),
            P(None, "shard"),
            P(None, "shard"),
            P("shard", None),
        ),
        (rows, rows),
    )


def solution(mesh):
    groups, shards = mesh.devices.shape

    def run(*args):
        head_count = args[7].shape[0]
        if 2 * shards == head_count == len(SEND):
            axes = ("pair", "member", "shard")
            used = Mesh(mesh.devices.reshape(groups // 2, 2, shards), axes)
            body, group = head_body, ("pair", "member")
        else:
            used, body, group = mesh, spread_body, ("group",)
        in_specs, out_specs = specs(group)
        return jax.shard_map(
            body, mesh=used, in_specs=in_specs, out_specs=out_specs, check_vma=False
        )(*args)

    return run
```

```python
import functools

import jax
import jax.numpy as jnp
from jax import lax
from jax.experimental import pallas as pl
from jax.experimental.pallas import tpu as pltpu
from jax.sharding import Mesh
from jax.sharding import PartitionSpec as P

ITERS = 4


precise = lax.Precision.HIGHEST

VMEM = pl.BlockSpec(memory_space=pltpu.VMEM)
SMEM = pl.BlockSpec(memory_space=pltpu.SMEM)


def partner(value, axis, apart):
    mask = 2**apart
    pairs = [(source, source ^ mask) for source in range(lax.axis_size(axis))]
    return lax.ppermute(value, axis, pairs)


def scaled_norm(row_vals, gain_vec):
    wide_rows = row_vals.astype(jnp.float32)
    factor = lax.rsqrt(jnp.mean(wide_rows * wide_rows, axis=-1, keepdims=True) + 1e-05)
    return (wide_rows * factor * gain_vec).astype(jnp.bfloat16)


def unit_rows(vectors):
    return vectors * lax.rsqrt(jnp.sum(vectors * vectors, axis=-1, keepdims=True) + 1e-06)


def slot_weights(owner_hot, decay_rows, log_weight, page_fill):
    page_len = log_weight.shape[2]
    slot_decay = jnp.dot(owner_hot, decay_rows, precision=precise)
    live_mask = (jnp.arange(page_len)[None, :] < page_fill[:, None]).astype(jnp.float32)
    return slot_decay[:, :, None] * jnp.exp(log_weight.astype(jnp.float32)) * live_mask[:, None, :]


def slot_terms(key_rows, source_rows, owner_hot, slot_weight, directions):
    slot_count, page_len, width_all = key_rows.shape
    head_count = slot_weight.shape[1]
    head_size = width_all // head_count
    member_count = owner_hot.shape[1]
    slot_dir = jnp.dot(owner_hot, directions.reshape(member_count, width_all), precision=precise)
    slot_dir = slot_dir.reshape(slot_count, head_count, head_size)
    key_wide = key_rows.astype(jnp.float32).reshape(slot_count, page_len, head_count, head_size)
    scores = jnp.einsum("sthd,shd->sht", key_wide, slot_dir, precision=precise)
    source_wide = source_rows.astype(jnp.float32).reshape(
        slot_count, page_len, head_count, head_size
    )
    contribution = jnp.einsum("sht,sthd->shd", slot_weight * scores, source_wide, precision=precise)
    summed = jnp.dot(owner_hot.T, contribution.reshape(slot_count, width_all), precision=precise)
    return summed.reshape(member_count, head_count, head_size)


def new_term(vectors, source_rows, strength_rows, key_new):
    return (
        strength_rows[:, :, None] * source_rows * jnp.sum(key_new * vectors, axis=-1, keepdims=True)
    )


def conjugate(query_rows, key_new, value_new, strength_rows, ridge_term, reduce_fn):
    solution = jnp.zeros_like(query_rows)
    residual = query_rows
    direction = query_rows
    res_norm = jnp.sum(residual * residual, axis=-1)
    for iteration in range(ITERS):
        image_vec = (
            reduce_fn(direction, False)
            + new_term(direction, key_new, strength_rows, key_new)
            + ridge_term[None, :, None] * direction
        )
        step_size = res_norm / jnp.sum(direction * image_vec, axis=-1)
        solution = solution + step_size[:, :, None] * direction
        residual = residual - step_size[:, :, None] * image_vec
        next_norm = jnp.sum(residual * residual, axis=-1)
        direction = residual + (next_norm / res_norm)[:, :, None] * direction
        res_norm = next_norm
    return reduce_fn(solution, True) + new_term(solution, value_new, strength_rows, key_new)


def pair_order(mine, theirs, parity):
    first = jnp.where(parity == 0, mine, theirs)
    second = jnp.where(parity == 0, theirs, mine)
    return jnp.concatenate([first, second], axis=0)


def spread_body(
    tokens,
    norm_gain,
    qkv_weight,
    conv_weight,
    conv_state,
    mesa_gates,
    mesa_bias,
    ridge_term,
    key_cache,
    value_cache,
    log_weight,
    page_owner,
    page_fill,
    out_weight,
    mlp_gain,
    gate_weight,
    up_weight,
    down_weight,
):
    req_rows = tokens.shape[0]
    group_rows = req_rows * lax.axis_size("shard")
    head_count = ridge_term.shape[0]
    width_all = key_cache.shape[2]
    head_size = width_all // head_count
    parity = lax.axis_index("group") % 2
    normed = scaled_norm(tokens, norm_gain)
    fresh_proj = jnp.dot(
        lax.all_gather(normed, "shard", axis=0, tiled=True),
        qkv_weight,
        preferred_element_type=jnp.float32,
    )
    past_rows = conv_state.astype(jnp.float32)
    pre_conv = (
        conv_weight[3] * fresh_proj
        + conv_weight[0] * past_rows[:, 0]
        + conv_weight[1] * past_rows[:, 1]
        + conv_weight[2] * past_rows[:, 2]
    )
    mixed_cols = jax.nn.silu(pre_conv).astype(jnp.bfloat16)
    home_rows = lax.all_to_all(mixed_cols, "shard", split_axis=0, concat_axis=1, tiled=True)
    split_rows = home_rows.astype(jnp.float32).reshape(req_rows, 3, head_count, head_size)
    query_home = unit_rows(split_rows[:, 0])
    key_home = unit_rows(split_rows[:, 1])
    value_home = split_rows[:, 2]
    gate_vals = jax.nn.sigmoid(
        jnp.dot(normed, mesa_gates, preferred_element_type=jnp.float32) + mesa_bias
    )
    decay_home = gate_vals[:, :head_count]
    strength_home = gate_vals[:, head_count:]
    owner_hot = (page_owner[:, None] == jnp.arange(2 * group_rows)[None, :]).astype(jnp.float32)
    stored = {}

    def cache_pass(directions, decay_grp, with_values):
        far_dirs, far_decay = partner((directions, decay_grp), "group", 0)
        pair_dirs = pair_order(directions, far_dirs, parity)
        pair_decay = pair_order(decay_grp, far_decay, parity)
        if "weight" not in stored:
            stored["weight"] = slot_weights(owner_hot, pair_decay, log_weight, page_fill)
        source_rows = value_cache if with_values else key_cache
        summed = slot_terms(key_cache, source_rows, owner_hot, stored["weight"], pair_dirs)
        mine = jnp.where(parity == 0, summed[:group_rows], summed[group_rows:])
        theirs = jnp.where(parity == 0, summed[group_rows:], summed[:group_rows])
        returned = partner(theirs, "group", 0)
        return mine + returned

    def reduce_home(vectors, with_values):
        directions, decay_grp = (
            lax.all_gather(vectors, "shard", axis=0, tiled=True),
            lax.all_gather(decay_home, "shard", axis=0, tiled=True),
        )
        return lax.psum_scatter(
            cache_pass(directions, decay_grp, with_values), "shard", scatter_dimension=0, tiled=True
        )

    found = conjugate(query_home, key_home, value_home, strength_home, ridge_term, reduce_home)
    retrieved = found.reshape(req_rows, width_all).astype(jnp.bfloat16)
    columns = lax.all_to_all(retrieved, "shard", split_axis=1, concat_axis=0, tiled=True)
    attended = lax.psum_scatter(
        jnp.dot(columns, out_weight, preferred_element_type=jnp.float32),
        "shard",
        scatter_dimension=0,
        tiled=True,
    )
    mid_rows = (tokens.astype(jnp.float32) + attended).astype(jnp.bfloat16)
    mlp_in = scaled_norm(mid_rows, mlp_gain)
    piece_rows = lax.all_gather(mlp_in, "shard", axis=0, tiled=True)
    gate_part = jnp.dot(piece_rows, gate_weight, preferred_element_type=jnp.float32)
    up_part = jnp.dot(piece_rows, up_weight, preferred_element_type=jnp.float32)
    hidden_rows = (jax.nn.silu(gate_part) * up_part).astype(jnp.bfloat16)
    down_part = lax.psum_scatter(
        jnp.dot(hidden_rows, down_weight, preferred_element_type=jnp.float32),
        "shard",
        scatter_dimension=0,
        tiled=True,
    )
    layer_out = (mid_rows.astype(jnp.float32) + down_part).astype(jnp.bfloat16)
    return (retrieved, layer_out)


TILE = 8
MASKED = -1e38
PAIR = ("shard", "member")
PARAMS = pltpu.CompilerParams(vmem_limit_bytes=16 * 1024 * 1024)
PAST, TAP, GAIN, BIAS, RIDGE = slice(0, 8), slice(8, 9), slice(9, 10), slice(10, 11), slice(11, 12)
GATES = slice(16, 32)

SEND = ((0, 0), (2, 2), (5, 5), (7, 7), (1, 4), (4, 1), (3, 6), (6, 3))
FROM = tuple((b, a) if a & 2 else (a, b) for a, b in SEND)
EARLY = 4
HELD = 4


def split_pair(value):
    high = value.astype(jnp.bfloat16)
    low = (value - high.astype(jnp.float32)).astype(jnp.bfloat16)
    return high, low


def hot(rows, columns, target_fn):
    row = lax.broadcasted_iota(jnp.int32, (rows, columns), 0)
    column = lax.broadcasted_iota(jnp.int32, (rows, columns), 1)
    return jnp.where(column == target_fn(row), 1.0, 0.0).astype(jnp.bfloat16)


def here():
    return lax.axis_index("shard") * 2 + lax.axis_index("member")


def at_step(table, step, me):
    return me ^ jnp.where((me & 2) == 0, table[step][0], table[step][1])


def silu(value):
    return value / (1.0 + jnp.exp(-value))


def cut_kernel(key_hbm, value_hbm, *refs):
    *piece_refs, stage_ref, sems = refs
    slots = key_hbm.shape[0]
    head_size = piece_refs[0].shape[2]
    me = here()
    loads = [
        pltpu.make_async_copy(source.at[slot], stage_ref.at[part, slot], sems.at[part * slots + slot])
        for part, source in enumerate((key_hbm, value_hbm))
        for slot in range(slots)
    ]
    for load in loads:
        load.start()
    starts = [
        pl.multiple_of(at_step(SEND, step, me) * head_size, head_size)
        for step in range(len(piece_refs))
    ]
    for part in range(2):
        for slot in range(slots):
            place = part * slots + slot
            loads[place].wait()
            for start, piece_ref in zip(starts, piece_refs):
                piece_ref[place] = stage_ref[part, slot, :, pl.ds(start, head_size)]


def pack_kernel(
    tokens_hbm,
    logs_hbm,
    owner_hbm,
    fill_hbm,
    past_hbm,
    tap_hbm,
    gain_hbm,
    gates_hbm,
    bias_hbm,
    ridge_hbm,
    send_ref,
    misc_ref,
    tokens_ref,
    logs_ref,
    owner_ref,
    fill_ref,
    state_ref,
    gates_ref,
    tap_ref,
    gain_ref,
    bias_ref,
    ridge_ref,
    sems,
):
    req_rows, width = tokens_ref.shape
    slots, head_count, page = logs_ref.shape
    copies = [
        pltpu.make_async_copy(source, target, sems.at[place])
        for place, (source, target) in enumerate(
            [
                (owner_hbm, owner_ref),
                (fill_hbm, fill_ref),
                (tokens_hbm, tokens_ref),
                (logs_hbm, logs_ref),
                (past_hbm, state_ref),
                (tap_hbm, tap_ref),
                (gain_hbm, gain_ref),
                (gates_hbm, gates_ref),
                (bias_hbm, bias_ref),
                (ridge_hbm, ridge_ref),
            ]
        )
    ]
    for copy in copies:
        copy.start()
    for copy in copies:
        copy.wait()

    tokens = tokens_ref[...].astype(jnp.float32)
    rows = [
        tokens[row : row + 1, first : first + page]
        for row in range(req_rows)
        for first in range(0, width, page)
    ]
    tile = jnp.concatenate(rows, axis=0).astype(jnp.bfloat16)
    packed = tile.shape[0] + TILE
    spot = lax.broadcasted_iota(jnp.int32, (head_count, page), 1)
    logs = []
    lane = lax.broadcasted_iota(jnp.int32, (1, page), 1)
    owners = jnp.zeros((1, page), jnp.float32)
    for slot in range(slots):
        rows = logs_ref[slot].astype(jnp.float32)
        logs.append(jnp.where(spot < fill_ref[slot], rows, MASKED))
        owners = jnp.where(lane == slot, owner_ref[slot].astype(jnp.float32), owners)
    rest = jnp.zeros((TILE - slots - 1, page), jnp.float32)
    for head in range(head_count):
        rows = [log[head : head + 1, :] for log in logs]
        side = jnp.concatenate([*rows, owners, rest], axis=0).astype(jnp.bfloat16)
        send_ref[head * packed : head * packed + tile.shape[0], :] = tile
        send_ref[head * packed + tile.shape[0] : (head + 1) * packed, :] = side

    past = tap_ref[0:1, :] * state_ref[0].astype(jnp.float32)
    past = past + tap_ref[1:2, :] * state_ref[1].astype(jnp.float32)
    past = past + tap_ref[2:3, :] * state_ref[2].astype(jnp.float32)
    columns = past.shape[1]
    misc_ref[PAST, :columns] = past
    misc_ref[TAP, :columns] = tap_ref[3:4, :]
    misc_ref[GAIN, :] = gain_ref[...]
    misc_ref[BIAS, : 2 * head_count] = bias_ref[...]
    ridges = jnp.zeros((1, page), jnp.float32)
    for head in range(head_count):
        ridges = jnp.where(lane == head, ridge_ref[head], ridges)
    misc_ref[RIDGE, :page] = ridges
    misc_ref[GATES, :] = gates_ref[...].astype(jnp.float32)


def project_kernel(
    shards,
    req_rows,
    slots,
    head_count,
    pack_ref,
    misc_ref,
    qkv_hbm,
    send_ref,
    tokens_ref,
    weight_ref,
    owner_ref,
    strength_ref,
    mixed_ref,
    qkv_ref,
    sems,
):
    chunk = qkv_ref.shape[0] // sems.shape[0]
    loads = [
        pltpu.make_async_copy(
            qkv_hbm.at[pl.ds(part * chunk, chunk)],
            qkv_ref.at[pl.ds(part * chunk, chunk)],
            sems.at[part],
        )
        for part in range(sems.shape[0])
    ]
    for load in loads:
        load.start()
    shard = lax.axis_index("shard")
    member = lax.axis_index("member")
    head = here()
    group_rows = shards * req_rows
    pair_rows = 2 * group_rows
    width = misc_ref.shape[1]
    columns = qkv_ref.shape[1]
    page = weight_ref.shape[1]
    head_size = send_ref.shape[1]
    blocks = columns // head_size
    parts = width // page
    packed = pack_ref.shape[0]
    tall = packed // (2 * shards)

    def rows_of(first, count):
        def home_of(row):
            request = row % count + first
            x = request // group_rows
            s = (request % group_rows) // req_rows
            return (s * 2 + x) * tall + request % req_rows * parts + row // count

        picked = jnp.dot(
            hot(count * parts, packed, home_of), pack_ref[...], preferred_element_type=jnp.float32
        )
        return jnp.concatenate(
            [picked[part * count : (part + 1) * count] for part in range(parts)], axis=1
        )

    own_tokens = rows_of(member * group_rows, group_rows)
    tokens_ref[...] = own_tokens
    own = scaled_norm(own_tokens, misc_ref[GAIN, :])
    normed = scaled_norm(rows_of(0, pair_rows), misc_ref[GAIN, :])
    raw = lax.dot_general(
        normed,
        misc_ref[GATES, :].astype(jnp.bfloat16),
        (((1,), (1,)), ((), ())),
        preferred_element_type=jnp.float32,
    )
    gate_vals = 1.0 / (1.0 + jnp.exp(-(raw + misc_ref[BIAS, : 2 * head_count])))
    column = lax.broadcasted_iota(jnp.int32, gate_vals.shape, 1)
    decay = jnp.sum(jnp.where(column == head, gate_vals, 0.0), axis=1, keepdims=True)
    strength = jnp.sum(
        jnp.where(column == head + head_count, gate_vals, 0.0), axis=1, keepdims=True
    )
    strength_ref[:pair_rows, :] = jnp.broadcast_to(strength, (pair_rows, head_size))
    ridges = misc_ref[RIDGE, :page]
    spot = lax.broadcasted_iota(jnp.int32, ridges.shape, 1)
    ridge = jnp.sum(jnp.where(spot == head, ridges, 0.0), axis=1, keepdims=True)
    strength_ref[pair_rows:, :] = jnp.broadcast_to(ridge, (TILE, head_size))

    all_slots = 2 * shards * slots
    side = tall - TILE
    pick_slot = hot(all_slots, packed, lambda row: (row // slots) * tall + side + row % slots)
    logs = jnp.dot(pick_slot, pack_ref[...], preferred_element_type=jnp.float32)
    pick_owner = hot(all_slots, packed, lambda row: (row // slots) * tall + side + slots)
    owners = jnp.dot(pick_owner, pack_ref[...], preferred_element_type=jnp.float32)
    at_slot = hot(all_slots, page, lambda row: row % slots).astype(jnp.float32)
    owner = jnp.sum(at_slot * owners, axis=1, keepdims=True).astype(jnp.int32)
    owner_ref[...] = jnp.broadcast_to(owner, owner_ref.shape)
    request = lax.broadcasted_iota(jnp.int32, (all_slots, pair_rows), 1)
    owner_hot = jnp.where(request == owner, 1.0, 0.0)
    wide_decay = jnp.broadcast_to(decay, (pair_rows, page))
    slot_decay = jnp.dot(
        owner_hot, wide_decay, precision=precise, preferred_element_type=jnp.float32
    )
    weight_ref[...] = slot_decay * jnp.exp(logs)

    for load in loads:
        load.wait()
    fresh = jnp.dot(own, qkv_ref[...], preferred_element_type=jnp.float32)
    before = misc_ref[TAP, :columns] * fresh + misc_ref[PAST, :columns]
    mixed_ref[...] = silu(before)
    for target in range(head_count):
        place = jnp.int32(0)
        for part in range(3):
            local = target + part * head_count - shard * blocks
            place = jnp.where((local >= 0) & (local < blocks), local, place)
        start = pl.multiple_of(place * head_size, head_size)
        send_ref[target * group_rows : (target + 1) * group_rows, :] = mixed_ref[
            :, pl.ds(start, head_size)
        ].astype(jnp.bfloat16)


def add_pieces(first, owner_ref, weight_ref, piece_refs, gram_ref):
    me = here()
    slots = piece_refs[0].shape[0] // 2
    for step, piece_ref in enumerate(piece_refs, first):
        for spot in range(slots):
            slot = at_step(FROM, step, me) * slots + spot
            keys = piece_ref[spot]
            both = jnp.concatenate([keys, piece_ref[slots + spot]], axis=1)
            turned = keys.T.astype(jnp.float32) * weight_ref[pl.ds(slot, 1), :]
            piece = jnp.dot(
                jnp.concatenate(split_pair(turned), axis=1),
                jnp.concatenate([both, both], axis=0),
                preferred_element_type=jnp.float32,
            )
            owner = owner_ref[slot, 0]
            gram_ref[owner] = gram_ref[owner] + piece


def gram_kernel(owner_ref, weight_ref, *refs):
    *piece_refs, gram_ref = refs
    gram_ref[...] = jnp.zeros_like(gram_ref)
    add_pieces(0, owner_ref, weight_ref, piece_refs, gram_ref)


def solve_kernel(
    first, head_count, blocks, owner_ref, weight_ref, mixed_ref, strength_ref, before_ref, *refs
):
    *piece_refs, own_ref, other_ref, gram_ref, rows_ref = refs
    del before_ref
    head = here()
    member = lax.axis_index("member")
    pair_rows, head_size, _ = gram_ref.shape
    add_pieces(first, owner_ref, weight_ref, piece_refs, gram_ref)

    def columns_of(block):
        first = pl.multiple_of(block // blocks * pair_rows, pair_rows)
        return mixed_ref[pl.ds(first, pair_rows), :].astype(jnp.float32)

    query = unit_rows(columns_of(head))
    key_new = unit_rows(columns_of(head + head_count))
    value_new = columns_of(head + 2 * head_count)
    strength = strength_ref[:pair_rows, :]
    ridge = strength_ref[pair_rows : pair_rows + 1, :]

    def image_of(vectors, columns):
        turned = vectors.T
        pieces = []
        for row in range(pair_rows):
            spread = jnp.broadcast_to(turned[:, row : row + 1], (head_size, head_size))
            pieces.append(jnp.sum(gram_ref[row, :, columns] * spread, axis=0, keepdims=True))
        return jnp.concatenate(pieces, axis=0)

    found = jnp.zeros_like(query)
    residual = query
    direction = query
    res_norm = jnp.sum(residual * residual, axis=-1, keepdims=True)
    for iteration in range(ITERS):
        along = jnp.sum(key_new * direction, axis=-1, keepdims=True)
        image = image_of(direction, slice(0, head_size))
        image = image + strength * key_new * along + ridge * direction
        step = res_norm / jnp.sum(direction * image, axis=-1, keepdims=True)
        found = found + step * direction
        residual = residual - step * image
        next_norm = jnp.sum(residual * residual, axis=-1, keepdims=True)
        direction = residual + (next_norm / res_norm) * direction
        res_norm = next_norm

    total = image_of(found, slice(head_size, 2 * head_size))
    total = total + strength * value_new * jnp.sum(key_new * found, axis=-1, keepdims=True)
    rows_ref[...] = total
    half = pair_rows // 2
    mine = pl.multiple_of(member * half, half)
    theirs = pl.multiple_of((1 - member) * half, half)
    own_ref[...] = rows_ref[pl.ds(mine, half), :].astype(jnp.bfloat16)
    other_ref[...] = rows_ref[pl.ds(theirs, half), :].astype(jnp.bfloat16)


def out_kernel(own_ref, come_ref, out_ref, send_ref):
    first = lax.axis_index("member") == 0
    width = out_ref.shape[1]
    own = own_ref[...].astype(jnp.float32)
    come = come_ref[...].astype(jnp.float32)
    heads = jnp.concatenate([jnp.where(first, own, come), jnp.where(first, come, own)], axis=1)
    heads = heads.astype(jnp.bfloat16)
    part = jnp.dot(heads, out_ref[...], preferred_element_type=jnp.float32)
    send_ref[:, :width] = part.astype(jnp.bfloat16)
    send_ref[:, width:] = heads


def home_rows(value, req_rows):
    first = lax.axis_index("shard") * req_rows
    row = lax.broadcasted_iota(jnp.int32, value.shape, 0)
    picked = [
        jnp.sum(jnp.where(row == first + i, value, 0.0), axis=0, keepdims=True)
        for i in range(req_rows)
    ]
    return jnp.concatenate(picked, axis=0)


def mlp_kernel(
    shards,
    tokens_ref,
    gain_ref,
    gate_ref,
    up_ref,
    down_ref,
    *refs,
):
    part_refs, refs = refs[:shards], refs[shards:]
    mid_ref, retrieved_ref, *send_refs, down_scr, heads_ref = refs
    shard = lax.axis_index("shard")
    group_rows, width = tokens_ref.shape
    req_rows = mid_ref.shape[0]
    span = part_refs[0].shape[1] - width
    attended = part_refs[0][:, :width].astype(jnp.float32)
    for part_ref in part_refs[1:]:
        attended += part_ref[:, :width].astype(jnp.float32)
    mid_rows = (tokens_ref[...] + attended).astype(jnp.bfloat16)
    mlp_in = scaled_norm(mid_rows, gain_ref[...])
    contract = (((1,), (1,)), ((), ()))
    gate_part = lax.dot_general(
        mlp_in, gate_ref[...], contract, preferred_element_type=jnp.float32
    )
    up_part = lax.dot_general(mlp_in, up_ref[...], contract, preferred_element_type=jnp.float32)
    hidden = (silu(gate_part) * up_part).astype(jnp.bfloat16)
    down = jnp.dot(hidden, down_ref[...], preferred_element_type=jnp.float32)
    down_scr[...] = down.reshape(down_scr.shape)
    rows = send_refs[0].shape[0]
    for apart, send_ref in enumerate(send_refs):
        send_ref[...] = down_scr[pl.ds(pl.multiple_of((shard ^ apart) * rows, rows), rows), :]
    mid_ref[...] = home_rows(mid_rows.astype(jnp.float32), mid_ref.shape[0])
    for apart, part_ref in enumerate(part_refs):
        first = pl.multiple_of((shard ^ apart) * span, span)
        heads_ref[:, pl.ds(first, span)] = home_rows(
            part_ref[:, width:].astype(jnp.float32), req_rows
        )
    retrieved_ref[...] = heads_ref[...].astype(jnp.bfloat16)


def finish_kernel(mid_ref, *refs):
    *down_refs, layer_ref = refs
    total = down_refs[0][...]
    for down_ref in down_refs[1:]:
        total = total + down_ref[...]
    layer_ref[...] = (mid_ref[...] + total.reshape(mid_ref.shape)).astype(jnp.bfloat16)


def head_body(
    tokens,
    norm_gain,
    qkv_weight,
    conv_weight,
    conv_state,
    mesa_gates,
    mesa_bias,
    ridge_term,
    key_cache,
    value_cache,
    log_weight,
    page_owner,
    page_fill,
    out_weight,
    mlp_gain,
    gate_weight,
    up_weight,
    down_weight,
):
    shards = lax.axis_size("shard")
    devices = 2 * shards
    req_rows, width = tokens.shape
    slots, page, _ = key_cache.shape
    head_count = ridge_term.shape[0]
    head_size = width // head_count
    group_rows = shards * req_rows
    pair_rows = 2 * group_rows
    all_slots = devices * slots
    columns = qkv_weight.shape[1]
    shape = jax.ShapeDtypeStruct
    bf16, f32 = jnp.bfloat16, jnp.float32

    def exchange(value, axes):
        return lax.all_to_all(value, axes, split_axis=0, concat_axis=0, tiled=True)

    def spot(number):
        return number % 2 * shards + number // 2

    hbm = pl.BlockSpec(memory_space=pltpu.HBM)
    past_rows = jnp.transpose(conv_state, (1, 0, 2))
    gates = mesa_gates.T

    def pinned(*values):
        return [pltpu.with_memory_space_constraint(value, pltpu.HBM) for value in values]

    pieces = pl.pallas_call(
        cut_kernel,
        out_shape=(shape((2 * slots, page, head_size), bf16),) * devices,
        in_specs=[hbm] * 2,
        out_specs=(VMEM,) * devices,
        scratch_shapes=[
            pltpu.VMEM((2, *key_cache.shape), bf16),
            pltpu.SemaphoreType.DMA((2 * slots,)),
        ],
        compiler_params=PARAMS,
        name="cut",
    )(*pinned(key_cache, value_cache))

    def move(step):
        pairs = [
            (spot(source), spot(source ^ SEND[step][source >> 1 & 1])) for source in range(devices)
        ]
        return lax.ppermute(pieces[step], ("member", "shard"), pairs)

    moved = [pieces[0]] + [move(step) for step in range(1, 1 + EARLY)]
    tokens, pieces, moved[1] = lax.optimization_barrier((tokens, pieces, moved[1]))
    pack, misc = pl.pallas_call(
        pack_kernel,
        out_shape=(
            shape((devices * (req_rows * width // page + TILE), page), bf16),
            shape((GATES.stop, width), f32),
        ),
        in_specs=[hbm] * 10,
        out_specs=(VMEM,) * 2,
        scratch_shapes=[
            pltpu.VMEM(tokens.shape, bf16),
            pltpu.VMEM(log_weight.shape, bf16),
            pltpu.SMEM(page_owner.shape, jnp.int32),
            pltpu.SMEM(page_fill.shape, jnp.int32),
            pltpu.VMEM(past_rows.shape, bf16),
            pltpu.VMEM(gates.shape, bf16),
            pltpu.VMEM(conv_weight.shape, f32),
            pltpu.VMEM((1, width), f32),
            pltpu.VMEM((1, 2 * head_count), f32),
            pltpu.SMEM(ridge_term.shape, f32),
            pltpu.SemaphoreType.DMA((10,)),
        ],
        compiler_params=PARAMS,
        name="pack",
    )(
        *pinned(
            tokens,
            log_weight,
            page_owner,
            page_fill,
            past_rows,
            conv_weight,
            norm_gain[None, :],
            gates,
            mesa_bias[None, :],
            ridge_term,
        )
    )
    packs = exchange(pack, PAIR)

    pieces, packs = lax.optimization_barrier((pieces, packs))
    moved += [move(step) for step in range(1 + EARLY, devices)]

    mixed, own_tokens, weight, owner, strength = pl.pallas_call(
        functools.partial(project_kernel, shards, req_rows, slots, head_count),
        out_shape=(
            shape((devices * group_rows, head_size), bf16),
            shape((group_rows, width), f32),
            shape((all_slots, page), f32),
            shape((all_slots, page), jnp.int32),
            shape((pair_rows + TILE, head_size), f32),
        ),
        in_specs=[VMEM] * 2 + [hbm],
        out_specs=(VMEM,) * 5,
        scratch_shapes=[
            pltpu.VMEM((group_rows, columns), f32),
            pltpu.VMEM(qkv_weight.shape, bf16),
            pltpu.SemaphoreType.DMA((4,)),
        ],
        compiler_params=PARAMS,
        name="project",
    )(packs, misc, *pinned(qkv_weight))

    held = HELD
    gram = pl.pallas_call(
        gram_kernel,
        out_shape=shape((pair_rows, head_size, 2 * head_size), f32),
        in_specs=[SMEM] + [VMEM] * (1 + held),
        out_specs=VMEM,
        compiler_params=PARAMS,
        name="gram",
    )(owner, weight, *moved[:held])
    mixed, gram = lax.optimization_barrier((mixed, gram))
    all_mixed = exchange(mixed, PAIR)
    all_mixed, owner, weight, gram = lax.optimization_barrier((all_mixed, owner, weight, gram))

    own_head, other_head, _ = pl.pallas_call(
        functools.partial(solve_kernel, held, head_count, columns // head_size),
        out_shape=(
            shape((group_rows, head_size), bf16),
            shape((group_rows, head_size), bf16),
            pltpu.VMEM(gram.shape, f32),
        ),
        in_specs=[SMEM] + [VMEM] * (4 + devices - held),
        out_specs=(VMEM,) * 3,
        input_output_aliases={4: 2},
        scratch_shapes=[pltpu.VMEM((pair_rows, head_size), f32)],
        compiler_params=PARAMS,
        name="solve",
    )(
        owner,
        weight,
        all_mixed,
        strength,
        pltpu.with_memory_space_constraint(gram, pltpu.VMEM),
        *moved[held:],
    )
    part = pl.pallas_call(
        out_kernel,
        out_shape=shape((group_rows, width + 2 * head_size), bf16),
        in_specs=[VMEM] * 3,
        out_specs=VMEM,
        compiler_params=PARAMS,
        name="out",
    )(own_head, lax.ppermute(other_head, "member", [(0, 1), (1, 0)]), out_weight)

    def over_shards(sent):
        arrived = [sent[0]]
        for apart in range(1, shards):
            pairs = [(source, source ^ apart) for source in range(shards)]
            arrived.append(lax.ppermute(sent[apart], "shard", pairs))
        return arrived

    parts = over_shards([part] * shards)

    mid_home, retrieved, *down = pl.pallas_call(
        functools.partial(mlp_kernel, shards),
        out_shape=(
            shape((req_rows, width), f32),
            shape((req_rows, width), bf16),
        )
        + (shape((req_rows * head_count, head_size), f32),) * shards,
        in_specs=[VMEM] * (5 + shards),
        out_specs=(VMEM,) * (2 + shards),
        scratch_shapes=[
            pltpu.VMEM((group_rows * head_count, head_size), f32),
            pltpu.VMEM((req_rows, width), f32),
        ],
        compiler_params=PARAMS,
        name="mlp",
    )(
        own_tokens,
        mlp_gain[None, :],
        gate_weight.T,
        up_weight.T,
        down_weight,
        *parts,
    )
    layer_out = pl.pallas_call(
        finish_kernel,
        out_shape=shape((req_rows, width), bf16),
        in_specs=[VMEM] * (1 + shards),
        out_specs=VMEM,
        compiler_params=PARAMS,
        name="finish",
    )(mid_home, *over_shards(down))
    return (retrieved, layer_out)


def specs(group):
    rows = P((*group, "shard"))
    return (
        (
            rows,
            P(),
            P(None, "shard"),
            P(None, "shard"),
            P(group, None, "shard"),
            P(),
            P(),
            P(),
            rows,
            rows,
            rows,
            rows,
            rows,
            P("shard", None),
            P(),
            P(None, "shard"),
            P(None, "shard"),
            P("shard", None),
        ),
        (rows, rows),
    )


def solution(mesh):
    groups, shards = mesh.devices.shape

    def run(*args):
        head_count = args[7].shape[0]
        if 2 * shards == head_count == len(SEND):
            axes = ("pair", "member", "shard")
            used = Mesh(mesh.devices.reshape(groups // 2, 2, shards), axes)
            body, group = head_body, ("pair", "member")
        else:
            used, body, group = mesh, spread_body, ("group",)
        in_specs, out_specs = specs(group)
        return jax.shard_map(
            body, mesh=used, in_specs=in_specs, out_specs=out_specs, check_vma=False
        )(*args)

    return run
```

```python
import functools

import jax
import jax.numpy as jnp
from jax import lax
from jax.experimental import pallas as pl
from jax.experimental.pallas import tpu as pltpu
from jax.sharding import Mesh
from jax.sharding import PartitionSpec as P

ITERS = 4


precise = lax.Precision.HIGHEST

VMEM = pl.BlockSpec(memory_space=pltpu.VMEM)
SMEM = pl.BlockSpec(memory_space=pltpu.SMEM)


def partner(value, axis, apart):
    mask = 2**apart
    pairs = [(source, source ^ mask) for source in range(lax.axis_size(axis))]
    return lax.ppermute(value, axis, pairs)


def scaled_norm(row_vals, gain_vec):
    wide_rows = row_vals.astype(jnp.float32)
    factor = lax.rsqrt(jnp.mean(wide_rows * wide_rows, axis=-1, keepdims=True) + 1e-05)
    return (wide_rows * factor * gain_vec).astype(jnp.bfloat16)


def unit_rows(vectors):
    return vectors * lax.rsqrt(jnp.sum(vectors * vectors, axis=-1, keepdims=True) + 1e-06)


def slot_weights(owner_hot, decay_rows, log_weight, page_fill):
    page_len = log_weight.shape[2]
    slot_decay = jnp.dot(owner_hot, decay_rows, precision=precise)
    live_mask = (jnp.arange(page_len)[None, :] < page_fill[:, None]).astype(jnp.float32)
    return slot_decay[:, :, None] * jnp.exp(log_weight.astype(jnp.float32)) * live_mask[:, None, :]


def slot_terms(key_rows, source_rows, owner_hot, slot_weight, directions):
    slot_count, page_len, width_all = key_rows.shape
    head_count = slot_weight.shape[1]
    head_size = width_all // head_count
    member_count = owner_hot.shape[1]
    slot_dir = jnp.dot(owner_hot, directions.reshape(member_count, width_all), precision=precise)
    slot_dir = slot_dir.reshape(slot_count, head_count, head_size)
    key_wide = key_rows.astype(jnp.float32).reshape(slot_count, page_len, head_count, head_size)
    scores = jnp.einsum("sthd,shd->sht", key_wide, slot_dir, precision=precise)
    source_wide = source_rows.astype(jnp.float32).reshape(
        slot_count, page_len, head_count, head_size
    )
    contribution = jnp.einsum("sht,sthd->shd", slot_weight * scores, source_wide, precision=precise)
    summed = jnp.dot(owner_hot.T, contribution.reshape(slot_count, width_all), precision=precise)
    return summed.reshape(member_count, head_count, head_size)


def new_term(vectors, source_rows, strength_rows, key_new):
    return (
        strength_rows[:, :, None] * source_rows * jnp.sum(key_new * vectors, axis=-1, keepdims=True)
    )


def conjugate(query_rows, key_new, value_new, strength_rows, ridge_term, reduce_fn):
    solution = jnp.zeros_like(query_rows)
    residual = query_rows
    direction = query_rows
    res_norm = jnp.sum(residual * residual, axis=-1)
    for iteration in range(ITERS):
        image_vec = (
            reduce_fn(direction, False)
            + new_term(direction, key_new, strength_rows, key_new)
            + ridge_term[None, :, None] * direction
        )
        step_size = res_norm / jnp.sum(direction * image_vec, axis=-1)
        solution = solution + step_size[:, :, None] * direction
        residual = residual - step_size[:, :, None] * image_vec
        next_norm = jnp.sum(residual * residual, axis=-1)
        direction = residual + (next_norm / res_norm)[:, :, None] * direction
        res_norm = next_norm
    return reduce_fn(solution, True) + new_term(solution, value_new, strength_rows, key_new)


def pair_order(mine, theirs, parity):
    first = jnp.where(parity == 0, mine, theirs)
    second = jnp.where(parity == 0, theirs, mine)
    return jnp.concatenate([first, second], axis=0)


def spread_body(
    tokens,
    norm_gain,
    qkv_weight,
    conv_weight,
    conv_state,
    mesa_gates,
    mesa_bias,
    ridge_term,
    key_cache,
    value_cache,
    log_weight,
    page_owner,
    page_fill,
    out_weight,
    mlp_gain,
    gate_weight,
    up_weight,
    down_weight,
):
    req_rows = tokens.shape[0]
    group_rows = req_rows * lax.axis_size("shard")
    head_count = ridge_term.shape[0]
    width_all = key_cache.shape[2]
    head_size = width_all // head_count
    parity = lax.axis_index("group") % 2
    normed = scaled_norm(tokens, norm_gain)
    fresh_proj = jnp.dot(
        lax.all_gather(normed, "shard", axis=0, tiled=True),
        qkv_weight,
        preferred_element_type=jnp.float32,
    )
    past_rows = conv_state.astype(jnp.float32)
    pre_conv = (
        conv_weight[3] * fresh_proj
        + conv_weight[0] * past_rows[:, 0]
        + conv_weight[1] * past_rows[:, 1]
        + conv_weight[2] * past_rows[:, 2]
    )
    mixed_cols = jax.nn.silu(pre_conv).astype(jnp.bfloat16)
    home_rows = lax.all_to_all(mixed_cols, "shard", split_axis=0, concat_axis=1, tiled=True)
    split_rows = home_rows.astype(jnp.float32).reshape(req_rows, 3, head_count, head_size)
    query_home = unit_rows(split_rows[:, 0])
    key_home = unit_rows(split_rows[:, 1])
    value_home = split_rows[:, 2]
    gate_vals = jax.nn.sigmoid(
        jnp.dot(normed, mesa_gates, preferred_element_type=jnp.float32) + mesa_bias
    )
    decay_home = gate_vals[:, :head_count]
    strength_home = gate_vals[:, head_count:]
    owner_hot = (page_owner[:, None] == jnp.arange(2 * group_rows)[None, :]).astype(jnp.float32)
    stored = {}

    def cache_pass(directions, decay_grp, with_values):
        far_dirs, far_decay = partner((directions, decay_grp), "group", 0)
        pair_dirs = pair_order(directions, far_dirs, parity)
        pair_decay = pair_order(decay_grp, far_decay, parity)
        if "weight" not in stored:
            stored["weight"] = slot_weights(owner_hot, pair_decay, log_weight, page_fill)
        source_rows = value_cache if with_values else key_cache
        summed = slot_terms(key_cache, source_rows, owner_hot, stored["weight"], pair_dirs)
        mine = jnp.where(parity == 0, summed[:group_rows], summed[group_rows:])
        theirs = jnp.where(parity == 0, summed[group_rows:], summed[:group_rows])
        returned = partner(theirs, "group", 0)
        return mine + returned

    def reduce_home(vectors, with_values):
        directions, decay_grp = (
            lax.all_gather(vectors, "shard", axis=0, tiled=True),
            lax.all_gather(decay_home, "shard", axis=0, tiled=True),
        )
        return lax.psum_scatter(
            cache_pass(directions, decay_grp, with_values), "shard", scatter_dimension=0, tiled=True
        )

    found = conjugate(query_home, key_home, value_home, strength_home, ridge_term, reduce_home)
    retrieved = found.reshape(req_rows, width_all).astype(jnp.bfloat16)
    columns = lax.all_to_all(retrieved, "shard", split_axis=1, concat_axis=0, tiled=True)
    attended = lax.psum_scatter(
        jnp.dot(columns, out_weight, preferred_element_type=jnp.float32),
        "shard",
        scatter_dimension=0,
        tiled=True,
    )
    mid_rows = (tokens.astype(jnp.float32) + attended).astype(jnp.bfloat16)
    mlp_in = scaled_norm(mid_rows, mlp_gain)
    piece_rows = lax.all_gather(mlp_in, "shard", axis=0, tiled=True)
    gate_part = jnp.dot(piece_rows, gate_weight, preferred_element_type=jnp.float32)
    up_part = jnp.dot(piece_rows, up_weight, preferred_element_type=jnp.float32)
    hidden_rows = (jax.nn.silu(gate_part) * up_part).astype(jnp.bfloat16)
    down_part = lax.psum_scatter(
        jnp.dot(hidden_rows, down_weight, preferred_element_type=jnp.float32),
        "shard",
        scatter_dimension=0,
        tiled=True,
    )
    layer_out = (mid_rows.astype(jnp.float32) + down_part).astype(jnp.bfloat16)
    return (retrieved, layer_out)


TILE = 8
MASKED = -1e38
PAIR = ("shard", "member")
PARAMS = pltpu.CompilerParams(vmem_limit_bytes=16 * 1024 * 1024)
PAST, TAP, GAIN, BIAS, RIDGE = slice(0, 8), slice(8, 9), slice(9, 10), slice(10, 11), slice(11, 12)
GATES = slice(16, 32)

SEND = ((0, 0), (2, 2), (5, 5), (7, 7), (1, 4), (4, 1), (3, 6), (6, 3))
FROM = tuple((b, a) if a & 2 else (a, b) for a, b in SEND)
EARLY = 4
HELD = 4


def split_pair(value):
    high = value.astype(jnp.bfloat16)
    low = (value - high.astype(jnp.float32)).astype(jnp.bfloat16)
    return high, low


def hot(rows, columns, target_fn):
    row = lax.broadcasted_iota(jnp.int32, (rows, columns), 0)
    column = lax.broadcasted_iota(jnp.int32, (rows, columns), 1)
    return jnp.where(column == target_fn(row), 1.0, 0.0).astype(jnp.bfloat16)


def here():
    return lax.axis_index("shard") * 2 + lax.axis_index("member")


def at_step(table, step, me):
    return me ^ jnp.where((me & 2) == 0, table[step][0], table[step][1])


def silu(value):
    return value / (1.0 + jnp.exp(-value))


def cut_kernel(key_hbm, value_hbm, *refs):
    *piece_refs, stage_ref, sems = refs
    slots = key_hbm.shape[0]
    head_size = piece_refs[0].shape[2]
    me = here()
    loads = [
        pltpu.make_async_copy(source.at[slot], stage_ref.at[part, slot], sems.at[part * slots + slot])
        for part, source in enumerate((key_hbm, value_hbm))
        for slot in range(slots)
    ]
    for load in loads:
        load.start()
    starts = [
        pl.multiple_of(at_step(SEND, step, me) * head_size, head_size)
        for step in range(len(piece_refs))
    ]
    for part in range(2):
        for slot in range(slots):
            place = part * slots + slot
            loads[place].wait()
            for start, piece_ref in zip(starts, piece_refs):
                piece_ref[place] = stage_ref[part, slot, :, pl.ds(start, head_size)]


def pack_kernel(
    tokens_hbm,
    logs_hbm,
    owner_hbm,
    fill_hbm,
    past_hbm,
    tap_hbm,
    gain_hbm,
    gates_hbm,
    bias_hbm,
    ridge_hbm,
    send_ref,
    misc_ref,
    tokens_ref,
    logs_ref,
    owner_ref,
    fill_ref,
    state_ref,
    gates_ref,
    tap_ref,
    gain_ref,
    bias_ref,
    ridge_ref,
    sems,
):
    req_rows, width = tokens_ref.shape
    slots, head_count, page = logs_ref.shape
    copies = [
        pltpu.make_async_copy(source, target, sems.at[place])
        for place, (source, target) in enumerate(
            [
                (owner_hbm, owner_ref),
                (fill_hbm, fill_ref),
                (tokens_hbm, tokens_ref),
                (logs_hbm, logs_ref),
                (past_hbm, state_ref),
                (tap_hbm, tap_ref),
                (gain_hbm, gain_ref),
                (gates_hbm, gates_ref),
                (bias_hbm, bias_ref),
                (ridge_hbm, ridge_ref),
            ]
        )
    ]
    for copy in copies:
        copy.start()
    for copy in copies:
        copy.wait()

    tokens = tokens_ref[...].astype(jnp.float32)
    rows = [
        tokens[row : row + 1, first : first + page]
        for row in range(req_rows)
        for first in range(0, width, page)
    ]
    tile = jnp.concatenate(rows, axis=0).astype(jnp.bfloat16)
    packed = tile.shape[0] + TILE
    spot = lax.broadcasted_iota(jnp.int32, (head_count, page), 1)
    logs = []
    lane = lax.broadcasted_iota(jnp.int32, (1, page), 1)
    owners = jnp.zeros((1, page), jnp.float32)
    for slot in range(slots):
        rows = logs_ref[slot].astype(jnp.float32)
        logs.append(jnp.where(spot < fill_ref[slot], rows, MASKED))
        owners = jnp.where(lane == slot, owner_ref[slot].astype(jnp.float32), owners)
    rest = jnp.zeros((TILE - slots - 1, page), jnp.float32)
    for head in range(head_count):
        rows = [log[head : head + 1, :] for log in logs]
        side = jnp.concatenate([*rows, owners, rest], axis=0).astype(jnp.bfloat16)
        send_ref[head * packed : head * packed + tile.shape[0], :] = tile
        send_ref[head * packed + tile.shape[0] : (head + 1) * packed, :] = side

    past = tap_ref[0:1, :] * state_ref[0].astype(jnp.float32)
    past = past + tap_ref[1:2, :] * state_ref[1].astype(jnp.float32)
    past = past + tap_ref[2:3, :] * state_ref[2].astype(jnp.float32)
    columns = past.shape[1]
    misc_ref[PAST, :columns] = past
    misc_ref[TAP, :columns] = tap_ref[3:4, :]
    misc_ref[GAIN, :] = gain_ref[...]
    misc_ref[BIAS, : 2 * head_count] = bias_ref[...]
    ridges = jnp.zeros((1, page), jnp.float32)
    for head in range(head_count):
        ridges = jnp.where(lane == head, ridge_ref[head], ridges)
    misc_ref[RIDGE, :page] = ridges
    misc_ref[GATES, :] = gates_ref[...].astype(jnp.float32)


def project_kernel(
    shards,
    req_rows,
    slots,
    head_count,
    pack_ref,
    misc_ref,
    qkv_hbm,
    send_ref,
    tokens_ref,
    weight_ref,
    owner_ref,
    strength_ref,
    mixed_ref,
    qkv_ref,
    sems,
):
    chunk = qkv_ref.shape[0] // sems.shape[0]
    loads = [
        pltpu.make_async_copy(
            qkv_hbm.at[pl.ds(part * chunk, chunk)],
            qkv_ref.at[pl.ds(part * chunk, chunk)],
            sems.at[part],
        )
        for part in range(sems.shape[0])
    ]
    for load in loads:
        load.start()
    shard = lax.axis_index("shard")
    member = lax.axis_index("member")
    head = here()
    group_rows = shards * req_rows
    pair_rows = 2 * group_rows
    width = misc_ref.shape[1]
    columns = qkv_ref.shape[1]
    page = weight_ref.shape[1]
    head_size = send_ref.shape[1]
    blocks = columns // head_size
    parts = width // page
    packed = pack_ref.shape[0]
    tall = packed // (2 * shards)

    def rows_of(first, count):
        def home_of(row):
            request = row % count + first
            x = request // group_rows
            s = (request % group_rows) // req_rows
            return (s * 2 + x) * tall + request % req_rows * parts + row // count

        picked = jnp.dot(
            hot(count * parts, packed, home_of), pack_ref[...], preferred_element_type=jnp.float32
        )
        return jnp.concatenate(
            [picked[part * count : (part + 1) * count] for part in range(parts)], axis=1
        )

    own_tokens = rows_of(member * group_rows, group_rows)
    tokens_ref[...] = own_tokens
    own = scaled_norm(own_tokens, misc_ref[GAIN, :])
    normed = scaled_norm(rows_of(0, pair_rows), misc_ref[GAIN, :])
    raw = lax.dot_general(
        normed,
        misc_ref[GATES, :].astype(jnp.bfloat16),
        (((1,), (1,)), ((), ())),
        preferred_element_type=jnp.float32,
    )
    gate_vals = 1.0 / (1.0 + jnp.exp(-(raw + misc_ref[BIAS, : 2 * head_count])))
    column = lax.broadcasted_iota(jnp.int32, gate_vals.shape, 1)
    decay = jnp.sum(jnp.where(column == head, gate_vals, 0.0), axis=1, keepdims=True)
    strength = jnp.sum(
        jnp.where(column == head + head_count, gate_vals, 0.0), axis=1, keepdims=True
    )
    strength_ref[:pair_rows, :] = jnp.broadcast_to(strength, (pair_rows, head_size))
    ridges = misc_ref[RIDGE, :page]
    spot = lax.broadcasted_iota(jnp.int32, ridges.shape, 1)
    ridge = jnp.sum(jnp.where(spot == head, ridges, 0.0), axis=1, keepdims=True)
    strength_ref[pair_rows:, :] = jnp.broadcast_to(ridge, (TILE, head_size))

    all_slots = 2 * shards * slots
    side = tall - TILE
    pick_slot = hot(all_slots, packed, lambda row: (row // slots) * tall + side + row % slots)
    logs = jnp.dot(pick_slot, pack_ref[...], preferred_element_type=jnp.float32)
    pick_owner = hot(all_slots, packed, lambda row: (row // slots) * tall + side + slots)
    owners = jnp.dot(pick_owner, pack_ref[...], preferred_element_type=jnp.float32)
    at_slot = hot(all_slots, page, lambda row: row % slots).astype(jnp.float32)
    owner = jnp.sum(at_slot * owners, axis=1, keepdims=True).astype(jnp.int32)
    owner_ref[...] = jnp.broadcast_to(owner, owner_ref.shape)
    request = lax.broadcasted_iota(jnp.int32, (all_slots, pair_rows), 1)
    owner_hot = jnp.where(request == owner, 1.0, 0.0)
    wide_decay = jnp.broadcast_to(decay, (pair_rows, page))
    slot_decay = jnp.dot(
        owner_hot, wide_decay, precision=precise, preferred_element_type=jnp.float32
    )
    weight_ref[...] = slot_decay * jnp.exp(logs)

    for load in loads:
        load.wait()
    fresh = jnp.dot(own, qkv_ref[...], preferred_element_type=jnp.float32)
    before = misc_ref[TAP, :columns] * fresh + misc_ref[PAST, :columns]
    mixed_ref[...] = silu(before)
    for target in range(head_count):
        place = jnp.int32(0)
        for part in range(3):
            local = target + part * head_count - shard * blocks
            place = jnp.where((local >= 0) & (local < blocks), local, place)
        start = pl.multiple_of(place * head_size, head_size)
        send_ref[target * group_rows : (target + 1) * group_rows, :] = mixed_ref[
            :, pl.ds(start, head_size)
        ].astype(jnp.bfloat16)


def add_pieces(first, owner_ref, weight_ref, piece_refs, gram_ref):
    me = here()
    slots = piece_refs[0].shape[0] // 2
    for step, piece_ref in enumerate(piece_refs, first):
        for spot in range(slots):
            slot = at_step(FROM, step, me) * slots + spot
            keys = piece_ref[spot]
            both = jnp.concatenate([keys, piece_ref[slots + spot]], axis=1)
            turned = keys.T.astype(jnp.float32) * weight_ref[pl.ds(slot, 1), :]
            piece = jnp.dot(
                jnp.concatenate(split_pair(turned), axis=1),
                jnp.concatenate([both, both], axis=0),
                preferred_element_type=jnp.float32,
            )
            owner = owner_ref[slot, 0]
            gram_ref[owner] = gram_ref[owner] + piece


def gram_kernel(owner_ref, weight_ref, *refs):
    *piece_refs, gram_ref = refs
    gram_ref[...] = jnp.zeros_like(gram_ref)
    add_pieces(0, owner_ref, weight_ref, piece_refs, gram_ref)


def solve_kernel(
    first, head_count, blocks, owner_ref, weight_ref, mixed_ref, strength_ref, before_ref, *refs
):
    *piece_refs, own_ref, other_ref, gram_ref, rows_ref = refs
    del before_ref
    head = here()
    member = lax.axis_index("member")
    pair_rows, head_size, _ = gram_ref.shape
    add_pieces(first, owner_ref, weight_ref, piece_refs, gram_ref)

    def columns_of(block):
        first = pl.multiple_of(block // blocks * pair_rows, pair_rows)
        return mixed_ref[pl.ds(first, pair_rows), :].astype(jnp.float32)

    query = unit_rows(columns_of(head))
    key_new = unit_rows(columns_of(head + head_count))
    value_new = columns_of(head + 2 * head_count)
    strength = strength_ref[:pair_rows, :]
    ridge = strength_ref[pair_rows : pair_rows + 1, :]

    def image_of(vectors, columns):
        turned = vectors.T
        pieces = []
        for row in range(pair_rows):
            spread = jnp.broadcast_to(turned[:, row : row + 1], (head_size, head_size))
            pieces.append(jnp.sum(gram_ref[row, :, columns] * spread, axis=0, keepdims=True))
        return jnp.concatenate(pieces, axis=0)

    found = jnp.zeros_like(query)
    residual = query
    direction = query
    res_norm = jnp.sum(residual * residual, axis=-1, keepdims=True)
    for iteration in range(ITERS):
        along = jnp.sum(key_new * direction, axis=-1, keepdims=True)
        image = image_of(direction, slice(0, head_size))
        image = image + strength * key_new * along + ridge * direction
        step = res_norm / jnp.sum(direction * image, axis=-1, keepdims=True)
        found = found + step * direction
        residual = residual - step * image
        next_norm = jnp.sum(residual * residual, axis=-1, keepdims=True)
        direction = residual + (next_norm / res_norm) * direction
        res_norm = next_norm

    total = image_of(found, slice(head_size, 2 * head_size))
    total = total + strength * value_new * jnp.sum(key_new * found, axis=-1, keepdims=True)
    rows_ref[...] = total
    half = pair_rows // 2
    mine = pl.multiple_of(member * half, half)
    theirs = pl.multiple_of((1 - member) * half, half)
    own_ref[...] = rows_ref[pl.ds(mine, half), :].astype(jnp.bfloat16)
    other_ref[...] = rows_ref[pl.ds(theirs, half), :].astype(jnp.bfloat16)


def out_kernel(own_ref, come_ref, out_ref, send_ref):
    first = lax.axis_index("member") == 0
    width = out_ref.shape[1]
    own = own_ref[...].astype(jnp.float32)
    come = come_ref[...].astype(jnp.float32)
    heads = jnp.concatenate([jnp.where(first, own, come), jnp.where(first, come, own)], axis=1)
    heads = heads.astype(jnp.bfloat16)
    part = jnp.dot(heads, out_ref[...], preferred_element_type=jnp.float32)
    send_ref[:, :width] = part.astype(jnp.bfloat16)
    send_ref[:, width:] = heads


def home_rows(value, req_rows):
    first = lax.axis_index("shard") * req_rows
    row = lax.broadcasted_iota(jnp.int32, value.shape, 0)
    picked = [
        jnp.sum(jnp.where(row == first + i, value, 0.0), axis=0, keepdims=True)
        for i in range(req_rows)
    ]
    return jnp.concatenate(picked, axis=0)


def mlp_kernel(
    shards,
    tokens_ref,
    gain_ref,
    gate_ref,
    up_ref,
    down_ref,
    *refs,
):
    part_refs, refs = refs[:shards], refs[shards:]
    mid_ref, retrieved_ref, *send_refs, down_scr, heads_ref = refs
    shard = lax.axis_index("shard")
    group_rows, width = tokens_ref.shape
    req_rows = mid_ref.shape[0]
    span = part_refs[0].shape[1] - width
    attended = part_refs[0][:, :width].astype(jnp.float32)
    for part_ref in part_refs[1:]:
        attended += part_ref[:, :width].astype(jnp.float32)
    mid_rows = (tokens_ref[...] + attended).astype(jnp.bfloat16)
    mlp_in = scaled_norm(mid_rows, gain_ref[...])
    contract = (((1,), (1,)), ((), ()))
    gate_part = lax.dot_general(
        mlp_in, gate_ref[...], contract, preferred_element_type=jnp.float32
    )
    up_part = lax.dot_general(mlp_in, up_ref[...], contract, preferred_element_type=jnp.float32)
    hidden = (silu(gate_part) * up_part).astype(jnp.bfloat16)
    down = jnp.dot(hidden, down_ref[...], preferred_element_type=jnp.float32)
    down_scr[...] = down.reshape(down_scr.shape)
    rows = send_refs[0].shape[0]
    for apart, send_ref in enumerate(send_refs):
        send_ref[...] = down_scr[pl.ds(pl.multiple_of((shard ^ apart) * rows, rows), rows), :]
    mid_ref[...] = home_rows(mid_rows.astype(jnp.float32), mid_ref.shape[0])
    for apart, part_ref in enumerate(part_refs):
        first = pl.multiple_of((shard ^ apart) * span, span)
        heads_ref[:, pl.ds(first, span)] = home_rows(
            part_ref[:, width:].astype(jnp.float32), req_rows
        )
    retrieved_ref[...] = heads_ref[...].astype(jnp.bfloat16)


def finish_kernel(mid_ref, *refs):
    *down_refs, layer_ref = refs
    total = down_refs[0][...]
    for down_ref in down_refs[1:]:
        total = total + down_ref[...]
    layer_ref[...] = (mid_ref[...] + total.reshape(mid_ref.shape)).astype(jnp.bfloat16)


def head_body(
    tokens,
    norm_gain,
    qkv_weight,
    conv_weight,
    conv_state,
    mesa_gates,
    mesa_bias,
    ridge_term,
    key_cache,
    value_cache,
    log_weight,
    page_owner,
    page_fill,
    out_weight,
    mlp_gain,
    gate_weight,
    up_weight,
    down_weight,
):
    shards = lax.axis_size("shard")
    devices = 2 * shards
    req_rows, width = tokens.shape
    slots, page, _ = key_cache.shape
    head_count = ridge_term.shape[0]
    head_size = width // head_count
    group_rows = shards * req_rows
    pair_rows = 2 * group_rows
    all_slots = devices * slots
    columns = qkv_weight.shape[1]
    shape = jax.ShapeDtypeStruct
    bf16, f32 = jnp.bfloat16, jnp.float32

    def exchange(value, axes):
        return lax.all_to_all(value, axes, split_axis=0, concat_axis=0, tiled=True)

    def spot(number):
        return number % 2 * shards + number // 2

    hbm = pl.BlockSpec(memory_space=pltpu.HBM)
    past_rows = jnp.transpose(conv_state, (1, 0, 2))
    gates = mesa_gates.T

    def pinned(*values):
        return [pltpu.with_memory_space_constraint(value, pltpu.HBM) for value in values]

    pieces = pl.pallas_call(
        cut_kernel,
        out_shape=(shape((2 * slots, page, head_size), bf16),) * devices,
        in_specs=[hbm] * 2,
        out_specs=(VMEM,) * devices,
        scratch_shapes=[
            pltpu.VMEM((2, *key_cache.shape), bf16),
            pltpu.SemaphoreType.DMA((2 * slots,)),
        ],
        compiler_params=PARAMS,
        name="cut",
    )(*pinned(key_cache, value_cache))

    def move(step):
        pairs = [
            (spot(source), spot(source ^ SEND[step][source >> 1 & 1])) for source in range(devices)
        ]
        return lax.ppermute(pieces[step], ("member", "shard"), pairs)

    moved = [pieces[0], move(1)]
    tokens, pieces = lax.optimization_barrier((tokens, pieces))
    pack, misc = pl.pallas_call(
        pack_kernel,
        out_shape=(
            shape((devices * (req_rows * width // page + TILE), page), bf16),
            shape((GATES.stop, width), f32),
        ),
        in_specs=[hbm] * 10,
        out_specs=(VMEM,) * 2,
        scratch_shapes=[
            pltpu.VMEM(tokens.shape, bf16),
            pltpu.VMEM(log_weight.shape, bf16),
            pltpu.SMEM(page_owner.shape, jnp.int32),
            pltpu.SMEM(page_fill.shape, jnp.int32),
            pltpu.VMEM(past_rows.shape, bf16),
            pltpu.VMEM(gates.shape, bf16),
            pltpu.VMEM(conv_weight.shape, f32),
            pltpu.VMEM((1, width), f32),
            pltpu.VMEM((1, 2 * head_count), f32),
            pltpu.SMEM(ridge_term.shape, f32),
            pltpu.SemaphoreType.DMA((10,)),
        ],
        compiler_params=PARAMS,
        name="pack",
    )(
        *pinned(
            tokens,
            log_weight,
            page_owner,
            page_fill,
            past_rows,
            conv_weight,
            norm_gain[None, :],
            gates,
            mesa_bias[None, :],
            ridge_term,
        )
    )
    pieces, pack, misc = lax.optimization_barrier((pieces, pack, misc))
    moved += [move(step) for step in range(2, 1 + EARLY)]
    packs = exchange(pack, PAIR)

    pieces, packs = lax.optimization_barrier((pieces, packs))
    moved += [move(step) for step in range(1 + EARLY, devices)]

    mixed, own_tokens, weight, owner, strength = pl.pallas_call(
        functools.partial(project_kernel, shards, req_rows, slots, head_count),
        out_shape=(
            shape((devices * group_rows, head_size), bf16),
            shape((group_rows, width), f32),
            shape((all_slots, page), f32),
            shape((all_slots, page), jnp.int32),
            shape((pair_rows + TILE, head_size), f32),
        ),
        in_specs=[VMEM] * 2 + [hbm],
        out_specs=(VMEM,) * 5,
        scratch_shapes=[
            pltpu.VMEM((group_rows, columns), f32),
            pltpu.VMEM(qkv_weight.shape, bf16),
            pltpu.SemaphoreType.DMA((4,)),
        ],
        compiler_params=PARAMS,
        name="project",
    )(packs, misc, *pinned(qkv_weight))

    held = HELD
    gram = pl.pallas_call(
        gram_kernel,
        out_shape=shape((pair_rows, head_size, 2 * head_size), f32),
        in_specs=[SMEM] + [VMEM] * (1 + held),
        out_specs=VMEM,
        compiler_params=PARAMS,
        name="gram",
    )(owner, weight, *moved[:held])
    mixed, gram = lax.optimization_barrier((mixed, gram))
    all_mixed = exchange(mixed, PAIR)
    all_mixed, owner, weight, gram = lax.optimization_barrier((all_mixed, owner, weight, gram))

    own_head, other_head, _ = pl.pallas_call(
        functools.partial(solve_kernel, held, head_count, columns // head_size),
        out_shape=(
            shape((group_rows, head_size), bf16),
            shape((group_rows, head_size), bf16),
            pltpu.VMEM(gram.shape, f32),
        ),
        in_specs=[SMEM] + [VMEM] * (4 + devices - held),
        out_specs=(VMEM,) * 3,
        input_output_aliases={4: 2},
        scratch_shapes=[pltpu.VMEM((pair_rows, head_size), f32)],
        compiler_params=PARAMS,
        name="solve",
    )(
        owner,
        weight,
        all_mixed,
        strength,
        pltpu.with_memory_space_constraint(gram, pltpu.VMEM),
        *moved[held:],
    )
    part = pl.pallas_call(
        out_kernel,
        out_shape=shape((group_rows, width + 2 * head_size), bf16),
        in_specs=[VMEM] * 3,
        out_specs=VMEM,
        compiler_params=PARAMS,
        name="out",
    )(own_head, lax.ppermute(other_head, "member", [(0, 1), (1, 0)]), out_weight)

    def over_shards(sent):
        arrived = [sent[0]]
        for apart in range(1, shards):
            pairs = [(source, source ^ apart) for source in range(shards)]
            arrived.append(lax.ppermute(sent[apart], "shard", pairs))
        return arrived

    parts = over_shards([part] * shards)

    mid_home, retrieved, *down = pl.pallas_call(
        functools.partial(mlp_kernel, shards),
        out_shape=(
            shape((req_rows, width), f32),
            shape((req_rows, width), bf16),
        )
        + (shape((req_rows * head_count, head_size), f32),) * shards,
        in_specs=[VMEM] * (5 + shards),
        out_specs=(VMEM,) * (2 + shards),
        scratch_shapes=[
            pltpu.VMEM((group_rows * head_count, head_size), f32),
            pltpu.VMEM((req_rows, width), f32),
        ],
        compiler_params=PARAMS,
        name="mlp",
    )(
        own_tokens,
        mlp_gain[None, :],
        gate_weight.T,
        up_weight.T,
        down_weight,
        *parts,
    )
    layer_out = pl.pallas_call(
        finish_kernel,
        out_shape=shape((req_rows, width), bf16),
        in_specs=[VMEM] * (1 + shards),
        out_specs=VMEM,
        compiler_params=PARAMS,
        name="finish",
    )(mid_home, *over_shards(down))
    return (retrieved, layer_out)


def specs(group):
    rows = P((*group, "shard"))
    return (
        (
            rows,
            P(),
            P(None, "shard"),
            P(None, "shard"),
            P(group, None, "shard"),
            P(),
            P(),
            P(),
            rows,
            rows,
            rows,
            rows,
            rows,
            P("shard", None),
            P(),
            P(None, "shard"),
            P(None, "shard"),
            P("shard", None),
        ),
        (rows, rows),
    )


def solution(mesh):
    groups, shards = mesh.devices.shape

    def run(*args):
        head_count = args[7].shape[0]
        if 2 * shards == head_count == len(SEND):
            axes = ("pair", "member", "shard")
            used = Mesh(mesh.devices.reshape(groups // 2, 2, shards), axes)
            body, group = head_body, ("pair", "member")
        else:
            used, body, group = mesh, spread_body, ("group",)
        in_specs, out_specs = specs(group)
        return jax.shard_map(
            body, mesh=used, in_specs=in_specs, out_specs=out_specs, check_vma=False
        )(*args)

    return run
```

```python
import functools

import jax
import jax.numpy as jnp
from jax import lax
from jax.experimental import pallas as pl
from jax.experimental.pallas import tpu as pltpu
from jax.sharding import Mesh
from jax.sharding import PartitionSpec as P

ITERS = 4


precise = lax.Precision.HIGHEST

VMEM = pl.BlockSpec(memory_space=pltpu.VMEM)
SMEM = pl.BlockSpec(memory_space=pltpu.SMEM)


def partner(value, axis, apart):
    mask = 2**apart
    pairs = [(source, source ^ mask) for source in range(lax.axis_size(axis))]
    return lax.ppermute(value, axis, pairs)


def scaled_norm(row_vals, gain_vec):
    wide_rows = row_vals.astype(jnp.float32)
    factor = lax.rsqrt(jnp.mean(wide_rows * wide_rows, axis=-1, keepdims=True) + 1e-05)
    return (wide_rows * factor * gain_vec).astype(jnp.bfloat16)


def unit_rows(vectors):
    return vectors * lax.rsqrt(jnp.sum(vectors * vectors, axis=-1, keepdims=True) + 1e-06)


def slot_weights(owner_hot, decay_rows, log_weight, page_fill):
    page_len = log_weight.shape[2]
    slot_decay = jnp.dot(owner_hot, decay_rows, precision=precise)
    live_mask = (jnp.arange(page_len)[None, :] < page_fill[:, None]).astype(jnp.float32)
    return slot_decay[:, :, None] * jnp.exp(log_weight.astype(jnp.float32)) * live_mask[:, None, :]


def slot_terms(key_rows, source_rows, owner_hot, slot_weight, directions):
    slot_count, page_len, width_all = key_rows.shape
    head_count = slot_weight.shape[1]
    head_size = width_all // head_count
    member_count = owner_hot.shape[1]
    slot_dir = jnp.dot(owner_hot, directions.reshape(member_count, width_all), precision=precise)
    slot_dir = slot_dir.reshape(slot_count, head_count, head_size)
    key_wide = key_rows.astype(jnp.float32).reshape(slot_count, page_len, head_count, head_size)
    scores = jnp.einsum("sthd,shd->sht", key_wide, slot_dir, precision=precise)
    source_wide = source_rows.astype(jnp.float32).reshape(
        slot_count, page_len, head_count, head_size
    )
    contribution = jnp.einsum("sht,sthd->shd", slot_weight * scores, source_wide, precision=precise)
    summed = jnp.dot(owner_hot.T, contribution.reshape(slot_count, width_all), precision=precise)
    return summed.reshape(member_count, head_count, head_size)


def new_term(vectors, source_rows, strength_rows, key_new):
    return (
        strength_rows[:, :, None] * source_rows * jnp.sum(key_new * vectors, axis=-1, keepdims=True)
    )


def conjugate(query_rows, key_new, value_new, strength_rows, ridge_term, reduce_fn):
    solution = jnp.zeros_like(query_rows)
    residual = query_rows
    direction = query_rows
    res_norm = jnp.sum(residual * residual, axis=-1)
    for iteration in range(ITERS):
        image_vec = (
            reduce_fn(direction, False)
            + new_term(direction, key_new, strength_rows, key_new)
            + ridge_term[None, :, None] * direction
        )
        step_size = res_norm / jnp.sum(direction * image_vec, axis=-1)
        solution = solution + step_size[:, :, None] * direction
        residual = residual - step_size[:, :, None] * image_vec
        next_norm = jnp.sum(residual * residual, axis=-1)
        direction = residual + (next_norm / res_norm)[:, :, None] * direction
        res_norm = next_norm
    return reduce_fn(solution, True) + new_term(solution, value_new, strength_rows, key_new)


def pair_order(mine, theirs, parity):
    first = jnp.where(parity == 0, mine, theirs)
    second = jnp.where(parity == 0, theirs, mine)
    return jnp.concatenate([first, second], axis=0)


def spread_body(
    tokens,
    norm_gain,
    qkv_weight,
    conv_weight,
    conv_state,
    mesa_gates,
    mesa_bias,
    ridge_term,
    key_cache,
    value_cache,
    log_weight,
    page_owner,
    page_fill,
    out_weight,
    mlp_gain,
    gate_weight,
    up_weight,
    down_weight,
):
    req_rows = tokens.shape[0]
    group_rows = req_rows * lax.axis_size("shard")
    head_count = ridge_term.shape[0]
    width_all = key_cache.shape[2]
    head_size = width_all // head_count
    parity = lax.axis_index("group") % 2
    normed = scaled_norm(tokens, norm_gain)
    fresh_proj = jnp.dot(
        lax.all_gather(normed, "shard", axis=0, tiled=True),
        qkv_weight,
        preferred_element_type=jnp.float32,
    )
    past_rows = conv_state.astype(jnp.float32)
    pre_conv = (
        conv_weight[3] * fresh_proj
        + conv_weight[0] * past_rows[:, 0]
        + conv_weight[1] * past_rows[:, 1]
        + conv_weight[2] * past_rows[:, 2]
    )
    mixed_cols = jax.nn.silu(pre_conv).astype(jnp.bfloat16)
    home_rows = lax.all_to_all(mixed_cols, "shard", split_axis=0, concat_axis=1, tiled=True)
    split_rows = home_rows.astype(jnp.float32).reshape(req_rows, 3, head_count, head_size)
    query_home = unit_rows(split_rows[:, 0])
    key_home = unit_rows(split_rows[:, 1])
    value_home = split_rows[:, 2]
    gate_vals = jax.nn.sigmoid(
        jnp.dot(normed, mesa_gates, preferred_element_type=jnp.float32) + mesa_bias
    )
    decay_home = gate_vals[:, :head_count]
    strength_home = gate_vals[:, head_count:]
    owner_hot = (page_owner[:, None] == jnp.arange(2 * group_rows)[None, :]).astype(jnp.float32)
    stored = {}

    def cache_pass(directions, decay_grp, with_values):
        far_dirs, far_decay = partner((directions, decay_grp), "group", 0)
        pair_dirs = pair_order(directions, far_dirs, parity)
        pair_decay = pair_order(decay_grp, far_decay, parity)
        if "weight" not in stored:
            stored["weight"] = slot_weights(owner_hot, pair_decay, log_weight, page_fill)
        source_rows = value_cache if with_values else key_cache
        summed = slot_terms(key_cache, source_rows, owner_hot, stored["weight"], pair_dirs)
        mine = jnp.where(parity == 0, summed[:group_rows], summed[group_rows:])
        theirs = jnp.where(parity == 0, summed[group_rows:], summed[:group_rows])
        returned = partner(theirs, "group", 0)
        return mine + returned

    def reduce_home(vectors, with_values):
        directions, decay_grp = (
            lax.all_gather(vectors, "shard", axis=0, tiled=True),
            lax.all_gather(decay_home, "shard", axis=0, tiled=True),
        )
        return lax.psum_scatter(
            cache_pass(directions, decay_grp, with_values), "shard", scatter_dimension=0, tiled=True
        )

    found = conjugate(query_home, key_home, value_home, strength_home, ridge_term, reduce_home)
    retrieved = found.reshape(req_rows, width_all).astype(jnp.bfloat16)
    columns = lax.all_to_all(retrieved, "shard", split_axis=1, concat_axis=0, tiled=True)
    attended = lax.psum_scatter(
        jnp.dot(columns, out_weight, preferred_element_type=jnp.float32),
        "shard",
        scatter_dimension=0,
        tiled=True,
    )
    mid_rows = (tokens.astype(jnp.float32) + attended).astype(jnp.bfloat16)
    mlp_in = scaled_norm(mid_rows, mlp_gain)
    piece_rows = lax.all_gather(mlp_in, "shard", axis=0, tiled=True)
    gate_part = jnp.dot(piece_rows, gate_weight, preferred_element_type=jnp.float32)
    up_part = jnp.dot(piece_rows, up_weight, preferred_element_type=jnp.float32)
    hidden_rows = (jax.nn.silu(gate_part) * up_part).astype(jnp.bfloat16)
    down_part = lax.psum_scatter(
        jnp.dot(hidden_rows, down_weight, preferred_element_type=jnp.float32),
        "shard",
        scatter_dimension=0,
        tiled=True,
    )
    layer_out = (mid_rows.astype(jnp.float32) + down_part).astype(jnp.bfloat16)
    return (retrieved, layer_out)


TILE = 8
MASKED = -1e38
PAIR = ("shard", "member")
PARAMS = pltpu.CompilerParams(vmem_limit_bytes=16 * 1024 * 1024)
PAST, TAP, GAIN, BIAS, RIDGE = slice(0, 8), slice(8, 9), slice(9, 10), slice(10, 11), slice(11, 12)
GATES = slice(16, 32)

SEND = ((0, 0), (5, 5), (2, 2), (7, 7), (1, 4), (4, 1), (3, 6), (6, 3))
FROM = tuple((b, a) if a & 2 else (a, b) for a, b in SEND)
EARLY = 4
HELD = 4


def split_pair(value):
    high = value.astype(jnp.bfloat16)
    low = (value - high.astype(jnp.float32)).astype(jnp.bfloat16)
    return high, low


def hot(rows, columns, target_fn):
    row = lax.broadcasted_iota(jnp.int32, (rows, columns), 0)
    column = lax.broadcasted_iota(jnp.int32, (rows, columns), 1)
    return jnp.where(column == target_fn(row), 1.0, 0.0).astype(jnp.bfloat16)


def here():
    return lax.axis_index("shard") * 2 + lax.axis_index("member")


def at_step(table, step, me):
    return me ^ jnp.where((me & 2) == 0, table[step][0], table[step][1])


def silu(value):
    return value / (1.0 + jnp.exp(-value))


def cut_kernel(key_hbm, value_hbm, *refs):
    *piece_refs, stage_ref, sems = refs
    slots = key_hbm.shape[0]
    head_size = piece_refs[0].shape[2]
    me = here()
    loads = [
        pltpu.make_async_copy(source.at[slot], stage_ref.at[part, slot], sems.at[part * slots + slot])
        for part, source in enumerate((key_hbm, value_hbm))
        for slot in range(slots)
    ]
    for load in loads:
        load.start()
    starts = [
        pl.multiple_of(at_step(SEND, step, me) * head_size, head_size)
        for step in range(len(piece_refs))
    ]
    for part in range(2):
        for slot in range(slots):
            place = part * slots + slot
            loads[place].wait()
            for start, piece_ref in zip(starts, piece_refs):
                piece_ref[place] = stage_ref[part, slot, :, pl.ds(start, head_size)]


def pack_kernel(
    tokens_hbm,
    logs_hbm,
    owner_hbm,
    fill_hbm,
    past_hbm,
    tap_hbm,
    gain_hbm,
    gates_hbm,
    bias_hbm,
    ridge_hbm,
    send_ref,
    misc_ref,
    tokens_ref,
    logs_ref,
    owner_ref,
    fill_ref,
    state_ref,
    gates_ref,
    tap_ref,
    gain_ref,
    bias_ref,
    ridge_ref,
    sems,
):
    req_rows, width = tokens_ref.shape
    slots, head_count, page = logs_ref.shape
    copies = [
        pltpu.make_async_copy(source, target, sems.at[place])
        for place, (source, target) in enumerate(
            [
                (owner_hbm, owner_ref),
                (fill_hbm, fill_ref),
                (tokens_hbm, tokens_ref),
                (logs_hbm, logs_ref),
                (past_hbm, state_ref),
                (tap_hbm, tap_ref),
                (gain_hbm, gain_ref),
                (gates_hbm, gates_ref),
                (bias_hbm, bias_ref),
                (ridge_hbm, ridge_ref),
            ]
        )
    ]
    for copy in copies:
        copy.start()
    for copy in copies:
        copy.wait()

    tokens = tokens_ref[...].astype(jnp.float32)
    rows = [
        tokens[row : row + 1, first : first + page]
        for row in range(req_rows)
        for first in range(0, width, page)
    ]
    tile = jnp.concatenate(rows, axis=0).astype(jnp.bfloat16)
    packed = tile.shape[0] + TILE
    spot = lax.broadcasted_iota(jnp.int32, (head_count, page), 1)
    logs = []
    lane = lax.broadcasted_iota(jnp.int32, (1, page), 1)
    owners = jnp.zeros((1, page), jnp.float32)
    for slot in range(slots):
        rows = logs_ref[slot].astype(jnp.float32)
        logs.append(jnp.where(spot < fill_ref[slot], rows, MASKED))
        owners = jnp.where(lane == slot, owner_ref[slot].astype(jnp.float32), owners)
    rest = jnp.zeros((TILE - slots - 1, page), jnp.float32)
    for head in range(head_count):
        rows = [log[head : head + 1, :] for log in logs]
        side = jnp.concatenate([*rows, owners, rest], axis=0).astype(jnp.bfloat16)
        send_ref[head * packed : head * packed + tile.shape[0], :] = tile
        send_ref[head * packed + tile.shape[0] : (head + 1) * packed, :] = side

    past = tap_ref[0:1, :] * state_ref[0].astype(jnp.float32)
    past = past + tap_ref[1:2, :] * state_ref[1].astype(jnp.float32)
    past = past + tap_ref[2:3, :] * state_ref[2].astype(jnp.float32)
    columns = past.shape[1]
    misc_ref[PAST, :columns] = past
    misc_ref[TAP, :columns] = tap_ref[3:4, :]
    misc_ref[GAIN, :] = gain_ref[...]
    misc_ref[BIAS, : 2 * head_count] = bias_ref[...]
    ridges = jnp.zeros((1, page), jnp.float32)
    for head in range(head_count):
        ridges = jnp.where(lane == head, ridge_ref[head], ridges)
    misc_ref[RIDGE, :page] = ridges
    misc_ref[GATES, :] = gates_ref[...].astype(jnp.float32)


def project_kernel(
    shards,
    req_rows,
    slots,
    head_count,
    pack_ref,
    misc_ref,
    qkv_hbm,
    send_ref,
    tokens_ref,
    weight_ref,
    owner_ref,
    strength_ref,
    mixed_ref,
    qkv_ref,
    sems,
):
    chunk = qkv_ref.shape[0] // sems.shape[0]
    loads = [
        pltpu.make_async_copy(
            qkv_hbm.at[pl.ds(part * chunk, chunk)],
            qkv_ref.at[pl.ds(part * chunk, chunk)],
            sems.at[part],
        )
        for part in range(sems.shape[0])
    ]
    for load in loads:
        load.start()
    shard = lax.axis_index("shard")
    member = lax.axis_index("member")
    head = here()
    group_rows = shards * req_rows
    pair_rows = 2 * group_rows
    width = misc_ref.shape[1]
    columns = qkv_ref.shape[1]
    page = weight_ref.shape[1]
    head_size = send_ref.shape[1]
    blocks = columns // head_size
    parts = width // page
    packed = pack_ref.shape[0]
    tall = packed // (2 * shards)

    def rows_of(first, count):
        def home_of(row):
            request = row % count + first
            x = request // group_rows
            s = (request % group_rows) // req_rows
            return (s * 2 + x) * tall + request % req_rows * parts + row // count

        picked = jnp.dot(
            hot(count * parts, packed, home_of), pack_ref[...], preferred_element_type=jnp.float32
        )
        return jnp.concatenate(
            [picked[part * count : (part + 1) * count] for part in range(parts)], axis=1
        )

    own_tokens = rows_of(member * group_rows, group_rows)
    tokens_ref[...] = own_tokens
    own = scaled_norm(own_tokens, misc_ref[GAIN, :])
    normed = scaled_norm(rows_of(0, pair_rows), misc_ref[GAIN, :])
    raw = lax.dot_general(
        normed,
        misc_ref[GATES, :].astype(jnp.bfloat16),
        (((1,), (1,)), ((), ())),
        preferred_element_type=jnp.float32,
    )
    gate_vals = 1.0 / (1.0 + jnp.exp(-(raw + misc_ref[BIAS, : 2 * head_count])))
    column = lax.broadcasted_iota(jnp.int32, gate_vals.shape, 1)
    decay = jnp.sum(jnp.where(column == head, gate_vals, 0.0), axis=1, keepdims=True)
    strength = jnp.sum(
        jnp.where(column == head + head_count, gate_vals, 0.0), axis=1, keepdims=True
    )
    strength_ref[:pair_rows, :] = jnp.broadcast_to(strength, (pair_rows, head_size))
    ridges = misc_ref[RIDGE, :page]
    spot = lax.broadcasted_iota(jnp.int32, ridges.shape, 1)
    ridge = jnp.sum(jnp.where(spot == head, ridges, 0.0), axis=1, keepdims=True)
    strength_ref[pair_rows:, :] = jnp.broadcast_to(ridge, (TILE, head_size))

    all_slots = 2 * shards * slots
    side = tall - TILE
    pick_slot = hot(all_slots, packed, lambda row: (row // slots) * tall + side + row % slots)
    logs = jnp.dot(pick_slot, pack_ref[...], preferred_element_type=jnp.float32)
    pick_owner = hot(all_slots, packed, lambda row: (row // slots) * tall + side + slots)
    owners = jnp.dot(pick_owner, pack_ref[...], preferred_element_type=jnp.float32)
    at_slot = hot(all_slots, page, lambda row: row % slots).astype(jnp.float32)
    owner = jnp.sum(at_slot * owners, axis=1, keepdims=True).astype(jnp.int32)
    owner_ref[...] = jnp.broadcast_to(owner, owner_ref.shape)
    request = lax.broadcasted_iota(jnp.int32, (all_slots, pair_rows), 1)
    owner_hot = jnp.where(request == owner, 1.0, 0.0)
    wide_decay = jnp.broadcast_to(decay, (pair_rows, page))
    slot_decay = jnp.dot(
        owner_hot, wide_decay, precision=precise, preferred_element_type=jnp.float32
    )
    weight_ref[...] = slot_decay * jnp.exp(logs)

    for load in loads:
        load.wait()
    fresh = jnp.dot(own, qkv_ref[...], preferred_element_type=jnp.float32)
    before = misc_ref[TAP, :columns] * fresh + misc_ref[PAST, :columns]
    mixed_ref[...] = silu(before)
    for target in range(head_count):
        place = jnp.int32(0)
        for part in range(3):
            local = target + part * head_count - shard * blocks
            place = jnp.where((local >= 0) & (local < blocks), local, place)
        start = pl.multiple_of(place * head_size, head_size)
        send_ref[target * group_rows : (target + 1) * group_rows, :] = mixed_ref[
            :, pl.ds(start, head_size)
        ].astype(jnp.bfloat16)


def add_pieces(first, owner_ref, weight_ref, piece_refs, gram_ref):
    me = here()
    slots = piece_refs[0].shape[0] // 2
    for step, piece_ref in enumerate(piece_refs, first):
        for spot in range(slots):
            slot = at_step(FROM, step, me) * slots + spot
            keys = piece_ref[spot]
            both = jnp.concatenate([keys, piece_ref[slots + spot]], axis=1)
            turned = keys.T.astype(jnp.float32) * weight_ref[pl.ds(slot, 1), :]
            piece = jnp.dot(
                jnp.concatenate(split_pair(turned), axis=1),
                jnp.concatenate([both, both], axis=0),
                preferred_element_type=jnp.float32,
            )
            owner = owner_ref[slot, 0]
            gram_ref[owner] = gram_ref[owner] + piece


def gram_kernel(owner_ref, weight_ref, *refs):
    *piece_refs, gram_ref = refs
    gram_ref[...] = jnp.zeros_like(gram_ref)
    add_pieces(0, owner_ref, weight_ref, piece_refs, gram_ref)


def solve_kernel(
    first, head_count, blocks, owner_ref, weight_ref, mixed_ref, strength_ref, before_ref, *refs
):
    *piece_refs, own_ref, other_ref, gram_ref, rows_ref = refs
    del before_ref
    head = here()
    member = lax.axis_index("member")
    pair_rows, head_size, _ = gram_ref.shape
    add_pieces(first, owner_ref, weight_ref, piece_refs, gram_ref)

    def columns_of(block):
        first = pl.multiple_of(block // blocks * pair_rows, pair_rows)
        return mixed_ref[pl.ds(first, pair_rows), :].astype(jnp.float32)

    query = unit_rows(columns_of(head))
    key_new = unit_rows(columns_of(head + head_count))
    value_new = columns_of(head + 2 * head_count)
    strength = strength_ref[:pair_rows, :]
    ridge = strength_ref[pair_rows : pair_rows + 1, :]

    def image_of(vectors, columns):
        turned = vectors.T
        pieces = []
        for row in range(pair_rows):
            spread = jnp.broadcast_to(turned[:, row : row + 1], (head_size, head_size))
            pieces.append(jnp.sum(gram_ref[row, :, columns] * spread, axis=0, keepdims=True))
        return jnp.concatenate(pieces, axis=0)

    found = jnp.zeros_like(query)
    residual = query
    direction = query
    res_norm = jnp.sum(residual * residual, axis=-1, keepdims=True)
    for iteration in range(ITERS):
        along = jnp.sum(key_new * direction, axis=-1, keepdims=True)
        image = image_of(direction, slice(0, head_size))
        image = image + strength * key_new * along + ridge * direction
        step = res_norm / jnp.sum(direction * image, axis=-1, keepdims=True)
        found = found + step * direction
        residual = residual - step * image
        next_norm = jnp.sum(residual * residual, axis=-1, keepdims=True)
        direction = residual + (next_norm / res_norm) * direction
        res_norm = next_norm

    total = image_of(found, slice(head_size, 2 * head_size))
    total = total + strength * value_new * jnp.sum(key_new * found, axis=-1, keepdims=True)
    rows_ref[...] = total
    half = pair_rows // 2
    mine = pl.multiple_of(member * half, half)
    theirs = pl.multiple_of((1 - member) * half, half)
    own_ref[...] = rows_ref[pl.ds(mine, half), :].astype(jnp.bfloat16)
    other_ref[...] = rows_ref[pl.ds(theirs, half), :].astype(jnp.bfloat16)


def out_kernel(own_ref, come_ref, out_ref, send_ref):
    first = lax.axis_index("member") == 0
    width = out_ref.shape[1]
    own = own_ref[...].astype(jnp.float32)
    come = come_ref[...].astype(jnp.float32)
    heads = jnp.concatenate([jnp.where(first, own, come), jnp.where(first, come, own)], axis=1)
    heads = heads.astype(jnp.bfloat16)
    part = jnp.dot(heads, out_ref[...], preferred_element_type=jnp.float32)
    send_ref[:, :width] = part.astype(jnp.bfloat16)
    send_ref[:, width:] = heads


def home_rows(value, req_rows):
    first = lax.axis_index("shard") * req_rows
    row = lax.broadcasted_iota(jnp.int32, value.shape, 0)
    picked = [
        jnp.sum(jnp.where(row == first + i, value, 0.0), axis=0, keepdims=True)
        for i in range(req_rows)
    ]
    return jnp.concatenate(picked, axis=0)


def mlp_kernel(
    shards,
    tokens_ref,
    gain_ref,
    gate_ref,
    up_ref,
    down_ref,
    *refs,
):
    part_refs, refs = refs[:shards], refs[shards:]
    mid_ref, retrieved_ref, *send_refs, down_scr, heads_ref = refs
    shard = lax.axis_index("shard")
    group_rows, width = tokens_ref.shape
    req_rows = mid_ref.shape[0]
    span = part_refs[0].shape[1] - width
    attended = part_refs[0][:, :width].astype(jnp.float32)
    for part_ref in part_refs[1:]:
        attended += part_ref[:, :width].astype(jnp.float32)
    mid_rows = (tokens_ref[...] + attended).astype(jnp.bfloat16)
    mlp_in = scaled_norm(mid_rows, gain_ref[...])
    contract = (((1,), (1,)), ((), ()))
    gate_part = lax.dot_general(
        mlp_in, gate_ref[...], contract, preferred_element_type=jnp.float32
    )
    up_part = lax.dot_general(mlp_in, up_ref[...], contract, preferred_element_type=jnp.float32)
    hidden = (silu(gate_part) * up_part).astype(jnp.bfloat16)
    down = jnp.dot(hidden, down_ref[...], preferred_element_type=jnp.float32)
    down_scr[...] = down.reshape(down_scr.shape)
    rows = send_refs[0].shape[0]
    for apart, send_ref in enumerate(send_refs):
        send_ref[...] = down_scr[pl.ds(pl.multiple_of((shard ^ apart) * rows, rows), rows), :]
    mid_ref[...] = home_rows(mid_rows.astype(jnp.float32), mid_ref.shape[0])
    for apart, part_ref in enumerate(part_refs):
        first = pl.multiple_of((shard ^ apart) * span, span)
        heads_ref[:, pl.ds(first, span)] = home_rows(
            part_ref[:, width:].astype(jnp.float32), req_rows
        )
    retrieved_ref[...] = heads_ref[...].astype(jnp.bfloat16)


def finish_kernel(mid_ref, *refs):
    *down_refs, layer_ref = refs
    total = down_refs[0][...]
    for down_ref in down_refs[1:]:
        total = total + down_ref[...]
    layer_ref[...] = (mid_ref[...] + total.reshape(mid_ref.shape)).astype(jnp.bfloat16)


def head_body(
    tokens,
    norm_gain,
    qkv_weight,
    conv_weight,
    conv_state,
    mesa_gates,
    mesa_bias,
    ridge_term,
    key_cache,
    value_cache,
    log_weight,
    page_owner,
    page_fill,
    out_weight,
    mlp_gain,
    gate_weight,
    up_weight,
    down_weight,
):
    shards = lax.axis_size("shard")
    devices = 2 * shards
    req_rows, width = tokens.shape
    slots, page, _ = key_cache.shape
    head_count = ridge_term.shape[0]
    head_size = width // head_count
    group_rows = shards * req_rows
    pair_rows = 2 * group_rows
    all_slots = devices * slots
    columns = qkv_weight.shape[1]
    shape = jax.ShapeDtypeStruct
    bf16, f32 = jnp.bfloat16, jnp.float32

    def exchange(value, axes):
        return lax.all_to_all(value, axes, split_axis=0, concat_axis=0, tiled=True)

    def spot(number):
        return number % 2 * shards + number // 2

    hbm = pl.BlockSpec(memory_space=pltpu.HBM)
    past_rows = jnp.transpose(conv_state, (1, 0, 2))
    gates = mesa_gates.T

    def pinned(*values):
        return [pltpu.with_memory_space_constraint(value, pltpu.HBM) for value in values]

    pieces = pl.pallas_call(
        cut_kernel,
        out_shape=(shape((2 * slots, page, head_size), bf16),) * devices,
        in_specs=[hbm] * 2,
        out_specs=(VMEM,) * devices,
        scratch_shapes=[
            pltpu.VMEM((2, *key_cache.shape), bf16),
            pltpu.SemaphoreType.DMA((2 * slots,)),
        ],
        compiler_params=PARAMS,
        name="cut",
    )(*pinned(key_cache, value_cache))

    def move(step):
        pairs = [
            (spot(source), spot(source ^ SEND[step][source >> 1 & 1])) for source in range(devices)
        ]
        return lax.ppermute(pieces[step], ("member", "shard"), pairs)

    moved = [pieces[0]] + [move(step) for step in range(1, 1 + EARLY)]
    tokens, pieces = lax.optimization_barrier((tokens, pieces))
    pack, misc = pl.pallas_call(
        pack_kernel,
        out_shape=(
            shape((devices * (req_rows * width // page + TILE), page), bf16),
            shape((GATES.stop, width), f32),
        ),
        in_specs=[hbm] * 10,
        out_specs=(VMEM,) * 2,
        scratch_shapes=[
            pltpu.VMEM(tokens.shape, bf16),
            pltpu.VMEM(log_weight.shape, bf16),
            pltpu.SMEM(page_owner.shape, jnp.int32),
            pltpu.SMEM(page_fill.shape, jnp.int32),
            pltpu.VMEM(past_rows.shape, bf16),
            pltpu.VMEM(gates.shape, bf16),
            pltpu.VMEM(conv_weight.shape, f32),
            pltpu.VMEM((1, width), f32),
            pltpu.VMEM((1, 2 * head_count), f32),
            pltpu.SMEM(ridge_term.shape, f32),
            pltpu.SemaphoreType.DMA((10,)),
        ],
        compiler_params=PARAMS,
        name="pack",
    )(
        *pinned(
            tokens,
            log_weight,
            page_owner,
            page_fill,
            past_rows,
            conv_weight,
            norm_gain[None, :],
            gates,
            mesa_bias[None, :],
            ridge_term,
        )
    )
    packs = exchange(pack, PAIR)

    pieces, packs = lax.optimization_barrier((pieces, packs))
    moved += [move(step) for step in range(1 + EARLY, devices)]

    mixed, own_tokens, weight, owner, strength = pl.pallas_call(
        functools.partial(project_kernel, shards, req_rows, slots, head_count),
        out_shape=(
            shape((devices * group_rows, head_size), bf16),
            shape((group_rows, width), f32),
            shape((all_slots, page), f32),
            shape((all_slots, page), jnp.int32),
            shape((pair_rows + TILE, head_size), f32),
        ),
        in_specs=[VMEM] * 2 + [hbm],
        out_specs=(VMEM,) * 5,
        scratch_shapes=[
            pltpu.VMEM((group_rows, columns), f32),
            pltpu.VMEM(qkv_weight.shape, bf16),
            pltpu.SemaphoreType.DMA((4,)),
        ],
        compiler_params=PARAMS,
        name="project",
    )(packs, misc, *pinned(qkv_weight))

    held = HELD
    gram = pl.pallas_call(
        gram_kernel,
        out_shape=shape((pair_rows, head_size, 2 * head_size), f32),
        in_specs=[SMEM] + [VMEM] * (1 + held),
        out_specs=VMEM,
        compiler_params=PARAMS,
        name="gram",
    )(owner, weight, *moved[:held])
    mixed, gram = lax.optimization_barrier((mixed, gram))
    all_mixed = exchange(mixed, PAIR)
    all_mixed, owner, weight, gram = lax.optimization_barrier((all_mixed, owner, weight, gram))

    own_head, other_head, _ = pl.pallas_call(
        functools.partial(solve_kernel, held, head_count, columns // head_size),
        out_shape=(
            shape((group_rows, head_size), bf16),
            shape((group_rows, head_size), bf16),
            pltpu.VMEM(gram.shape, f32),
        ),
        in_specs=[SMEM] + [VMEM] * (4 + devices - held),
        out_specs=(VMEM,) * 3,
        input_output_aliases={4: 2},
        scratch_shapes=[pltpu.VMEM((pair_rows, head_size), f32)],
        compiler_params=PARAMS,
        name="solve",
    )(
        owner,
        weight,
        all_mixed,
        strength,
        pltpu.with_memory_space_constraint(gram, pltpu.VMEM),
        *moved[held:],
    )
    part = pl.pallas_call(
        out_kernel,
        out_shape=shape((group_rows, width + 2 * head_size), bf16),
        in_specs=[VMEM] * 3,
        out_specs=VMEM,
        compiler_params=PARAMS,
        name="out",
    )(own_head, lax.ppermute(other_head, "member", [(0, 1), (1, 0)]), out_weight)

    def over_shards(sent):
        arrived = [sent[0]]
        for apart in range(1, shards):
            pairs = [(source, source ^ apart) for source in range(shards)]
            arrived.append(lax.ppermute(sent[apart], "shard", pairs))
        return arrived

    parts = over_shards([part] * shards)

    mid_home, retrieved, *down = pl.pallas_call(
        functools.partial(mlp_kernel, shards),
        out_shape=(
            shape((req_rows, width), f32),
            shape((req_rows, width), bf16),
        )
        + (shape((req_rows * head_count, head_size), f32),) * shards,
        in_specs=[VMEM] * (5 + shards),
        out_specs=(VMEM,) * (2 + shards),
        scratch_shapes=[
            pltpu.VMEM((group_rows * head_count, head_size), f32),
            pltpu.VMEM((req_rows, width), f32),
        ],
        compiler_params=PARAMS,
        name="mlp",
    )(
        own_tokens,
        mlp_gain[None, :],
        gate_weight.T,
        up_weight.T,
        down_weight,
        *parts,
    )
    layer_out = pl.pallas_call(
        finish_kernel,
        out_shape=shape((req_rows, width), bf16),
        in_specs=[VMEM] * (1 + shards),
        out_specs=VMEM,
        compiler_params=PARAMS,
        name="finish",
    )(mid_home, *over_shards(down))
    return (retrieved, layer_out)


def specs(group):
    rows = P((*group, "shard"))
    return (
        (
            rows,
            P(),
            P(None, "shard"),
            P(None, "shard"),
            P(group, None, "shard"),
            P(),
            P(),
            P(),
            rows,
            rows,
            rows,
            rows,
            rows,
            P("shard", None),
            P(),
            P(None, "shard"),
            P(None, "shard"),
            P("shard", None),
        ),
        (rows, rows),
    )


def solution(mesh):
    groups, shards = mesh.devices.shape

    def run(*args):
        head_count = args[7].shape[0]
        if 2 * shards == head_count == len(SEND):
            axes = ("pair", "member", "shard")
            used = Mesh(mesh.devices.reshape(groups // 2, 2, shards), axes)
            body, group = head_body, ("pair", "member")
        else:
            used, body, group = mesh, spread_body, ("group",)
        in_specs, out_specs = specs(group)
        return jax.shard_map(
            body, mesh=used, in_specs=in_specs, out_specs=out_specs, check_vma=False
        )(*args)

    return run
```

```python
import functools

import jax
import jax.numpy as jnp
from jax import lax
from jax.experimental import pallas as pl
from jax.experimental.pallas import tpu as pltpu
from jax.sharding import Mesh
from jax.sharding import PartitionSpec as P

ITERS = 4


precise = lax.Precision.HIGHEST

VMEM = pl.BlockSpec(memory_space=pltpu.VMEM)
SMEM = pl.BlockSpec(memory_space=pltpu.SMEM)


def partner(value, axis, apart):
    mask = 2**apart
    pairs = [(source, source ^ mask) for source in range(lax.axis_size(axis))]
    return lax.ppermute(value, axis, pairs)


def scaled_norm(row_vals, gain_vec):
    wide_rows = row_vals.astype(jnp.float32)
    factor = lax.rsqrt(jnp.mean(wide_rows * wide_rows, axis=-1, keepdims=True) + 1e-05)
    return (wide_rows * factor * gain_vec).astype(jnp.bfloat16)


def unit_rows(vectors):
    return vectors * lax.rsqrt(jnp.sum(vectors * vectors, axis=-1, keepdims=True) + 1e-06)


def slot_weights(owner_hot, decay_rows, log_weight, page_fill):
    page_len = log_weight.shape[2]
    slot_decay = jnp.dot(owner_hot, decay_rows, precision=precise)
    live_mask = (jnp.arange(page_len)[None, :] < page_fill[:, None]).astype(jnp.float32)
    return slot_decay[:, :, None] * jnp.exp(log_weight.astype(jnp.float32)) * live_mask[:, None, :]


def slot_terms(key_rows, source_rows, owner_hot, slot_weight, directions):
    slot_count, page_len, width_all = key_rows.shape
    head_count = slot_weight.shape[1]
    head_size = width_all // head_count
    member_count = owner_hot.shape[1]
    slot_dir = jnp.dot(owner_hot, directions.reshape(member_count, width_all), precision=precise)
    slot_dir = slot_dir.reshape(slot_count, head_count, head_size)
    key_wide = key_rows.astype(jnp.float32).reshape(slot_count, page_len, head_count, head_size)
    scores = jnp.einsum("sthd,shd->sht", key_wide, slot_dir, precision=precise)
    source_wide = source_rows.astype(jnp.float32).reshape(
        slot_count, page_len, head_count, head_size
    )
    contribution = jnp.einsum("sht,sthd->shd", slot_weight * scores, source_wide, precision=precise)
    summed = jnp.dot(owner_hot.T, contribution.reshape(slot_count, width_all), precision=precise)
    return summed.reshape(member_count, head_count, head_size)


def new_term(vectors, source_rows, strength_rows, key_new):
    return (
        strength_rows[:, :, None] * source_rows * jnp.sum(key_new * vectors, axis=-1, keepdims=True)
    )


def conjugate(query_rows, key_new, value_new, strength_rows, ridge_term, reduce_fn):
    solution = jnp.zeros_like(query_rows)
    residual = query_rows
    direction = query_rows
    res_norm = jnp.sum(residual * residual, axis=-1)
    for iteration in range(ITERS):
        image_vec = (
            reduce_fn(direction, False)
            + new_term(direction, key_new, strength_rows, key_new)
            + ridge_term[None, :, None] * direction
        )
        step_size = res_norm / jnp.sum(direction * image_vec, axis=-1)
        solution = solution + step_size[:, :, None] * direction
        residual = residual - step_size[:, :, None] * image_vec
        next_norm = jnp.sum(residual * residual, axis=-1)
        direction = residual + (next_norm / res_norm)[:, :, None] * direction
        res_norm = next_norm
    return reduce_fn(solution, True) + new_term(solution, value_new, strength_rows, key_new)


def pair_order(mine, theirs, parity):
    first = jnp.where(parity == 0, mine, theirs)
    second = jnp.where(parity == 0, theirs, mine)
    return jnp.concatenate([first, second], axis=0)


def spread_body(
    tokens,
    norm_gain,
    qkv_weight,
    conv_weight,
    conv_state,
    mesa_gates,
    mesa_bias,
    ridge_term,
    key_cache,
    value_cache,
    log_weight,
    page_owner,
    page_fill,
    out_weight,
    mlp_gain,
    gate_weight,
    up_weight,
    down_weight,
):
    req_rows = tokens.shape[0]
    group_rows = req_rows * lax.axis_size("shard")
    head_count = ridge_term.shape[0]
    width_all = key_cache.shape[2]
    head_size = width_all // head_count
    parity = lax.axis_index("group") % 2
    normed = scaled_norm(tokens, norm_gain)
    fresh_proj = jnp.dot(
        lax.all_gather(normed, "shard", axis=0, tiled=True),
        qkv_weight,
        preferred_element_type=jnp.float32,
    )
    past_rows = conv_state.astype(jnp.float32)
    pre_conv = (
        conv_weight[3] * fresh_proj
        + conv_weight[0] * past_rows[:, 0]
        + conv_weight[1] * past_rows[:, 1]
        + conv_weight[2] * past_rows[:, 2]
    )
    mixed_cols = jax.nn.silu(pre_conv).astype(jnp.bfloat16)
    home_rows = lax.all_to_all(mixed_cols, "shard", split_axis=0, concat_axis=1, tiled=True)
    split_rows = home_rows.astype(jnp.float32).reshape(req_rows, 3, head_count, head_size)
    query_home = unit_rows(split_rows[:, 0])
    key_home = unit_rows(split_rows[:, 1])
    value_home = split_rows[:, 2]
    gate_vals = jax.nn.sigmoid(
        jnp.dot(normed, mesa_gates, preferred_element_type=jnp.float32) + mesa_bias
    )
    decay_home = gate_vals[:, :head_count]
    strength_home = gate_vals[:, head_count:]
    owner_hot = (page_owner[:, None] == jnp.arange(2 * group_rows)[None, :]).astype(jnp.float32)
    stored = {}

    def cache_pass(directions, decay_grp, with_values):
        far_dirs, far_decay = partner((directions, decay_grp), "group", 0)
        pair_dirs = pair_order(directions, far_dirs, parity)
        pair_decay = pair_order(decay_grp, far_decay, parity)
        if "weight" not in stored:
            stored["weight"] = slot_weights(owner_hot, pair_decay, log_weight, page_fill)
        source_rows = value_cache if with_values else key_cache
        summed = slot_terms(key_cache, source_rows, owner_hot, stored["weight"], pair_dirs)
        mine = jnp.where(parity == 0, summed[:group_rows], summed[group_rows:])
        theirs = jnp.where(parity == 0, summed[group_rows:], summed[:group_rows])
        returned = partner(theirs, "group", 0)
        return mine + returned

    def reduce_home(vectors, with_values):
        directions, decay_grp = (
            lax.all_gather(vectors, "shard", axis=0, tiled=True),
            lax.all_gather(decay_home, "shard", axis=0, tiled=True),
        )
        return lax.psum_scatter(
            cache_pass(directions, decay_grp, with_values), "shard", scatter_dimension=0, tiled=True
        )

    found = conjugate(query_home, key_home, value_home, strength_home, ridge_term, reduce_home)
    retrieved = found.reshape(req_rows, width_all).astype(jnp.bfloat16)
    columns = lax.all_to_all(retrieved, "shard", split_axis=1, concat_axis=0, tiled=True)
    attended = lax.psum_scatter(
        jnp.dot(columns, out_weight, preferred_element_type=jnp.float32),
        "shard",
        scatter_dimension=0,
        tiled=True,
    )
    mid_rows = (tokens.astype(jnp.float32) + attended).astype(jnp.bfloat16)
    mlp_in = scaled_norm(mid_rows, mlp_gain)
    piece_rows = lax.all_gather(mlp_in, "shard", axis=0, tiled=True)
    gate_part = jnp.dot(piece_rows, gate_weight, preferred_element_type=jnp.float32)
    up_part = jnp.dot(piece_rows, up_weight, preferred_element_type=jnp.float32)
    hidden_rows = (jax.nn.silu(gate_part) * up_part).astype(jnp.bfloat16)
    down_part = lax.psum_scatter(
        jnp.dot(hidden_rows, down_weight, preferred_element_type=jnp.float32),
        "shard",
        scatter_dimension=0,
        tiled=True,
    )
    layer_out = (mid_rows.astype(jnp.float32) + down_part).astype(jnp.bfloat16)
    return (retrieved, layer_out)


TILE = 8
MASKED = -1e38
PAIR = ("shard", "member")
PARAMS = pltpu.CompilerParams(vmem_limit_bytes=16 * 1024 * 1024)
PAST, TAP, GAIN, BIAS, RIDGE = slice(0, 8), slice(8, 9), slice(9, 10), slice(10, 11), slice(11, 12)
GATES = slice(16, 32)

SEND = ((0, 0), (5, 5), (2, 2), (7, 7), (1, 4), (4, 1), (3, 6), (6, 3))
FROM = tuple((b, a) if a & 2 else (a, b) for a, b in SEND)
EARLY = 4
HELD = 4


def split_pair(value):
    high = value.astype(jnp.bfloat16)
    low = (value - high.astype(jnp.float32)).astype(jnp.bfloat16)
    return high, low


def hot(rows, columns, target_fn):
    row = lax.broadcasted_iota(jnp.int32, (rows, columns), 0)
    column = lax.broadcasted_iota(jnp.int32, (rows, columns), 1)
    return jnp.where(column == target_fn(row), 1.0, 0.0).astype(jnp.bfloat16)


def here():
    return lax.axis_index("shard") * 2 + lax.axis_index("member")


def at_step(table, step, me):
    return me ^ jnp.where((me & 2) == 0, table[step][0], table[step][1])


def silu(value):
    return value / (1.0 + jnp.exp(-value))


def cut_kernel(
    key_hbm,
    value_hbm,
    tokens_hbm,
    logs_hbm,
    owner_hbm,
    fill_hbm,
    past_hbm,
    tap_hbm,
    gain_hbm,
    gates_hbm,
    bias_hbm,
    ridge_hbm,
    send_ref,
    misc_ref,
    *refs,
):
    *piece_refs, tokens_ref, logs_ref, owner_ref, fill_ref, state_ref, gates_ref = refs[:-7]
    tap_ref, gain_ref, bias_ref, ridge_ref, stage_ref, small_sems, sems = refs[-7:]
    slots = key_hbm.shape[0]
    head_size = piece_refs[0].shape[2]
    me = here()
    loads = [
        pltpu.make_async_copy(source.at[slot], stage_ref.at[part, slot], sems.at[part * slots + slot])
        for part, source in enumerate((key_hbm, value_hbm))
        for slot in range(slots)
    ]
    for load in loads:
        load.start()
    req_rows, width = tokens_ref.shape
    slots, head_count, page = logs_ref.shape
    copies = [
        pltpu.make_async_copy(source, target, small_sems.at[place])
        for place, (source, target) in enumerate(
            [
                (owner_hbm, owner_ref),
                (fill_hbm, fill_ref),
                (tokens_hbm, tokens_ref),
                (logs_hbm, logs_ref),
                (past_hbm, state_ref),
                (tap_hbm, tap_ref),
                (gain_hbm, gain_ref),
                (gates_hbm, gates_ref),
                (bias_hbm, bias_ref),
                (ridge_hbm, ridge_ref),
            ]
        )
    ]
    for copy in copies:
        copy.start()
    starts = [
        pl.multiple_of(at_step(SEND, step, me) * head_size, head_size)
        for step in range(len(piece_refs))
    ]
    for part in range(2):
        for slot in range(slots):
            place = part * slots + slot
            loads[place].wait()
            for start, piece_ref in zip(starts, piece_refs):
                piece_ref[place] = stage_ref[part, slot, :, pl.ds(start, head_size)]

    for copy in copies:
        copy.wait()

    tokens = tokens_ref[...].astype(jnp.float32)
    rows = [
        tokens[row : row + 1, first : first + page]
        for row in range(req_rows)
        for first in range(0, width, page)
    ]
    tile = jnp.concatenate(rows, axis=0).astype(jnp.bfloat16)
    packed = tile.shape[0] + TILE
    spot = lax.broadcasted_iota(jnp.int32, (head_count, page), 1)
    logs = []
    lane = lax.broadcasted_iota(jnp.int32, (1, page), 1)
    owners = jnp.zeros((1, page), jnp.float32)
    for slot in range(slots):
        rows = logs_ref[slot].astype(jnp.float32)
        logs.append(jnp.where(spot < fill_ref[slot], rows, MASKED))
        owners = jnp.where(lane == slot, owner_ref[slot].astype(jnp.float32), owners)
    rest = jnp.zeros((TILE - slots - 1, page), jnp.float32)
    for head in range(head_count):
        rows = [log[head : head + 1, :] for log in logs]
        side = jnp.concatenate([*rows, owners, rest], axis=0).astype(jnp.bfloat16)
        send_ref[head * packed : head * packed + tile.shape[0], :] = tile
        send_ref[head * packed + tile.shape[0] : (head + 1) * packed, :] = side

    past = tap_ref[0:1, :] * state_ref[0].astype(jnp.float32)
    past = past + tap_ref[1:2, :] * state_ref[1].astype(jnp.float32)
    past = past + tap_ref[2:3, :] * state_ref[2].astype(jnp.float32)
    columns = past.shape[1]
    misc_ref[PAST, :columns] = past
    misc_ref[TAP, :columns] = tap_ref[3:4, :]
    misc_ref[GAIN, :] = gain_ref[...]
    misc_ref[BIAS, : 2 * head_count] = bias_ref[...]
    ridges = jnp.zeros((1, page), jnp.float32)
    for head in range(head_count):
        ridges = jnp.where(lane == head, ridge_ref[head], ridges)
    misc_ref[RIDGE, :page] = ridges
    misc_ref[GATES, :] = gates_ref[...].astype(jnp.float32)


def project_kernel(
    shards,
    req_rows,
    slots,
    head_count,
    pack_ref,
    misc_ref,
    qkv_hbm,
    send_ref,
    tokens_ref,
    weight_ref,
    owner_ref,
    strength_ref,
    mixed_ref,
    qkv_ref,
    sems,
):
    chunk = qkv_ref.shape[0] // sems.shape[0]
    loads = [
        pltpu.make_async_copy(
            qkv_hbm.at[pl.ds(part * chunk, chunk)],
            qkv_ref.at[pl.ds(part * chunk, chunk)],
            sems.at[part],
        )
        for part in range(sems.shape[0])
    ]
    for load in loads:
        load.start()
    shard = lax.axis_index("shard")
    member = lax.axis_index("member")
    head = here()
    group_rows = shards * req_rows
    pair_rows = 2 * group_rows
    width = misc_ref.shape[1]
    columns = qkv_ref.shape[1]
    page = weight_ref.shape[1]
    head_size = send_ref.shape[1]
    blocks = columns // head_size
    parts = width // page
    packed = pack_ref.shape[0]
    tall = packed // (2 * shards)

    def rows_of(first, count):
        def home_of(row):
            request = row % count + first
            x = request // group_rows
            s = (request % group_rows) // req_rows
            return (s * 2 + x) * tall + request % req_rows * parts + row // count

        picked = jnp.dot(
            hot(count * parts, packed, home_of), pack_ref[...], preferred_element_type=jnp.float32
        )
        return jnp.concatenate(
            [picked[part * count : (part + 1) * count] for part in range(parts)], axis=1
        )

    own_tokens = rows_of(member * group_rows, group_rows)
    tokens_ref[...] = own_tokens
    own = scaled_norm(own_tokens, misc_ref[GAIN, :])
    normed = scaled_norm(rows_of(0, pair_rows), misc_ref[GAIN, :])
    raw = lax.dot_general(
        normed,
        misc_ref[GATES, :].astype(jnp.bfloat16),
        (((1,), (1,)), ((), ())),
        preferred_element_type=jnp.float32,
    )
    gate_vals = 1.0 / (1.0 + jnp.exp(-(raw + misc_ref[BIAS, : 2 * head_count])))
    column = lax.broadcasted_iota(jnp.int32, gate_vals.shape, 1)
    decay = jnp.sum(jnp.where(column == head, gate_vals, 0.0), axis=1, keepdims=True)
    strength = jnp.sum(
        jnp.where(column == head + head_count, gate_vals, 0.0), axis=1, keepdims=True
    )
    strength_ref[:pair_rows, :] = jnp.broadcast_to(strength, (pair_rows, head_size))
    ridges = misc_ref[RIDGE, :page]
    spot = lax.broadcasted_iota(jnp.int32, ridges.shape, 1)
    ridge = jnp.sum(jnp.where(spot == head, ridges, 0.0), axis=1, keepdims=True)
    strength_ref[pair_rows:, :] = jnp.broadcast_to(ridge, (TILE, head_size))

    all_slots = 2 * shards * slots
    side = tall - TILE
    pick_slot = hot(all_slots, packed, lambda row: (row // slots) * tall + side + row % slots)
    logs = jnp.dot(pick_slot, pack_ref[...], preferred_element_type=jnp.float32)
    pick_owner = hot(all_slots, packed, lambda row: (row // slots) * tall + side + slots)
    owners = jnp.dot(pick_owner, pack_ref[...], preferred_element_type=jnp.float32)
    at_slot = hot(all_slots, page, lambda row: row % slots).astype(jnp.float32)
    owner = jnp.sum(at_slot * owners, axis=1, keepdims=True).astype(jnp.int32)
    owner_ref[...] = jnp.broadcast_to(owner, owner_ref.shape)
    request = lax.broadcasted_iota(jnp.int32, (all_slots, pair_rows), 1)
    owner_hot = jnp.where(request == owner, 1.0, 0.0)
    wide_decay = jnp.broadcast_to(decay, (pair_rows, page))
    slot_decay = jnp.dot(
        owner_hot, wide_decay, precision=precise, preferred_element_type=jnp.float32
    )
    weight_ref[...] = slot_decay * jnp.exp(logs)

    for load in loads:
        load.wait()
    fresh = jnp.dot(own, qkv_ref[...], preferred_element_type=jnp.float32)
    before = misc_ref[TAP, :columns] * fresh + misc_ref[PAST, :columns]
    mixed_ref[...] = silu(before)
    for target in range(head_count):
        place = jnp.int32(0)
        for part in range(3):
            local = target + part * head_count - shard * blocks
            place = jnp.where((local >= 0) & (local < blocks), local, place)
        start = pl.multiple_of(place * head_size, head_size)
        send_ref[target * group_rows : (target + 1) * group_rows, :] = mixed_ref[
            :, pl.ds(start, head_size)
        ].astype(jnp.bfloat16)


def add_pieces(first, owner_ref, weight_ref, piece_refs, gram_ref):
    me = here()
    slots = piece_refs[0].shape[0] // 2
    for step, piece_ref in enumerate(piece_refs, first):
        for spot in range(slots):
            slot = at_step(FROM, step, me) * slots + spot
            keys = piece_ref[spot]
            both = jnp.concatenate([keys, piece_ref[slots + spot]], axis=1)
            turned = keys.T.astype(jnp.float32) * weight_ref[pl.ds(slot, 1), :]
            piece = jnp.dot(
                jnp.concatenate(split_pair(turned), axis=1),
                jnp.concatenate([both, both], axis=0),
                preferred_element_type=jnp.float32,
            )
            owner = owner_ref[slot, 0]
            gram_ref[owner] = gram_ref[owner] + piece


def gram_kernel(owner_ref, weight_ref, *refs):
    *piece_refs, gram_ref = refs
    gram_ref[...] = jnp.zeros_like(gram_ref)
    add_pieces(0, owner_ref, weight_ref, piece_refs, gram_ref)


def solve_kernel(
    first, head_count, blocks, owner_ref, weight_ref, mixed_ref, strength_ref, before_ref, *refs
):
    *piece_refs, own_ref, other_ref, gram_ref, rows_ref = refs
    del before_ref
    head = here()
    member = lax.axis_index("member")
    pair_rows, head_size, _ = gram_ref.shape
    add_pieces(first, owner_ref, weight_ref, piece_refs, gram_ref)

    def columns_of(block):
        first = pl.multiple_of(block // blocks * pair_rows, pair_rows)
        return mixed_ref[pl.ds(first, pair_rows), :].astype(jnp.float32)

    query = unit_rows(columns_of(head))
    key_new = unit_rows(columns_of(head + head_count))
    value_new = columns_of(head + 2 * head_count)
    strength = strength_ref[:pair_rows, :]
    ridge = strength_ref[pair_rows : pair_rows + 1, :]

    def image_of(vectors, columns):
        turned = vectors.T
        pieces = []
        for row in range(pair_rows):
            spread = jnp.broadcast_to(turned[:, row : row + 1], (head_size, head_size))
            pieces.append(jnp.sum(gram_ref[row, :, columns] * spread, axis=0, keepdims=True))
        return jnp.concatenate(pieces, axis=0)

    found = jnp.zeros_like(query)
    residual = query
    direction = query
    res_norm = jnp.sum(residual * residual, axis=-1, keepdims=True)
    for iteration in range(ITERS):
        along = jnp.sum(key_new * direction, axis=-1, keepdims=True)
        image = image_of(direction, slice(0, head_size))
        image = image + strength * key_new * along + ridge * direction
        step = res_norm / jnp.sum(direction * image, axis=-1, keepdims=True)
        found = found + step * direction
        residual = residual - step * image
        next_norm = jnp.sum(residual * residual, axis=-1, keepdims=True)
        direction = residual + (next_norm / res_norm) * direction
        res_norm = next_norm

    total = image_of(found, slice(head_size, 2 * head_size))
    total = total + strength * value_new * jnp.sum(key_new * found, axis=-1, keepdims=True)
    rows_ref[...] = total
    half = pair_rows // 2
    mine = pl.multiple_of(member * half, half)
    theirs = pl.multiple_of((1 - member) * half, half)
    own_ref[...] = rows_ref[pl.ds(mine, half), :].astype(jnp.bfloat16)
    other_ref[...] = rows_ref[pl.ds(theirs, half), :].astype(jnp.bfloat16)


def out_kernel(own_ref, come_ref, out_ref, send_ref):
    first = lax.axis_index("member") == 0
    width = out_ref.shape[1]
    own = own_ref[...].astype(jnp.float32)
    come = come_ref[...].astype(jnp.float32)
    heads = jnp.concatenate([jnp.where(first, own, come), jnp.where(first, come, own)], axis=1)
    heads = heads.astype(jnp.bfloat16)
    part = jnp.dot(heads, out_ref[...], preferred_element_type=jnp.float32)
    send_ref[:, :width] = part.astype(jnp.bfloat16)
    send_ref[:, width:] = heads


def home_rows(value, req_rows):
    first = lax.axis_index("shard") * req_rows
    row = lax.broadcasted_iota(jnp.int32, value.shape, 0)
    picked = [
        jnp.sum(jnp.where(row == first + i, value, 0.0), axis=0, keepdims=True)
        for i in range(req_rows)
    ]
    return jnp.concatenate(picked, axis=0)


def mlp_kernel(
    shards,
    tokens_ref,
    gain_ref,
    gate_ref,
    up_ref,
    down_ref,
    *refs,
):
    part_refs, refs = refs[:shards], refs[shards:]
    mid_ref, retrieved_ref, *send_refs, down_scr, heads_ref = refs
    shard = lax.axis_index("shard")
    group_rows, width = tokens_ref.shape
    req_rows = mid_ref.shape[0]
    span = part_refs[0].shape[1] - width
    attended = part_refs[0][:, :width].astype(jnp.float32)
    for part_ref in part_refs[1:]:
        attended += part_ref[:, :width].astype(jnp.float32)
    mid_rows = (tokens_ref[...] + attended).astype(jnp.bfloat16)
    mlp_in = scaled_norm(mid_rows, gain_ref[...])
    contract = (((1,), (1,)), ((), ()))
    gate_part = lax.dot_general(
        mlp_in, gate_ref[...], contract, preferred_element_type=jnp.float32
    )
    up_part = lax.dot_general(mlp_in, up_ref[...], contract, preferred_element_type=jnp.float32)
    hidden = (silu(gate_part) * up_part).astype(jnp.bfloat16)
    down = jnp.dot(hidden, down_ref[...], preferred_element_type=jnp.float32)
    down_scr[...] = down.reshape(down_scr.shape)
    rows = send_refs[0].shape[0]
    for apart, send_ref in enumerate(send_refs):
        send_ref[...] = down_scr[pl.ds(pl.multiple_of((shard ^ apart) * rows, rows), rows), :]
    mid_ref[...] = home_rows(mid_rows.astype(jnp.float32), mid_ref.shape[0])
    for apart, part_ref in enumerate(part_refs):
        first = pl.multiple_of((shard ^ apart) * span, span)
        heads_ref[:, pl.ds(first, span)] = home_rows(
            part_ref[:, width:].astype(jnp.float32), req_rows
        )
    retrieved_ref[...] = heads_ref[...].astype(jnp.bfloat16)


def finish_kernel(mid_ref, *refs):
    *down_refs, layer_ref = refs
    total = down_refs[0][...]
    for down_ref in down_refs[1:]:
        total = total + down_ref[...]
    layer_ref[...] = (mid_ref[...] + total.reshape(mid_ref.shape)).astype(jnp.bfloat16)


def head_body(
    tokens,
    norm_gain,
    qkv_weight,
    conv_weight,
    conv_state,
    mesa_gates,
    mesa_bias,
    ridge_term,
    key_cache,
    value_cache,
    log_weight,
    page_owner,
    page_fill,
    out_weight,
    mlp_gain,
    gate_weight,
    up_weight,
    down_weight,
):
    shards = lax.axis_size("shard")
    devices = 2 * shards
    req_rows, width = tokens.shape
    slots, page, _ = key_cache.shape
    head_count = ridge_term.shape[0]
    head_size = width // head_count
    group_rows = shards * req_rows
    pair_rows = 2 * group_rows
    all_slots = devices * slots
    columns = qkv_weight.shape[1]
    shape = jax.ShapeDtypeStruct
    bf16, f32 = jnp.bfloat16, jnp.float32

    def exchange(value, axes):
        return lax.all_to_all(value, axes, split_axis=0, concat_axis=0, tiled=True)

    def spot(number):
        return number % 2 * shards + number // 2

    hbm = pl.BlockSpec(memory_space=pltpu.HBM)
    past_rows = jnp.transpose(conv_state, (1, 0, 2))
    gates = mesa_gates.T

    def pinned(*values):
        return [pltpu.with_memory_space_constraint(value, pltpu.HBM) for value in values]

    pack, misc, *pieces = pl.pallas_call(
        cut_kernel,
        out_shape=(
            shape((devices * (req_rows * width // page + TILE), page), bf16),
            shape((GATES.stop, width), f32),
        )
        + (shape((2 * slots, page, head_size), bf16),) * devices,
        in_specs=[hbm] * 12,
        out_specs=(VMEM,) * (2 + devices),
        scratch_shapes=[
            pltpu.VMEM(tokens.shape, bf16),
            pltpu.VMEM(log_weight.shape, bf16),
            pltpu.SMEM(page_owner.shape, jnp.int32),
            pltpu.SMEM(page_fill.shape, jnp.int32),
            pltpu.VMEM(past_rows.shape, bf16),
            pltpu.VMEM(gates.shape, bf16),
            pltpu.VMEM(conv_weight.shape, f32),
            pltpu.VMEM((1, width), f32),
            pltpu.VMEM((1, 2 * head_count), f32),
            pltpu.SMEM(ridge_term.shape, f32),
            pltpu.VMEM((2, *key_cache.shape), bf16),
            pltpu.SemaphoreType.DMA((10,)),
            pltpu.SemaphoreType.DMA((2 * slots,)),
        ],
        compiler_params=PARAMS,
        name="cut",
    )(
        *pinned(
            key_cache,
            value_cache,
            tokens,
            log_weight,
            page_owner,
            page_fill,
            past_rows,
            conv_weight,
            norm_gain[None, :],
            gates,
            mesa_bias[None, :],
            ridge_term,
        )
    )

    def move(step):
        pairs = [
            (spot(source), spot(source ^ SEND[step][source >> 1 & 1])) for source in range(devices)
        ]
        return lax.ppermute(pieces[step], ("member", "shard"), pairs)

    moved = [pieces[0]] + [move(step) for step in range(1, 1 + EARLY)]
    packs = exchange(pack, PAIR)

    pieces, packs = lax.optimization_barrier((pieces, packs))
    moved += [move(step) for step in range(1 + EARLY, devices)]

    mixed, own_tokens, weight, owner, strength = pl.pallas_call(
        functools.partial(project_kernel, shards, req_rows, slots, head_count),
        out_shape=(
            shape((devices * group_rows, head_size), bf16),
            shape((group_rows, width), f32),
            shape((all_slots, page), f32),
            shape((all_slots, page), jnp.int32),
            shape((pair_rows + TILE, head_size), f32),
        ),
        in_specs=[VMEM] * 2 + [hbm],
        out_specs=(VMEM,) * 5,
        scratch_shapes=[
            pltpu.VMEM((group_rows, columns), f32),
            pltpu.VMEM(qkv_weight.shape, bf16),
            pltpu.SemaphoreType.DMA((4,)),
        ],
        compiler_params=PARAMS,
        name="project",
    )(packs, misc, *pinned(qkv_weight))

    held = HELD
    gram = pl.pallas_call(
        gram_kernel,
        out_shape=shape((pair_rows, head_size, 2 * head_size), f32),
        in_specs=[SMEM] + [VMEM] * (1 + held),
        out_specs=VMEM,
        compiler_params=PARAMS,
        name="gram",
    )(owner, weight, *moved[:held])
    mixed, gram = lax.optimization_barrier((mixed, gram))
    all_mixed = exchange(mixed, PAIR)
    all_mixed, owner, weight, gram = lax.optimization_barrier((all_mixed, owner, weight, gram))

    own_head, other_head, _ = pl.pallas_call(
        functools.partial(solve_kernel, held, head_count, columns // head_size),
        out_shape=(
            shape((group_rows, head_size), bf16),
            shape((group_rows, head_size), bf16),
            pltpu.VMEM(gram.shape, f32),
        ),
        in_specs=[SMEM] + [VMEM] * (4 + devices - held),
        out_specs=(VMEM,) * 3,
        input_output_aliases={4: 2},
        scratch_shapes=[pltpu.VMEM((pair_rows, head_size), f32)],
        compiler_params=PARAMS,
        name="solve",
    )(
        owner,
        weight,
        all_mixed,
        strength,
        pltpu.with_memory_space_constraint(gram, pltpu.VMEM),
        *moved[held:],
    )
    part = pl.pallas_call(
        out_kernel,
        out_shape=shape((group_rows, width + 2 * head_size), bf16),
        in_specs=[VMEM] * 3,
        out_specs=VMEM,
        compiler_params=PARAMS,
        name="out",
    )(own_head, lax.ppermute(other_head, "member", [(0, 1), (1, 0)]), out_weight)

    def over_shards(sent):
        arrived = [sent[0]]
        for apart in range(1, shards):
            pairs = [(source, source ^ apart) for source in range(shards)]
            arrived.append(lax.ppermute(sent[apart], "shard", pairs))
        return arrived

    parts = over_shards([part] * shards)

    mid_home, retrieved, *down = pl.pallas_call(
        functools.partial(mlp_kernel, shards),
        out_shape=(
            shape((req_rows, width), f32),
            shape((req_rows, width), bf16),
        )
        + (shape((req_rows * head_count, head_size), f32),) * shards,
        in_specs=[VMEM] * (5 + shards),
        out_specs=(VMEM,) * (2 + shards),
        scratch_shapes=[
            pltpu.VMEM((group_rows * head_count, head_size), f32),
            pltpu.VMEM((req_rows, width), f32),
        ],
        compiler_params=PARAMS,
        name="mlp",
    )(
        own_tokens,
        mlp_gain[None, :],
        gate_weight.T,
        up_weight.T,
        down_weight,
        *parts,
    )
    layer_out = pl.pallas_call(
        finish_kernel,
        out_shape=shape((req_rows, width), bf16),
        in_specs=[VMEM] * (1 + shards),
        out_specs=VMEM,
        compiler_params=PARAMS,
        name="finish",
    )(mid_home, *over_shards(down))
    return (retrieved, layer_out)


def specs(group):
    rows = P((*group, "shard"))
    return (
        (
            rows,
            P(),
            P(None, "shard"),
            P(None, "shard"),
            P(group, None, "shard"),
            P(),
            P(),
            P(),
            rows,
            rows,
            rows,
            rows,
            rows,
            P("shard", None),
            P(),
            P(None, "shard"),
            P(None, "shard"),
            P("shard", None),
        ),
        (rows, rows),
    )


def solution(mesh):
    groups, shards = mesh.devices.shape

    def run(*args):
        head_count = args[7].shape[0]
        if 2 * shards == head_count == len(SEND):
            axes = ("pair", "member", "shard")
            used = Mesh(mesh.devices.reshape(groups // 2, 2, shards), axes)
            body, group = head_body, ("pair", "member")
        else:
            used, body, group = mesh, spread_body, ("group",)
        in_specs, out_specs = specs(group)
        return jax.shard_map(
            body, mesh=used, in_specs=in_specs, out_specs=out_specs, check_vma=False
        )(*args)

    return run
```

```python
import functools

import jax
import jax.numpy as jnp
from jax import lax
from jax.experimental import pallas as pl
from jax.experimental.pallas import tpu as pltpu
from jax.sharding import Mesh
from jax.sharding import PartitionSpec as P

ITERS = 4


precise = lax.Precision.HIGHEST

VMEM = pl.BlockSpec(memory_space=pltpu.VMEM)
SMEM = pl.BlockSpec(memory_space=pltpu.SMEM)


def partner(value, axis, apart):
    mask = 2**apart
    pairs = [(source, source ^ mask) for source in range(lax.axis_size(axis))]
    return lax.ppermute(value, axis, pairs)


def scaled_norm(row_vals, gain_vec):
    wide_rows = row_vals.astype(jnp.float32)
    factor = lax.rsqrt(jnp.mean(wide_rows * wide_rows, axis=-1, keepdims=True) + 1e-05)
    return (wide_rows * factor * gain_vec).astype(jnp.bfloat16)


def unit_rows(vectors):
    return vectors * lax.rsqrt(jnp.sum(vectors * vectors, axis=-1, keepdims=True) + 1e-06)


def slot_weights(owner_hot, decay_rows, log_weight, page_fill):
    page_len = log_weight.shape[2]
    slot_decay = jnp.dot(owner_hot, decay_rows, precision=precise)
    live_mask = (jnp.arange(page_len)[None, :] < page_fill[:, None]).astype(jnp.float32)
    return slot_decay[:, :, None] * jnp.exp(log_weight.astype(jnp.float32)) * live_mask[:, None, :]


def slot_terms(key_rows, source_rows, owner_hot, slot_weight, directions):
    slot_count, page_len, width_all = key_rows.shape
    head_count = slot_weight.shape[1]
    head_size = width_all // head_count
    member_count = owner_hot.shape[1]
    slot_dir = jnp.dot(owner_hot, directions.reshape(member_count, width_all), precision=precise)
    slot_dir = slot_dir.reshape(slot_count, head_count, head_size)
    key_wide = key_rows.astype(jnp.float32).reshape(slot_count, page_len, head_count, head_size)
    scores = jnp.einsum("sthd,shd->sht", key_wide, slot_dir, precision=precise)
    source_wide = source_rows.astype(jnp.float32).reshape(
        slot_count, page_len, head_count, head_size
    )
    contribution = jnp.einsum("sht,sthd->shd", slot_weight * scores, source_wide, precision=precise)
    summed = jnp.dot(owner_hot.T, contribution.reshape(slot_count, width_all), precision=precise)
    return summed.reshape(member_count, head_count, head_size)


def new_term(vectors, source_rows, strength_rows, key_new):
    return (
        strength_rows[:, :, None] * source_rows * jnp.sum(key_new * vectors, axis=-1, keepdims=True)
    )


def conjugate(query_rows, key_new, value_new, strength_rows, ridge_term, reduce_fn):
    solution = jnp.zeros_like(query_rows)
    residual = query_rows
    direction = query_rows
    res_norm = jnp.sum(residual * residual, axis=-1)
    for iteration in range(ITERS):
        image_vec = (
            reduce_fn(direction, False)
            + new_term(direction, key_new, strength_rows, key_new)
            + ridge_term[None, :, None] * direction
        )
        step_size = res_norm / jnp.sum(direction * image_vec, axis=-1)
        solution = solution + step_size[:, :, None] * direction
        residual = residual - step_size[:, :, None] * image_vec
        next_norm = jnp.sum(residual * residual, axis=-1)
        direction = residual + (next_norm / res_norm)[:, :, None] * direction
        res_norm = next_norm
    return reduce_fn(solution, True) + new_term(solution, value_new, strength_rows, key_new)


def pair_order(mine, theirs, parity):
    first = jnp.where(parity == 0, mine, theirs)
    second = jnp.where(parity == 0, theirs, mine)
    return jnp.concatenate([first, second], axis=0)


def spread_body(
    tokens,
    norm_gain,
    qkv_weight,
    conv_weight,
    conv_state,
    mesa_gates,
    mesa_bias,
    ridge_term,
    key_cache,
    value_cache,
    log_weight,
    page_owner,
    page_fill,
    out_weight,
    mlp_gain,
    gate_weight,
    up_weight,
    down_weight,
):
    req_rows = tokens.shape[0]
    group_rows = req_rows * lax.axis_size("shard")
    head_count = ridge_term.shape[0]
    width_all = key_cache.shape[2]
    head_size = width_all // head_count
    parity = lax.axis_index("group") % 2
    normed = scaled_norm(tokens, norm_gain)
    fresh_proj = jnp.dot(
        lax.all_gather(normed, "shard", axis=0, tiled=True),
        qkv_weight,
        preferred_element_type=jnp.float32,
    )
    past_rows = conv_state.astype(jnp.float32)
    pre_conv = (
        conv_weight[3] * fresh_proj
        + conv_weight[0] * past_rows[:, 0]
        + conv_weight[1] * past_rows[:, 1]
        + conv_weight[2] * past_rows[:, 2]
    )
    mixed_cols = jax.nn.silu(pre_conv).astype(jnp.bfloat16)
    home_rows = lax.all_to_all(mixed_cols, "shard", split_axis=0, concat_axis=1, tiled=True)
    split_rows = home_rows.astype(jnp.float32).reshape(req_rows, 3, head_count, head_size)
    query_home = unit_rows(split_rows[:, 0])
    key_home = unit_rows(split_rows[:, 1])
    value_home = split_rows[:, 2]
    gate_vals = jax.nn.sigmoid(
        jnp.dot(normed, mesa_gates, preferred_element_type=jnp.float32) + mesa_bias
    )
    decay_home = gate_vals[:, :head_count]
    strength_home = gate_vals[:, head_count:]
    owner_hot = (page_owner[:, None] == jnp.arange(2 * group_rows)[None, :]).astype(jnp.float32)
    stored = {}

    def cache_pass(directions, decay_grp, with_values):
        far_dirs, far_decay = partner((directions, decay_grp), "group", 0)
        pair_dirs = pair_order(directions, far_dirs, parity)
        pair_decay = pair_order(decay_grp, far_decay, parity)
        if "weight" not in stored:
            stored["weight"] = slot_weights(owner_hot, pair_decay, log_weight, page_fill)
        source_rows = value_cache if with_values else key_cache
        summed = slot_terms(key_cache, source_rows, owner_hot, stored["weight"], pair_dirs)
        mine = jnp.where(parity == 0, summed[:group_rows], summed[group_rows:])
        theirs = jnp.where(parity == 0, summed[group_rows:], summed[:group_rows])
        returned = partner(theirs, "group", 0)
        return mine + returned

    def reduce_home(vectors, with_values):
        directions, decay_grp = (
            lax.all_gather(vectors, "shard", axis=0, tiled=True),
            lax.all_gather(decay_home, "shard", axis=0, tiled=True),
        )
        return lax.psum_scatter(
            cache_pass(directions, decay_grp, with_values), "shard", scatter_dimension=0, tiled=True
        )

    found = conjugate(query_home, key_home, value_home, strength_home, ridge_term, reduce_home)
    retrieved = found.reshape(req_rows, width_all).astype(jnp.bfloat16)
    columns = lax.all_to_all(retrieved, "shard", split_axis=1, concat_axis=0, tiled=True)
    attended = lax.psum_scatter(
        jnp.dot(columns, out_weight, preferred_element_type=jnp.float32),
        "shard",
        scatter_dimension=0,
        tiled=True,
    )
    mid_rows = (tokens.astype(jnp.float32) + attended).astype(jnp.bfloat16)
    mlp_in = scaled_norm(mid_rows, mlp_gain)
    piece_rows = lax.all_gather(mlp_in, "shard", axis=0, tiled=True)
    gate_part = jnp.dot(piece_rows, gate_weight, preferred_element_type=jnp.float32)
    up_part = jnp.dot(piece_rows, up_weight, preferred_element_type=jnp.float32)
    hidden_rows = (jax.nn.silu(gate_part) * up_part).astype(jnp.bfloat16)
    down_part = lax.psum_scatter(
        jnp.dot(hidden_rows, down_weight, preferred_element_type=jnp.float32),
        "shard",
        scatter_dimension=0,
        tiled=True,
    )
    layer_out = (mid_rows.astype(jnp.float32) + down_part).astype(jnp.bfloat16)
    return (retrieved, layer_out)


TILE = 8
MASKED = -1e38
PAIR = ("shard", "member")
PARAMS = pltpu.CompilerParams(vmem_limit_bytes=16 * 1024 * 1024)
PAST, TAP, GAIN, BIAS, RIDGE = slice(0, 8), slice(8, 9), slice(9, 10), slice(10, 11), slice(11, 12)
GATES = slice(16, 32)

SEND = ((0, 0), (5, 5), (2, 2), (7, 7), (1, 4), (4, 1), (3, 6), (6, 3))
FROM = tuple((b, a) if a & 2 else (a, b) for a, b in SEND)
EARLY = 4
HELD = 4


def split_pair(value):
    high = value.astype(jnp.bfloat16)
    low = (value - high.astype(jnp.float32)).astype(jnp.bfloat16)
    return high, low


def hot(rows, columns, target_fn):
    row = lax.broadcasted_iota(jnp.int32, (rows, columns), 0)
    column = lax.broadcasted_iota(jnp.int32, (rows, columns), 1)
    return jnp.where(column == target_fn(row), 1.0, 0.0).astype(jnp.bfloat16)


def here():
    return lax.axis_index("shard") * 2 + lax.axis_index("member")


def at_step(table, step, me):
    return me ^ jnp.where((me & 2) == 0, table[step][0], table[step][1])


def silu(value):
    return value / (1.0 + jnp.exp(-value))


def cut_kernel(
    key_hbm,
    value_hbm,
    tokens_hbm,
    logs_hbm,
    owner_hbm,
    fill_hbm,
    past_hbm,
    tap_hbm,
    gain_hbm,
    gates_hbm,
    bias_hbm,
    ridge_hbm,
    send_ref,
    misc_ref,
    *refs,
):
    *piece_refs, tokens_ref, logs_ref, owner_ref, fill_ref, state_ref, gates_ref = refs[:-7]
    tap_ref, gain_ref, bias_ref, ridge_ref, stage_ref, small_sems, sems = refs[-7:]
    slots = key_hbm.shape[0]
    head_size = piece_refs[0].shape[2]
    me = here()
    loads = [
        pltpu.make_async_copy(source.at[slot], stage_ref.at[part, slot], sems.at[part * slots + slot])
        for part, source in enumerate((key_hbm, value_hbm))
        for slot in range(slots)
    ]
    req_rows, width = tokens_ref.shape
    slots, head_count, page = logs_ref.shape
    copies = [
        pltpu.make_async_copy(source, target, small_sems.at[place])
        for place, (source, target) in enumerate(
            [
                (owner_hbm, owner_ref),
                (fill_hbm, fill_ref),
                (tokens_hbm, tokens_ref),
                (logs_hbm, logs_ref),
                (past_hbm, state_ref),
                (tap_hbm, tap_ref),
                (gain_hbm, gain_ref),
                (gates_hbm, gates_ref),
                (bias_hbm, bias_ref),
                (ridge_hbm, ridge_ref),
            ]
        )
    ]
    for copy in copies:
        copy.start()
    for load in loads:
        load.start()
    for copy in copies:
        copy.wait()

    tokens = tokens_ref[...].astype(jnp.float32)
    rows = [
        tokens[row : row + 1, first : first + page]
        for row in range(req_rows)
        for first in range(0, width, page)
    ]
    tile = jnp.concatenate(rows, axis=0).astype(jnp.bfloat16)
    packed = tile.shape[0] + TILE
    spot = lax.broadcasted_iota(jnp.int32, (head_count, page), 1)
    logs = []
    lane = lax.broadcasted_iota(jnp.int32, (1, page), 1)
    owners = jnp.zeros((1, page), jnp.float32)
    for slot in range(slots):
        rows = logs_ref[slot].astype(jnp.float32)
        logs.append(jnp.where(spot < fill_ref[slot], rows, MASKED))
        owners = jnp.where(lane == slot, owner_ref[slot].astype(jnp.float32), owners)
    rest = jnp.zeros((TILE - slots - 1, page), jnp.float32)
    for head in range(head_count):
        rows = [log[head : head + 1, :] for log in logs]
        side = jnp.concatenate([*rows, owners, rest], axis=0).astype(jnp.bfloat16)
        send_ref[head * packed : head * packed + tile.shape[0], :] = tile
        send_ref[head * packed + tile.shape[0] : (head + 1) * packed, :] = side

    past = tap_ref[0:1, :] * state_ref[0].astype(jnp.float32)
    past = past + tap_ref[1:2, :] * state_ref[1].astype(jnp.float32)
    past = past + tap_ref[2:3, :] * state_ref[2].astype(jnp.float32)
    columns = past.shape[1]
    misc_ref[PAST, :columns] = past
    misc_ref[TAP, :columns] = tap_ref[3:4, :]
    misc_ref[GAIN, :] = gain_ref[...]
    misc_ref[BIAS, : 2 * head_count] = bias_ref[...]
    ridges = jnp.zeros((1, page), jnp.float32)
    for head in range(head_count):
        ridges = jnp.where(lane == head, ridge_ref[head], ridges)
    misc_ref[RIDGE, :page] = ridges
    misc_ref[GATES, :] = gates_ref[...].astype(jnp.float32)

    starts = [
        pl.multiple_of(at_step(SEND, step, me) * head_size, head_size)
        for step in range(len(piece_refs))
    ]
    for part in range(2):
        for slot in range(slots):
            place = part * slots + slot
            loads[place].wait()
            for start, piece_ref in zip(starts, piece_refs):
                piece_ref[place] = stage_ref[part, slot, :, pl.ds(start, head_size)]


def project_kernel(
    shards,
    req_rows,
    slots,
    head_count,
    pack_ref,
    misc_ref,
    qkv_hbm,
    send_ref,
    tokens_ref,
    weight_ref,
    owner_ref,
    strength_ref,
    mixed_ref,
    qkv_ref,
    sems,
):
    chunk = qkv_ref.shape[0] // sems.shape[0]
    loads = [
        pltpu.make_async_copy(
            qkv_hbm.at[pl.ds(part * chunk, chunk)],
            qkv_ref.at[pl.ds(part * chunk, chunk)],
            sems.at[part],
        )
        for part in range(sems.shape[0])
    ]
    for load in loads:
        load.start()
    shard = lax.axis_index("shard")
    member = lax.axis_index("member")
    head = here()
    group_rows = shards * req_rows
    pair_rows = 2 * group_rows
    width = misc_ref.shape[1]
    columns = qkv_ref.shape[1]
    page = weight_ref.shape[1]
    head_size = send_ref.shape[1]
    blocks = columns // head_size
    parts = width // page
    packed = pack_ref.shape[0]
    tall = packed // (2 * shards)

    def rows_of(first, count):
        def home_of(row):
            request = row % count + first
            x = request // group_rows
            s = (request % group_rows) // req_rows
            return (s * 2 + x) * tall + request % req_rows * parts + row // count

        picked = jnp.dot(
            hot(count * parts, packed, home_of), pack_ref[...], preferred_element_type=jnp.float32
        )
        return jnp.concatenate(
            [picked[part * count : (part + 1) * count] for part in range(parts)], axis=1
        )

    own_tokens = rows_of(member * group_rows, group_rows)
    tokens_ref[...] = own_tokens
    own = scaled_norm(own_tokens, misc_ref[GAIN, :])
    normed = scaled_norm(rows_of(0, pair_rows), misc_ref[GAIN, :])
    raw = lax.dot_general(
        normed,
        misc_ref[GATES, :].astype(jnp.bfloat16),
        (((1,), (1,)), ((), ())),
        preferred_element_type=jnp.float32,
    )
    gate_vals = 1.0 / (1.0 + jnp.exp(-(raw + misc_ref[BIAS, : 2 * head_count])))
    column = lax.broadcasted_iota(jnp.int32, gate_vals.shape, 1)
    decay = jnp.sum(jnp.where(column == head, gate_vals, 0.0), axis=1, keepdims=True)
    strength = jnp.sum(
        jnp.where(column == head + head_count, gate_vals, 0.0), axis=1, keepdims=True
    )
    strength_ref[:pair_rows, :] = jnp.broadcast_to(strength, (pair_rows, head_size))
    ridges = misc_ref[RIDGE, :page]
    spot = lax.broadcasted_iota(jnp.int32, ridges.shape, 1)
    ridge = jnp.sum(jnp.where(spot == head, ridges, 0.0), axis=1, keepdims=True)
    strength_ref[pair_rows:, :] = jnp.broadcast_to(ridge, (TILE, head_size))

    all_slots = 2 * shards * slots
    side = tall - TILE
    pick_slot = hot(all_slots, packed, lambda row: (row // slots) * tall + side + row % slots)
    logs = jnp.dot(pick_slot, pack_ref[...], preferred_element_type=jnp.float32)
    pick_owner = hot(all_slots, packed, lambda row: (row // slots) * tall + side + slots)
    owners = jnp.dot(pick_owner, pack_ref[...], preferred_element_type=jnp.float32)
    at_slot = hot(all_slots, page, lambda row: row % slots).astype(jnp.float32)
    owner = jnp.sum(at_slot * owners, axis=1, keepdims=True).astype(jnp.int32)
    owner_ref[...] = jnp.broadcast_to(owner, owner_ref.shape)
    request = lax.broadcasted_iota(jnp.int32, (all_slots, pair_rows), 1)
    owner_hot = jnp.where(request == owner, 1.0, 0.0)
    wide_decay = jnp.broadcast_to(decay, (pair_rows, page))
    slot_decay = jnp.dot(
        owner_hot, wide_decay, precision=precise, preferred_element_type=jnp.float32
    )
    weight_ref[...] = slot_decay * jnp.exp(logs)

    for load in loads:
        load.wait()
    fresh = jnp.dot(own, qkv_ref[...], preferred_element_type=jnp.float32)
    before = misc_ref[TAP, :columns] * fresh + misc_ref[PAST, :columns]
    mixed_ref[...] = silu(before)
    for target in range(head_count):
        place = jnp.int32(0)
        for part in range(3):
            local = target + part * head_count - shard * blocks
            place = jnp.where((local >= 0) & (local < blocks), local, place)
        start = pl.multiple_of(place * head_size, head_size)
        send_ref[target * group_rows : (target + 1) * group_rows, :] = mixed_ref[
            :, pl.ds(start, head_size)
        ].astype(jnp.bfloat16)


def add_pieces(first, owner_ref, weight_ref, piece_refs, gram_ref):
    me = here()
    slots = piece_refs[0].shape[0] // 2
    for step, piece_ref in enumerate(piece_refs, first):
        for spot in range(slots):
            slot = at_step(FROM, step, me) * slots + spot
            keys = piece_ref[spot]
            both = jnp.concatenate([keys, piece_ref[slots + spot]], axis=1)
            turned = keys.T.astype(jnp.float32) * weight_ref[pl.ds(slot, 1), :]
            piece = jnp.dot(
                jnp.concatenate(split_pair(turned), axis=1),
                jnp.concatenate([both, both], axis=0),
                preferred_element_type=jnp.float32,
            )
            owner = owner_ref[slot, 0]
            gram_ref[owner] = gram_ref[owner] + piece


def gram_kernel(owner_ref, weight_ref, *refs):
    *piece_refs, gram_ref = refs
    gram_ref[...] = jnp.zeros_like(gram_ref)
    add_pieces(0, owner_ref, weight_ref, piece_refs, gram_ref)


def solve_kernel(
    first, head_count, blocks, owner_ref, weight_ref, mixed_ref, strength_ref, before_ref, *refs
):
    *piece_refs, own_ref, other_ref, gram_ref, rows_ref = refs
    del before_ref
    head = here()
    member = lax.axis_index("member")
    pair_rows, head_size, _ = gram_ref.shape
    add_pieces(first, owner_ref, weight_ref, piece_refs, gram_ref)

    def columns_of(block):
        first = pl.multiple_of(block // blocks * pair_rows, pair_rows)
        return mixed_ref[pl.ds(first, pair_rows), :].astype(jnp.float32)

    query = unit_rows(columns_of(head))
    key_new = unit_rows(columns_of(head + head_count))
    value_new = columns_of(head + 2 * head_count)
    strength = strength_ref[:pair_rows, :]
    ridge = strength_ref[pair_rows : pair_rows + 1, :]

    def image_of(vectors, columns):
        turned = vectors.T
        pieces = []
        for row in range(pair_rows):
            spread = jnp.broadcast_to(turned[:, row : row + 1], (head_size, head_size))
            pieces.append(jnp.sum(gram_ref[row, :, columns] * spread, axis=0, keepdims=True))
        return jnp.concatenate(pieces, axis=0)

    found = jnp.zeros_like(query)
    residual = query
    direction = query
    res_norm = jnp.sum(residual * residual, axis=-1, keepdims=True)
    for iteration in range(ITERS):
        along = jnp.sum(key_new * direction, axis=-1, keepdims=True)
        image = image_of(direction, slice(0, head_size))
        image = image + strength * key_new * along + ridge * direction
        step = res_norm / jnp.sum(direction * image, axis=-1, keepdims=True)
        found = found + step * direction
        residual = residual - step * image
        next_norm = jnp.sum(residual * residual, axis=-1, keepdims=True)
        direction = residual + (next_norm / res_norm) * direction
        res_norm = next_norm

    total = image_of(found, slice(head_size, 2 * head_size))
    total = total + strength * value_new * jnp.sum(key_new * found, axis=-1, keepdims=True)
    rows_ref[...] = total
    half = pair_rows // 2
    mine = pl.multiple_of(member * half, half)
    theirs = pl.multiple_of((1 - member) * half, half)
    own_ref[...] = rows_ref[pl.ds(mine, half), :].astype(jnp.bfloat16)
    other_ref[...] = rows_ref[pl.ds(theirs, half), :].astype(jnp.bfloat16)


def out_kernel(own_ref, come_ref, out_ref, send_ref):
    first = lax.axis_index("member") == 0
    width = out_ref.shape[1]
    own = own_ref[...].astype(jnp.float32)
    come = come_ref[...].astype(jnp.float32)
    heads = jnp.concatenate([jnp.where(first, own, come), jnp.where(first, come, own)], axis=1)
    heads = heads.astype(jnp.bfloat16)
    part = jnp.dot(heads, out_ref[...], preferred_element_type=jnp.float32)
    send_ref[:, :width] = part.astype(jnp.bfloat16)
    send_ref[:, width:] = heads


def home_rows(value, req_rows):
    first = lax.axis_index("shard") * req_rows
    row = lax.broadcasted_iota(jnp.int32, value.shape, 0)
    picked = [
        jnp.sum(jnp.where(row == first + i, value, 0.0), axis=0, keepdims=True)
        for i in range(req_rows)
    ]
    return jnp.concatenate(picked, axis=0)


def mlp_kernel(
    shards,
    tokens_ref,
    gain_ref,
    gate_ref,
    up_ref,
    down_ref,
    *refs,
):
    part_refs, refs = refs[:shards], refs[shards:]
    mid_ref, retrieved_ref, *send_refs, down_scr, heads_ref = refs
    shard = lax.axis_index("shard")
    group_rows, width = tokens_ref.shape
    req_rows = mid_ref.shape[0]
    span = part_refs[0].shape[1] - width
    attended = part_refs[0][:, :width].astype(jnp.float32)
    for part_ref in part_refs[1:]:
        attended += part_ref[:, :width].astype(jnp.float32)
    mid_rows = (tokens_ref[...] + attended).astype(jnp.bfloat16)
    mlp_in = scaled_norm(mid_rows, gain_ref[...])
    contract = (((1,), (1,)), ((), ()))
    gate_part = lax.dot_general(
        mlp_in, gate_ref[...], contract, preferred_element_type=jnp.float32
    )
    up_part = lax.dot_general(mlp_in, up_ref[...], contract, preferred_element_type=jnp.float32)
    hidden = (silu(gate_part) * up_part).astype(jnp.bfloat16)
    down = jnp.dot(hidden, down_ref[...], preferred_element_type=jnp.float32)
    down_scr[...] = down.reshape(down_scr.shape)
    rows = send_refs[0].shape[0]
    for apart, send_ref in enumerate(send_refs):
        send_ref[...] = down_scr[pl.ds(pl.multiple_of((shard ^ apart) * rows, rows), rows), :]
    mid_ref[...] = home_rows(mid_rows.astype(jnp.float32), mid_ref.shape[0])
    for apart, part_ref in enumerate(part_refs):
        first = pl.multiple_of((shard ^ apart) * span, span)
        heads_ref[:, pl.ds(first, span)] = home_rows(
            part_ref[:, width:].astype(jnp.float32), req_rows
        )
    retrieved_ref[...] = heads_ref[...].astype(jnp.bfloat16)


def finish_kernel(mid_ref, *refs):
    *down_refs, layer_ref = refs
    total = down_refs[0][...]
    for down_ref in down_refs[1:]:
        total = total + down_ref[...]
    layer_ref[...] = (mid_ref[...] + total.reshape(mid_ref.shape)).astype(jnp.bfloat16)


def head_body(
    tokens,
    norm_gain,
    qkv_weight,
    conv_weight,
    conv_state,
    mesa_gates,
    mesa_bias,
    ridge_term,
    key_cache,
    value_cache,
    log_weight,
    page_owner,
    page_fill,
    out_weight,
    mlp_gain,
    gate_weight,
    up_weight,
    down_weight,
):
    shards = lax.axis_size("shard")
    devices = 2 * shards
    req_rows, width = tokens.shape
    slots, page, _ = key_cache.shape
    head_count = ridge_term.shape[0]
    head_size = width // head_count
    group_rows = shards * req_rows
    pair_rows = 2 * group_rows
    all_slots = devices * slots
    columns = qkv_weight.shape[1]
    shape = jax.ShapeDtypeStruct
    bf16, f32 = jnp.bfloat16, jnp.float32

    def exchange(value, axes):
        return lax.all_to_all(value, axes, split_axis=0, concat_axis=0, tiled=True)

    def spot(number):
        return number % 2 * shards + number // 2

    hbm = pl.BlockSpec(memory_space=pltpu.HBM)
    past_rows = jnp.transpose(conv_state, (1, 0, 2))
    gates = mesa_gates.T

    def pinned(*values):
        return [pltpu.with_memory_space_constraint(value, pltpu.HBM) for value in values]

    pack, misc, *pieces = pl.pallas_call(
        cut_kernel,
        out_shape=(
            shape((devices * (req_rows * width // page + TILE), page), bf16),
            shape((GATES.stop, width), f32),
        )
        + (shape((2 * slots, page, head_size), bf16),) * devices,
        in_specs=[hbm] * 12,
        out_specs=(VMEM,) * (2 + devices),
        scratch_shapes=[
            pltpu.VMEM(tokens.shape, bf16),
            pltpu.VMEM(log_weight.shape, bf16),
            pltpu.SMEM(page_owner.shape, jnp.int32),
            pltpu.SMEM(page_fill.shape, jnp.int32),
            pltpu.VMEM(past_rows.shape, bf16),
            pltpu.VMEM(gates.shape, bf16),
            pltpu.VMEM(conv_weight.shape, f32),
            pltpu.VMEM((1, width), f32),
            pltpu.VMEM((1, 2 * head_count), f32),
            pltpu.SMEM(ridge_term.shape, f32),
            pltpu.VMEM((2, *key_cache.shape), bf16),
            pltpu.SemaphoreType.DMA((10,)),
            pltpu.SemaphoreType.DMA((2 * slots,)),
        ],
        compiler_params=PARAMS,
        name="cut",
    )(
        *pinned(
            key_cache,
            value_cache,
            tokens,
            log_weight,
            page_owner,
            page_fill,
            past_rows,
            conv_weight,
            norm_gain[None, :],
            gates,
            mesa_bias[None, :],
            ridge_term,
        )
    )

    def move(step):
        pairs = [
            (spot(source), spot(source ^ SEND[step][source >> 1 & 1])) for source in range(devices)
        ]
        return lax.ppermute(pieces[step], ("member", "shard"), pairs)

    moved = [pieces[0]] + [move(step) for step in range(1, 1 + EARLY)]
    packs = exchange(pack, PAIR)

    pieces, packs = lax.optimization_barrier((pieces, packs))
    moved += [move(step) for step in range(1 + EARLY, devices)]

    mixed, own_tokens, weight, owner, strength = pl.pallas_call(
        functools.partial(project_kernel, shards, req_rows, slots, head_count),
        out_shape=(
            shape((devices * group_rows, head_size), bf16),
            shape((group_rows, width), f32),
            shape((all_slots, page), f32),
            shape((all_slots, page), jnp.int32),
            shape((pair_rows + TILE, head_size), f32),
        ),
        in_specs=[VMEM] * 2 + [hbm],
        out_specs=(VMEM,) * 5,
        scratch_shapes=[
            pltpu.VMEM((group_rows, columns), f32),
            pltpu.VMEM(qkv_weight.shape, bf16),
            pltpu.SemaphoreType.DMA((4,)),
        ],
        compiler_params=PARAMS,
        name="project",
    )(packs, misc, *pinned(qkv_weight))

    held = HELD
    gram = pl.pallas_call(
        gram_kernel,
        out_shape=shape((pair_rows, head_size, 2 * head_size), f32),
        in_specs=[SMEM] + [VMEM] * (1 + held),
        out_specs=VMEM,
        compiler_params=PARAMS,
        name="gram",
    )(owner, weight, *moved[:held])
    mixed, gram = lax.optimization_barrier((mixed, gram))
    all_mixed = exchange(mixed, PAIR)
    all_mixed, owner, weight, gram = lax.optimization_barrier((all_mixed, owner, weight, gram))

    own_head, other_head, _ = pl.pallas_call(
        functools.partial(solve_kernel, held, head_count, columns // head_size),
        out_shape=(
            shape((group_rows, head_size), bf16),
            shape((group_rows, head_size), bf16),
            pltpu.VMEM(gram.shape, f32),
        ),
        in_specs=[SMEM] + [VMEM] * (4 + devices - held),
        out_specs=(VMEM,) * 3,
        input_output_aliases={4: 2},
        scratch_shapes=[pltpu.VMEM((pair_rows, head_size), f32)],
        compiler_params=PARAMS,
        name="solve",
    )(
        owner,
        weight,
        all_mixed,
        strength,
        pltpu.with_memory_space_constraint(gram, pltpu.VMEM),
        *moved[held:],
    )
    part = pl.pallas_call(
        out_kernel,
        out_shape=shape((group_rows, width + 2 * head_size), bf16),
        in_specs=[VMEM] * 3,
        out_specs=VMEM,
        compiler_params=PARAMS,
        name="out",
    )(own_head, lax.ppermute(other_head, "member", [(0, 1), (1, 0)]), out_weight)

    def over_shards(sent):
        arrived = [sent[0]]
        for apart in range(1, shards):
            pairs = [(source, source ^ apart) for source in range(shards)]
            arrived.append(lax.ppermute(sent[apart], "shard", pairs))
        return arrived

    parts = over_shards([part] * shards)

    mid_home, retrieved, *down = pl.pallas_call(
        functools.partial(mlp_kernel, shards),
        out_shape=(
            shape((req_rows, width), f32),
            shape((req_rows, width), bf16),
        )
        + (shape((req_rows * head_count, head_size), f32),) * shards,
        in_specs=[VMEM] * (5 + shards),
        out_specs=(VMEM,) * (2 + shards),
        scratch_shapes=[
            pltpu.VMEM((group_rows * head_count, head_size), f32),
            pltpu.VMEM((req_rows, width), f32),
        ],
        compiler_params=PARAMS,
        name="mlp",
    )(
        own_tokens,
        mlp_gain[None, :],
        gate_weight.T,
        up_weight.T,
        down_weight,
        *parts,
    )
    layer_out = pl.pallas_call(
        finish_kernel,
        out_shape=shape((req_rows, width), bf16),
        in_specs=[VMEM] * (1 + shards),
        out_specs=VMEM,
        compiler_params=PARAMS,
        name="finish",
    )(mid_home, *over_shards(down))
    return (retrieved, layer_out)


def specs(group):
    rows = P((*group, "shard"))
    return (
        (
            rows,
            P(),
            P(None, "shard"),
            P(None, "shard"),
            P(group, None, "shard"),
            P(),
            P(),
            P(),
            rows,
            rows,
            rows,
            rows,
            rows,
            P("shard", None),
            P(),
            P(None, "shard"),
            P(None, "shard"),
            P("shard", None),
        ),
        (rows, rows),
    )


def solution(mesh):
    groups, shards = mesh.devices.shape

    def run(*args):
        head_count = args[7].shape[0]
        if 2 * shards == head_count == len(SEND):
            axes = ("pair", "member", "shard")
            used = Mesh(mesh.devices.reshape(groups // 2, 2, shards), axes)
            body, group = head_body, ("pair", "member")
        else:
            used, body, group = mesh, spread_body, ("group",)
        in_specs, out_specs = specs(group)
        return jax.shard_map(
            body, mesh=used, in_specs=in_specs, out_specs=out_specs, check_vma=False
        )(*args)

    return run
```
